32 devices in a mesh: dp: 8 (over y, x, core), tensor: 4 (over z).
Axes of the slice: x: 2, y: 2, z: 4, core: 2. Of those that a mesh axis runs over, the one named last changes fastest.
Arguments:
- layer_input: bfloat16 [8192, 2048], P(('dp', 'tensor')), may hold values from -6 to 6
- ln_gain: float32 [2048], replicated, may hold values from 0.5 to 1.5
- ln_bias: float32 [2048], replicated, may hold values from -1 to 1
- w_query: bfloat16 [2048, 2048], P('dp', 'tensor'), may hold values from -0.125 to 0.125
- b_query: float32 [2048], P('tensor'), may hold values from -1.5 to 1.5
- w_key: bfloat16 [2048, 2048], P('dp', 'tensor'), may hold values from -0.125 to 0.125
- b_key: float32 [2048], P('tensor'), may hold values from -1.5 to 1.5
- w_value: bfloat16 [2048, 2048], P('dp', 'tensor'), may hold values from -0.125 to 0.125
- b_value: float32 [2048], P('tensor'), may hold values from -1.5 to 1.5
- w_out: bfloat16 [2048, 2048], P('tensor', 'dp'), may hold values from -2 to 2
- b_out: float32 [2048], replicated, may hold values from -1 to 1
- w_up: bfloat16 [2048, 8192], P('dp', 'tensor'), may hold values from -0.125 to 0.125
- b_up: float32 [8192], P('tensor'), may hold values from -2.5 to 2.5
- w_down: bfloat16 [8192, 2048], P('tensor', 'dp'), may hold values from -0.125 to 0.125
- b_down: float32 [2048], replicated, may hold values from -1 to 1
- prefix: int32 [8], P('dp'), may hold values from 102 to 512
- cotangent: bfloat16 [8192, 2048], P(('dp', 'tensor')), may hold values from -6 to 6
Outputs:
- layer_out: bfloat16 [8192, 2048], P(('dp', 'tensor'))
- d_input: float32 [8192, 2048], P(('dp', 'tensor'))
- d_ln_gain: float32 [2048], replicated
- d_ln_bias: float32 [2048], replicated
- d_w_query: float32 [2048, 2048], P('dp', 'tensor')
- d_b_query: float32 [2048], P('tensor')
- d_w_key: float32 [2048, 2048], P('dp', 'tensor')
- d_b_key: float32 [2048], P('tensor')
- d_w_value: float32 [2048, 2048], P('dp', 'tensor')
- d_b_value: float32 [2048], P('tensor')
- d_w_out: float32 [2048, 2048], P('tensor', 'dp')
- d_b_out: float32 [2048], replicated
- d_w_up: float32 [2048, 8192], P('dp', 'tensor')
- d_b_up: float32 [8192], P('tensor')
- d_w_down: float32 [8192, 2048], P('tensor', 'dp')
- d_b_down: float32 [2048], replicated
The draws below stay inside these ranges and needn't reach their ends.
All inputs are finite; a program needn't handle non-finite values.
Results may differ from the reference program's by a relative error of at most 0.012.
The reference program's roundings to bfloat16 on the way count: a program that leaves them out, or rounds other values in their place, can miss the bound.
Values may be sent and summed in bfloat16 or wider, within the bound.
A program may use at most 256 MiB of HBM per device.

```python
import math
import jax
import jax.numpy as jnp
from jax import lax

D = 2048
HEADS = 32
HEAD_DIM = 64
ROT_DIM = 32
FF = 8192
SEQ = 1024
SEQS = 8
TOKENS = 8192


def with_ends(drawn, rng, smallest, largest):
    longest = drawn.shape.index(max(drawn.shape))
    spots = []
    for shift in (0, 1):
        where = [jax.random.randint(jax.random.fold_in(rng, axis), (), 0, length) for axis, length in enumerate(drawn.shape)]
        where[longest] = (where[longest] + shift) % drawn.shape[longest]
        spots.append(tuple(where))
    return drawn.at[spots[0]].set(smallest).at[spots[1]].set(largest)


def shard_levels(stream_key, extent, split, smallest, largest):
    def one(position, blocks):
        heights = jax.random.uniform(jax.random.fold_in(jax.random.fold_in(stream_key, 6), position), (blocks,), jnp.float32, smallest / len(split), largest / len(split))
        return jnp.repeat(jnp.exp(heights), extent[position] // blocks).reshape((-1,) + (1,) * (len(extent) - position - 1))

    factor_of = one(*split[0])
    for cut in split[1:]:
        factor_of = factor_of * one(*cut)
    return factor_of


def gaussian(stream_key, shape, scale, reach, cuts=(), kind=jnp.bfloat16):
    values = jax.random.normal(stream_key, shape, jnp.float32) * scale
    if len(cuts) > 0:
        values = shard_levels(stream_key, shape, cuts, -0.22, 0.18) * values
    return jnp.clip(values, min=-reach, max=reach).astype(kind)


def setup_inputs(seed: int = 0) -> dict:
    key_list = jax.random.split(jax.random.key(seed), 18)
    return {
        "layer_input": gaussian(key_list[0], (TOKENS, D), 1.0, 6.0, ((0, 32),)),
        "ln_gain": jnp.clip(1.0 + 0.1 * jax.random.normal(key_list[1], (D,), jnp.float32), 0.5, 1.5),
        "ln_bias": gaussian(key_list[2], (D,), 0.2, 1.0, (), jnp.float32),
        "w_query": gaussian(key_list[3], (D, D), D ** -0.5, 0.125, ((0, 8), (1, 4))),
        "b_query": gaussian(key_list[4], (D,), 0.3, 1.5, ((0, 4),), jnp.float32),
        "w_key": gaussian(key_list[5], (D, D), D ** -0.5, 0.125, ((0, 8), (1, 4))),
        "b_key": gaussian(key_list[6], (D,), 0.3, 1.5, ((0, 4),), jnp.float32),
        "w_value": gaussian(key_list[7], (D, D), D ** -0.5, 0.125, ((0, 8), (1, 4))),
        "b_value": gaussian(key_list[8], (D,), 0.3, 1.5, ((0, 4),), jnp.float32),
        "w_out": gaussian(key_list[9], (D, D), (max(D // 256, 2)) ** -0.5, 2.0, ((0, 4), (1, 8))),
        "b_out": gaussian(key_list[10], (D,), 0.2, 1.0, (), jnp.float32),
        "w_up": gaussian(key_list[11], (D, FF), D ** -0.5, 0.125, ((0, 8), (1, 4))),
        "b_up": gaussian(key_list[12], (FF,), 0.5, 2.5, ((0, 4),), jnp.float32),
        "w_down": gaussian(key_list[13], (FF, D), (FF // 4) ** -0.5, 0.125, ((0, 4), (1, 8))),
        "b_down": gaussian(key_list[14], (D,), 0.2, 1.0, (), jnp.float32),
        "prefix": with_ends(jax.random.randint(key_list[15], (SEQS,), SEQ // 10, SEQ // 2 + 1), jax.random.fold_in(key_list[15], 1), SEQ // 10, (SEQ // 2 + 1) - 1).astype(jnp.int32),
        "cotangent": gaussian(key_list[16], (TOKENS, D), 1.0, 6.0, ((0, 32),)),
    }


@jax.custom_vjp
def low(v):
    return lax.optimization_barrier(v.astype(jnp.bfloat16)).astype(jnp.float32)

@jax.custom_vjp
def low_back(v):
    return v

def low_keep(v):
    return (low(v), None)

def low_pass(kept, grad):
    return (grad,)

def back_keep(v):
    return (v, None)

def back_low(kept, grad):
    return (low(grad),)
low.defvjp(low_keep, low_pass)
low_back.defvjp(back_keep, back_low)
epsilon = 1e-05
rope_base = 10000.0
masked_score = -1e+30
highest = lax.Precision.HIGHEST

def rotate(tensor, positions, direction):
    half_dim = ROT_DIM // 2
    freqs = rope_base ** (-(jnp.arange(half_dim).astype(jnp.float32) * 2.0 / ROT_DIM))
    angles = positions.astype(jnp.float32)[:, None] * freqs[None, :]
    cosine = jnp.cos(angles)[:, None, :]
    sine = direction * jnp.sin(angles)[:, None, :]
    first = tensor[..., :half_dim]
    second = tensor[..., half_dim:ROT_DIM]
    return jnp.concatenate([first * cosine - second * sine, second * cosine + first * sine, tensor[..., ROT_DIM:]], axis=-1)

def attend(query, key, value, prefix_len):
    block_rows = min(512, SEQ)
    positions = jnp.arange(SEQ).astype(jnp.int32)
    score_scale = 1.0 / math.sqrt(HEAD_DIM)

    def one_block(offset):
        query_rows = lax.dynamic_slice_in_dim(query, offset, block_rows, 0)
        scores = low_back(jnp.einsum('qhd,khd->hqk', query_rows, key, precision=highest) * score_scale)
        query_pos = offset + jnp.arange(block_rows).astype(jnp.int32)
        seen = (positions[None, :] <= query_pos[:, None]) | (positions[None, :] < prefix_len)
        scores = jnp.where(seen[None], scores, masked_score)
        probs = low(jax.nn.softmax(scores, axis=-1))
        return jnp.einsum('hqk,khd->qhd', probs, value, precision=highest)
    offsets = (jnp.arange(SEQ // block_rows) * block_rows).astype(jnp.int32)
    blocks = lax.map(jax.checkpoint(one_block), offsets)
    return blocks.reshape(SEQ, HEADS * HEAD_DIM)

def layer(input_seq, params, prefix_len):
    ln_gain, ln_bias, w_query, b_query, w_key, b_key, w_value, b_value, w_out, b_out, w_up, b_up, w_down, b_down = params
    row_mean = lax.optimization_barrier(jnp.mean(input_seq, axis=-1, keepdims=True))
    centred = input_seq - row_mean
    variance = lax.optimization_barrier(jnp.mean(centred * centred, axis=-1, keepdims=True))
    normed = low(centred * lax.rsqrt(variance + epsilon) * ln_gain + ln_bias)
    positions = jnp.arange(SEQ).astype(jnp.int32)
    query_pre = low_back(jnp.dot(normed, w_query, precision=highest) + b_query)
    key_pre = low_back(jnp.dot(normed, w_key, precision=highest) + b_key)
    value_pre = low_back(jnp.dot(normed, w_value, precision=highest) + b_value)
    query = low(rotate(query_pre.reshape(SEQ, HEADS, HEAD_DIM), positions, 1.0))
    key = low(rotate(key_pre.reshape(SEQ, HEADS, HEAD_DIM), positions, 1.0))
    value = low(value_pre.reshape(SEQ, HEADS, HEAD_DIM))
    attn = low(low_back(attend(query, key, value, prefix_len)))
    up_pre = low_back(jnp.dot(normed, w_up, precision=highest) + b_up)
    hidden = low(jax.nn.gelu(up_pre, approximate=True))
    branch = low_back(jnp.dot(attn, w_out, precision=highest) + jnp.dot(hidden, w_down, precision=highest))
    return input_seq + branch + b_out + b_down

def reference(layer_input, ln_gain, ln_bias, w_query, b_query, w_key, b_key, w_value, b_value, w_out, b_out, w_up, b_up, w_down, b_down, prefix, cotangent):
    floats = tuple((item.astype(jnp.float32) for item in (layer_input, ln_gain, ln_bias, w_query, b_query, w_key, b_key, w_value, b_value, w_out, b_out, w_up, b_up, w_down, b_down)))

    def forward(*inputs):
        input_all = inputs[0].reshape(SEQS, SEQ, D)
        params = inputs[1:]

        def step(carry, item):
            return (carry, layer(item[0], params, item[1]))
        unused, outputs = lax.scan(jax.checkpoint(step), jnp.zeros((), jnp.float32), (input_all, prefix))
        return outputs.reshape(TOKENS, D)
    result, pull = jax.vjp(forward, *floats)
    grads = pull(cotangent.astype(jnp.float32))
    return (result.astype(jnp.bfloat16), grads[0], grads[1], grads[2], grads[3], grads[4], grads[5], grads[6], grads[7], grads[8], grads[9], grads[10], grads[11], grads[12], grads[13], grads[14])
```

```python
import functools
import math

import jax
import jax.numpy as jnp
from jax import lax
from jax.experimental import pallas as pl
from jax.experimental.pallas import tpu as pltpu
from jax.sharding import PartitionSpec as P

HEAD_DIM = 64
ROT_DIM = 32
MESH = pl.DeviceIdType.MESH
BF = jnp.bfloat16
F32 = jnp.float32

epsilon = 1e-05
rope_base = 10000.0
masked_score = -1e30
root = math.sqrt(2.0 / math.pi)


def nn(a, b):
    return jnp.dot(a, b, preferred_element_type=F32)


def nt(a, b):
    return lax.dot_general(a, b, (((1,), (1,)), ((), ())), preferred_element_type=F32)


def tn(a, b):
    return lax.dot_general(a, b, (((0,), (0,)), ((), ())), preferred_element_type=F32)


def rows_at(index, size):
    return pl.ds(pl.multiple_of(index * size, size), size)


def flip(index, bit):
    return index + bit - 2 * bit * lax.rem(index // bit, 2)


class Copies:
    def __init__(self, send, recv):
        self.send, self.recv, self.count, self.sent = send, recv, 0, []

    def new(self):
        self.count += 1
        return self.count - 1

    def make(self, k, src, dst, device):
        return pltpu.make_async_remote_copy(
            src, dst, self.send.at[k], self.recv.at[k], device_id=device, device_id_type=MESH
        )

    def start(self, k, src, dst, device):
        copy = self.make(k, src, dst, device)
        copy.start()
        self.sent.append(copy)

    def wait(self, k, dst, device):
        self.make(k, dst, dst, device).wait_recv()

    def finish(self):
        for copy in self.sent:
            copy.wait_send()


class Spread:
    def __init__(self, copies, view, me, z):
        self.c, self.view, self.me, self.z = copies, view, me, z
        self.k = [copies.new() for _ in range(9)]

    def dev(self, bit):
        return (flip(self.me, bit), self.z)

    def own(self):
        v = self.view(self.me)
        self.c.start(self.k[1], v, v, self.dev(2))
        self.c.start(self.k[2], v, v, self.dev(4))
        self.c.start(self.k[0], v, v, self.dev(1))

    def forward(self):
        c, x, y = self.c, flip(self.me, 2), flip(self.me, 4)
        c.wait(self.k[1], self.view(x), self.dev(2))
        v = self.view(x, 0)
        c.start(self.k[3], v, v, self.dev(4))
        c.wait(self.k[2], self.view(y), self.dev(4))
        v = self.view(y, 1)
        c.start(self.k[4], v, v, self.dev(2))
        v = self.view(x)
        c.start(self.k[5], v, v, self.dev(1))
        v = self.view(y)
        c.start(self.k[6], v, v, self.dev(1))

    def last(self):
        c, far = self.c, flip(flip(self.me, 2), 4)
        c.wait(self.k[3], self.view(far, 0), self.dev(4))
        c.wait(self.k[4], self.view(far, 1), self.dev(2))
        v = self.view(far)
        c.start(self.k[7], v, v, self.dev(1))

    def ready(self):
        c, s = self.c, flip(self.me, 1)
        c.wait(self.k[0], self.view(s), self.dev(1))
        c.wait(self.k[5], self.view(flip(s, 2)), self.dev(1))
        c.wait(self.k[6], self.view(flip(s, 4)), self.dev(1))
        c.wait(self.k[7], self.view(flip(flip(s, 2), 4)), self.dev(1))


class Line:
    def __init__(self, copies, buf, size, n, me, z):
        self.c, self.buf, self.size, self.n, self.me, self.z = copies, buf, size, n, me, z
        self.k = [(copies.new(), copies.new()) for _ in range(n - 1)]

    def block(self, j):
        return self.buf.at[rows_at(jnp.clip(j, 0, self.n - 1), self.size), :]

    def start(self, s):
        z, n = self.z, self.n
        up, down = self.block(z - s), self.block(z + s)

        @pl.when((z >= s) & (z < n - 1))
        def _():
            self.c.make(self.k[s][0], up, up, (self.me, jnp.minimum(z + 1, n - 1))).start()

        @pl.when((z + s <= n - 1) & (z > 0))
        def _():
            self.c.make(self.k[s][1], down, down, (self.me, jnp.maximum(z - 1, 0))).start()

    def recv(self, s):
        z, n = self.z, self.n
        up, down = self.block(z - 1 - s), self.block(z + 1 + s)

        @pl.when(z >= s + 1)
        def _():
            self.c.make(self.k[s][0], up, up, (self.me, jnp.minimum(z + 1, n - 1))).wait_recv()

        @pl.when(z + 1 + s <= n - 1)
        def _():
            self.c.make(self.k[s][1], down, down, (self.me, jnp.maximum(z - 1, 0))).wait_recv()

    def finish(self):
        z, n = self.z, self.n
        for s in range(n - 1):
            block = self.block(z)

            @pl.when((z >= s) & (z < n - 1))
            def _():
                self.c.make(self.k[s][0], block, block, (self.me, jnp.minimum(z + 1, n - 1))).wait_send()

            @pl.when((z + s <= n - 1) & (z > 0))
            def _():
                self.c.make(self.k[s][1], block, block, (self.me, jnp.maximum(z - 1, 0))).wait_send()


def turned(x, table, sign):
    return (
        x * table[0]
        + pltpu.roll(x, 112, 1) * (table[1] * sign)
        + pltpu.roll(x, 16, 1) * (table[2] * sign)
    )


def gather_forward(
    n,
    prefix,
    x,
    cot,
    wq,
    wk,
    wv,
    wo,
    wu,
    wd,
    gain,
    bias,
    bqkv,
    bu,
    table,
    normed,
    cots,
    w_qkv,
    w_up,
    qkv,
    joined,
    branch,
    attn_grad,
    up_grad,
    lse,
    w_dn,
    slope,
    own_x,
    send,
    recv,
    local,
):
    me, z = lax.axis_index("dp"), lax.axis_index("tensor")
    size, d = x.shape
    length = n * size
    width = wq.shape[1]
    ff = wu.shape[1]
    shard = wq.shape[0]
    lanes = wo.shape[1]

    barrier = pltpu.get_barrier_semaphore()
    for bit in (1, 2, 4):
        pl.semaphore_signal(barrier, 1, device_id=(flip(me, bit), z), device_id_type=MESH)

    @pl.when(z > 0)
    def _():
        pl.semaphore_signal(barrier, 1, device_id=(me, jnp.maximum(z - 1, 0)), device_id_type=MESH)

    @pl.when(z < n - 1)
    def _():
        pl.semaphore_signal(barrier, 1, device_id=(me, jnp.minimum(z + 1, n - 1)), device_id_type=MESH)

    mine, cols = rows_at(me, shard), rows_at(me, lanes)
    loads = [
        pltpu.make_async_copy(x, own_x, local.at[0]),
        pltpu.make_async_copy(wq, w_qkv.at[mine, pl.ds(0, width)], local.at[1]),
        pltpu.make_async_copy(wk, w_qkv.at[mine, pl.ds(width, width)], local.at[2]),
        pltpu.make_async_copy(wv, w_qkv.at[mine, pl.ds(2 * width, width)], local.at[3]),
        pltpu.make_async_copy(wu, w_up.at[mine, :], local.at[4]),
        pltpu.make_async_copy(wo, w_dn.at[pl.ds(0, width), cols], local.at[5]),
        pltpu.make_async_copy(wd, w_dn.at[pl.ds(width, ff), cols], local.at[6]),
        pltpu.make_async_copy(cot, cots.at[rows_at(z, size), :], local.at[7]),
    ]
    for load in loads:
        load.start()

    copies = Copies(send, recv)

    def row_view(buf):
        def view(i, half=None):
            if half is None:
                return buf.at[rows_at(i, shard), :]
            h = shard // 2
            return buf.at[pl.ds(pl.multiple_of(i * shard + half * h, h), h), :]

        return view

    def col_view(first, count):
        def view(i, half=None):
            if half is None:
                return w_dn.at[pl.ds(first, count), rows_at(i, lanes)]
            h = count // 2
            return w_dn.at[pl.ds(first + half * h, h), rows_at(i, lanes)]

        return view

    s_qkv = Spread(copies, row_view(w_qkv), me, z)
    s_up = Spread(copies, row_view(w_up), me, z)
    s_dn = [Spread(copies, col_view(0, width + ff // 2), me, z), Spread(copies, col_view(width + ff // 2, ff // 2), me, z)]
    l_n = Line(copies, normed, size, n, me, z)
    l_c = Line(copies, cots, size, n, me, z)

    order = [z, flip(z, 1), flip(z, 2), flip(flip(z, 1), 2)]

    def norm(r, carry):
        rows = rows_at(r, 64)
        v = own_x[rows, :].astype(F32)
        mean = jnp.mean(v, axis=-1, keepdims=True)
        c = v - mean
        inv = lax.rsqrt(jnp.mean(c * c, axis=-1, keepdims=True) + epsilon)
        out = (c * inv) * gain[...] + bias[...]
        normed[pl.ds(pl.multiple_of(z * size + r * 64, 64), 64), :] = out.astype(BF)
        return carry

    def project(j):
        rows = rows_at(j, size)
        for part in range(3):
            acc = nn(normed[rows, :], w_qkv[:, part * width : (part + 1) * width])
            acc = acc + bqkv[:, part * width : (part + 1) * width]
            for p in range(width // 128):
                piece = acc[:, p * 128 : (p + 1) * 128]
                if part < 2:
                    tab = [table[i, rows, :] for i in range(3)]
                    piece = turned(piece, tab, 1.0)
                    if part == 0:
                        piece = piece * (1.0 / math.sqrt(HEAD_DIM))
                qkv[rows, part * width + p * 128 : part * width + (p + 1) * 128] = piece.astype(BF)

    def raise_(j):
        rows = rows_at(j, size)
        tile = 512

        @pl.loop(0, ff // tile)
        def _(t):
            cs = rows_at(t, tile)
            u = nn(normed[rows, :], w_up[:, cs]) + bu[:, cs]
            sq = u * u
            th = jnp.tanh(root * u * (1.0 + 0.044715 * sq))
            half = 0.5 * (1.0 + th)
            joined[rows, pl.ds(pl.multiple_of(width + t * tile, tile), tile)] = (u * half).astype(BF)
            slope[rows, cs] = (
                half + 0.5 * u * (1.0 - th * th) * (root * (1.0 + 3 * 0.044715 * sq))
            ).astype(BF)

    def attend(first, count):
        block = length // 4

        @pl.loop(first, first + count)
        def _(p):
            ps = rows_at(p, 128)
            head = lax.broadcasted_iota(jnp.int32, (1, 128), 1) // HEAD_DIM
            for b in range(4):
                nk = max(b + 1, 2) * block
                qs = pl.ds(b * block, block)
                q = qkv[qs, ps]
                k = qkv[pl.ds(0, nk), pl.ds(pl.multiple_of(width + p * 128, 128), 128)]
                v = qkv[pl.ds(0, nk), pl.ds(pl.multiple_of(2 * width + p * 128, 128), 128)]
                limit = jnp.maximum(
                    b * block + lax.broadcasted_iota(jnp.int32, (block, 1), 0), prefix[0] - 1
                )
                seen = lax.broadcasted_iota(jnp.int32, (block, nk), 1) <= limit
                outs = []
                for h in range(2):
                    s = nt(jnp.where(head == h, q, jnp.zeros_like(q)), k)
                    s = jnp.where(seen, s, masked_score)
                    top = jnp.max(s, axis=-1, keepdims=True)
                    e = jnp.exp(s - top)
                    total = jnp.sum(e, axis=-1, keepdims=True)
                    probs = (e * (1.0 / total)).astype(BF)
                    outs.append(nn(probs, v))
                    lane = lax.broadcasted_iota(jnp.int32, (1, 128), 1)
                    lse[qs, :] = jnp.where(lane == 2 * p + h, top + jnp.log(total), lse[qs, :])
                joined[qs, ps] = jnp.where(head == 0, outs[0], outs[1]).astype(BF)

    def lower(j):
        rows = rows_at(j, size)
        tile = 512

        @pl.loop(0, d // tile)
        def _(t):
            branch[rows, rows_at(t, tile)] = nn(joined[rows, :], w_dn[:, rows_at(t, tile)]).astype(BF)

    def back_down(j):
        rows = rows_at(j, size)
        tile = 512
        attn_grad[rows, :] = nt(cots[rows, :], w_dn[:width, :]).astype(BF)

        @pl.loop(0, ff // tile)
        def _(t):
            g = nt(cots[rows, :], w_dn[pl.ds(pl.multiple_of(width + t * tile, tile), tile), :])
            cs = rows_at(t, tile)
            up_grad[rows, cs] = (g * slope[rows, cs].astype(F32)).astype(BF)

    signals = 3 + jnp.where(z > 0, 1, 0) + jnp.where(z < n - 1, 1, 0)
    pl.semaphore_wait(barrier, signals)

    for i in (1, 2, 3):
        loads[i].wait()
    s_qkv.own()
    loads[0].wait()
    lax.fori_loop(0, size // 64, norm, 0)
    l_n.start(0)
    loads[4].wait()
    s_up.own()
    lse[...] = jnp.zeros_like(lse)
    s_qkv.forward()
    l_n.recv(0)
    l_n.start(1)
    s_qkv.last()
    loads[5].wait()
    loads[6].wait()
    s_dn[0].own()
    s_qkv.ready()
    project(order[0])
    s_up.forward()
    project(order[1])
    l_n.recv(1)
    l_n.start(2)
    s_up.last()
    s_dn[1].own()
    project(order[2])
    s_up.ready()
    raise_(order[0])
    s_dn[0].forward()
    raise_(order[1])
    l_n.recv(2)
    loads[7].wait()
    l_c.start(0)
    s_dn[0].last()
    project(order[3])
    raise_(order[2])
    s_dn[1].forward()
    raise_(order[3])
    attend(0, 2)
    l_c.recv(0)
    l_c.start(1)
    s_dn[1].last()
    attend(2, 2)
    for s in s_dn:
        s.ready()
    back_down(order[0])
    back_down(order[1])
    l_c.recv(1)
    l_c.start(2)
    lower(order[0])
    lower(order[1])
    lower(order[2])
    lower(order[3])
    back_down(order[2])
    l_c.recv(2)
    back_down(order[3])
    l_n.finish()
    l_c.finish()
    copies.finish()


def tables(length):
    half = ROT_DIM // 2
    freqs = rope_base ** (-(jnp.arange(half).astype(F32) * 2.0 / ROT_DIM))
    angles = jnp.arange(length).astype(F32)[:, None] * freqs[None, :]
    cos, sin = jnp.cos(angles), jnp.sin(angles)
    one, zero = jnp.ones((length, HEAD_DIM - ROT_DIM), F32), jnp.zeros((length, half), F32)
    wide = jnp.zeros((length, HEAD_DIM - ROT_DIM), F32)
    c = jnp.concatenate([cos, cos, one], 1)
    s1 = jnp.concatenate([-sin, zero, wide], 1)
    s2 = jnp.concatenate([zero, sin, wide], 1)
    return jnp.stack([jnp.concatenate([t, t], 1) for t in (c, s1, s2)])


def forward_call(n, prefix, x, cot, wq, wk, wv, wo, wu, wd, gain, bias, bq, bk, bv, bu):
    size, d = x.shape
    length, width, ff = n * size, wq.shape[1], wu.shape[1]
    vm, hbm = pl.BlockSpec(memory_space=pltpu.VMEM), pl.BlockSpec(memory_space=pl.ANY)
    shape = lambda s, t=BF: jax.ShapeDtypeStruct(s, t)
    return pl.pallas_call(
        functools.partial(gather_forward, n),
        out_shape=(
            shape((length, d)),
            shape((length, d)),
            shape((d, 3 * width)),
            shape((d, ff)),
            shape((length, 3 * width)),
            shape((length, width + ff)),
            shape((length, d)),
            shape((length, width)),
            shape((length, ff)),
            shape((length, 128), F32),
        ),
        in_specs=[pl.BlockSpec(memory_space=pltpu.SMEM)] + [hbm] * 8 + [vm] * 5,
        out_specs=(vm,) * 10,
        scratch_shapes=[
            pltpu.VMEM((width + ff, d), BF),
            pltpu.VMEM((length, ff), BF),
            pltpu.VMEM((size, d), BF),
            pltpu.SemaphoreType.DMA((48,)),
            pltpu.SemaphoreType.DMA((48,)),
            pltpu.SemaphoreType.DMA((8,)),
        ],
        compiler_params=pltpu.CompilerParams(
            collective_id=1, has_side_effects=True, vmem_limit_bytes=63 << 20
        ),
        cost_estimate=pl.CostEstimate(flops=50_000_000_000, bytes_accessed=100_000_000, transcendentals=0),
    )(
        prefix,
        x,
        cot,
        wq,
        wk,
        wv,
        wo,
        wu,
        wd,
        gain[None],
        bias[None],
        jnp.concatenate([bq, bk, bv])[None],
        bu[None],
        tables(length),
    )


def rotate(tensor, positions, direction):
    half_dim = ROT_DIM // 2
    freqs = rope_base ** (-(jnp.arange(half_dim).astype(jnp.float32) * 2.0 / ROT_DIM))
    angles = positions.astype(jnp.float32)[:, None] * freqs[None, :]
    cosine = jnp.cos(angles)[:, None, :]
    sine = direction * jnp.sin(angles)[:, None, :]
    first = tensor[..., :half_dim]
    second = tensor[..., half_dim:ROT_DIM]
    return jnp.concatenate(
        [first * cosine - second * sine, second * cosine + first * sine, tensor[..., ROT_DIM:]],
        axis=-1,
    )


def times_transposed(left, right):
    return lax.dot_general(
        left, right, (((1,), (1,)), ((), ())), preferred_element_type=jnp.float32
    )


def rows_transposed(left, right):
    return lax.dot_general(
        left, right, (((0,), (0,)), ((), ())), preferred_element_type=jnp.float32
    )


def plain_on_device(
    layer_input,
    ln_gain,
    ln_bias,
    w_query,
    b_query,
    w_key,
    b_key,
    w_value,
    b_value,
    w_out,
    b_out,
    w_up,
    b_up,
    w_down,
    b_down,
    prefix,
    cotangent,
):
    local_width = w_query.shape[1]
    hidden_here = w_up.shape[1]
    heads_here = local_width // HEAD_DIM
    score_scale = 1.0 / math.sqrt(HEAD_DIM)
    prefix_len = prefix[0]
    input_float = layer_input.astype(jnp.float32)
    row_mean = jnp.mean(input_float, axis=-1, keepdims=True)
    centred = input_float - row_mean
    inverse = lax.rsqrt(jnp.mean(centred * centred, axis=-1, keepdims=True) + epsilon)
    unit_rows = centred * inverse
    normed = (unit_rows * ln_gain + ln_bias).astype(jnp.bfloat16)
    normed_all = lax.all_gather(normed, "tensor", axis=0, tiled=True)
    length = normed_all.shape[0]
    positions = jnp.arange(length)
    block_rows = min(512, length)
    block_count = length // block_rows
    pieces = (
        lax.all_gather(w_query, "dp", axis=0, tiled=True),
        lax.all_gather(w_key, "dp", axis=0, tiled=True),
        lax.all_gather(w_value, "dp", axis=0, tiled=True),
        lax.all_gather(w_up, "dp", axis=0, tiled=True),
    )
    columns = normed_all
    query_acc, key_acc, value_acc, up_acc = tuple(
        (jnp.dot(columns, piece, preferred_element_type=jnp.float32) for piece in pieces)
    )
    query_pre = (query_acc + b_query).reshape(length, heads_here, HEAD_DIM)
    key_pre = (key_acc + b_key).reshape(length, heads_here, HEAD_DIM)
    query = rotate(query_pre, positions, 1.0).astype(jnp.bfloat16)
    key = rotate(key_pre, positions, 1.0).astype(jnp.bfloat16)
    value = (value_acc + b_value).reshape(length, heads_here, HEAD_DIM).astype(jnp.bfloat16)
    up_pre = up_acc + b_up
    hidden = jax.nn.gelu(up_pre, approximate=True).astype(jnp.bfloat16)

    def scores_for(query_rows, offset):
        raw = (
            jnp.einsum("qhd,khd->hqk", query_rows, key, preferred_element_type=jnp.float32)
            * score_scale
        )
        query_pos = offset + jnp.arange(block_rows)
        seen = (positions[None, :] <= query_pos[:, None]) | (positions[None, :] < prefix_len)
        return jnp.where(seen[None], raw, masked_score)

    def attend_block(index):
        offset = index * block_rows
        query_rows = lax.dynamic_slice_in_dim(query, offset, block_rows, 0)
        scores = scores_for(query_rows, offset)
        row_max = jnp.max(scores, axis=-1, keepdims=True)
        expo = jnp.exp(scores - row_max)
        totals = jnp.sum(expo, axis=-1, keepdims=True)
        probs_low = (expo / totals).astype(jnp.bfloat16)
        out_rows = jnp.einsum("hqk,khd->qhd", probs_low, value, preferred_element_type=jnp.float32)
        return (out_rows, (row_max + jnp.log(totals))[..., 0])

    indices = jnp.arange(block_count)
    out_blocks, log_totals = lax.map(attend_block, indices)
    attn = out_blocks.reshape(length, local_width).astype(jnp.bfloat16)
    pieces = (
        lax.all_gather(w_out, "dp", axis=1, tiled=True),
        lax.all_gather(w_down, "dp", axis=1, tiled=True),
    )
    part = jnp.dot(attn, pieces[0], preferred_element_type=jnp.float32) + jnp.dot(
        hidden, pieces[1], preferred_element_type=jnp.float32
    )
    partial_value = part
    branch = lax.psum_scatter(partial_value, "tensor", scatter_dimension=0, tiled=True)
    layer_out = (input_float + branch + b_out + b_down).astype(jnp.bfloat16)
    grad_all = lax.all_gather(cotangent, "tensor", axis=0, tiled=True)
    pieces = (
        lax.all_gather(w_out, "dp", axis=1, tiled=True),
        lax.all_gather(w_down, "dp", axis=1, tiled=True),
    )
    columns = grad_all
    attn_grad = times_transposed(columns, pieces[0])
    hidden_grad = times_transposed(columns, pieces[1])
    down_joined = jnp.concatenate([attn, hidden], axis=1)
    unused, gelu_pull = jax.vjp(lambda inner: jax.nn.gelu(inner, approximate=True), up_pre)
    up_grad_low = gelu_pull(hidden_grad)[0].astype(jnp.bfloat16)
    attn_grad_low = attn_grad.astype(jnp.bfloat16).reshape(length, heads_here, HEAD_DIM)

    def back_block(carry, item):
        key_grad, value_grad = carry
        index, lse_rows = item
        offset = index * block_rows
        query_rows = lax.dynamic_slice_in_dim(query, offset, block_rows, 0)
        grad_rows = lax.dynamic_slice_in_dim(attn_grad_low, offset, block_rows, 0)
        scores = scores_for(query_rows, offset)
        probs = jnp.exp(scores - lse_rows[..., None])
        value_grad = value_grad + jnp.einsum(
            "hqk,qhd->khd",
            probs.astype(jnp.bfloat16),
            grad_rows,
            preferred_element_type=jnp.float32,
        )
        prob_grad = jnp.einsum("qhd,khd->hqk", grad_rows, value, preferred_element_type=jnp.float32)
        delta = jnp.sum(probs * prob_grad, axis=-1, keepdims=True)
        score_grad = (probs * (prob_grad - delta)).astype(jnp.bfloat16)
        query_grad = (
            jnp.einsum("hqk,khd->qhd", score_grad, key, preferred_element_type=jnp.float32)
            * score_scale
        )
        key_grad = (
            key_grad
            + jnp.einsum("hqk,qhd->khd", score_grad, query_rows, preferred_element_type=jnp.float32)
            * score_scale
        )
        return ((key_grad, value_grad), query_grad)

    state_zeros = jnp.zeros((length, heads_here, HEAD_DIM), jnp.float32)
    (key_grad, value_grad), query_blocks = lax.scan(
        back_block, (state_zeros, state_zeros), (indices, log_totals)
    )
    query_grad = query_blocks.reshape(length, heads_here, HEAD_DIM)
    q_grad_low = (
        rotate(query_grad, positions, -1.0).reshape(length, local_width).astype(jnp.bfloat16)
    )
    k_grad_low = rotate(key_grad, positions, -1.0).reshape(length, local_width).astype(jnp.bfloat16)
    v_grad_low = value_grad.reshape(length, local_width).astype(jnp.bfloat16)
    up_joined = jnp.concatenate([q_grad_low, k_grad_low, v_grad_low, up_grad_low], axis=1)
    columns = grad_all
    joined_rows = lax.psum_scatter(
        jnp.concatenate(
            [rows_transposed(columns, down_joined), rows_transposed(normed_all, up_joined)], axis=1
        ),
        "dp",
        scatter_dimension=0,
        tiled=True,
    )
    down_rows = joined_rows[:, : local_width + hidden_here]
    up_rows = joined_rows[:, local_width + hidden_here :]
    d_w_out = down_rows[:, :local_width].T
    d_w_down = down_rows[:, local_width:].T
    d_w_query = up_rows[:, :local_width]
    d_w_key = up_rows[:, local_width : 2 * local_width]
    d_w_value = up_rows[:, 2 * local_width : 3 * local_width]
    d_w_up = up_rows[:, 3 * local_width :]
    pieces = (
        lax.all_gather(w_query, "dp", axis=0, tiled=True),
        lax.all_gather(w_key, "dp", axis=0, tiled=True),
        lax.all_gather(w_value, "dp", axis=0, tiled=True),
        lax.all_gather(w_up, "dp", axis=0, tiled=True),
    )
    part = (
        times_transposed(q_grad_low, pieces[0])
        + times_transposed(k_grad_low, pieces[1])
        + times_transposed(v_grad_low, pieces[2])
        + times_transposed(up_grad_low, pieces[3])
    )
    own_grad = lax.psum_scatter(part, "tensor", scatter_dimension=0, tiled=True)
    scaled_grad = own_grad * ln_gain
    norm_part = inverse * (
        scaled_grad
        - jnp.mean(scaled_grad, axis=-1, keepdims=True)
        - unit_rows * jnp.mean(scaled_grad * unit_rows, axis=-1, keepdims=True)
    )
    cot_float = cotangent.astype(jnp.float32)
    d_input = cot_float + norm_part
    d_ln_gain, d_ln_bias, d_b_out = lax.psum(
        (
            jnp.sum(own_grad * unit_rows, axis=0),
            jnp.sum(own_grad, axis=0),
            jnp.sum(cot_float, axis=0),
        ),
        ("dp", "tensor"),
    )
    d_b_query, d_b_key, d_b_value, d_b_up = lax.psum(
        (
            jnp.sum(q_grad_low.astype(jnp.float32), axis=0),
            jnp.sum(k_grad_low.astype(jnp.float32), axis=0),
            jnp.sum(v_grad_low.astype(jnp.float32), axis=0),
            jnp.sum(up_grad_low.astype(jnp.float32), axis=0),
        ),
        "dp",
    )
    return (
        layer_out,
        d_input,
        d_ln_gain,
        d_ln_bias,
        d_w_query,
        d_b_query,
        d_w_key,
        d_b_key,
        d_w_value,
        d_b_value,
        d_w_out,
        d_b_out,
        d_w_up,
        d_b_up,
        d_w_down,
        d_b_out,
    )


def on_device(
    layer_input, ln_gain, ln_bias, w_query, b_query, w_key, b_key, w_value, b_value,
    w_out, b_out, w_up, b_up, w_down, b_down, prefix, cotangent,
):
    n = lax.axis_size("tensor")
    local_width = w_query.shape[1]
    hidden_here = w_up.shape[1]
    heads_here = local_width // HEAD_DIM
    score_scale = 1.0 / math.sqrt(HEAD_DIM)
    prefix_len = prefix[0]
    input_float = layer_input.astype(jnp.float32)
    row_mean = jnp.mean(input_float, axis=-1, keepdims=True)
    centred = input_float - row_mean
    inverse = lax.rsqrt(jnp.mean(centred * centred, axis=-1, keepdims=True) + epsilon)
    unit_rows = centred * inverse
    normed_all, grad_all, w_qkv, w_up_all, qkv, joined, part, attn_grad, up_grad_low, lse = forward_call(
        n, prefix, layer_input, cotangent, w_query, w_key, w_value, w_out, w_up, w_down,
        ln_gain, ln_bias, b_query, b_key, b_value, b_up,
    )
    length = normed_all.shape[0]
    positions = jnp.arange(length)
    block_rows = min(512, length)
    block_count = length // block_rows
    query, key, value = (
        qkv[:, i * local_width : (i + 1) * local_width].reshape(length, heads_here, HEAD_DIM)
        for i in range(3)
    )
    log_totals = lse[:, :heads_here].T.reshape(heads_here, block_count, block_rows).transpose(1, 0, 2)

    def scores_for(query_rows, offset):
        raw = jnp.einsum("qhd,khd->hqk", query_rows, key, preferred_element_type=jnp.float32)
        query_pos = offset + jnp.arange(block_rows)
        seen = (positions[None, :] <= query_pos[:, None]) | (positions[None, :] < prefix_len)
        return jnp.where(seen[None], raw, masked_score)

    indices = jnp.arange(block_count)
    branch = lax.psum_scatter(part.astype(F32), "tensor", scatter_dimension=0, tiled=True)
    layer_out = (input_float + branch + b_out + b_down).astype(jnp.bfloat16)
    attn_grad_low = attn_grad.reshape(length, heads_here, HEAD_DIM)

    def back_block(carry, item):
        key_grad, value_grad = carry
        index, lse_rows = item
        offset = index * block_rows
        query_rows = lax.dynamic_slice_in_dim(query, offset, block_rows, 0)
        grad_rows = lax.dynamic_slice_in_dim(attn_grad_low, offset, block_rows, 0)
        scores = scores_for(query_rows, offset)
        probs = jnp.exp(scores - lse_rows[..., None])
        value_grad = value_grad + jnp.einsum(
            "hqk,qhd->khd", probs.astype(jnp.bfloat16), grad_rows, preferred_element_type=jnp.float32
        )
        prob_grad = jnp.einsum("qhd,khd->hqk", grad_rows, value, preferred_element_type=jnp.float32)
        delta = jnp.sum(probs * prob_grad, axis=-1, keepdims=True)
        score_grad = (probs * (prob_grad - delta)).astype(jnp.bfloat16)
        query_grad = (
            jnp.einsum("hqk,khd->qhd", score_grad, key, preferred_element_type=jnp.float32) * score_scale
        )
        key_grad = key_grad + jnp.einsum(
            "hqk,qhd->khd", score_grad, query_rows, preferred_element_type=jnp.float32
        )
        return ((key_grad, value_grad), query_grad)

    state_zeros = jnp.zeros((length, heads_here, HEAD_DIM), jnp.float32)
    (key_grad, value_grad), query_blocks = lax.scan(
        back_block, (state_zeros, state_zeros), (indices, log_totals)
    )
    query_grad = query_blocks.reshape(length, heads_here, HEAD_DIM)
    q_grad_low = rotate(query_grad, positions, -1.0).reshape(length, local_width).astype(jnp.bfloat16)
    k_grad_low = rotate(key_grad, positions, -1.0).reshape(length, local_width).astype(jnp.bfloat16)
    v_grad_low = value_grad.reshape(length, local_width).astype(jnp.bfloat16)
    up_joined = jnp.concatenate([q_grad_low, k_grad_low, v_grad_low, up_grad_low], axis=1)
    joined_rows = lax.psum_scatter(
        jnp.concatenate(
            [rows_transposed(grad_all, joined), rows_transposed(normed_all, up_joined)], axis=1
        ),
        "dp",
        scatter_dimension=0,
        tiled=True,
    )
    down_rows = joined_rows[:, : local_width + hidden_here]
    up_rows = joined_rows[:, local_width + hidden_here :]
    d_w_out = down_rows[:, :local_width].T
    d_w_down = down_rows[:, local_width:].T
    d_w_query = up_rows[:, :local_width]
    d_w_key = up_rows[:, local_width : 2 * local_width]
    d_w_value = up_rows[:, 2 * local_width : 3 * local_width]
    d_w_up = up_rows[:, 3 * local_width :]
    part = times_transposed(up_joined[:, : 3 * local_width], w_qkv) + times_transposed(up_grad_low, w_up_all)
    own_grad = lax.psum_scatter(part, "tensor", scatter_dimension=0, tiled=True)
    scaled_grad = own_grad * ln_gain
    norm_part = inverse * (
        scaled_grad
        - jnp.mean(scaled_grad, axis=-1, keepdims=True)
        - unit_rows * jnp.mean(scaled_grad * unit_rows, axis=-1, keepdims=True)
    )
    cot_float = cotangent.astype(jnp.float32)
    d_input = cot_float + norm_part
    d_ln_gain, d_ln_bias, d_b_out = lax.psum(
        (
            jnp.sum(own_grad * unit_rows, axis=0),
            jnp.sum(own_grad, axis=0),
            jnp.sum(cot_float, axis=0),
        ),
        ("dp", "tensor"),
    )
    sums = lax.psum(jnp.sum(up_joined.astype(jnp.float32), axis=0), "dp")
    d_b_query, d_b_key, d_b_value = (sums[i * local_width : (i + 1) * local_width] for i in range(3))
    d_b_up = sums[3 * local_width :]
    return (
        layer_out, d_input, d_ln_gain, d_ln_bias, d_w_query, d_b_query, d_w_key, d_b_key,
        d_w_value, d_b_value, d_w_out, d_b_out, d_w_up, d_b_up, d_w_down, d_b_out,
    )


def solution(mesh):
    fits = mesh.shape["dp"] == 8 and mesh.shape["tensor"] == 4
    return jax.shard_map(
        on_device if fits else plain_on_device,
        mesh=mesh,
        in_specs=(
            P(("dp", "tensor"), None),
            P(),
            P(),
            P("dp", "tensor"),
            P("tensor"),
            P("dp", "tensor"),
            P("tensor"),
            P("dp", "tensor"),
            P("tensor"),
            P("tensor", "dp"),
            P(),
            P("dp", "tensor"),
            P("tensor"),
            P("tensor", "dp"),
            P(),
            P("dp"),
            P(("dp", "tensor"), None),
        ),
        out_specs=(
            P(("dp", "tensor"), None),
            P(("dp", "tensor"), None),
            P(),
            P(),
            P("dp", "tensor"),
            P("tensor"),
            P("dp", "tensor"),
            P("tensor"),
            P("dp", "tensor"),
            P("tensor"),
            P("tensor", "dp"),
            P(),
            P("dp", "tensor"),
            P("tensor"),
            P("tensor", "dp"),
            P(),
        ),
        check_vma=False,
    )
```

```python
import functools
import math

import jax
import jax.numpy as jnp
import numpy as np
from jax import lax
from jax.experimental import pallas as pl
from jax.experimental.pallas import tpu as pltpu
from jax.sharding import PartitionSpec as P

HEAD_DIM = 64
ROT_DIM = 32
MESH = pl.DeviceIdType.MESH
BF = jnp.bfloat16
F32 = jnp.float32

epsilon = 1e-05
rope_base = 10000.0
masked_score = -1e30
root = math.sqrt(2.0 / math.pi)


def nn(a, b):
    return jnp.dot(a, b, preferred_element_type=F32)


def nt(a, b):
    return lax.dot_general(a, b, (((1,), (1,)), ((), ())), preferred_element_type=F32)


def tn(a, b):
    return lax.dot_general(a, b, (((0,), (0,)), ((), ())), preferred_element_type=F32)


def rows_at(index, size):
    return pl.ds(pl.multiple_of(index * size, size), size)


def flip(index, bit):
    return index + bit - 2 * bit * lax.rem(index // bit, 2)


class Copies:
    def __init__(self, send, recv):
        self.send, self.recv, self.count, self.sent = send, recv, 0, []

    def new(self):
        self.count += 1
        return self.count - 1

    def make(self, k, src, dst, device):
        return pltpu.make_async_remote_copy(
            src, dst, self.send.at[k], self.recv.at[k], device_id=device, device_id_type=MESH
        )

    def start(self, k, src, dst, device):
        copy = self.make(k, src, dst, device)
        copy.start()
        self.sent.append(copy)

    def wait(self, k, dst, device):
        self.make(k, dst, dst, device).wait_recv()

    def finish(self):
        for copy in self.sent:
            copy.wait_send()


class Spread:
    def __init__(self, copies, view, me, z):
        self.c, self.view, self.me, self.z = copies, view, me, z
        self.k = [copies.new() for _ in range(9)]

    def dev(self, bit):
        return (flip(self.me, bit), self.z)

    def own(self):
        v = self.view(self.me)
        self.c.start(self.k[1], v, v, self.dev(2))
        self.c.start(self.k[2], v, v, self.dev(4))
        self.c.start(self.k[0], v, v, self.dev(1))

    def forward(self):
        c, x, y = self.c, flip(self.me, 2), flip(self.me, 4)
        c.wait(self.k[1], self.view(x), self.dev(2))
        v = self.view(x, 0)
        c.start(self.k[3], v, v, self.dev(4))
        c.wait(self.k[2], self.view(y), self.dev(4))
        v = self.view(y, 1)
        c.start(self.k[4], v, v, self.dev(2))
        v = self.view(x)
        c.start(self.k[5], v, v, self.dev(1))
        v = self.view(y)
        c.start(self.k[6], v, v, self.dev(1))

    def last(self):
        c, far = self.c, flip(flip(self.me, 2), 4)
        c.wait(self.k[3], self.view(far, 0), self.dev(4))
        c.wait(self.k[4], self.view(far, 1), self.dev(2))
        v = self.view(far)
        c.start(self.k[7], v, v, self.dev(1))

    def ready(self):
        c, s = self.c, flip(self.me, 1)
        c.wait(self.k[0], self.view(s), self.dev(1))
        c.wait(self.k[5], self.view(flip(s, 2)), self.dev(1))
        c.wait(self.k[6], self.view(flip(s, 4)), self.dev(1))
        c.wait(self.k[7], self.view(flip(flip(s, 2), 4)), self.dev(1))


class Line:
    def __init__(self, copies, buf, size, n, me, z):
        self.c, self.buf, self.size, self.n, self.me, self.z = copies, buf, size, n, me, z
        self.k = [(copies.new(), copies.new()) for _ in range(n - 1)]

    def block(self, j):
        return self.buf.at[rows_at(jnp.clip(j, 0, self.n - 1), self.size), :]

    def start(self, s):
        z, n = self.z, self.n
        up, down = self.block(z - s), self.block(z + s)

        @pl.when((z >= s) & (z < n - 1))
        def _():
            self.c.make(self.k[s][0], up, up, (self.me, jnp.minimum(z + 1, n - 1))).start()

        @pl.when((z + s <= n - 1) & (z > 0))
        def _():
            self.c.make(self.k[s][1], down, down, (self.me, jnp.maximum(z - 1, 0))).start()

    def recv(self, s):
        z, n = self.z, self.n
        up, down = self.block(z - 1 - s), self.block(z + 1 + s)

        @pl.when(z >= s + 1)
        def _():
            self.c.make(self.k[s][0], up, up, (self.me, jnp.minimum(z + 1, n - 1))).wait_recv()

        @pl.when(z + 1 + s <= n - 1)
        def _():
            self.c.make(self.k[s][1], down, down, (self.me, jnp.maximum(z - 1, 0))).wait_recv()

    def finish(self):
        z, n = self.z, self.n
        for s in range(n - 1):
            block = self.block(z)

            @pl.when((z >= s) & (z < n - 1))
            def _():
                self.c.make(self.k[s][0], block, block, (self.me, jnp.minimum(z + 1, n - 1))).wait_send()

            @pl.when((z + s <= n - 1) & (z > 0))
            def _():
                self.c.make(self.k[s][1], block, block, (self.me, jnp.maximum(z - 1, 0))).wait_send()


def turned(x, table, sign):
    return (
        x * table[0]
        + pltpu.roll(x, 112, 1) * (table[1] * sign)
        + pltpu.roll(x, 16, 1) * (table[2] * sign)
    )


def gather_forward(
    n,
    prefix,
    x,
    cot,
    wq,
    wk,
    wv,
    wo,
    wu,
    wd,
    gain,
    bias,
    bqkv,
    bu,
    table,
    normed,
    cots,
    w_qkv,
    w_up,
    qkv,
    joined,
    branch,
    attn_grad,
    up_grad,
    lse_out,
    w_dn,
    slope,
    own_x,
    lse,
    send,
    recv,
    local,
):
    me, z = lax.axis_index("dp"), lax.axis_index("tensor")
    size, d = x.shape
    length = n * size
    width = wq.shape[1]
    ff = wu.shape[1]
    shard = wq.shape[0]
    lanes = wo.shape[1]

    barrier = pltpu.get_barrier_semaphore()
    for bit in (1, 2, 4):
        pl.semaphore_signal(barrier, 1, device_id=(flip(me, bit), z), device_id_type=MESH)

    @pl.when(z > 0)
    def _():
        pl.semaphore_signal(barrier, 1, device_id=(me, jnp.maximum(z - 1, 0)), device_id_type=MESH)

    @pl.when(z < n - 1)
    def _():
        pl.semaphore_signal(barrier, 1, device_id=(me, jnp.minimum(z + 1, n - 1)), device_id_type=MESH)

    mine, cols = rows_at(me, shard), rows_at(me, lanes)
    loads = [
        pltpu.make_async_copy(x, own_x, local.at[0]),
        pltpu.make_async_copy(wq, w_qkv.at[mine, pl.ds(0, width)], local.at[1]),
        pltpu.make_async_copy(wk, w_qkv.at[mine, pl.ds(width, width)], local.at[2]),
        pltpu.make_async_copy(wv, w_qkv.at[mine, pl.ds(2 * width, width)], local.at[3]),
        pltpu.make_async_copy(wu, w_up.at[mine, :], local.at[4]),
        pltpu.make_async_copy(wo, w_dn.at[pl.ds(0, width), cols], local.at[5]),
        pltpu.make_async_copy(wd, w_dn.at[pl.ds(width, ff), cols], local.at[6]),
        pltpu.make_async_copy(cot, cots.at[rows_at(z, size), :], local.at[7]),
    ]
    for load in loads:
        load.start()

    copies = Copies(send, recv)

    def row_view(buf):
        def view(i, half=None):
            if half is None:
                return buf.at[rows_at(i, shard), :]
            h = shard // 2
            return buf.at[pl.ds(pl.multiple_of(i * shard + half * h, h), h), :]

        return view

    def col_view(first, count):
        def view(i, half=None):
            if half is None:
                return w_dn.at[pl.ds(first, count), rows_at(i, lanes)]
            h = count // 2
            return w_dn.at[pl.ds(first + half * h, h), rows_at(i, lanes)]

        return view

    s_qkv = Spread(copies, row_view(w_qkv), me, z)
    s_up = Spread(copies, row_view(w_up), me, z)
    s_dn = [Spread(copies, col_view(0, width + ff // 2), me, z), Spread(copies, col_view(width + ff // 2, ff // 2), me, z)]
    l_n = Line(copies, normed, size, n, me, z)
    l_c = Line(copies, cots, size, n, me, z)

    order = [z, flip(z, 1), flip(z, 2), flip(flip(z, 1), 2)]

    def norm(r, carry):
        rows = rows_at(r, 64)
        v = own_x[rows, :].astype(F32)
        mean = jnp.mean(v, axis=-1, keepdims=True)
        c = v - mean
        inv = lax.rsqrt(jnp.mean(c * c, axis=-1, keepdims=True) + epsilon)
        out = (c * inv) * gain[...] + bias[...]
        normed[pl.ds(pl.multiple_of(z * size + r * 64, 64), 64), :] = out.astype(BF)
        return carry

    def project(j):
        rows = rows_at(j, size)
        for part in range(3):
            acc = nn(normed[rows, :], w_qkv[:, part * width : (part + 1) * width])
            acc = acc + bqkv[:, part * width : (part + 1) * width]
            for p in range(width // 128):
                piece = acc[:, p * 128 : (p + 1) * 128]
                if part < 2:
                    tab = [table[i, rows, :] for i in range(3)]
                    piece = turned(piece, tab, 1.0)
                    if part == 0:
                        piece = piece * (1.0 / math.sqrt(HEAD_DIM))
                qkv[rows, part * width + p * 128 : part * width + (p + 1) * 128] = piece.astype(BF)

    def raise_(j):
        rows = rows_at(j, size)
        tile = 512

        @pl.loop(0, ff // tile)
        def _(t):
            cs = rows_at(t, tile)
            u = nn(normed[rows, :], w_up[:, cs]) + bu[:, cs]
            sq = u * u
            th = jnp.tanh(root * u * (1.0 + 0.044715 * sq))
            half = 0.5 * (1.0 + th)
            joined[rows, pl.ds(pl.multiple_of(width + t * tile, tile), tile)] = (u * half).astype(BF)
            slope[rows, cs] = (
                half + 0.5 * u * (1.0 - th * th) * (root * (1.0 + 3 * 0.044715 * sq))
            ).astype(BF)

    def attend(first, count):
        block = length // 4

        @pl.loop(first, first + count)
        def _(p):
            ps = rows_at(p, 128)
            head = lax.broadcasted_iota(jnp.int32, (1, 128), 1) // HEAD_DIM
            for b in range(4):
                nk = max(b + 1, 2) * block
                qs = pl.ds(b * block, block)
                q = qkv[qs, ps]
                k = qkv[pl.ds(0, nk), pl.ds(pl.multiple_of(width + p * 128, 128), 128)]
                v = qkv[pl.ds(0, nk), pl.ds(pl.multiple_of(2 * width + p * 128, 128), 128)]
                limit = jnp.maximum(
                    b * block + lax.broadcasted_iota(jnp.int32, (block, 1), 0), prefix[0] - 1
                )
                seen = lax.broadcasted_iota(jnp.int32, (block, nk), 1) <= limit
                outs = []
                for h in range(2):
                    s = nt(jnp.where(head == h, q, jnp.zeros_like(q)), k)
                    s = jnp.where(seen, s, masked_score)
                    top = jnp.max(s, axis=-1, keepdims=True)
                    e = jnp.exp(s - top)
                    total = jnp.sum(e, axis=-1, keepdims=True)
                    probs = (e * (1.0 / total)).astype(BF)
                    outs.append(nn(probs, v))
                    lane = lax.broadcasted_iota(jnp.int32, (1, 128), 1)
                    lse[qs, :] = jnp.where(lane == 2 * p + h, top + jnp.log(total), lse[qs, :])
                joined[qs, ps] = jnp.where(head == 0, outs[0], outs[1]).astype(BF)

    def lower(j):
        rows = rows_at(j, size)
        tile = 512

        @pl.loop(0, d // tile)
        def _(t):
            branch[rows, rows_at(t, tile)] = nn(joined[rows, :], w_dn[:, rows_at(t, tile)]).astype(BF)

    def back_down(j):
        rows = rows_at(j, size)
        tile = 512
        attn_grad[rows, :] = nt(cots[rows, :], w_dn[:width, :]).astype(BF)

        @pl.loop(0, ff // tile)
        def _(t):
            g = nt(cots[rows, :], w_dn[pl.ds(pl.multiple_of(width + t * tile, tile), tile), :])
            cs = rows_at(t, tile)
            up_grad[rows, cs] = (g * slope[rows, cs].astype(F32)).astype(BF)

    signals = 3 + jnp.where(z > 0, 1, 0) + jnp.where(z < n - 1, 1, 0)
    pl.semaphore_wait(barrier, signals)

    for i in (1, 2, 3):
        loads[i].wait()
    s_qkv.own()
    loads[0].wait()
    lax.fori_loop(0, size // 64, norm, 0)
    l_n.start(0)
    loads[4].wait()
    s_up.own()
    lse[...] = jnp.zeros_like(lse)
    s_qkv.forward()
    l_n.recv(0)
    l_n.start(1)
    s_qkv.last()
    loads[5].wait()
    loads[6].wait()
    s_dn[0].own()
    s_qkv.ready()
    project(order[0])
    s_up.forward()
    project(order[1])
    l_n.recv(1)
    l_n.start(2)
    s_up.last()
    s_dn[1].own()
    project(order[2])
    s_up.ready()
    raise_(order[0])
    s_dn[0].forward()
    raise_(order[1])
    l_n.recv(2)
    loads[7].wait()
    l_c.start(0)
    s_dn[0].last()
    project(order[3])
    raise_(order[2])
    s_dn[1].forward()
    raise_(order[3])
    attend(0, 2)
    l_c.recv(0)
    l_c.start(1)
    s_dn[1].last()
    attend(2, 2)
    lse_out[...] = lse[...].T[: lse_out.shape[0], :]
    for s in s_dn:
        s.ready()
    back_down(order[0])
    back_down(order[1])
    l_c.recv(1)
    l_c.start(2)
    lower(order[0])
    lower(order[1])
    lower(order[2])
    lower(order[3])
    back_down(order[2])
    l_c.recv(2)
    back_down(order[3])
    l_n.finish()
    l_c.finish()
    copies.finish()


def tables(length):
    half = ROT_DIM // 2
    freqs = rope_base ** (-(np.arange(half).astype(np.float32) * 2.0 / ROT_DIM))
    angles = np.arange(length).astype(np.float32)[:, None] * freqs[None, :].astype(np.float32)
    cos, sin = np.cos(angles), np.sin(angles)
    rest = np.zeros((length, HEAD_DIM - ROT_DIM), np.float32)
    none = np.zeros((length, half), np.float32)
    c = np.concatenate([cos, cos, rest + 1.0], 1)
    s1 = np.concatenate([-sin, none, rest], 1)
    s2 = np.concatenate([none, sin, rest], 1)
    return jnp.asarray(np.stack([np.concatenate([t, t], 1) for t in (c, s1, s2)]).astype(np.float32))


def forward_call(n, prefix, x, cot, wq, wk, wv, wo, wu, wd, gain, bias, bq, bk, bv, bu):
    size, d = x.shape
    length, width, ff = n * size, wq.shape[1], wu.shape[1]
    vm, hbm = pl.BlockSpec(memory_space=pltpu.VMEM), pl.BlockSpec(memory_space=pl.ANY)
    shape = lambda s, t=BF: jax.ShapeDtypeStruct(s, t)
    return pl.pallas_call(
        functools.partial(gather_forward, n),
        out_shape=(
            shape((length, d)),
            shape((length, d)),
            shape((d, 3 * width)),
            shape((d, ff)),
            shape((length, 3 * width)),
            shape((length, width + ff)),
            shape((length, d)),
            shape((length, width)),
            shape((length, ff)),
            shape((width // HEAD_DIM, length), F32),
        ),
        in_specs=[pl.BlockSpec(memory_space=pltpu.SMEM)] + [hbm] * 8 + [vm] * 5,
        out_specs=(vm,) * 10,
        scratch_shapes=[
            pltpu.VMEM((width + ff, d), BF),
            pltpu.VMEM((length, ff), BF),
            pltpu.VMEM((size, d), BF),
            pltpu.VMEM((length, 128), F32),
            pltpu.SemaphoreType.DMA((48,)),
            pltpu.SemaphoreType.DMA((48,)),
            pltpu.SemaphoreType.DMA((8,)),
        ],
        compiler_params=pltpu.CompilerParams(
            collective_id=1, has_side_effects=True, vmem_limit_bytes=63 << 20
        ),
        cost_estimate=pl.CostEstimate(flops=50_000_000_000, bytes_accessed=100_000_000, transcendentals=0),
    )(
        prefix,
        x,
        cot,
        wq,
        wk,
        wv,
        wo,
        wu,
        wd,
        gain[None],
        bias[None],
        jnp.concatenate([bq, bk, bv])[None],
        bu[None],
        tables(length),
    )


class Fold:
    def __init__(self, part, slots, send, recv, first, size, n, me, z):
        self.part, self.slots, self.send, self.recv, self.first = part, slots, send, recv, first
        self.size, self.n, self.me, self.z = size, n, me, z

    def copy(self, way, s, block):
        z, n = self.z, self.n
        to = jnp.minimum(z + 1, n - 1) if way == 0 else jnp.maximum(z - 1, 0)
        return pltpu.make_async_remote_copy(
            self.part.at[rows_at(block, self.size), :],
            self.slots.at[way, s],
            self.send.at[self.first + way * (n - 1) + s],
            self.recv.at[self.first + way * (n - 1) + s],
            device_id=(self.me, to),
            device_id_type=MESH,
        )

    def step(self, tau):
        n = self.n
        for way in range(2):
            far = self.z if way == 0 else n - 1 - self.z
            s = jnp.clip(tau - far, 0, n - 2)
            goal = n - 1 - s if way == 0 else s
            if tau > 0:

                @pl.when((far >= 1) & (far <= tau))
                def _():
                    self.copy(way, s, goal).wait_recv()

            if 0 < tau < n - 1:

                @pl.when((far >= 1) & (far <= tau))
                def _():
                    @pl.loop(0, self.size // 64)
                    def _(r):
                        rows = pl.ds(pl.multiple_of(goal * self.size + r * 64, 64), 64)
                        self.part[rows, :] = (
                            self.part[rows, :].astype(F32) + self.slots[way, s, rows_at(r, 64), :].astype(F32)
                        ).astype(BF)

            if tau < n - 1:

                @pl.when(far <= tau)
                def _():
                    self.copy(way, s, goal).start()

    def own(self, r, count):
        z, n = self.z, self.n
        up = self.slots[0, jnp.clip(n - 1 - z, 0, n - 2), rows_at(r, count), :].astype(F32)
        down = self.slots[1, jnp.clip(z, 0, n - 2), rows_at(r, count), :].astype(F32)
        here = self.part[pl.ds(pl.multiple_of(z * self.size + r * count, count), count), :].astype(F32)
        up = jnp.where(z > 0, up, jnp.zeros_like(up))
        down = jnp.where(z < n - 1, down, jnp.zeros_like(down))
        return here + up + down

    def finish(self):
        n = self.n
        for s in range(n - 1):
            for way in range(2):
                far = self.z if way == 0 else n - 1 - self.z

                @pl.when(n - 1 - s - far > 0)
                def _():
                    self.copy(way, s, self.z).wait_send()


PIECE = 512
OWN_SLOTS = 4
SIB_SLOTS = 4
LAG = 2
LINK_SLOTS = 2 + 2 * LAG


def backward_scatter(
    n,
    prefix,
    x,
    normed,
    cots,
    w_qkv,
    w_up,
    qkv,
    joined,
    branch,
    attn_grad,
    up_grad,
    lse,
    table,
    gain,
    b_sum,
    layer_out,
    d_input,
    d_in,
    d_dn,
    d_bias,
    d_all,
    own_x,
    cot,
    grads,
    d_attn,
    n_block,
    n_turned,
    j_block,
    j_turned,
    wq_block,
    wu_block,
    part_b,
    part_g,
    fold_slots,
    sib_out,
    sib_in,
    own_low,
    own_sum,
    link_in,
    acc,
    d_rows,
    narrow,
    wide,
    wide_z,
    sums,
    fold_send,
    fold_recv,
    sib_send,
    sib_recv,
    link_send,
    link_recv,
    out_sem,
    local,
    stream,
    small_send,
    small_recv,
    zfree,
):
    me, z = lax.axis_index("dp"), lax.axis_index("tensor")
    size, d = x.shape
    length = n * size
    width = attn_grad.shape[1]
    ff = up_grad.shape[1]
    lanes = d // 8
    down_pieces = (width + ff) // PIECE
    up_pieces = (3 * width + ff) // PIECE
    pieces = down_pieces + up_pieces
    core = lax.rem(me, 2)
    sib = (flip(me, 1), z)

    barrier = pltpu.get_barrier_semaphore()
    peers = []
    for k in range(1, 8):
        to = me
        for bit in (1, 2, 4):
            if k & bit:
                to = flip(to, bit)
        peers.append(to)
        pl.semaphore_signal(barrier, 1, device_id=(to, z), device_id_type=MESH)
    others = [lax.rem(z + k, n) for k in range(1, n)]
    for to in others:
        pl.semaphore_signal(barrier, 1, device_id=(me, to), device_id_type=MESH)

    def load(k, src, dst):
        return pltpu.make_async_copy(src, dst, local.at[k])

    loads = [
        load(0, branch, part_b),
        load(1, cots, cot),
        load(2, qkv, grads.at[:, pl.ds(0, 3 * width)]),
        load(3, attn_grad, d_attn),
        load(4, up_grad, grads.at[:, pl.ds(3 * width, ff)]),
        load(5, x, own_x),
    ]

    def j_load(p):
        return pltpu.make_async_copy(
            joined.at[:, rows_at(jnp.minimum(p, down_pieces - 1), PIECE)],
            j_block.at[lax.rem(p, 2)],
            stream.at[lax.rem(p, 2)],
        )

    def w_loads(t):
        return [
            pltpu.make_async_copy(w_qkv.at[rows_at(t, PIECE), :], wq_block, stream.at[2]),
            pltpu.make_async_copy(w_up.at[rows_at(t, PIECE), :], wu_block, stream.at[3]),
        ]

    def n_load(j):
        return pltpu.make_async_copy(normed.at[rows_at(j, size), :], n_block, stream.at[4])

    j_load(0).start()
    for l in loads:
        l.start()
    for l in w_loads(0) + [n_load(0)]:
        l.start()

    fold_b = Fold(part_b, fold_slots, fold_send, fold_recv, 0, size, n, me, z)
    fold_g = Fold(part_g, fold_slots, fold_send, fold_recv, 2 * (n - 1), size, n, me, z)

    links = [flip(flip(me, 2), 4), flip(me, 2), flip(me, 4)]
    goals = links + [me]

    def sib_copy(p):
        return pltpu.make_async_remote_copy(
            sib_out.at[lax.rem(p, 2)],
            sib_in.at[lax.rem(p, SIB_SLOTS)],
            sib_send.at[lax.rem(p, 2)],
            sib_recv.at[lax.rem(p, SIB_SLOTS)],
            device_id=sib,
            device_id_type=MESH,
        )

    def link_copy(p, r):
        return pltpu.make_async_remote_copy(
            own_low.at[lax.rem(p, OWN_SLOTS), r],
            link_in.at[lax.rem(p, LINK_SLOTS), r],
            link_send.at[lax.rem(p, OWN_SLOTS), r],
            link_recv.at[lax.rem(p, LINK_SLOTS), r],
            device_id=(links[r], z),
            device_id_type=MESH,
        )

    def out_copies(p):
        src = own_sum.at[lax.rem(p, OWN_SLOTS)]
        sem = out_sem.at[lax.rem(p, OWN_SLOTS)]
        half = PIECE // 2
        down = [
            pltpu.make_async_copy(
                src.at[:, pl.ds(i * half, half)],
                d_dn.at[pl.ds(pl.multiple_of(jnp.minimum(p, down_pieces - 1) * PIECE + i * half, half), half), :],
                sem.at[i],
            )
            for i in range(2)
        ]
        up = [
            pltpu.make_async_copy(
                src.at[:, pl.ds(i * half, half)],
                d_in.at[
                    :,
                    pl.ds(
                        pl.multiple_of(up_column(p) + i * half, half),
                        half,
                    ),
                ],
                sem.at[i],
            )
            for i in range(2)
        ]
        return down, up

    def up_column(p):
        t = jnp.clip(p - down_pieces, 0, up_pieces - 1)
        return lax.rem(t + 3 * width // PIECE, up_pieces) * PIECE

    def first_down(p):
        slot, out = lax.rem(p, OWN_SLOTS), lax.rem(p, 2)
        j_load(p).wait()

        @pl.when(p + 1 < down_pieces)
        def _():
            j_load(p + 1).start()

        j_turned[...] = j_block[lax.rem(p, 2)].T
        half = PIECE // 2
        for r, goal in enumerate(goals):
            for mine in range(2):
                to = flip(goal, 1) if mine == 0 else goal
                t = nn(j_turned[...], cot[:, rows_at(to, lanes)])
                for i in range(2):
                    v = t[i * half : (i + 1) * half, :]
                    cs = pl.ds(i * half, half)
                    if mine == 0:
                        sib_out[out, r, :, cs] = v.astype(BF)
                    elif r < 3:
                        own_low[slot, r, :, cs] = v.astype(BF)
                    else:
                        own_sum[slot, :, cs] = v

    def first_up(p):
        slot, out = lax.rem(p, OWN_SLOTS), lax.rem(p, 2)
        g = grads[:, pl.ds(pl.multiple_of(up_column(p), PIECE), PIECE)]
        for r, goal in enumerate(goals):
            for mine in range(2):
                to = flip(goal, 1) if mine == 0 else goal
                t = nn(n_turned[rows_at(to, lanes), :], g)
                if mine == 0:
                    sib_out[out, r] = t.astype(BF)
                elif r < 3:
                    own_low[slot, r] = t.astype(BF)
                else:
                    own_sum[slot] = t

    def stage_one(p):
        @pl.when(p >= 2)
        def _():
            sib_copy(p - 2).wait_send()

        @pl.when(p >= OWN_SLOTS)
        def _():
            for c in out_copies(p - OWN_SLOTS)[0]:
                c.wait()

        @pl.when(p < down_pieces)
        def _():
            first_down(p)

        @pl.when(p >= down_pieces)
        def _():
            first_up(p)

        sib_copy(p).start()

    def stage_two(p):
        slot = lax.rem(p, OWN_SLOTS)
        inn = lax.rem(p, SIB_SLOTS)
        sib_copy(p).wait_recv()
        for r in range(3):
            own_low[slot, r] = (own_low[slot, r].astype(F32) + sib_in[inn, r].astype(F32)).astype(BF)
            link_copy(p, r).start()
        own_sum[slot] = own_sum[slot] + sib_in[inn, 3].astype(F32)

    def stage_three(p):
        slot = lax.rem(p, OWN_SLOTS)
        inn = lax.rem(p, LINK_SLOTS)
        for r in range(3):
            link_copy(p, r).wait_recv()
        own_sum[slot] = (
            (own_sum[slot] + link_in[inn, 0].astype(F32)) + link_in[inn, 1].astype(F32)
        ) + link_in[inn, 2].astype(F32)
        for r in range(3):
            link_copy(p, r).wait_send()
        down, up = out_copies(p)

        @pl.when(p < down_pieces)
        def _():
            for c in down:
                c.start()

        @pl.when(p >= down_pieces)
        def _():
            for c in up:
                c.start()

    def attend_back(p):
        block = length // 4
        ps = rows_at(p, 128)
        ks = pl.ds(pl.multiple_of(width + p * 128, 128), 128)
        vs = pl.ds(pl.multiple_of(2 * width + p * 128, 128), 128)
        head = lax.broadcasted_iota(jnp.int32, (1, 128), 1) // HEAD_DIM
        acc[...] = jnp.zeros_like(acc)
        for b in range(4):
            nk = max(b + 1, 2) * block
            qs, kr = pl.ds(b * block, block), pl.ds(0, nk)
            limit = jnp.maximum(
                b * block + lax.broadcasted_iota(jnp.int32, (1, block), 1), prefix[0] - 1
            )

            @pl.loop(0, 2)
            def _(h):
                only = lambda a: jnp.where(head == h, a, jnp.zeros_like(a))
                k, v = grads[kr, ks], grads[kr, vs]
                qh, gh = only(grads[qs, ps]), only(d_attn[qs, ps])
                s = nt(k, qh)
                seen = lax.broadcasted_iota(jnp.int32, (nk, block), 0) <= limit
                probs = jnp.where(seen, jnp.exp(s - lse[pl.ds(2 * p + h, 1), qs]), 0.0)
                acc[2, kr, :] += nn(probs.astype(BF), gh)
                dp = nt(v, gh)
                delta = jnp.sum(probs * dp, axis=0, keepdims=True)
                ds = (probs * (dp - delta)).astype(BF)
                acc[1, kr, :] += nn(ds, qh)
                acc[0, qs, :] += tn(ds, only(k)) * (1.0 / math.sqrt(HEAD_DIM))

        tab = [table[i] for i in range(3)]
        grads[:, ps] = turned(acc[0], tab, -1.0).astype(BF)
        grads[:, ks] = turned(acc[1], tab, -1.0).astype(BF)
        grads[:, vs] = acc[2].astype(BF)

    def normed_back(t):
        for l in w_loads(t):
            l.wait()

        @pl.loop(0, length // 512)
        def _(m):
            rows = rows_at(m, 512)
            part_g[rows, t * PIECE : (t + 1) * PIECE] = (
                nt(grads[rows, : 3 * width], wq_block[...]) + nt(grads[rows, 3 * width :], wu_block[...])
            ).astype(BF)

        if t + 1 < d // PIECE:
            for l in w_loads(t + 1):
                l.start()

    def turn(j):
        n_load(j).wait()
        n_turned[:, j * size : (j + 1) * size] = n_block[...].T
        if j + 1 < n:
            n_load(j + 1).start()

    def small(k, src, dst, to):
        return pltpu.make_async_remote_copy(
            src, dst, small_send.at[k], small_recv.at[k], device_id=to, device_id_type=MESH
        )

    def bias_sums():
        for i in range(up_pieces):
            narrow[me, i : i + 1, :] = jnp.sum(
                grads[:, i * PIECE : (i + 1) * PIECE].astype(F32), axis=0, keepdims=True
            )
        for k, to in enumerate(peers):
            small(k, narrow.at[me], narrow.at[me], (to, z)).start()

    def branch_end():
        loads[5].wait()

        @pl.loop(0, size // 32)
        def _(r):
            rows = pl.ds(pl.multiple_of(z * size + r * 32, 32), 32)
            v = own_x[rows_at(r, 32), :].astype(F32) + fold_b.own(r, 32) + b_sum[0:1, :] + b_sum[1:2, :]
            part_b[rows, :] = v.astype(BF)

        out = load(0, part_b.at[rows_at(z, size), :], layer_out)
        out.start()
        fold_b.finish()

        @pl.when(z > 0)
        def _():
            pl.semaphore_signal(zfree.at[0], 1, device_id=(me, jnp.maximum(z - 1, 0)), device_id_type=MESH)

        @pl.when(z < n - 1)
        def _():
            pl.semaphore_signal(zfree.at[1], 1, device_id=(me, jnp.minimum(z + 1, n - 1)), device_id_type=MESH)

        out.wait()

    def fold_free():
        @pl.when(z < n - 1)
        def _():
            pl.semaphore_wait(zfree.at[0], 1)

        @pl.when(z > 0)
        def _():
            pl.semaphore_wait(zfree.at[1], 1)

    def input_end():
        sums[...] = jnp.zeros_like(sums)

        def chunk(r):
            return pltpu.make_async_copy(
                d_rows.at[lax.rem(r, 2)], d_input.at[rows_at(r, 32), :], local.at[lax.rem(r, 2)]
            )

        @pl.loop(0, size // 32)
        def _(r):
            grad = fold_g.own(r, 32)
            v = own_x[rows_at(r, 32), :].astype(F32)
            c = v - jnp.mean(v, axis=-1, keepdims=True)
            inv = lax.rsqrt(jnp.mean(c * c, axis=-1, keepdims=True) + epsilon)
            unit = c * inv
            own_cot = cot[pl.ds(pl.multiple_of(z * size + r * 32, 32), 32), :].astype(F32)
            gu = grad * unit
            sums[0:1, :] += jnp.sum(gu, axis=0, keepdims=True)
            sums[1:2, :] += jnp.sum(grad, axis=0, keepdims=True)
            sums[2:3, :] += jnp.sum(own_cot, axis=0, keepdims=True)
            scaled = grad * gain[...]

            @pl.when(r >= 2)
            def _():
                chunk(r - 2).wait()

            d_rows[lax.rem(r, 2)] = own_cot + inv * (
                scaled
                - jnp.mean(scaled, axis=-1, keepdims=True)
                - unit * jnp.mean(scaled * unit, axis=-1, keepdims=True)
            )
            chunk(r).start()

        for i in range(3):
            for q in range(4):
                wide[me, 4 * i + q : 4 * i + q + 1, :] = sums[i : i + 1, q * PIECE : (q + 1) * PIECE]
        for k, to in enumerate(peers):
            small(8 + k, wide.at[me], wide.at[me], (to, z)).start()
        for k, to in enumerate(peers):
            small(8 + k, wide.at[to], wide.at[to], (to, z)).wait_recv()
        total = wide[0]
        for i in range(1, 8):
            total = total + wide[i]
        wide_z[z] = total
        for k, to in enumerate(others):
            small(16 + k, wide_z.at[z], wide_z.at[z], (me, to)).start()
        for k in range(n - 1):
            origin = lax.rem(z + n - 1 - k, n)
            small(16 + k, wide_z.at[origin], wide_z.at[origin], (me, origin)).wait_recv()
        total = wide_z[0]
        for i in range(1, n):
            total = total + wide_z[i]
        d_all[...] = total
        for k, to in enumerate(peers):
            small(k, narrow.at[to], narrow.at[to], (to, z)).wait_recv()
        total = narrow[0]
        for i in range(1, 8):
            total = total + narrow[i]
        d_bias[...] = total
        for k, to in enumerate(peers):
            small(k, narrow.at[me], narrow.at[me], (to, z)).wait_send()
            small(8 + k, wide.at[me], wide.at[me], (to, z)).wait_send()
        for k, to in enumerate(others):
            small(16 + k, wide_z.at[z], wide_z.at[z], (me, to)).wait_send()
        for r in range(2):
            chunk(size // 32 - 2 + r).wait()

    narrow[me] = jnp.zeros(narrow.shape[1:], F32)
    wide[me] = jnp.zeros(wide.shape[1:], F32)
    pl.semaphore_wait(barrier, 7 + n - 1)

    tasks = {}

    def at(p, *work):
        tasks.setdefault(p, []).extend(work)

    loads[0].wait()
    fold_b.step(0)
    for l in loads[1:5]:
        l.wait()

    at(2, lambda: fold_b.step(1))
    at(4, lambda: turn(0), lambda: normed_back(0), lambda: turn(1), bias_sums, lambda: turn(2), lambda: fold_b.step(2))
    at(4, lambda: turn(3))
    at(5, lambda: normed_back(1))
    at(6, lambda: normed_back(2))
    at(7, lambda: normed_back(3), lambda: fold_b.step(3), branch_end, fold_free, lambda: fold_g.step(0))
    at(9, lambda: fold_g.step(1))
    at(11, lambda: fold_g.step(2))
    at(13, lambda: fold_g.step(3))

    @pl.loop(0, pieces + 1 + LAG)
    def _(p):
        @pl.when(p < pieces)
        def _():
            stage_one(p)

        @pl.when((p >= 1) & (p <= pieces))
        def _():
            stage_two(p - 1)

        @pl.when(p >= 1 + LAG)
        def _():
            stage_three(p - 1 - LAG)

        @pl.when(p < width // 128)
        def _():
            attend_back(p)

        for k, work in tasks.items():

            @pl.when(p == k)
            def _():
                for w in work:
                    w()

    for p in range(2):
        sib_copy(pieces - 2 + p).wait_send()
    for p in range(OWN_SLOTS):
        for c in out_copies(pieces - OWN_SLOTS + p)[1]:
            c.wait()
    input_end()
    fold_g.finish()


def backward_call(n, prefix, x, normed, cots, w_qkv, w_up, qkv, joined, branch, attn_grad, up_grad, lse, gain, b_out, b_down):
    size, d = x.shape
    length, width, ff = n * size, attn_grad.shape[1], up_grad.shape[1]
    vm, hbm = pl.BlockSpec(memory_space=pltpu.VMEM), pl.BlockSpec(memory_space=pl.ANY)
    shape = lambda s, t=BF: jax.ShapeDtypeStruct(s, t)
    dma = pltpu.SemaphoreType.DMA
    half = PIECE // 2
    return pl.pallas_call(
        functools.partial(backward_scatter, n),
        out_shape=(
            shape((size, d)),
            shape((size, d), F32),
            shape((d // 8, 3 * width + ff), F32),
            shape((width + ff, d // 8), F32),
            shape((8, PIECE), F32),
            shape((16, PIECE), F32),
        ),
        in_specs=[pl.BlockSpec(memory_space=pltpu.SMEM)] + [hbm] * 10 + [vm] * 4,
        out_specs=(hbm,) * 4 + (vm,) * 2,
        scratch_shapes=[
            pltpu.VMEM((size, d), BF),
            pltpu.VMEM((length, d), BF),
            pltpu.VMEM((length, 3 * width + ff), BF),
            pltpu.VMEM((length, width), BF),
            pltpu.VMEM((size, d), BF),
            pltpu.VMEM((d, length), BF),
            pltpu.VMEM((2, length, PIECE), BF),
            pltpu.VMEM((PIECE, length), BF),
            pltpu.VMEM((PIECE, 3 * width), BF),
            pltpu.VMEM((PIECE, ff), BF),
            pltpu.VMEM((length, d), BF),
            pltpu.VMEM((length, d), BF),
            pltpu.VMEM((2, n - 1, size, d), BF),
            pltpu.VMEM((2, 4, half, PIECE), BF),
            pltpu.VMEM((SIB_SLOTS, 4, half, PIECE), BF),
            pltpu.VMEM((OWN_SLOTS, 3, half, PIECE), BF),
            pltpu.VMEM((OWN_SLOTS, half, PIECE), F32),
            pltpu.VMEM((LINK_SLOTS, 3, half, PIECE), BF),
            pltpu.VMEM((3, length, 128), F32),
            pltpu.VMEM((2, 32, d), F32),
            pltpu.VMEM((8, 8, PIECE), F32),
            pltpu.VMEM((8, 16, PIECE), F32),
            pltpu.VMEM((n, 16, PIECE), F32),
            pltpu.VMEM((8, d), F32),
            dma((4 * (n - 1),)),
            dma((4 * (n - 1),)),
            dma((2,)),
            dma((SIB_SLOTS,)),
            dma((OWN_SLOTS, 3)),
            dma((LINK_SLOTS, 3)),
            dma((OWN_SLOTS, 2)),
            dma((6,)),
            dma((5,)),
            dma((16 + n - 1,)),
            dma((16 + n - 1,)),
            pltpu.SemaphoreType.REGULAR((2,)),
        ],
        compiler_params=pltpu.CompilerParams(
            collective_id=2, has_side_effects=True, vmem_limit_bytes=63 << 20
        ),
        cost_estimate=pl.CostEstimate(flops=60_000_000_000, bytes_accessed=100_000_000, transcendentals=0),
    )(
        prefix, x, normed, cots, w_qkv, w_up, qkv, joined, branch, attn_grad, up_grad, lse,
        tables(length), gain[None], jnp.stack([b_out, b_down]),
    )


def rotate(tensor, positions, direction):
    half_dim = ROT_DIM // 2
    freqs = rope_base ** (-(jnp.arange(half_dim).astype(jnp.float32) * 2.0 / ROT_DIM))
    angles = positions.astype(jnp.float32)[:, None] * freqs[None, :]
    cosine = jnp.cos(angles)[:, None, :]
    sine = direction * jnp.sin(angles)[:, None, :]
    first = tensor[..., :half_dim]
    second = tensor[..., half_dim:ROT_DIM]
    return jnp.concatenate(
        [first * cosine - second * sine, second * cosine + first * sine, tensor[..., ROT_DIM:]],
        axis=-1,
    )


def times_transposed(left, right):
    return lax.dot_general(
        left, right, (((1,), (1,)), ((), ())), preferred_element_type=jnp.float32
    )


def rows_transposed(left, right):
    return lax.dot_general(
        left, right, (((0,), (0,)), ((), ())), preferred_element_type=jnp.float32
    )


def plain_on_device(
    layer_input,
    ln_gain,
    ln_bias,
    w_query,
    b_query,
    w_key,
    b_key,
    w_value,
    b_value,
    w_out,
    b_out,
    w_up,
    b_up,
    w_down,
    b_down,
    prefix,
    cotangent,
):
    local_width = w_query.shape[1]
    hidden_here = w_up.shape[1]
    heads_here = local_width // HEAD_DIM
    score_scale = 1.0 / math.sqrt(HEAD_DIM)
    prefix_len = prefix[0]
    input_float = layer_input.astype(jnp.float32)
    row_mean = jnp.mean(input_float, axis=-1, keepdims=True)
    centred = input_float - row_mean
    inverse = lax.rsqrt(jnp.mean(centred * centred, axis=-1, keepdims=True) + epsilon)
    unit_rows = centred * inverse
    normed = (unit_rows * ln_gain + ln_bias).astype(jnp.bfloat16)
    normed_all = lax.all_gather(normed, "tensor", axis=0, tiled=True)
    length = normed_all.shape[0]
    positions = jnp.arange(length)
    block_rows = min(512, length)
    block_count = length // block_rows
    pieces = (
        lax.all_gather(w_query, "dp", axis=0, tiled=True),
        lax.all_gather(w_key, "dp", axis=0, tiled=True),
        lax.all_gather(w_value, "dp", axis=0, tiled=True),
        lax.all_gather(w_up, "dp", axis=0, tiled=True),
    )
    columns = normed_all
    query_acc, key_acc, value_acc, up_acc = tuple(
        (jnp.dot(columns, piece, preferred_element_type=jnp.float32) for piece in pieces)
    )
    query_pre = (query_acc + b_query).reshape(length, heads_here, HEAD_DIM)
    key_pre = (key_acc + b_key).reshape(length, heads_here, HEAD_DIM)
    query = rotate(query_pre, positions, 1.0).astype(jnp.bfloat16)
    key = rotate(key_pre, positions, 1.0).astype(jnp.bfloat16)
    value = (value_acc + b_value).reshape(length, heads_here, HEAD_DIM).astype(jnp.bfloat16)
    up_pre = up_acc + b_up
    hidden = jax.nn.gelu(up_pre, approximate=True).astype(jnp.bfloat16)

    def scores_for(query_rows, offset):
        raw = (
            jnp.einsum("qhd,khd->hqk", query_rows, key, preferred_element_type=jnp.float32)
            * score_scale
        )
        query_pos = offset + jnp.arange(block_rows)
        seen = (positions[None, :] <= query_pos[:, None]) | (positions[None, :] < prefix_len)
        return jnp.where(seen[None], raw, masked_score)

    def attend_block(index):
        offset = index * block_rows
        query_rows = lax.dynamic_slice_in_dim(query, offset, block_rows, 0)
        scores = scores_for(query_rows, offset)
        row_max = jnp.max(scores, axis=-1, keepdims=True)
        expo = jnp.exp(scores - row_max)
        totals = jnp.sum(expo, axis=-1, keepdims=True)
        probs_low = (expo / totals).astype(jnp.bfloat16)
        out_rows = jnp.einsum("hqk,khd->qhd", probs_low, value, preferred_element_type=jnp.float32)
        return (out_rows, (row_max + jnp.log(totals))[..., 0])

    indices = jnp.arange(block_count)
    out_blocks, log_totals = lax.map(attend_block, indices)
    attn = out_blocks.reshape(length, local_width).astype(jnp.bfloat16)
    pieces = (
        lax.all_gather(w_out, "dp", axis=1, tiled=True),
        lax.all_gather(w_down, "dp", axis=1, tiled=True),
    )
    part = jnp.dot(attn, pieces[0], preferred_element_type=jnp.float32) + jnp.dot(
        hidden, pieces[1], preferred_element_type=jnp.float32
    )
    partial_value = part
    branch = lax.psum_scatter(partial_value, "tensor", scatter_dimension=0, tiled=True)
    layer_out = (input_float + branch + b_out + b_down).astype(jnp.bfloat16)
    grad_all = lax.all_gather(cotangent, "tensor", axis=0, tiled=True)
    pieces = (
        lax.all_gather(w_out, "dp", axis=1, tiled=True),
        lax.all_gather(w_down, "dp", axis=1, tiled=True),
    )
    columns = grad_all
    attn_grad = times_transposed(columns, pieces[0])
    hidden_grad = times_transposed(columns, pieces[1])
    down_joined = jnp.concatenate([attn, hidden], axis=1)
    unused, gelu_pull = jax.vjp(lambda inner: jax.nn.gelu(inner, approximate=True), up_pre)
    up_grad_low = gelu_pull(hidden_grad)[0].astype(jnp.bfloat16)
    attn_grad_low = attn_grad.astype(jnp.bfloat16).reshape(length, heads_here, HEAD_DIM)

    def back_block(carry, item):
        key_grad, value_grad = carry
        index, lse_rows = item
        offset = index * block_rows
        query_rows = lax.dynamic_slice_in_dim(query, offset, block_rows, 0)
        grad_rows = lax.dynamic_slice_in_dim(attn_grad_low, offset, block_rows, 0)
        scores = scores_for(query_rows, offset)
        probs = jnp.exp(scores - lse_rows[..., None])
        value_grad = value_grad + jnp.einsum(
            "hqk,qhd->khd",
            probs.astype(jnp.bfloat16),
            grad_rows,
            preferred_element_type=jnp.float32,
        )
        prob_grad = jnp.einsum("qhd,khd->hqk", grad_rows, value, preferred_element_type=jnp.float32)
        delta = jnp.sum(probs * prob_grad, axis=-1, keepdims=True)
        score_grad = (probs * (prob_grad - delta)).astype(jnp.bfloat16)
        query_grad = (
            jnp.einsum("hqk,khd->qhd", score_grad, key, preferred_element_type=jnp.float32)
            * score_scale
        )
        key_grad = (
            key_grad
            + jnp.einsum("hqk,qhd->khd", score_grad, query_rows, preferred_element_type=jnp.float32)
            * score_scale
        )
        return ((key_grad, value_grad), query_grad)

    state_zeros = jnp.zeros((length, heads_here, HEAD_DIM), jnp.float32)
    (key_grad, value_grad), query_blocks = lax.scan(
        back_block, (state_zeros, state_zeros), (indices, log_totals)
    )
    query_grad = query_blocks.reshape(length, heads_here, HEAD_DIM)
    q_grad_low = (
        rotate(query_grad, positions, -1.0).reshape(length, local_width).astype(jnp.bfloat16)
    )
    k_grad_low = rotate(key_grad, positions, -1.0).reshape(length, local_width).astype(jnp.bfloat16)
    v_grad_low = value_grad.reshape(length, local_width).astype(jnp.bfloat16)
    up_joined = jnp.concatenate([q_grad_low, k_grad_low, v_grad_low, up_grad_low], axis=1)
    columns = grad_all
    joined_rows = lax.psum_scatter(
        jnp.concatenate(
            [rows_transposed(columns, down_joined), rows_transposed(normed_all, up_joined)], axis=1
        ),
        "dp",
        scatter_dimension=0,
        tiled=True,
    )
    down_rows = joined_rows[:, : local_width + hidden_here]
    up_rows = joined_rows[:, local_width + hidden_here :]
    d_w_out = down_rows[:, :local_width].T
    d_w_down = down_rows[:, local_width:].T
    d_w_query = up_rows[:, :local_width]
    d_w_key = up_rows[:, local_width : 2 * local_width]
    d_w_value = up_rows[:, 2 * local_width : 3 * local_width]
    d_w_up = up_rows[:, 3 * local_width :]
    pieces = (
        lax.all_gather(w_query, "dp", axis=0, tiled=True),
        lax.all_gather(w_key, "dp", axis=0, tiled=True),
        lax.all_gather(w_value, "dp", axis=0, tiled=True),
        lax.all_gather(w_up, "dp", axis=0, tiled=True),
    )
    part = (
        times_transposed(q_grad_low, pieces[0])
        + times_transposed(k_grad_low, pieces[1])
        + times_transposed(v_grad_low, pieces[2])
        + times_transposed(up_grad_low, pieces[3])
    )
    own_grad = lax.psum_scatter(part, "tensor", scatter_dimension=0, tiled=True)
    scaled_grad = own_grad * ln_gain
    norm_part = inverse * (
        scaled_grad
        - jnp.mean(scaled_grad, axis=-1, keepdims=True)
        - unit_rows * jnp.mean(scaled_grad * unit_rows, axis=-1, keepdims=True)
    )
    cot_float = cotangent.astype(jnp.float32)
    d_input = cot_float + norm_part
    d_ln_gain, d_ln_bias, d_b_out = lax.psum(
        (
            jnp.sum(own_grad * unit_rows, axis=0),
            jnp.sum(own_grad, axis=0),
            jnp.sum(cot_float, axis=0),
        ),
        ("dp", "tensor"),
    )
    d_b_query, d_b_key, d_b_value, d_b_up = lax.psum(
        (
            jnp.sum(q_grad_low.astype(jnp.float32), axis=0),
            jnp.sum(k_grad_low.astype(jnp.float32), axis=0),
            jnp.sum(v_grad_low.astype(jnp.float32), axis=0),
            jnp.sum(up_grad_low.astype(jnp.float32), axis=0),
        ),
        "dp",
    )
    return (
        layer_out,
        d_input,
        d_ln_gain,
        d_ln_bias,
        d_w_query,
        d_b_query,
        d_w_key,
        d_b_key,
        d_w_value,
        d_b_value,
        d_w_out,
        d_b_out,
        d_w_up,
        d_b_up,
        d_w_down,
        d_b_out,
    )


def on_device(
    layer_input, ln_gain, ln_bias, w_query, b_query, w_key, b_key, w_value, b_value,
    w_out, b_out, w_up, b_up, w_down, b_down, prefix, cotangent,
):
    n = lax.axis_size("tensor")
    width = w_query.shape[1]
    normed, cots, w_qkv, w_up_all, qkv, joined, branch, attn_grad, up_grad, lse = forward_call(
        n, prefix, layer_input, cotangent, w_query, w_key, w_value, w_out, w_up, w_down,
        ln_gain, ln_bias, b_query, b_key, b_value, b_up,
    )
    layer_out, d_input, d_in, d_dn, d_bias, d_all = backward_call(
        n, prefix, layer_input, normed, cots, w_qkv, w_up_all, qkv, joined, branch, attn_grad,
        up_grad, lse, ln_gain, b_out, b_down,
    )
    flat, bias = d_all.reshape(-1), d_bias.reshape(-1)
    d = layer_input.shape[1]
    d_ln_gain, d_ln_bias, d_b_out = (flat[i * d : (i + 1) * d] for i in range(3))
    d_w_query, d_w_key, d_w_value = (d_in[:, i * width : (i + 1) * width] for i in range(3))
    d_b_query, d_b_key, d_b_value = (bias[i * width : (i + 1) * width] for i in range(3))
    return (
        layer_out, d_input, d_ln_gain, d_ln_bias, d_w_query, d_b_query, d_w_key, d_b_key,
        d_w_value, d_b_value, d_dn[:width], d_b_out, d_in[:, 3 * width :],
        bias[3 * width : 3 * width + w_up.shape[1]], d_dn[width:], d_b_out,
    )


def solution(mesh):
    fits = mesh.shape["dp"] == 8 and mesh.shape["tensor"] == 4
    return jax.shard_map(
        on_device if fits else plain_on_device,
        mesh=mesh,
        in_specs=(
            P(("dp", "tensor"), None),
            P(),
            P(),
            P("dp", "tensor"),
            P("tensor"),
            P("dp", "tensor"),
            P("tensor"),
            P("dp", "tensor"),
            P("tensor"),
            P("tensor", "dp"),
            P(),
            P("dp", "tensor"),
            P("tensor"),
            P("tensor", "dp"),
            P(),
            P("dp"),
            P(("dp", "tensor"), None),
        ),
        out_specs=(
            P(("dp", "tensor"), None),
            P(("dp", "tensor"), None),
            P(),
            P(),
            P("dp", "tensor"),
            P("tensor"),
            P("dp", "tensor"),
            P("tensor"),
            P("dp", "tensor"),
            P("tensor"),
            P("tensor", "dp"),
            P(),
            P("dp", "tensor"),
            P("tensor"),
            P("tensor", "dp"),
            P(),
        ),
        check_vma=False,
    )
```

```python
import functools
import math

import jax
import jax.numpy as jnp
import numpy as np
from jax import lax
from jax.experimental import pallas as pl
from jax.experimental.pallas import tpu as pltpu
from jax.sharding import PartitionSpec as P

HEAD_DIM = 64
ROT_DIM = 32
MESH = pl.DeviceIdType.MESH
BF = jnp.bfloat16
F32 = jnp.float32

epsilon = 1e-05
rope_base = 10000.0
masked_score = -1e30
root = math.sqrt(2.0 / math.pi)


def nn(a, b):
    return jnp.dot(a, b, preferred_element_type=F32)


def nt(a, b):
    return lax.dot_general(a, b, (((1,), (1,)), ((), ())), preferred_element_type=F32)


def tn(a, b):
    return lax.dot_general(a, b, (((0,), (0,)), ((), ())), preferred_element_type=F32)


def rows_at(index, size):
    return pl.ds(pl.multiple_of(index * size, size), size)


def flip(index, bit):
    return index + bit - 2 * bit * lax.rem(index // bit, 2)


class Copies:
    def __init__(self, send, recv):
        self.send, self.recv, self.count, self.sent = send, recv, 0, []

    def new(self):
        self.count += 1
        return self.count - 1

    def make(self, k, src, dst, device):
        return pltpu.make_async_remote_copy(
            src, dst, self.send.at[k], self.recv.at[k], device_id=device, device_id_type=MESH
        )

    def start(self, k, src, dst, device):
        copy = self.make(k, src, dst, device)
        copy.start()
        self.sent.append(copy)

    def wait(self, k, dst, device):
        self.make(k, dst, dst, device).wait_recv()

    def finish(self):
        for copy in self.sent:
            copy.wait_send()


class Spread:
    def __init__(self, copies, view, me, z):
        self.c, self.view, self.me, self.z = copies, view, me, z
        self.k = [copies.new() for _ in range(9)]

    def dev(self, bit):
        return (flip(self.me, bit), self.z)

    def own(self):
        v = self.view(self.me)
        self.c.start(self.k[1], v, v, self.dev(2))
        self.c.start(self.k[2], v, v, self.dev(4))
        self.c.start(self.k[0], v, v, self.dev(1))

    def forward(self):
        c, x, y = self.c, flip(self.me, 2), flip(self.me, 4)
        c.wait(self.k[1], self.view(x), self.dev(2))
        v = self.view(x, 0)
        c.start(self.k[3], v, v, self.dev(4))
        c.wait(self.k[2], self.view(y), self.dev(4))
        v = self.view(y, 1)
        c.start(self.k[4], v, v, self.dev(2))
        v = self.view(x)
        c.start(self.k[5], v, v, self.dev(1))
        v = self.view(y)
        c.start(self.k[6], v, v, self.dev(1))

    def last(self):
        c, far = self.c, flip(flip(self.me, 2), 4)
        c.wait(self.k[3], self.view(far, 0), self.dev(4))
        c.wait(self.k[4], self.view(far, 1), self.dev(2))
        v = self.view(far)
        c.start(self.k[7], v, v, self.dev(1))

    def ready(self):
        c, s = self.c, flip(self.me, 1)
        c.wait(self.k[0], self.view(s), self.dev(1))
        c.wait(self.k[5], self.view(flip(s, 2)), self.dev(1))
        c.wait(self.k[6], self.view(flip(s, 4)), self.dev(1))
        c.wait(self.k[7], self.view(flip(flip(s, 2), 4)), self.dev(1))


class Line:
    CHUNKS = 4

    def __init__(self, copies, buf, size, n, me, z):
        self.c, self.buf, self.size, self.n, self.me, self.z = copies, buf, size // self.CHUNKS, n, me, z
        self.k = [[[copies.new() for _ in range(self.CHUNKS)] for _ in range(2)] for _ in range(n - 1)]

    def copy(self, s, way, c, block):
        z, n = self.z, self.n
        to = jnp.minimum(z + 1, n - 1) if way == 0 else jnp.maximum(z - 1, 0)
        v = self.buf.at[rows_at(jnp.clip(block, 0, n - 1) * self.CHUNKS + c, self.size), :]
        return self.c.make(self.k[s][way][c], v, v, (self.me, to))

    def far(self, way):
        return self.z if way == 0 else self.n - 1 - self.z

    def block(self, way, s):
        return self.z - s if way == 0 else self.z + s

    def own(self, c):
        for way in range(2):

            @pl.when(self.far(way) < self.n - 1)
            def _():
                self.copy(0, way, c, self.z).start()

    def event(self, s, c):
        for way in range(2):
            far = self.far(way)

            @pl.when(far >= s + 1)
            def _():
                self.copy(s, way, c, self.block(way, s + 1)).wait_recv()

            if s + 1 < self.n - 1:

                @pl.when((far >= s + 1) & (far < self.n - 1))
                def _():
                    self.copy(s + 1, way, c, self.block(way, s + 1)).start()

    def finish(self):
        for s in range(self.n - 1):
            for way in range(2):
                far = self.far(way)

                @pl.when((far >= s) & (far < self.n - 1))
                def _():
                    for c in range(self.CHUNKS):
                        self.copy(s, way, c, self.z).wait_send()


class Fold:
    def __init__(self, part, slots, send, recv, tiles, size, n, me, z):
        self.part, self.slots, self.send, self.recv = part, slots, send, recv
        self.tiles, self.size, self.n, self.me, self.z = list(tiles), size, n, me, z

    def far(self, way):
        return self.z if way == 0 else self.n - 1 - self.z

    def copy(self, way, t, i):
        z, n = self.z, self.n
        to = jnp.minimum(z + 1, n - 1) if way == 0 else jnp.maximum(z - 1, 0)
        goal = n - 1 - i if way == 0 else i
        k = self.tiles.index(t) * (n - 1) + i
        return pltpu.make_async_remote_copy(
            self.part.at[goal * self.size : (goal + 1) * self.size, t * PIECE : (t + 1) * PIECE],
            self.slots.at[way, k],
            self.send.at[way, k],
            self.recv.at[way, k],
            device_id=(self.me, to),
            device_id_type=MESH,
        )

    def first(self, t):
        for way in range(2):

            @pl.when(self.far(way) == 0)
            def _():
                for i in range(self.n - 1):
                    self.copy(way, t, i).start()

    def event(self, t, far):
        n = self.n
        for way in range(2):

            @pl.when(self.far(way) == far)
            def _():
                for i in range(n - far):
                    goal = n - 1 - i if way == 0 else i
                    k = self.tiles.index(t) * (n - 1) + i
                    self.copy(way, t, i).wait_recv()
                    at = (slice(goal * self.size, (goal + 1) * self.size), slice(t * PIECE, (t + 1) * PIECE))
                    self.part[at] = (self.part[at].astype(F32) + self.slots[way, k].astype(F32)).astype(BF)
                    if i < n - 1 - far:
                        self.copy(way, t, i).start()

    def finish(self):
        n = self.n
        for way in range(2):
            far = self.far(way)
            for i in range(n - 1):

                @pl.when(far < n - 1 - i)
                def _():
                    for t in self.tiles:
                        self.copy(way, t, i).wait_send()


PIECE = 512
EARLY = 2
ORDER = (
    "own.up0", "own.up1", "norm0", "nown0", "norm1", "nown1", "norm2", "nown2", "norm3", "nown3", "n00",
    "fwd.up0", "own.q0", "n01", "n02", "fwd.up1", "own.q1", "n03", "last.up0", "n10", "ready.up0", "raise00",
    "raise10", "n11", "fwd.q0", "n12", "last.up1", "ready.up1", "raise01", "n13", "cown", "raise11",
    "raise20", "fwd.q1", "own.dn0", "own.dn1", "n20", "raise21", "last.q0", "ready.q0", "n21", "last.q1",
    "ready.q1", "n22", "fwd.dn0", "own.dn2", "n23", "proj", "c00", "att0", "c01", "last.dn0", "fwd.dn1",
    "att1", "c02", "c03", "ready.dn0", "fwd.dn2", "raise30", "raise31", "c10", "ab0", "c11", "last.dn1",
    "last.dn2", "ab1", "c12", "c13", "ready.dn1", "ready.dn2", "lower0", "ffirst0", "lower1", "c20",
    "ffirst1", "lower2", "c21", "lower3", "ab2", "c22", "c23", "ab3", "f01", "hg0", "hg1", "hg2", "f11",
    "hg3", "f02", "kb", "f03", "f12", "f13",
)


def turned(x, table, sign):
    return (
        x * table[0]
        + pltpu.roll(x, 112, 1) * (table[1] * sign)
        + pltpu.roll(x, 16, 1) * (table[2] * sign)
    )


def gather_forward(
    n,
    prefix,
    x,
    cot,
    wq,
    wk,
    wv,
    wo,
    wu,
    wd,
    gain,
    bias,
    bqkv,
    bu,
    table,
    normed_out,
    cots_out,
    w_qkv_out,
    w_up_out,
    grads_out,
    joined_out,
    branch_out,
    normed,
    cots,
    w_qkv,
    w_up,
    w_dn,
    qkv,
    joined,
    slope,
    d_attn,
    d_key,
    d_value,
    own_x,
    lse,
    lse_row,
    fold_slots,
    send,
    recv,
    local,
    outs,
    fold_send,
    fold_recv,
):
    me, z = lax.axis_index("dp"), lax.axis_index("tensor")
    size, d = x.shape
    length = n * size
    width = wq.shape[1]
    ff = wu.shape[1]
    shard = wq.shape[0]
    lanes = wo.shape[1]
    branch = normed

    barrier = pltpu.get_barrier_semaphore()
    for bit in (1, 2, 4):
        pl.semaphore_signal(barrier, 1, device_id=(flip(me, bit), z), device_id_type=MESH)

    @pl.when(z > 0)
    def _():
        pl.semaphore_signal(barrier, 1, device_id=(me, jnp.maximum(z - 1, 0)), device_id_type=MESH)

    @pl.when(z < n - 1)
    def _():
        pl.semaphore_signal(barrier, 1, device_id=(me, jnp.minimum(z + 1, n - 1)), device_id_type=MESH)

    mine, cols = rows_at(me, shard), rows_at(me, lanes)
    loads = [
        pltpu.make_async_copy(x, own_x, local.at[0]),
        pltpu.make_async_copy(wu, w_up.at[mine, :], local.at[1]),
        pltpu.make_async_copy(wq, w_qkv.at[mine, pl.ds(0, width)], local.at[2]),
        pltpu.make_async_copy(wk, w_qkv.at[mine, pl.ds(width, width)], local.at[3]),
        pltpu.make_async_copy(wv, w_qkv.at[mine, pl.ds(2 * width, width)], local.at[4]),
        pltpu.make_async_copy(wo, w_dn.at[pl.ds(0, width), cols], local.at[5]),
        pltpu.make_async_copy(wd, w_dn.at[pl.ds(width, ff), cols], local.at[6]),
        pltpu.make_async_copy(cot, cots.at[rows_at(z, size), :], local.at[7]),
    ]
    for load in loads:
        load.start()

    stores = []

    def store(src, dst):
        copy = pltpu.make_async_copy(src, dst, outs.at[len(stores)])
        stores.append(copy)
        copy.start()
        return copy

    copies = Copies(send, recv)

    def row_view(buf, first, count):
        def view(i, half=None):
            h = count if half is None else count // 2
            start = i * shard + first + (0 if half is None else half * h)
            return buf.at[pl.ds(pl.multiple_of(start, h), h), :]

        return view

    def col_view(first, count):
        def view(i, half=None):
            if half is None:
                return w_dn.at[pl.ds(first, count), rows_at(i, lanes)]
            h = count // 2
            return w_dn.at[pl.ds(first + half * h, h), rows_at(i, lanes)]

        return view

    def row_col_view(first, count):
        def view(i, half=None):
            h = shard if half is None else shard // 2
            start = i * shard + (0 if half is None else half * h)
            return w_up.at[pl.ds(pl.multiple_of(start, h), h), pl.ds(first, count)]

        return view

    s_up = [Spread(copies, row_col_view(i * ff // 2, ff // 2), me, z) for i in range(2)]
    s_qkv = [Spread(copies, row_view(w_qkv, i * shard // 2, shard // 2), me, z) for i in range(2)]
    s_dn = [Spread(copies, col_view(*v), me, z) for v in ((0, width), (width, ff // 2), (width + ff // 2, ff // 2))]
    l_n = Line(copies, normed, size, n, me, z)
    l_c = Line(copies, cots, size, n, me, z)
    fold = Fold(branch, fold_slots, fold_send, fold_recv, range(EARLY), size, n, me, z)
    order = [z, flip(z, 1), flip(z, 2), flip(flip(z, 1), 2)]
    head = lax.broadcasted_iota(jnp.int32, (1, 128), 1) // HEAD_DIM

    def norm(r):
        rows = slice(r * 64, (r + 1) * 64)
        v = own_x[rows, :].astype(F32)
        mean = jnp.mean(v, axis=-1, keepdims=True)
        c = v - mean
        inv = lax.rsqrt(jnp.mean(c * c, axis=-1, keepdims=True) + epsilon)
        out = (c * inv) * gain[...] + bias[...]
        normed[pl.ds(pl.multiple_of(z * size + r * 64, 64), 64), :] = out.astype(BF)

    def project():
        tile = 512

        @pl.loop(0, length // tile)
        def _(m):
            rows = rows_at(m, tile)
            tab = [table[i, rows, :] for i in range(3)]
            for part in range(3):
                acc = nn(normed[rows, :], w_qkv[:, part * width : (part + 1) * width])
                acc = acc + bqkv[:, part * width : (part + 1) * width]
                for p in range(width // 128):
                    piece = acc[:, p * 128 : (p + 1) * 128]
                    if part < 2:
                        piece = turned(piece, tab, 1.0)
                        if part == 0:
                            piece = piece * (1.0 / math.sqrt(HEAD_DIM))
                    qkv[rows, part * width + p * 128 : part * width + (p + 1) * 128] = piece.astype(BF)

    def raise_(j, part):
        rows = rows_at(j, size)
        tile = 512

        @pl.loop(part * ff // tile // 2, (part + 1) * ff // tile // 2)
        def _(t):
            cs = rows_at(t, tile)
            u = nn(normed[rows, :], w_up[:, cs]) + bu[:, cs]
            sq = u * u
            th = jnp.tanh(root * u * (1.0 + 0.044715 * sq))
            half = 0.5 * (1.0 + th)
            joined[rows, pl.ds(pl.multiple_of(width + t * tile, tile), tile)] = (u * half).astype(BF)
            slope[rows, cs] = (
                half + 0.5 * u * (1.0 - th * th) * (root * (1.0 + 3 * 0.044715 * sq))
            ).astype(BF)

    block = length // 4

    def visible(b):
        return (b if b > 0 else 0), max(b + 1, 2)

    def attend(first, count):
        @pl.loop(first, first + count)
        def _(p):
            ps = rows_at(p, 128)
            ks = pl.ds(pl.multiple_of(width + p * 128, 128), 128)
            vs = pl.ds(pl.multiple_of(2 * width + p * 128, 128), 128)
            lane = lax.broadcasted_iota(jnp.int32, (1, 128), 1)
            for b in range(4):
                full, some = visible(b)
                qs = pl.ds(b * block, block)
                parts = [(0, full)] * (full > 0) + [(full, some)]
                limit = jnp.maximum(
                    b * block + lax.broadcasted_iota(jnp.int32, (block, 1), 0), prefix[0] - 1
                )
                outs_ = []
                for h in range(2):
                    q = qkv[qs, ps]
                    q = jnp.where(head == h, q, jnp.zeros_like(q))
                    scores = []
                    for lo, hi in parts:
                        kr = pl.ds(lo * block, (hi - lo) * block)
                        s = nt(q, qkv[kr, ks])
                        if lo == full:
                            at = lo * block + lax.broadcasted_iota(jnp.int32, s.shape, 1)
                            s = jnp.where(at <= limit, s, masked_score)
                        scores.append(s)
                    top = functools.reduce(jnp.maximum, [jnp.max(s, axis=-1, keepdims=True) for s in scores])
                    e = [jnp.exp(s - top) for s in scores]
                    total = sum(jnp.sum(v, axis=-1, keepdims=True) for v in e)
                    inv = 1.0 / total
                    outs_.append(
                        sum(
                            nn((v * inv).astype(BF), qkv[pl.ds(lo * block, (hi - lo) * block), vs])
                            for v, (lo, hi) in zip(e, parts)
                        )
                    )
                    lse[qs, :] = jnp.where(lane == 2 * p + h, top + jnp.log(total), lse[qs, :])
                joined[qs, ps] = jnp.where(head == 0, outs_[0], outs_[1]).astype(BF)

    def lower(t):
        @pl.loop(0, length // 512)
        def _(m):
            rows = rows_at(m, 512)
            branch[rows, t * PIECE : (t + 1) * PIECE] = nn(
                joined[rows, :], w_dn[:, t * PIECE : (t + 1) * PIECE]
            ).astype(BF)

    def hidden_back(j):
        rows = rows_at(j, size)
        tile = 512

        @pl.loop(0, ff // tile)
        def _(t):
            g = nt(cots[rows, :], w_dn[pl.ds(pl.multiple_of(width + t * tile, tile), tile), :])
            cs = rows_at(t, tile)
            slope[rows, cs] = (g * slope[rows, cs].astype(F32)).astype(BF)

    def attend_back(b):
        full, some = visible(b)
        qs = pl.ds(b * block, block)
        limit = jnp.maximum(b * block + lax.broadcasted_iota(jnp.int32, (1, block), 1), prefix[0] - 1)

        @pl.loop(0, width // 128)
        def _(p):
            ps = rows_at(p, 128)
            ks = pl.ds(pl.multiple_of(width + p * 128, 128), 128)
            vs = pl.ds(pl.multiple_of(2 * width + p * 128, 128), 128)
            only = lambda a, h: jnp.where(head == h, a, jnp.zeros_like(a))
            q, g = qkv[qs, ps], d_attn[:, ps]
            dq = None
            for h in range(2):
                qh, gh = only(q, h), only(g, h)
                kept = []
                delta = None
                for kb in range(some):
                    kr = pl.ds(kb * block, block)
                    probs = jnp.exp(nt(qkv[kr, ks], qh) - lse_row[pl.ds(2 * p + h, 1), qs])
                    if kb >= full:
                        at = kb * block + lax.broadcasted_iota(jnp.int32, (block, block), 0)
                        probs = jnp.where(at <= limit, probs, 0.0)
                    d_value[kr, ps] += nn(probs.astype(BF), gh)
                    d_probs = nt(qkv[kr, vs], gh)
                    kept.append((probs, d_probs))
                    add = jnp.sum(probs * d_probs, axis=0, keepdims=True)
                    delta = add if delta is None else delta + add
                for kb, (probs, d_probs) in enumerate(kept):
                    kr = pl.ds(kb * block, block)
                    ds = (probs * (d_probs - delta)).astype(BF)
                    d_key[kr, ps] += nn(ds, qh)
                    add = tn(ds, only(qkv[kr, ks], h))
                    dq = add if dq is None else dq + add
            tab = [table[i, qs, :] for i in range(3)]
            qkv[qs, ps] = turned(dq * (1.0 / math.sqrt(HEAD_DIM)), tab, -1.0).astype(BF)

    def back(k):
        d_attn[...] = nt(cots[rows_at(order[k], size), :], w_dn[:width, :]).astype(BF)
        for b in range(4):

            @pl.when(order[k] == b)
            def _():
                attend_back(b)

    def keys_back():
        @pl.loop(0, width // 128)
        def _(p):
            ps = rows_at(p, 128)
            ks = pl.ds(pl.multiple_of(width + p * 128, 128), 128)
            vs = pl.ds(pl.multiple_of(2 * width + p * 128, 128), 128)
            tab = [table[i] for i in range(3)]
            qkv[:, ks] = turned(d_key[:, ps], tab, -1.0).astype(BF)
            qkv[:, vs] = d_value[:, ps].astype(BF)

    signals = 3 + jnp.where(z > 0, 1, 0) + jnp.where(z < n - 1, 1, 0)
    pl.semaphore_wait(barrier, signals)

    n_stored = []
    part = functools.partial

    def clear():
        lse[...] = jnp.zeros_like(lse)
        d_key[...] = jnp.zeros_like(d_key)
        d_value[...] = jnp.zeros_like(d_value)

    def wait_loads(*which):
        for i in which:
            loads[i].wait()

    def heads_end():
        lse_row[...] = lse[...].T[: lse_row.shape[0], :]

    def branch_free():
        l_n.finish()
        n_stored[0].wait()

    todo = {
        "own.up0": [part(wait_loads, 1), s_up[0].own],
        "own.q0": [part(wait_loads, 2, 3, 4), s_qkv[0].own],
        "own.dn0": [part(wait_loads, 5), s_dn[0].own],
        "own.dn1": [part(wait_loads, 6), s_dn[1].own],
        "norm0": [part(wait_loads, 0), part(norm, 0)],
        "nown3": [part(l_n.own, 3), clear],
        "ready.up1": [s_up[1].ready, part(store, w_up, w_up_out)],
        "ready.q1": [s_qkv[1].ready, part(store, w_qkv, w_qkv_out)],
        "n23": [part(l_n.event, 2, 3), lambda: n_stored.append(store(normed, normed_out))],
        "cown": [part(wait_loads, 7)] + [part(l_c.own, c) for c in range(Line.CHUNKS)],
        "c23": [part(l_c.event, 2, 3), part(store, cots, cots_out)],
        "proj": [project],
        "att0": [part(attend, 0, 2)],
        "att1": [part(attend, 2, 2), heads_end],
        "raise31": [part(raise_, order[3], 1), part(store, joined, joined_out)],
        "lower0": [branch_free, part(lower, 0)],
        "hg3": [part(hidden_back, order[3]), part(store, slope, grads_out.at[:, pl.ds(3 * width, ff)])],
        "kb": [keys_back, part(store, qkv, grads_out.at[:, pl.ds(0, 3 * width)])],
    }
    for name, spreads in (("up", s_up), ("q", s_qkv), ("dn", s_dn)):
        for i, s in enumerate(spreads):
            for what, call in (("own", s.own), ("fwd", s.forward), ("last", s.last), ("ready", s.ready)):
                todo.setdefault(what + "." + name + str(i), [call])
    for c in range(Line.CHUNKS):
        todo.setdefault("norm" + str(c), [part(norm, c)])
        todo.setdefault("nown" + str(c), [part(l_n.own, c)])
        for s in range(n - 1):
            todo.setdefault("n" + str(s) + str(c), [part(l_n.event, s, c)])
            todo.setdefault("c" + str(s) + str(c), [part(l_c.event, s, c)])
    for k in range(4):
        for i in range(2):
            todo.setdefault("raise" + str(k) + str(i), [part(raise_, order[k], i)])
        todo.setdefault("hg" + str(k), [part(hidden_back, order[k])])
        todo.setdefault("ab" + str(k), [part(back, k)])
        todo.setdefault("lower" + str(k), [part(lower, k)])
        todo.setdefault("ffirst" + str(k), [part(fold.first, k)])
        for far in range(1, n):
            todo.setdefault("f" + str(k) + str(far), [part(fold.event, k, far)])
    for name in ORDER:
        for call in todo[name]:
            call()
    store(branch, branch_out)
    for copy in stores:
        if copy is not n_stored[0]:
            copy.wait()
    fold.finish()
    l_c.finish()
    copies.finish()


def tables(length):
    half = ROT_DIM // 2
    freqs = rope_base ** (-(np.arange(half).astype(np.float32) * 2.0 / ROT_DIM))
    angles = np.arange(length).astype(np.float32)[:, None] * freqs[None, :].astype(np.float32)
    cos, sin = np.cos(angles), np.sin(angles)
    rest = np.zeros((length, HEAD_DIM - ROT_DIM), np.float32)
    none = np.zeros((length, half), np.float32)
    c = np.concatenate([cos, cos, rest + 1.0], 1)
    s1 = np.concatenate([-sin, none, rest], 1)
    s2 = np.concatenate([none, sin, rest], 1)
    return jnp.asarray(np.stack([np.concatenate([t, t], 1) for t in (c, s1, s2)]).astype(np.float32))


def forward_call(n, prefix, x, cot, wq, wk, wv, wo, wu, wd, gain, bias, bq, bk, bv, bu):
    size, d = x.shape
    length, width, ff = n * size, wq.shape[1], wu.shape[1]
    vm, hbm = pl.BlockSpec(memory_space=pltpu.VMEM), pl.BlockSpec(memory_space=pl.ANY)
    shape = lambda s, t=BF: jax.ShapeDtypeStruct(s, t)
    dma = pltpu.SemaphoreType.DMA
    count = 7 * 9 + 2 * (n - 1) * 2 * Line.CHUNKS
    return pl.pallas_call(
        functools.partial(gather_forward, n),
        out_shape=(
            shape((length, d)),
            shape((length, d)),
            shape((d, 3 * width)),
            shape((d, ff)),
            shape((length, 3 * width + ff)),
            shape((length, width + ff)),
            shape((length, d)),
        ),
        in_specs=[pl.BlockSpec(memory_space=pltpu.SMEM)] + [hbm] * 8 + [vm] * 5,
        out_specs=(hbm,) * 7,
        scratch_shapes=[
            pltpu.VMEM((length, d), BF),
            pltpu.VMEM((length, d), BF),
            pltpu.VMEM((d, 3 * width), BF),
            pltpu.VMEM((d, ff), BF),
            pltpu.VMEM((width + ff, d), BF),
            pltpu.VMEM((length, 3 * width), BF),
            pltpu.VMEM((length, width + ff), BF),
            pltpu.VMEM((length, ff), BF),
            pltpu.VMEM((size, width), BF),
            pltpu.VMEM((length, width), F32),
            pltpu.VMEM((length, width), F32),
            pltpu.VMEM((size, d), BF),
            pltpu.VMEM((length, 128), F32),
            pltpu.VMEM((width // HEAD_DIM, length), F32),
            pltpu.VMEM((2, EARLY * (n - 1), size, PIECE), BF),
            dma((count,)),
            dma((count,)),
            dma((8,)),
            dma((8,)),
            dma((2, EARLY * (n - 1))),
            dma((2, EARLY * (n - 1))),
        ],
        compiler_params=pltpu.CompilerParams(
            collective_id=1, has_side_effects=True, vmem_limit_bytes=63 << 20
        ),
        cost_estimate=pl.CostEstimate(flops=50_000_000_000, bytes_accessed=100_000_000, transcendentals=0),
    )(
        prefix,
        x,
        cot,
        wq,
        wk,
        wv,
        wo,
        wu,
        wd,
        gain[None],
        bias[None],
        jnp.concatenate([bq, bk, bv])[None],
        bu[None],
        tables(length),
    )


SIB_SLOTS = 4
SLOTS = 4


def backward_scatter(
    n,
    x,
    normed,
    cots,
    w_qkv,
    w_up,
    grads_in,
    joined,
    branch,
    gain,
    b_sum,
    layer_out,
    d_input,
    d_in,
    d_dn,
    d_bias,
    d_all,
    own_x,
    cot,
    grads,
    n_block,
    n_turned,
    j_block,
    j_turned,
    wq_block,
    wu_block,
    part_b,
    part_g,
    slots_b,
    slots_g,
    sib_out,
    sib_in,
    own_low,
    own_sum,
    x_in,
    y_in,
    end_in,
    d_rows,
    narrow,
    wide,
    wide_z,
    sums,
    b_send,
    b_recv,
    g_send,
    g_recv,
    sib_send,
    sib_recv,
    link_send,
    link_recv,
    out_sem,
    local,
    stream,
    small_send,
    small_recv,
):
    me, z = lax.axis_index("dp"), lax.axis_index("tensor")
    size, d = x.shape
    length = n * size
    ff = w_up.shape[1]
    width = joined.shape[1] - ff
    lanes = d // 8
    down_pieces = (width + ff) // PIECE
    up_pieces = (3 * width + ff) // PIECE
    pieces = down_pieces + up_pieces
    half, quarter = PIECE // 2, PIECE // 4
    sib = (flip(me, 1), z)
    x_to, y_to = (flip(me, 2), z), (flip(me, 4), z)

    barrier = pltpu.get_barrier_semaphore()
    peers = []
    for k in range(1, 8):
        to = me
        for bit in (1, 2, 4):
            if k & bit:
                to = flip(to, bit)
        peers.append(to)
        pl.semaphore_signal(barrier, 1, device_id=(to, z), device_id_type=MESH)
    others = [lax.rem(z + k, n) for k in range(1, n)]
    for to in others:
        pl.semaphore_signal(barrier, 1, device_id=(me, to), device_id_type=MESH)

    def load(k, src, dst):
        return pltpu.make_async_copy(src, dst, local.at[k])

    loads = [
        load(0, branch, part_b),
        load(1, cots, cot),
        load(2, grads_in, grads),
        load(3, x, own_x),
    ]

    def j_load(p):
        return pltpu.make_async_copy(
            joined.at[:, rows_at(jnp.minimum(p, down_pieces - 1), PIECE)],
            j_block.at[lax.rem(p, 2)],
            stream.at[lax.rem(p, 2)],
        )

    def w_loads(t):
        return [
            pltpu.make_async_copy(w_qkv.at[rows_at(t, PIECE), :], wq_block.at[t % 2], stream.at[2 + t % 2]),
            pltpu.make_async_copy(w_up.at[rows_at(t, PIECE), :], wu_block.at[t % 2], stream.at[4 + t % 2]),
        ]

    def n_load(j):
        return pltpu.make_async_copy(normed.at[rows_at(j, size), :], n_block, stream.at[6])

    j_load(0).start()
    for l in loads:
        l.start()
    for l in w_loads(0) + w_loads(1) + [n_load(0)]:
        l.start()

    fold_b = Fold(part_b, slots_b, b_send, b_recv, range(EARLY, d // PIECE), size, n, me, z)
    fold_g = Fold(part_g, slots_g, g_send, g_recv, range(d // PIECE), size, n, me, z)

    goals = [flip(me, 2), flip(flip(me, 2), 4), flip(me, 4), me]

    def sib_copy(p):
        return pltpu.make_async_remote_copy(
            sib_out.at[lax.rem(p, 2)],
            sib_in.at[lax.rem(p, SIB_SLOTS)],
            sib_send.at[lax.rem(p, 2)],
            sib_recv.at[lax.rem(p, SIB_SLOTS)],
            device_id=sib,
            device_id_type=MESH,
        )

    def link_copy(k, p, src, dst, to):
        slot = lax.rem(p, SLOTS)
        return pltpu.make_async_remote_copy(
            src, dst, link_send.at[k, slot], link_recv.at[k, slot], device_id=to, device_id_type=MESH
        )

    def x_first(p):
        slot = lax.rem(p, SLOTS)
        return link_copy(0, p, own_low.at[slot, pl.ds(0, 2), pl.ds(0, quarter)], x_in.at[slot], x_to)

    def y_first(p):
        slot = lax.rem(p, SLOTS)
        return link_copy(1, p, own_low.at[slot, pl.ds(1, 2), pl.ds(quarter, quarter)], y_in.at[slot], y_to)

    def y_last(p):
        slot = lax.rem(p, SLOTS)
        return link_copy(2, p, own_low.at[slot, 2, pl.ds(0, quarter)], end_in.at[slot, 0], y_to)

    def x_last(p):
        slot = lax.rem(p, SLOTS)
        return link_copy(3, p, own_low.at[slot, 0, pl.ds(quarter, quarter)], end_in.at[slot, 1], x_to)

    def up_column(p):
        t = jnp.clip(p - down_pieces, 0, up_pieces - 1)
        return lax.rem(t + 3 * width // PIECE, up_pieces) * PIECE

    def out_copies(p):
        src = own_sum.at[lax.rem(p, SLOTS)]
        sem = out_sem.at[lax.rem(p, SLOTS)]
        row = jnp.minimum(p, down_pieces - 1) * PIECE
        down = [
            pltpu.make_async_copy(
                src.at[:, pl.ds(i * half, half)],
                d_dn.at[pl.ds(pl.multiple_of(row + i * half, half), half), :],
                sem.at[i],
            )
            for i in range(2)
        ]
        up = [
            pltpu.make_async_copy(
                src.at[:, pl.ds(i * half, half)],
                d_in.at[:, pl.ds(pl.multiple_of(up_column(p) + i * half, half), half)],
                sem.at[i],
            )
            for i in range(2)
        ]
        return down, up

    def first_down(p):
        slot, out = lax.rem(p, SLOTS), lax.rem(p, 2)
        j_load(p).wait()

        @pl.when(p + 1 < down_pieces)
        def _():
            j_load(p + 1).start()

        j_turned[...] = j_block[lax.rem(p, 2)].T
        for mine in range(2):
            for r, goal in enumerate(goals):
                to = flip(goal, 1) if mine == 0 else goal
                t = nn(j_turned[...], cot[:, rows_at(to, lanes)])
                for i in range(2):
                    v = t[i * half : (i + 1) * half, :]
                    cs = pl.ds(i * half, half)
                    if mine == 0:
                        sib_out[out, r, :, cs] = v.astype(BF)
                    elif r < 3:
                        own_low[slot, r, :, cs] = v.astype(BF)
                    else:
                        own_sum[slot, :, cs] = v
            if mine == 0:
                sib_copy(p).start()

    def first_up(p):
        slot, out = lax.rem(p, SLOTS), lax.rem(p, 2)
        g = grads[:, pl.ds(pl.multiple_of(up_column(p), PIECE), PIECE)]
        for mine in range(2):
            for r, goal in enumerate(goals):
                to = flip(goal, 1) if mine == 0 else goal
                t = nn(n_turned[rows_at(to, lanes), :], g)
                if mine == 0:
                    sib_out[out, r] = t.astype(BF)
                elif r < 3:
                    own_low[slot, r] = t.astype(BF)
                else:
                    own_sum[slot] = t
            if mine == 0:
                sib_copy(p).start()

    def stage_one(p):
        @pl.when(p >= 2)
        def _():
            sib_copy(p - 2).wait_send()

        @pl.when(p >= SLOTS)
        def _():
            for c in out_copies(p - SLOTS)[0]:
                c.wait()

        @pl.when(p < down_pieces)
        def _():
            first_down(p)

        @pl.when(p >= down_pieces)
        def _():
            first_up(p)

    def stage_two(p):
        slot, inn = lax.rem(p, SLOTS), lax.rem(p, SIB_SLOTS)
        sib_copy(p).wait_recv()
        a, b = pl.ds(0, quarter), pl.ds(quarter, quarter)

        def add(r, rows):
            own_low[slot, r, rows] = (own_low[slot, r, rows].astype(F32) + sib_in[inn, r, rows].astype(F32)).astype(BF)

        add(0, a)
        add(1, a)
        x_first(p).start()
        add(1, b)
        add(2, b)
        y_first(p).start()
        add(0, b)
        add(2, a)
        own_sum[slot] = own_sum[slot] + sib_in[inn, 3].astype(F32)

    def stage_three(p):
        slot = lax.rem(p, SLOTS)
        a, b = pl.ds(0, quarter), pl.ds(quarter, quarter)
        x_first(p).wait_recv()
        own_low[slot, 2, a] = (own_low[slot, 2, a].astype(F32) + x_in[slot, 1].astype(F32)).astype(BF)
        y_last(p).start()
        y_first(p).wait_recv()
        own_low[slot, 0, b] = (own_low[slot, 0, b].astype(F32) + y_in[slot, 0].astype(F32)).astype(BF)
        x_last(p).start()
        own_sum[slot, a] = own_sum[slot, a] + x_in[slot, 0].astype(F32)
        own_sum[slot, b] = own_sum[slot, b] + y_in[slot, 1].astype(F32)

    def stage_four(p):
        slot = lax.rem(p, SLOTS)
        a, b = pl.ds(0, quarter), pl.ds(quarter, quarter)
        y_last(p).wait_recv()
        own_sum[slot, a] = own_sum[slot, a] + end_in[slot, 0].astype(F32)
        x_last(p).wait_recv()
        own_sum[slot, b] = own_sum[slot, b] + end_in[slot, 1].astype(F32)
        down, up = out_copies(p)

        @pl.when(p < down_pieces)
        def _():
            for c in down:
                c.start()

        @pl.when(p >= down_pieces)
        def _():
            for c in up:
                c.start()

        for c in (x_first(p), y_first(p), x_last(p), y_last(p)):
            c.wait_send()

    def normed_back(t):
        for l in w_loads(t):
            l.wait()

        @pl.loop(0, length // 512)
        def _(m):
            rows = rows_at(m, 512)
            part_g[rows, t * PIECE : (t + 1) * PIECE] = (
                nt(grads[rows, : 3 * width], wq_block[t % 2]) + nt(grads[rows, 3 * width :], wu_block[t % 2])
            ).astype(BF)

        if t + 2 < d // PIECE:
            for l in w_loads(t + 2):
                l.start()
        fold_g.first(t)

    def turn(j):
        n_load(j).wait()
        n_turned[:, j * size : (j + 1) * size] = n_block[...].T
        if j + 1 < n:
            n_load(j + 1).start()

    def small(k, src, dst, to):
        return pltpu.make_async_remote_copy(
            src, dst, small_send.at[k], small_recv.at[k], device_id=to, device_id_type=MESH
        )

    def bias_sums():
        for i in range(up_pieces):
            narrow[me, i : i + 1, :] = jnp.sum(
                grads[:, i * PIECE : (i + 1) * PIECE].astype(F32), axis=0, keepdims=True
            )
        for k, to in enumerate(peers):
            small(k, narrow.at[me], narrow.at[me], (to, z)).start()

    def branch_end():
        @pl.loop(0, size // 32)
        def _(r):
            rows = pl.ds(pl.multiple_of(z * size + r * 32, 32), 32)
            v = own_x[rows_at(r, 32), :].astype(F32) + part_b[rows, :].astype(F32) + b_sum[0:1, :] + b_sum[1:2, :]
            part_b[rows, :] = v.astype(BF)

        load(0, part_b.at[rows_at(z, size), :], layer_out).start()

    def input_end():
        sums[...] = jnp.zeros_like(sums)

        def chunk(r):
            return pltpu.make_async_copy(
                d_rows.at[lax.rem(r, 2)], d_input.at[rows_at(r, 32), :], local.at[1 + lax.rem(r, 2)]
            )

        @pl.loop(0, size // 32)
        def _(r):
            mine = pl.ds(pl.multiple_of(z * size + r * 32, 32), 32)
            grad = part_g[mine, :].astype(F32)
            v = own_x[rows_at(r, 32), :].astype(F32)
            c = v - jnp.mean(v, axis=-1, keepdims=True)
            inv = lax.rsqrt(jnp.mean(c * c, axis=-1, keepdims=True) + epsilon)
            unit = c * inv
            own_cot = cot[mine, :].astype(F32)
            gu = grad * unit
            sums[0:1, :] += jnp.sum(gu, axis=0, keepdims=True)
            sums[1:2, :] += jnp.sum(grad, axis=0, keepdims=True)
            sums[2:3, :] += jnp.sum(own_cot, axis=0, keepdims=True)
            scaled = grad * gain[...]

            @pl.when(r >= 2)
            def _():
                chunk(r - 2).wait()

            d_rows[lax.rem(r, 2)] = own_cot + inv * (
                scaled
                - jnp.mean(scaled, axis=-1, keepdims=True)
                - unit * jnp.mean(scaled * unit, axis=-1, keepdims=True)
            )
            chunk(r).start()

        for i in range(3):
            for q in range(4):
                wide[me, 4 * i + q : 4 * i + q + 1, :] = sums[i : i + 1, q * PIECE : (q + 1) * PIECE]
        for k, to in enumerate(peers):
            small(8 + k, wide.at[me], wide.at[me], (to, z)).start()
        for r in range(2):
            chunk(size // 32 - 2 + r).wait()

    def small_end():
        for k, to in enumerate(peers):
            small(8 + k, wide.at[to], wide.at[to], (to, z)).wait_recv()
        total = wide[0]
        for i in range(1, 8):
            total = total + wide[i]
        wide_z[z] = total
        for k, to in enumerate(others):
            small(16 + k, wide_z.at[z], wide_z.at[z], (me, to)).start()

    def last_end():
        for k in range(n - 1):
            origin = lax.rem(z + n - 1 - k, n)
            small(16 + k, wide_z.at[origin], wide_z.at[origin], (me, origin)).wait_recv()
        total = wide_z[0]
        for i in range(1, n):
            total = total + wide_z[i]
        d_all[...] = total
        for k, to in enumerate(peers):
            small(k, narrow.at[to], narrow.at[to], (to, z)).wait_recv()
        total = narrow[0]
        for i in range(1, 8):
            total = total + narrow[i]
        d_bias[...] = total
        for k, to in enumerate(peers):
            small(k, narrow.at[me], narrow.at[me], (to, z)).wait_send()
            small(8 + k, wide.at[me], wide.at[me], (to, z)).wait_send()
        for k, to in enumerate(others):
            small(16 + k, wide_z.at[z], wide_z.at[z], (me, to)).wait_send()
        load(0, part_b.at[rows_at(z, size), :], layer_out).wait()

    narrow[me] = jnp.zeros(narrow.shape[1:], F32)
    wide[me] = jnp.zeros(wide.shape[1:], F32)
    pl.semaphore_wait(barrier, 7 + n - 1)

    tasks = {}

    def at(p, *work):
        tasks.setdefault(p, []).extend(work)

    loads[0].wait()
    for t in fold_b.tiles:
        fold_b.first(t)
    for l in loads[1:]:
        l.wait()

    part = functools.partial
    at(0, part(normed_back, 0))
    at(1, part(normed_back, 1))
    at(2, part(normed_back, 2))
    at(3, part(normed_back, 3), part(turn, 0), part(turn, 1))
    at(4, part(turn, 2), part(turn, 3), bias_sums)
    late = d // PIECE - EARLY
    for i in range(late):
        for far in range(1, n):
            at(2 * i + 1 + far, part(fold_b.event, EARLY + i, far))
    at(2 * late + 2, branch_end)
    for t in range(d // PIECE):
        for far in range(1, n):
            at(2 * (t + late) + 1 + far, part(fold_g.event, t, far))
    at(14, input_end, small_end, last_end)

    @pl.loop(0, max(pieces + 3, max(tasks) + 1))
    def _(p):
        @pl.when(p < pieces)
        def _():
            stage_one(p)

        @pl.when((p >= 1) & (p <= pieces))
        def _():
            stage_two(p - 1)

        @pl.when((p >= 2) & (p <= pieces + 1))
        def _():
            stage_three(p - 2)

        @pl.when((p >= 3) & (p <= pieces + 2))
        def _():
            stage_four(p - 3)

        for k, work in tasks.items():

            @pl.when(p == k)
            def _():
                for w in work:
                    w()

    for p in range(2):
        sib_copy(pieces - 2 + p).wait_send()
    for p in range(SLOTS):
        for c in out_copies(pieces - SLOTS + p)[1]:
            c.wait()
    fold_b.finish()
    fold_g.finish()


def backward_call(n, x, normed, cots, w_qkv, w_up, grads, joined, branch, gain, b_out, b_down):
    size, d = x.shape
    length, ff = n * size, w_up.shape[1]
    width = joined.shape[1] - ff
    vm, hbm = pl.BlockSpec(memory_space=pltpu.VMEM), pl.BlockSpec(memory_space=pl.ANY)
    shape = lambda s, t=BF: jax.ShapeDtypeStruct(s, t)
    dma = pltpu.SemaphoreType.DMA
    half, quarter = PIECE // 2, PIECE // 4
    late, tiles = (d // PIECE - EARLY) * (n - 1), d // PIECE * (n - 1)
    return pl.pallas_call(
        functools.partial(backward_scatter, n),
        out_shape=(
            shape((size, d)),
            shape((size, d), F32),
            shape((d // 8, 3 * width + ff), F32),
            shape((width + ff, d // 8), F32),
            shape((8, PIECE), F32),
            shape((16, PIECE), F32),
        ),
        in_specs=[hbm] * 8 + [vm] * 2,
        out_specs=(hbm,) * 4 + (vm,) * 2,
        scratch_shapes=[
            pltpu.VMEM((size, d), BF),
            pltpu.VMEM((length, d), BF),
            pltpu.VMEM((length, 3 * width + ff), BF),
            pltpu.VMEM((size, d), BF),
            pltpu.VMEM((d, length), BF),
            pltpu.VMEM((2, length, PIECE), BF),
            pltpu.VMEM((PIECE, length), BF),
            pltpu.VMEM((2, PIECE, 3 * width), BF),
            pltpu.VMEM((2, PIECE, ff), BF),
            pltpu.VMEM((length, d), BF),
            pltpu.VMEM((length, d), BF),
            pltpu.VMEM((2, late, size, PIECE), BF),
            pltpu.VMEM((2, tiles, size, PIECE), BF),
            pltpu.VMEM((2, 4, half, PIECE), BF),
            pltpu.VMEM((SIB_SLOTS, 4, half, PIECE), BF),
            pltpu.VMEM((SLOTS, 3, half, PIECE), BF),
            pltpu.VMEM((SLOTS, half, PIECE), F32),
            pltpu.VMEM((SLOTS, 2, quarter, PIECE), BF),
            pltpu.VMEM((SLOTS, 2, quarter, PIECE), BF),
            pltpu.VMEM((SLOTS, 2, quarter, PIECE), BF),
            pltpu.VMEM((2, 32, d), F32),
            pltpu.VMEM((8, 8, PIECE), F32),
            pltpu.VMEM((8, 16, PIECE), F32),
            pltpu.VMEM((n, 16, PIECE), F32),
            pltpu.VMEM((8, d), F32),
            dma((2, late)),
            dma((2, late)),
            dma((2, tiles)),
            dma((2, tiles)),
            dma((2,)),
            dma((SIB_SLOTS,)),
            dma((4, SLOTS)),
            dma((4, SLOTS)),
            dma((SLOTS, 2)),
            dma((4,)),
            dma((7,)),
            dma((16 + n - 1,)),
            dma((16 + n - 1,)),
        ],
        compiler_params=pltpu.CompilerParams(
            collective_id=2, has_side_effects=True, vmem_limit_bytes=63 << 20
        ),
        cost_estimate=pl.CostEstimate(flops=60_000_000_000, bytes_accessed=100_000_000, transcendentals=0),
    )(x, normed, cots, w_qkv, w_up, grads, joined, branch, gain[None], jnp.stack([b_out, b_down]))


def rotate(tensor, positions, direction):
    half_dim = ROT_DIM // 2
    freqs = rope_base ** (-(jnp.arange(half_dim).astype(jnp.float32) * 2.0 / ROT_DIM))
    angles = positions.astype(jnp.float32)[:, None] * freqs[None, :]
    cosine = jnp.cos(angles)[:, None, :]
    sine = direction * jnp.sin(angles)[:, None, :]
    first = tensor[..., :half_dim]
    second = tensor[..., half_dim:ROT_DIM]
    return jnp.concatenate(
        [first * cosine - second * sine, second * cosine + first * sine, tensor[..., ROT_DIM:]],
        axis=-1,
    )


def times_transposed(left, right):
    return lax.dot_general(
        left, right, (((1,), (1,)), ((), ())), preferred_element_type=jnp.float32
    )


def rows_transposed(left, right):
    return lax.dot_general(
        left, right, (((0,), (0,)), ((), ())), preferred_element_type=jnp.float32
    )


def plain_on_device(
    layer_input,
    ln_gain,
    ln_bias,
    w_query,
    b_query,
    w_key,
    b_key,
    w_value,
    b_value,
    w_out,
    b_out,
    w_up,
    b_up,
    w_down,
    b_down,
    prefix,
    cotangent,
):
    local_width = w_query.shape[1]
    hidden_here = w_up.shape[1]
    heads_here = local_width // HEAD_DIM
    score_scale = 1.0 / math.sqrt(HEAD_DIM)
    prefix_len = prefix[0]
    input_float = layer_input.astype(jnp.float32)
    row_mean = jnp.mean(input_float, axis=-1, keepdims=True)
    centred = input_float - row_mean
    inverse = lax.rsqrt(jnp.mean(centred * centred, axis=-1, keepdims=True) + epsilon)
    unit_rows = centred * inverse
    normed = (unit_rows * ln_gain + ln_bias).astype(jnp.bfloat16)
    normed_all = lax.all_gather(normed, "tensor", axis=0, tiled=True)
    length = normed_all.shape[0]
    positions = jnp.arange(length)
    block_rows = min(512, length)
    block_count = length // block_rows
    pieces = (
        lax.all_gather(w_query, "dp", axis=0, tiled=True),
        lax.all_gather(w_key, "dp", axis=0, tiled=True),
        lax.all_gather(w_value, "dp", axis=0, tiled=True),
        lax.all_gather(w_up, "dp", axis=0, tiled=True),
    )
    columns = normed_all
    query_acc, key_acc, value_acc, up_acc = tuple(
        (jnp.dot(columns, piece, preferred_element_type=jnp.float32) for piece in pieces)
    )
    query_pre = (query_acc + b_query).reshape(length, heads_here, HEAD_DIM)
    key_pre = (key_acc + b_key).reshape(length, heads_here, HEAD_DIM)
    query = rotate(query_pre, positions, 1.0).astype(jnp.bfloat16)
    key = rotate(key_pre, positions, 1.0).astype(jnp.bfloat16)
    value = (value_acc + b_value).reshape(length, heads_here, HEAD_DIM).astype(jnp.bfloat16)
    up_pre = up_acc + b_up
    hidden = jax.nn.gelu(up_pre, approximate=True).astype(jnp.bfloat16)

    def scores_for(query_rows, offset):
        raw = (
            jnp.einsum("qhd,khd->hqk", query_rows, key, preferred_element_type=jnp.float32)
            * score_scale
        )
        query_pos = offset + jnp.arange(block_rows)
        seen = (positions[None, :] <= query_pos[:, None]) | (positions[None, :] < prefix_len)
        return jnp.where(seen[None], raw, masked_score)

    def attend_block(index):
        offset = index * block_rows
        query_rows = lax.dynamic_slice_in_dim(query, offset, block_rows, 0)
        scores = scores_for(query_rows, offset)
        row_max = jnp.max(scores, axis=-1, keepdims=True)
        expo = jnp.exp(scores - row_max)
        totals = jnp.sum(expo, axis=-1, keepdims=True)
        probs_low = (expo / totals).astype(jnp.bfloat16)
        out_rows = jnp.einsum("hqk,khd->qhd", probs_low, value, preferred_element_type=jnp.float32)
        return (out_rows, (row_max + jnp.log(totals))[..., 0])

    indices = jnp.arange(block_count)
    out_blocks, log_totals = lax.map(attend_block, indices)
    attn = out_blocks.reshape(length, local_width).astype(jnp.bfloat16)
    pieces = (
        lax.all_gather(w_out, "dp", axis=1, tiled=True),
        lax.all_gather(w_down, "dp", axis=1, tiled=True),
    )
    part = jnp.dot(attn, pieces[0], preferred_element_type=jnp.float32) + jnp.dot(
        hidden, pieces[1], preferred_element_type=jnp.float32
    )
    partial_value = part
    branch = lax.psum_scatter(partial_value, "tensor", scatter_dimension=0, tiled=True)
    layer_out = (input_float + branch + b_out + b_down).astype(jnp.bfloat16)
    grad_all = lax.all_gather(cotangent, "tensor", axis=0, tiled=True)
    pieces = (
        lax.all_gather(w_out, "dp", axis=1, tiled=True),
        lax.all_gather(w_down, "dp", axis=1, tiled=True),
    )
    columns = grad_all
    attn_grad = times_transposed(columns, pieces[0])
    hidden_grad = times_transposed(columns, pieces[1])
    down_joined = jnp.concatenate([attn, hidden], axis=1)
    unused, gelu_pull = jax.vjp(lambda inner: jax.nn.gelu(inner, approximate=True), up_pre)
    up_grad_low = gelu_pull(hidden_grad)[0].astype(jnp.bfloat16)
    attn_grad_low = attn_grad.astype(jnp.bfloat16).reshape(length, heads_here, HEAD_DIM)

    def back_block(carry, item):
        key_grad, value_grad = carry
        index, lse_rows = item
        offset = index * block_rows
        query_rows = lax.dynamic_slice_in_dim(query, offset, block_rows, 0)
        grad_rows = lax.dynamic_slice_in_dim(attn_grad_low, offset, block_rows, 0)
        scores = scores_for(query_rows, offset)
        probs = jnp.exp(scores - lse_rows[..., None])
        value_grad = value_grad + jnp.einsum(
            "hqk,qhd->khd",
            probs.astype(jnp.bfloat16),
            grad_rows,
            preferred_element_type=jnp.float32,
        )
        prob_grad = jnp.einsum("qhd,khd->hqk", grad_rows, value, preferred_element_type=jnp.float32)
        delta = jnp.sum(probs * prob_grad, axis=-1, keepdims=True)
        score_grad = (probs * (prob_grad - delta)).astype(jnp.bfloat16)
        query_grad = (
            jnp.einsum("hqk,khd->qhd", score_grad, key, preferred_element_type=jnp.float32)
            * score_scale
        )
        key_grad = (
            key_grad
            + jnp.einsum("hqk,qhd->khd", score_grad, query_rows, preferred_element_type=jnp.float32)
            * score_scale
        )
        return ((key_grad, value_grad), query_grad)

    state_zeros = jnp.zeros((length, heads_here, HEAD_DIM), jnp.float32)
    (key_grad, value_grad), query_blocks = lax.scan(
        back_block, (state_zeros, state_zeros), (indices, log_totals)
    )
    query_grad = query_blocks.reshape(length, heads_here, HEAD_DIM)
    q_grad_low = (
        rotate(query_grad, positions, -1.0).reshape(length, local_width).astype(jnp.bfloat16)
    )
    k_grad_low = rotate(key_grad, positions, -1.0).reshape(length, local_width).astype(jnp.bfloat16)
    v_grad_low = value_grad.reshape(length, local_width).astype(jnp.bfloat16)
    up_joined = jnp.concatenate([q_grad_low, k_grad_low, v_grad_low, up_grad_low], axis=1)
    columns = grad_all
    joined_rows = lax.psum_scatter(
        jnp.concatenate(
            [rows_transposed(columns, down_joined), rows_transposed(normed_all, up_joined)], axis=1
        ),
        "dp",
        scatter_dimension=0,
        tiled=True,
    )
    down_rows = joined_rows[:, : local_width + hidden_here]
    up_rows = joined_rows[:, local_width + hidden_here :]
    d_w_out = down_rows[:, :local_width].T
    d_w_down = down_rows[:, local_width:].T
    d_w_query = up_rows[:, :local_width]
    d_w_key = up_rows[:, local_width : 2 * local_width]
    d_w_value = up_rows[:, 2 * local_width : 3 * local_width]
    d_w_up = up_rows[:, 3 * local_width :]
    pieces = (
        lax.all_gather(w_query, "dp", axis=0, tiled=True),
        lax.all_gather(w_key, "dp", axis=0, tiled=True),
        lax.all_gather(w_value, "dp", axis=0, tiled=True),
        lax.all_gather(w_up, "dp", axis=0, tiled=True),
    )
    part = (
        times_transposed(q_grad_low, pieces[0])
        + times_transposed(k_grad_low, pieces[1])
        + times_transposed(v_grad_low, pieces[2])
        + times_transposed(up_grad_low, pieces[3])
    )
    own_grad = lax.psum_scatter(part, "tensor", scatter_dimension=0, tiled=True)
    scaled_grad = own_grad * ln_gain
    norm_part = inverse * (
        scaled_grad
        - jnp.mean(scaled_grad, axis=-1, keepdims=True)
        - unit_rows * jnp.mean(scaled_grad * unit_rows, axis=-1, keepdims=True)
    )
    cot_float = cotangent.astype(jnp.float32)
    d_input = cot_float + norm_part
    d_ln_gain, d_ln_bias, d_b_out = lax.psum(
        (
            jnp.sum(own_grad * unit_rows, axis=0),
            jnp.sum(own_grad, axis=0),
            jnp.sum(cot_float, axis=0),
        ),
        ("dp", "tensor"),
    )
    d_b_query, d_b_key, d_b_value, d_b_up = lax.psum(
        (
            jnp.sum(q_grad_low.astype(jnp.float32), axis=0),
            jnp.sum(k_grad_low.astype(jnp.float32), axis=0),
            jnp.sum(v_grad_low.astype(jnp.float32), axis=0),
            jnp.sum(up_grad_low.astype(jnp.float32), axis=0),
        ),
        "dp",
    )
    return (
        layer_out,
        d_input,
        d_ln_gain,
        d_ln_bias,
        d_w_query,
        d_b_query,
        d_w_key,
        d_b_key,
        d_w_value,
        d_b_value,
        d_w_out,
        d_b_out,
        d_w_up,
        d_b_up,
        d_w_down,
        d_b_out,
    )


def on_device(
    layer_input, ln_gain, ln_bias, w_query, b_query, w_key, b_key, w_value, b_value,
    w_out, b_out, w_up, b_up, w_down, b_down, prefix, cotangent,
):
    n = lax.axis_size("tensor")
    width = w_query.shape[1]
    normed, cots, w_qkv, w_up_all, grads, joined, branch = forward_call(
        n, prefix, layer_input, cotangent, w_query, w_key, w_value, w_out, w_up, w_down,
        ln_gain, ln_bias, b_query, b_key, b_value, b_up,
    )
    layer_out, d_input, d_in, d_dn, d_bias, d_all = backward_call(
        n, layer_input, normed, cots, w_qkv, w_up_all, grads, joined, branch, ln_gain, b_out, b_down
    )
    flat, bias = d_all.reshape(-1), d_bias.reshape(-1)
    d = layer_input.shape[1]
    d_ln_gain, d_ln_bias, d_b_out = (flat[i * d : (i + 1) * d] for i in range(3))
    d_w_query, d_w_key, d_w_value = (d_in[:, i * width : (i + 1) * width] for i in range(3))
    d_b_query, d_b_key, d_b_value = (bias[i * width : (i + 1) * width] for i in range(3))
    return (
        layer_out, d_input, d_ln_gain, d_ln_bias, d_w_query, d_b_query, d_w_key, d_b_key,
        d_w_value, d_b_value, d_dn[:width], d_b_out, d_in[:, 3 * width :],
        bias[3 * width : 3 * width + w_up.shape[1]], d_dn[width:], d_b_out,
    )


def solution(mesh):
    fits = mesh.shape["dp"] == 8 and mesh.shape["tensor"] == 4
    return jax.shard_map(
        on_device if fits else plain_on_device,
        mesh=mesh,
        in_specs=(
            P(("dp", "tensor"), None),
            P(),
            P(),
            P("dp", "tensor"),
            P("tensor"),
            P("dp", "tensor"),
            P("tensor"),
            P("dp", "tensor"),
            P("tensor"),
            P("tensor", "dp"),
            P(),
            P("dp", "tensor"),
            P("tensor"),
            P("tensor", "dp"),
            P(),
            P("dp"),
            P(("dp", "tensor"), None),
        ),
        out_specs=(
            P(("dp", "tensor"), None),
            P(("dp", "tensor"), None),
            P(),
            P(),
            P("dp", "tensor"),
            P("tensor"),
            P("dp", "tensor"),
            P("tensor"),
            P("dp", "tensor"),
            P("tensor"),
            P("tensor", "dp"),
            P(),
            P("dp", "tensor"),
            P("tensor"),
            P("tensor", "dp"),
            P(),
        ),
        check_vma=False,
    )
```

```python
import functools
import math

import jax
import jax.numpy as jnp
import numpy as np
from jax import lax
from jax.experimental import pallas as pl
from jax.experimental.pallas import tpu as pltpu
from jax.sharding import PartitionSpec as P

HEAD_DIM = 64
ROT_DIM = 32
MESH = pl.DeviceIdType.MESH
BF = jnp.bfloat16
F32 = jnp.float32

epsilon = 1e-05
rope_base = 10000.0
masked_score = -1e30
root = math.sqrt(2.0 / math.pi)


def nn(a, b):
    return jnp.dot(a, b, preferred_element_type=F32)


def nt(a, b):
    return lax.dot_general(a, b, (((1,), (1,)), ((), ())), preferred_element_type=F32)


def tn(a, b):
    return lax.dot_general(a, b, (((0,), (0,)), ((), ())), preferred_element_type=F32)


def rows_at(index, size):
    return pl.ds(pl.multiple_of(index * size, size), size)


def flip(index, bit):
    return index + bit - 2 * bit * lax.rem(index // bit, 2)


class Copies:
    def __init__(self, send, recv):
        self.send, self.recv, self.count, self.sent = send, recv, 0, []

    def new(self):
        self.count += 1
        return self.count - 1

    def make(self, k, src, dst, device):
        return pltpu.make_async_remote_copy(
            src, dst, self.send.at[k], self.recv.at[k], device_id=device, device_id_type=MESH
        )

    def start(self, k, src, dst, device):
        copy = self.make(k, src, dst, device)
        copy.start()
        self.sent.append(copy)

    def wait(self, k, dst, device):
        self.make(k, dst, dst, device).wait_recv()

    def finish(self):
        for copy in self.sent:
            copy.wait_send()


class Spread:
    def __init__(self, copies, view, me, z):
        self.c, self.view, self.me, self.z = copies, view, me, z
        self.k = [copies.new() for _ in range(9)]

    def dev(self, bit):
        return (flip(self.me, bit), self.z)

    def own(self):
        v = self.view(self.me)
        self.c.start(self.k[1], v, v, self.dev(2))
        self.c.start(self.k[2], v, v, self.dev(4))
        self.c.start(self.k[0], v, v, self.dev(1))

    def forward(self):
        c, x, y = self.c, flip(self.me, 2), flip(self.me, 4)
        c.wait(self.k[1], self.view(x), self.dev(2))
        v = self.view(x, 0)
        c.start(self.k[3], v, v, self.dev(4))
        c.wait(self.k[2], self.view(y), self.dev(4))
        v = self.view(y, 1)
        c.start(self.k[4], v, v, self.dev(2))
        v = self.view(x)
        c.start(self.k[5], v, v, self.dev(1))
        v = self.view(y)
        c.start(self.k[6], v, v, self.dev(1))

    def last(self):
        c, far = self.c, flip(flip(self.me, 2), 4)
        c.wait(self.k[3], self.view(far, 0), self.dev(4))
        c.wait(self.k[4], self.view(far, 1), self.dev(2))
        v = self.view(far)
        c.start(self.k[7], v, v, self.dev(1))

    def ready(self):
        c, s = self.c, flip(self.me, 1)
        c.wait(self.k[0], self.view(s), self.dev(1))
        c.wait(self.k[5], self.view(flip(s, 2)), self.dev(1))
        c.wait(self.k[6], self.view(flip(s, 4)), self.dev(1))
        c.wait(self.k[7], self.view(flip(flip(s, 2), 4)), self.dev(1))


class Line:
    CHUNKS = 4

    def __init__(self, copies, buf, size, n, me, z):
        self.c, self.buf, self.size, self.n, self.me, self.z = copies, buf, size // self.CHUNKS, n, me, z
        self.k = [[[copies.new() for _ in range(self.CHUNKS)] for _ in range(2)] for _ in range(n - 1)]

    def copy(self, s, way, c, block):
        z, n = self.z, self.n
        to = jnp.minimum(z + 1, n - 1) if way == 0 else jnp.maximum(z - 1, 0)
        v = self.buf.at[rows_at(jnp.clip(block, 0, n - 1) * self.CHUNKS + c, self.size), :]
        return self.c.make(self.k[s][way][c], v, v, (self.me, to))

    def far(self, way):
        return self.z if way == 0 else self.n - 1 - self.z

    def block(self, way, s):
        return self.z - s if way == 0 else self.z + s

    def own(self, c):
        for way in range(2):

            @pl.when(self.far(way) < self.n - 1)
            def _():
                self.copy(0, way, c, self.z).start()

    def event(self, s, c):
        for way in range(2):
            far = self.far(way)

            @pl.when(far >= s + 1)
            def _():
                self.copy(s, way, c, self.block(way, s + 1)).wait_recv()

            if s + 1 < self.n - 1:

                @pl.when((far >= s + 1) & (far < self.n - 1))
                def _():
                    self.copy(s + 1, way, c, self.block(way, s + 1)).start()

    def finish(self):
        for s in range(self.n - 1):
            for way in range(2):
                far = self.far(way)

                @pl.when((far >= s) & (far < self.n - 1))
                def _():
                    for c in range(self.CHUNKS):
                        self.copy(s, way, c, self.z).wait_send()


class Fold:
    def __init__(self, part, slots, send, recv, tiles, size, n, me, z):
        self.part, self.slots, self.send, self.recv = part, slots, send, recv
        self.tiles, self.size, self.n, self.me, self.z = list(tiles), size, n, me, z

    def far(self, way):
        return self.z if way == 0 else self.n - 1 - self.z

    def copy(self, way, t, i):
        z, n = self.z, self.n
        to = jnp.minimum(z + 1, n - 1) if way == 0 else jnp.maximum(z - 1, 0)
        goal = n - 1 - i if way == 0 else i
        k = self.tiles.index(t) * (n - 1) + i
        return pltpu.make_async_remote_copy(
            self.part.at[goal * self.size : (goal + 1) * self.size, t * PIECE : (t + 1) * PIECE],
            self.slots.at[way, k],
            self.send.at[way, k],
            self.recv.at[way, k],
            device_id=(self.me, to),
            device_id_type=MESH,
        )

    def first(self, t):
        for way in range(2):

            @pl.when(self.far(way) == 0)
            def _():
                for i in range(self.n - 1):
                    self.copy(way, t, i).start()

    def event(self, t, far):
        n = self.n
        for way in range(2):

            @pl.when(self.far(way) == far)
            def _():
                for i in range(n - far):
                    goal = n - 1 - i if way == 0 else i
                    k = self.tiles.index(t) * (n - 1) + i
                    self.copy(way, t, i).wait_recv()
                    at = (slice(goal * self.size, (goal + 1) * self.size), slice(t * PIECE, (t + 1) * PIECE))
                    self.part[at] = (self.part[at].astype(F32) + self.slots[way, k].astype(F32)).astype(BF)
                    if i < n - 1 - far:
                        self.copy(way, t, i).start()

    def finish(self):
        n = self.n
        for way in range(2):
            far = self.far(way)
            for i in range(n - 1):

                @pl.when(far < n - 1 - i)
                def _():
                    for t in self.tiles:
                        self.copy(way, t, i).wait_send()


PIECE = 512
EARLY = 2
ORDER = (
    "own.up0", "own.up1", "norm0", "nown0", "norm1", "nown1", "norm2", "nown2", "norm3", "nown3", "n00",
    "fwd.up0", "own.q0", "n01", "n02", "fwd.up1", "own.q1", "n03", "last.up0", "n10", "ready.up0", "raise00",
    "raise10", "n11", "fwd.q0", "n12", "last.up1", "ready.up1", "raise01", "n13", "cown", "raise11",
    "raise20", "fwd.q1", "own.dn0", "own.dn1", "n20", "raise21", "last.q0", "ready.q0", "n21", "last.q1",
    "ready.q1", "n22", "fwd.dn0", "own.dn2", "n23", "proj", "c00", "att0", "c01", "last.dn0", "fwd.dn1",
    "att1", "c02", "c03", "ready.dn0", "fwd.dn2", "raise30", "raise31", "c10", "ab0", "c11", "last.dn1",
    "last.dn2", "ab1", "c12", "c13", "ready.dn1", "ready.dn2", "lower0", "ffirst0", "lower1", "c20",
    "ffirst1", "lower2", "c21", "lower3", "ab2", "c22", "c23", "ab3", "f01", "hg0", "hg1", "hg2", "f11",
    "hg3", "f02", "kb", "f03", "f12", "f13",
)


def turned(x, table, sign):
    return (
        x * table[0]
        + pltpu.roll(x, 112, 1) * (table[1] * sign)
        + pltpu.roll(x, 16, 1) * (table[2] * sign)
    )


def gather_forward(
    n,
    prefix,
    x,
    cot,
    wq,
    wk,
    wv,
    wo,
    wu,
    wd,
    gain,
    bias,
    bq,
    bk,
    bv,
    bu,
    table,
    normed_out,
    cots_out,
    w_qkv_out,
    w_up_out,
    grads_out,
    joined_out,
    branch_out,
    normed,
    cots,
    w_qkv,
    w_up,
    w_dn,
    qkv,
    joined,
    slope,
    d_attn,
    d_key,
    d_value,
    own_x,
    lse,
    lse_row,
    fold_slots,
    send,
    recv,
    local,
    outs,
    fold_send,
    fold_recv,
):
    me, z = lax.axis_index("dp"), lax.axis_index("tensor")
    size, d = x.shape
    length = n * size
    width = wq.shape[1]
    ff = wu.shape[1]
    shard = wq.shape[0]
    lanes = wo.shape[1]
    branch = normed

    barrier = pltpu.get_barrier_semaphore()
    for bit in (1, 2, 4):
        pl.semaphore_signal(barrier, 1, device_id=(flip(me, bit), z), device_id_type=MESH)

    @pl.when(z > 0)
    def _():
        pl.semaphore_signal(barrier, 1, device_id=(me, jnp.maximum(z - 1, 0)), device_id_type=MESH)

    @pl.when(z < n - 1)
    def _():
        pl.semaphore_signal(barrier, 1, device_id=(me, jnp.minimum(z + 1, n - 1)), device_id_type=MESH)

    mine, cols = rows_at(me, shard), rows_at(me, lanes)
    loads = [
        pltpu.make_async_copy(x, own_x, local.at[0]),
        pltpu.make_async_copy(wu, w_up.at[mine, :], local.at[1]),
        pltpu.make_async_copy(wq, w_qkv.at[mine, pl.ds(0, width)], local.at[2]),
        pltpu.make_async_copy(wk, w_qkv.at[mine, pl.ds(width, width)], local.at[3]),
        pltpu.make_async_copy(wv, w_qkv.at[mine, pl.ds(2 * width, width)], local.at[4]),
        pltpu.make_async_copy(wo, w_dn.at[pl.ds(0, width), cols], local.at[5]),
        pltpu.make_async_copy(wd, w_dn.at[pl.ds(width, ff), cols], local.at[6]),
        pltpu.make_async_copy(cot, cots.at[rows_at(z, size), :], local.at[7]),
    ]
    for load in loads:
        load.start()

    stores = []

    def store(src, dst):
        copy = pltpu.make_async_copy(src, dst, outs.at[len(stores)])
        stores.append(copy)
        copy.start()
        return copy

    copies = Copies(send, recv)

    def row_view(buf, first, count):
        def view(i, half=None):
            h = count if half is None else count // 2
            start = i * shard + first + (0 if half is None else half * h)
            return buf.at[pl.ds(pl.multiple_of(start, h), h), :]

        return view

    def col_view(first, count):
        def view(i, half=None):
            if half is None:
                return w_dn.at[pl.ds(first, count), rows_at(i, lanes)]
            h = count // 2
            return w_dn.at[pl.ds(first + half * h, h), rows_at(i, lanes)]

        return view

    def row_col_view(first, count):
        def view(i, half=None):
            h = shard if half is None else shard // 2
            start = i * shard + (0 if half is None else half * h)
            return w_up.at[pl.ds(pl.multiple_of(start, h), h), pl.ds(first, count)]

        return view

    s_up = [Spread(copies, row_col_view(i * ff // 2, ff // 2), me, z) for i in range(2)]
    s_qkv = [Spread(copies, row_view(w_qkv, i * shard // 2, shard // 2), me, z) for i in range(2)]
    s_dn = [Spread(copies, col_view(*v), me, z) for v in ((0, width), (width, ff // 2), (width + ff // 2, ff // 2))]
    l_n = Line(copies, normed, size, n, me, z)
    l_c = Line(copies, cots, size, n, me, z)
    fold = Fold(branch, fold_slots, fold_send, fold_recv, range(EARLY), size, n, me, z)
    order = [z, flip(z, 1), flip(z, 2), flip(flip(z, 1), 2)]
    head = lax.broadcasted_iota(jnp.int32, (1, 128), 1) // HEAD_DIM

    def norm(r):
        rows = slice(r * 64, (r + 1) * 64)
        v = own_x[rows, :].astype(F32)
        mean = jnp.mean(v, axis=-1, keepdims=True)
        c = v - mean
        inv = lax.rsqrt(jnp.mean(c * c, axis=-1, keepdims=True) + epsilon)
        out = (c * inv) * gain[...] + bias[...]
        normed[pl.ds(pl.multiple_of(z * size + r * 64, 64), 64), :] = out.astype(BF)

    def project():
        tile = 512

        @pl.loop(0, length // tile)
        def _(m):
            rows = rows_at(m, tile)
            tab = [table[i, rows, :] for i in range(3)]
            for part in range(3):
                acc = nn(normed[rows, :], w_qkv[:, part * width : (part + 1) * width])
                acc = acc + (bq, bk, bv)[part][...]
                for p in range(width // 128):
                    piece = acc[:, p * 128 : (p + 1) * 128]
                    if part < 2:
                        piece = turned(piece, tab, 1.0)
                        if part == 0:
                            piece = piece * (1.0 / math.sqrt(HEAD_DIM))
                    qkv[rows, part * width + p * 128 : part * width + (p + 1) * 128] = piece.astype(BF)

    def raise_(j, part):
        rows = rows_at(j, size)
        tile = 512

        @pl.loop(part * ff // tile // 2, (part + 1) * ff // tile // 2)
        def _(t):
            cs = rows_at(t, tile)
            u = nn(normed[rows, :], w_up[:, cs]) + bu[:, cs]
            sq = u * u
            th = jnp.tanh(root * u * (1.0 + 0.044715 * sq))
            half = 0.5 * (1.0 + th)
            joined[rows, pl.ds(pl.multiple_of(width + t * tile, tile), tile)] = (u * half).astype(BF)
            slope[rows, cs] = (
                half + 0.5 * u * (1.0 - th * th) * (root * (1.0 + 3 * 0.044715 * sq))
            ).astype(BF)

    block = length // 4

    def visible(b):
        return (b if b > 0 else 0), max(b + 1, 2)

    def attend(first, count):
        @pl.loop(first, first + count)
        def _(p):
            ps = rows_at(p, 128)
            ks = pl.ds(pl.multiple_of(width + p * 128, 128), 128)
            vs = pl.ds(pl.multiple_of(2 * width + p * 128, 128), 128)
            lane = lax.broadcasted_iota(jnp.int32, (1, 128), 1)
            for b in range(4):
                full, some = visible(b)
                qs = pl.ds(b * block, block)
                parts = [(0, full)] * (full > 0) + [(full, some)]
                limit = jnp.maximum(
                    b * block + lax.broadcasted_iota(jnp.int32, (block, 1), 0), prefix[0] - 1
                )
                outs_ = []
                for h in range(2):
                    q = qkv[qs, ps]
                    q = jnp.where(head == h, q, jnp.zeros_like(q))
                    scores = []
                    for lo, hi in parts:
                        kr = pl.ds(lo * block, (hi - lo) * block)
                        s = nt(q, qkv[kr, ks])
                        if lo == full:
                            at = lo * block + lax.broadcasted_iota(jnp.int32, s.shape, 1)
                            s = jnp.where(at <= limit, s, masked_score)
                        scores.append(s)
                    top = functools.reduce(jnp.maximum, [jnp.max(s, axis=-1, keepdims=True) for s in scores])
                    e = [jnp.exp(s - top) for s in scores]
                    total = sum(jnp.sum(v, axis=-1, keepdims=True) for v in e)
                    inv = 1.0 / total
                    outs_.append(
                        sum(
                            nn((v * inv).astype(BF), qkv[pl.ds(lo * block, (hi - lo) * block), vs])
                            for v, (lo, hi) in zip(e, parts)
                        )
                    )
                    lse[qs, :] = jnp.where(lane == 2 * p + h, top + jnp.log(total), lse[qs, :])
                joined[qs, ps] = jnp.where(head == 0, outs_[0], outs_[1]).astype(BF)

    def lower(t):
        @pl.loop(0, length // 512)
        def _(m):
            rows = rows_at(m, 512)
            branch[rows, t * PIECE : (t + 1) * PIECE] = nn(
                joined[rows, :], w_dn[:, t * PIECE : (t + 1) * PIECE]
            ).astype(BF)

    def hidden_back(j):
        rows = rows_at(j, size)
        tile = 512

        @pl.loop(0, ff // tile)
        def _(t):
            g = nt(cots[rows, :], w_dn[pl.ds(pl.multiple_of(width + t * tile, tile), tile), :])
            cs = rows_at(t, tile)
            slope[rows, cs] = (g * slope[rows, cs].astype(F32)).astype(BF)

    def attend_back(b):
        full, some = visible(b)
        qs = pl.ds(b * block, block)
        limit = jnp.maximum(b * block + lax.broadcasted_iota(jnp.int32, (1, block), 1), prefix[0] - 1)

        @pl.loop(0, width // 128)
        def _(p):
            ps = rows_at(p, 128)
            ks = pl.ds(pl.multiple_of(width + p * 128, 128), 128)
            vs = pl.ds(pl.multiple_of(2 * width + p * 128, 128), 128)
            only = lambda a, h: jnp.where(head == h, a, jnp.zeros_like(a))
            q, g = qkv[qs, ps], d_attn[:, ps]
            dq = None
            for h in range(2):
                qh, gh = only(q, h), only(g, h)
                kept = []
                delta = None
                for kb in range(some):
                    kr = pl.ds(kb * block, block)
                    probs = jnp.exp(nt(qkv[kr, ks], qh) - lse_row[pl.ds(2 * p + h, 1), qs])
                    if kb >= full:
                        at = kb * block + lax.broadcasted_iota(jnp.int32, (block, block), 0)
                        probs = jnp.where(at <= limit, probs, 0.0)
                    d_value[kr, ps] += nn(probs.astype(BF), gh)
                    d_probs = nt(qkv[kr, vs], gh)
                    kept.append((probs, d_probs))
                    add = jnp.sum(probs * d_probs, axis=0, keepdims=True)
                    delta = add if delta is None else delta + add
                for kb, (probs, d_probs) in enumerate(kept):
                    kr = pl.ds(kb * block, block)
                    ds = (probs * (d_probs - delta)).astype(BF)
                    d_key[kr, ps] += nn(ds, qh)
                    add = tn(ds, only(qkv[kr, ks], h))
                    dq = add if dq is None else dq + add
            tab = [table[i, qs, :] for i in range(3)]
            qkv[qs, ps] = turned(dq * (1.0 / math.sqrt(HEAD_DIM)), tab, -1.0).astype(BF)

    def back(k):
        d_attn[...] = nt(cots[rows_at(order[k], size), :], w_dn[:width, :]).astype(BF)
        for b in range(4):

            @pl.when(order[k] == b)
            def _():
                attend_back(b)

    def keys_back():
        @pl.loop(0, width // 128)
        def _(p):
            ps = rows_at(p, 128)
            ks = pl.ds(pl.multiple_of(width + p * 128, 128), 128)
            vs = pl.ds(pl.multiple_of(2 * width + p * 128, 128), 128)
            tab = [table[i] for i in range(3)]
            qkv[:, ks] = turned(d_key[:, ps], tab, -1.0).astype(BF)
            qkv[:, vs] = d_value[:, ps].astype(BF)

    signals = 3 + jnp.where(z > 0, 1, 0) + jnp.where(z < n - 1, 1, 0)
    pl.semaphore_wait(barrier, signals)

    n_stored = []
    part = functools.partial

    def clear():
        lse[...] = jnp.zeros_like(lse)
        d_key[...] = jnp.zeros_like(d_key)
        d_value[...] = jnp.zeros_like(d_value)

    def wait_loads(*which):
        for i in which:
            loads[i].wait()

    def heads_end():
        lse_row[...] = lse[...].T[: lse_row.shape[0], :]

    def branch_free():
        l_n.finish()
        n_stored[0].wait()

    todo = {
        "own.up0": [part(wait_loads, 1), s_up[0].own],
        "own.q0": [part(wait_loads, 2, 3, 4), s_qkv[0].own],
        "own.dn0": [part(wait_loads, 5), s_dn[0].own],
        "own.dn1": [part(wait_loads, 6), s_dn[1].own],
        "norm0": [part(wait_loads, 0), part(norm, 0)],
        "nown3": [part(l_n.own, 3), clear],
        "ready.up1": [s_up[1].ready, part(store, w_up, w_up_out)],
        "ready.q1": [s_qkv[1].ready, part(store, w_qkv, w_qkv_out)],
        "n23": [part(l_n.event, 2, 3), lambda: n_stored.append(store(normed, normed_out))],
        "cown": [part(wait_loads, 7)] + [part(l_c.own, c) for c in range(Line.CHUNKS)],
        "c23": [part(l_c.event, 2, 3), part(store, cots, cots_out)],
        "proj": [project],
        "att0": [part(attend, 0, 2)],
        "att1": [part(attend, 2, 2), heads_end],
        "raise31": [part(raise_, order[3], 1), part(store, joined, joined_out)],
        "lower0": [branch_free, part(lower, 0)],
        "hg3": [part(hidden_back, order[3]), part(store, slope, grads_out.at[:, pl.ds(3 * width, ff)])],
        "kb": [keys_back, part(store, qkv, grads_out.at[:, pl.ds(0, 3 * width)])],
    }
    for name, spreads in (("up", s_up), ("q", s_qkv), ("dn", s_dn)):
        for i, s in enumerate(spreads):
            for what, call in (("own", s.own), ("fwd", s.forward), ("last", s.last), ("ready", s.ready)):
                todo.setdefault(what + "." + name + str(i), [call])
    for c in range(Line.CHUNKS):
        todo.setdefault("norm" + str(c), [part(norm, c)])
        todo.setdefault("nown" + str(c), [part(l_n.own, c)])
        for s in range(n - 1):
            todo.setdefault("n" + str(s) + str(c), [part(l_n.event, s, c)])
            todo.setdefault("c" + str(s) + str(c), [part(l_c.event, s, c)])
    for k in range(4):
        for i in range(2):
            todo.setdefault("raise" + str(k) + str(i), [part(raise_, order[k], i)])
        todo.setdefault("hg" + str(k), [part(hidden_back, order[k])])
        todo.setdefault("ab" + str(k), [part(back, k)])
        todo.setdefault("lower" + str(k), [part(lower, k)])
        todo.setdefault("ffirst" + str(k), [part(fold.first, k)])
        for far in range(1, n):
            todo.setdefault("f" + str(k) + str(far), [part(fold.event, k, far)])
    for name in ORDER:
        for call in todo[name]:
            call()
    store(branch, branch_out)
    for copy in stores:
        if copy is not n_stored[0]:
            copy.wait()
    fold.finish()
    l_c.finish()
    copies.finish()


def tables(length):
    half = ROT_DIM // 2
    freqs = rope_base ** (-(np.arange(half).astype(np.float32) * 2.0 / ROT_DIM))
    angles = np.arange(length).astype(np.float32)[:, None] * freqs[None, :].astype(np.float32)
    cos, sin = np.cos(angles), np.sin(angles)
    rest = np.zeros((length, HEAD_DIM - ROT_DIM), np.float32)
    none = np.zeros((length, half), np.float32)
    c = np.concatenate([cos, cos, rest + 1.0], 1)
    s1 = np.concatenate([-sin, none, rest], 1)
    s2 = np.concatenate([none, sin, rest], 1)
    return jnp.asarray(np.stack([np.concatenate([t, t], 1) for t in (c, s1, s2)]).astype(np.float32))


def forward_call(n, prefix, x, cot, wq, wk, wv, wo, wu, wd, gain, bias, bq, bk, bv, bu):
    size, d = x.shape
    length, width, ff = n * size, wq.shape[1], wu.shape[1]
    vm, hbm = pl.BlockSpec(memory_space=pltpu.VMEM), pl.BlockSpec(memory_space=pl.ANY)
    shape = lambda s, t=BF: jax.ShapeDtypeStruct(s, t)
    dma = pltpu.SemaphoreType.DMA
    count = 7 * 9 + 2 * (n - 1) * 2 * Line.CHUNKS
    return pl.pallas_call(
        functools.partial(gather_forward, n),
        out_shape=(
            shape((length, d)),
            shape((length, d)),
            shape((d, 3 * width)),
            shape((d, ff)),
            shape((length, 3 * width + ff)),
            shape((length, width + ff)),
            shape((length, d)),
        ),
        in_specs=[pl.BlockSpec(memory_space=pltpu.SMEM)] + [hbm] * 8 + [vm] * 7,
        out_specs=(hbm,) * 7,
        scratch_shapes=[
            pltpu.VMEM((length, d), BF),
            pltpu.VMEM((length, d), BF),
            pltpu.VMEM((d, 3 * width), BF),
            pltpu.VMEM((d, ff), BF),
            pltpu.VMEM((width + ff, d), BF),
            pltpu.VMEM((length, 3 * width), BF),
            pltpu.VMEM((length, width + ff), BF),
            pltpu.VMEM((length, ff), BF),
            pltpu.VMEM((size, width), BF),
            pltpu.VMEM((length, width), F32),
            pltpu.VMEM((length, width), F32),
            pltpu.VMEM((size, d), BF),
            pltpu.VMEM((length, 128), F32),
            pltpu.VMEM((width // HEAD_DIM, length), F32),
            pltpu.VMEM((2, EARLY * (n - 1), size, PIECE), BF),
            dma((count,)),
            dma((count,)),
            dma((8,)),
            dma((8,)),
            dma((2, EARLY * (n - 1))),
            dma((2, EARLY * (n - 1))),
        ],
        compiler_params=pltpu.CompilerParams(
            collective_id=1, has_side_effects=True, vmem_limit_bytes=63 << 20
        ),
        cost_estimate=pl.CostEstimate(flops=50_000_000_000, bytes_accessed=100_000_000, transcendentals=0),
    )(
        prefix,
        x,
        cot,
        wq,
        wk,
        wv,
        wo,
        wu,
        wd,
        gain[None],
        bias[None],
        bq[None],
        bk[None],
        bv[None],
        bu[None],
        tables(length),
    )


SIB_SLOTS = 2
SLOTS = 4


def backward_scatter(
    n,
    x,
    normed,
    cots,
    w_qkv,
    w_up,
    grads_in,
    joined,
    branch,
    gain,
    b_out,
    b_down,
    layer_out,
    d_input,
    d_in,
    d_dn,
    d_bias,
    d_all,
    own_x,
    cot,
    grads,
    n_block,
    n_turned,
    j_block,
    j_turned,
    wq_block,
    wu_block,
    part_b,
    part_g,
    slots_b,
    slots_g,
    sib_out,
    sib_in,
    own_low,
    own_sum,
    x_in,
    y_in,
    end_in,
    d_rows,
    narrow,
    wide,
    wide_z,
    sums,
    b_send,
    b_recv,
    g_send,
    g_recv,
    sib_send,
    sib_recv,
    link_send,
    link_recv,
    out_sem,
    local,
    stream,
    small_send,
    small_recv,
):
    me, z = lax.axis_index("dp"), lax.axis_index("tensor")
    size, d = x.shape
    length = n * size
    ff = w_up.shape[1]
    width = joined.shape[1] - ff
    lanes = d // 8
    down_pieces = (width + ff) // PIECE
    up_pieces = (3 * width + ff) // PIECE
    pieces = down_pieces + up_pieces
    half, quarter = PIECE // 2, PIECE // 4
    sib = (flip(me, 1), z)
    x_to, y_to = (flip(me, 2), z), (flip(me, 4), z)

    barrier = pltpu.get_barrier_semaphore()
    peers = []
    for k in range(1, 8):
        to = me
        for bit in (1, 2, 4):
            if k & bit:
                to = flip(to, bit)
        peers.append(to)
        pl.semaphore_signal(barrier, 1, device_id=(to, z), device_id_type=MESH)
    others = [lax.rem(z + k, n) for k in range(1, n)]
    for to in others:
        pl.semaphore_signal(barrier, 1, device_id=(me, to), device_id_type=MESH)

    def load(k, src, dst):
        return pltpu.make_async_copy(src, dst, local.at[k])

    loads = [
        load(0, branch, part_b),
        load(1, cots, cot),
        load(2, grads_in, grads),
        load(3, x, own_x),
    ]

    def j_load(p):
        return pltpu.make_async_copy(
            joined.at[:, rows_at(jnp.minimum(p, down_pieces - 1), PIECE)],
            j_block.at[lax.rem(p, 2)],
            stream.at[lax.rem(p, 2)],
        )

    def w_loads(t):
        return [
            pltpu.make_async_copy(w_qkv.at[rows_at(t, PIECE), :], wq_block.at[t % 2], stream.at[2 + t % 2]),
            pltpu.make_async_copy(w_up.at[rows_at(t, PIECE), :], wu_block.at[t % 2], stream.at[4 + t % 2]),
        ]

    def n_load(j):
        return pltpu.make_async_copy(normed.at[rows_at(j, size), :], n_block, stream.at[6])

    j_load(0).start()
    for l in [loads[1], loads[0]] + [n_load(0)] + w_loads(0) + [loads[2], loads[3]] + w_loads(1):
        l.start()

    fold_b = Fold(part_b, slots_b, b_send, b_recv, range(EARLY, d // PIECE), size, n, me, z)
    fold_g = Fold(part_g, slots_g, g_send, g_recv, range(d // PIECE), size, n, me, z)

    goals = [flip(me, 2), flip(flip(me, 2), 4), flip(me, 4), me]

    def sib_copy(p):
        return pltpu.make_async_remote_copy(
            sib_out.at[lax.rem(p, 2)],
            sib_in.at[lax.rem(p, SIB_SLOTS)],
            sib_send.at[lax.rem(p, 2)],
            sib_recv.at[lax.rem(p, SIB_SLOTS)],
            device_id=sib,
            device_id_type=MESH,
        )

    def link_copy(k, p, src, dst, to):
        slot = lax.rem(p, SLOTS)
        return pltpu.make_async_remote_copy(
            src, dst, link_send.at[k, slot], link_recv.at[k, slot], device_id=to, device_id_type=MESH
        )

    def x_first(p):
        slot = lax.rem(p, SLOTS)
        return link_copy(0, p, own_low.at[slot, pl.ds(0, 2), pl.ds(0, quarter)], x_in.at[slot], x_to)

    def y_first(p):
        slot = lax.rem(p, SLOTS)
        return link_copy(1, p, own_low.at[slot, pl.ds(1, 2), pl.ds(quarter, quarter)], y_in.at[slot], y_to)

    def y_last(p):
        slot = lax.rem(p, SLOTS)
        return link_copy(2, p, own_low.at[slot, 2, pl.ds(0, quarter)], end_in.at[slot, 0], y_to)

    def x_last(p):
        slot = lax.rem(p, SLOTS)
        return link_copy(3, p, own_low.at[slot, 0, pl.ds(quarter, quarter)], end_in.at[slot, 1], x_to)

    def up_column(p):
        t = jnp.clip(p - down_pieces, 0, up_pieces - 1)
        return lax.rem(t + 3 * width // PIECE, up_pieces) * PIECE

    def out_copies(p):
        src = own_sum.at[lax.rem(p, SLOTS)]
        sem = out_sem.at[lax.rem(p, SLOTS)]
        row = jnp.minimum(p, down_pieces - 1) * PIECE
        down = [
            pltpu.make_async_copy(
                src.at[:, pl.ds(i * half, half)],
                d_dn.at[pl.ds(pl.multiple_of(row + i * half, half), half), :],
                sem.at[i],
            )
            for i in range(2)
        ]
        up = [
            pltpu.make_async_copy(
                src.at[:, pl.ds(i * half, half)],
                d_in.at[:, pl.ds(pl.multiple_of(up_column(p) + i * half, half), half)],
                sem.at[i],
            )
            for i in range(2)
        ]
        return down, up

    def first_down(p):
        slot, out = lax.rem(p, SLOTS), lax.rem(p, 2)
        j_load(p).wait()

        @pl.when(p + 1 < down_pieces)
        def _():
            j_load(p + 1).start()

        j_turned[...] = j_block[lax.rem(p, 2)].T
        for mine in range(2):
            for r, goal in enumerate(goals):
                to = flip(goal, 1) if mine == 0 else goal
                t = nn(j_turned[...], cot[:, rows_at(to, lanes)])
                for i in range(2):
                    v = t[i * half : (i + 1) * half, :]
                    cs = pl.ds(i * half, half)
                    if mine == 0:
                        sib_out[out, r, :, cs] = v.astype(BF)
                    elif r < 3:
                        own_low[slot, r, :, cs] = v.astype(BF)
                    else:
                        own_sum[slot, :, cs] = v
            if mine == 0:
                sib_copy(p).start()

    def first_up(p):
        slot, out = lax.rem(p, SLOTS), lax.rem(p, 2)
        g = grads[:, pl.ds(pl.multiple_of(up_column(p), PIECE), PIECE)]
        for mine in range(2):
            for r, goal in enumerate(goals):
                to = flip(goal, 1) if mine == 0 else goal
                t = nn(n_turned[rows_at(to, lanes), :], g)
                if mine == 0:
                    sib_out[out, r] = t.astype(BF)
                elif r < 3:
                    own_low[slot, r] = t.astype(BF)
                else:
                    own_sum[slot] = t
            if mine == 0:
                sib_copy(p).start()

    def stage_one(p):
        @pl.when(p >= 2)
        def _():
            sib_copy(p - 2).wait_send()

        @pl.when(p >= SLOTS)
        def _():
            for c in out_copies(p - SLOTS)[0]:
                c.wait()

        @pl.when(p < down_pieces)
        def _():
            first_down(p)

        @pl.when(p >= down_pieces)
        def _():
            first_up(p)

    def stage_two(p):
        slot, inn = lax.rem(p, SLOTS), lax.rem(p, SIB_SLOTS)
        sib_copy(p).wait_recv()
        a, b = pl.ds(0, quarter), pl.ds(quarter, quarter)

        def add(r, rows):
            own_low[slot, r, rows] = (own_low[slot, r, rows].astype(F32) + sib_in[inn, r, rows].astype(F32)).astype(BF)

        add(0, a)
        add(1, a)
        x_first(p).start()
        add(1, b)
        add(2, b)
        y_first(p).start()
        add(0, b)
        add(2, a)
        own_sum[slot] = own_sum[slot] + sib_in[inn, 3].astype(F32)

    def stage_three(p):
        slot = lax.rem(p, SLOTS)
        a, b = pl.ds(0, quarter), pl.ds(quarter, quarter)
        x_first(p).wait_recv()
        own_low[slot, 2, a] = (own_low[slot, 2, a].astype(F32) + x_in[slot, 1].astype(F32)).astype(BF)
        y_last(p).start()
        y_first(p).wait_recv()
        own_low[slot, 0, b] = (own_low[slot, 0, b].astype(F32) + y_in[slot, 0].astype(F32)).astype(BF)
        x_last(p).start()
        own_sum[slot, a] = own_sum[slot, a] + x_in[slot, 0].astype(F32)
        own_sum[slot, b] = own_sum[slot, b] + y_in[slot, 1].astype(F32)

    def stage_four(p):
        slot = lax.rem(p, SLOTS)
        a, b = pl.ds(0, quarter), pl.ds(quarter, quarter)
        y_last(p).wait_recv()
        own_sum[slot, a] = own_sum[slot, a] + end_in[slot, 0].astype(F32)
        x_last(p).wait_recv()
        own_sum[slot, b] = own_sum[slot, b] + end_in[slot, 1].astype(F32)
        down, up = out_copies(p)

        @pl.when(p < down_pieces)
        def _():
            for c in down:
                c.start()

        @pl.when(p >= down_pieces)
        def _():
            for c in up:
                c.start()

        for c in (x_first(p), y_first(p), x_last(p), y_last(p)):
            c.wait_send()

    def normed_back(t):
        for l in w_loads(t):
            l.wait()

        @pl.loop(0, length // 512)
        def _(m):
            rows = rows_at(m, 512)
            part_g[rows, t * PIECE : (t + 1) * PIECE] = (
                nt(grads[rows, : 3 * width], wq_block[t % 2]) + nt(grads[rows, 3 * width :], wu_block[t % 2])
            ).astype(BF)

        if t + 2 < d // PIECE:
            for l in w_loads(t + 2):
                l.start()
        fold_g.first(t)

    def turn(j):
        n_load(j).wait()
        n_turned[:, j * size : (j + 1) * size] = n_block[...].T
        if j + 1 < n:
            n_load(j + 1).start()

    def small(k, src, dst, to):
        return pltpu.make_async_remote_copy(
            src, dst, small_send.at[k], small_recv.at[k], device_id=to, device_id_type=MESH
        )

    def bias_sums():
        for i in range(up_pieces):
            narrow[me, i : i + 1, :] = jnp.sum(
                grads[:, i * PIECE : (i + 1) * PIECE].astype(F32), axis=0, keepdims=True
            )
        for k, to in enumerate(peers):
            small(k, narrow.at[me], narrow.at[me], (to, z)).start()

    def branch_end():
        loads[3].wait()

        @pl.loop(0, size // 32)
        def _(r):
            rows = pl.ds(pl.multiple_of(z * size + r * 32, 32), 32)
            v = own_x[rows_at(r, 32), :].astype(F32) + part_b[rows, :].astype(F32) + b_out[...] + b_down[...]
            part_b[rows, :] = v.astype(BF)

        load(0, part_b.at[rows_at(z, size), :], layer_out).start()

    def input_end():
        sums[...] = jnp.zeros_like(sums)

        def chunk(r):
            return pltpu.make_async_copy(
                d_rows.at[lax.rem(r, 2)], d_input.at[rows_at(r, 32), :], local.at[1 + lax.rem(r, 2)]
            )

        @pl.loop(0, size // 32)
        def _(r):
            mine = pl.ds(pl.multiple_of(z * size + r * 32, 32), 32)
            grad = part_g[mine, :].astype(F32)
            v = own_x[rows_at(r, 32), :].astype(F32)
            c = v - jnp.mean(v, axis=-1, keepdims=True)
            inv = lax.rsqrt(jnp.mean(c * c, axis=-1, keepdims=True) + epsilon)
            unit = c * inv
            own_cot = cot[mine, :].astype(F32)
            gu = grad * unit
            sums[0:1, :] += jnp.sum(gu, axis=0, keepdims=True)
            sums[1:2, :] += jnp.sum(grad, axis=0, keepdims=True)
            sums[2:3, :] += jnp.sum(own_cot, axis=0, keepdims=True)
            scaled = grad * gain[...]

            @pl.when(r >= 2)
            def _():
                chunk(r - 2).wait()

            d_rows[lax.rem(r, 2)] = own_cot + inv * (
                scaled
                - jnp.mean(scaled, axis=-1, keepdims=True)
                - unit * jnp.mean(scaled * unit, axis=-1, keepdims=True)
            )
            chunk(r).start()

        for i in range(3):
            for q in range(4):
                wide[me, 4 * i + q : 4 * i + q + 1, :] = sums[i : i + 1, q * PIECE : (q + 1) * PIECE]
        for k, to in enumerate(peers):
            small(8 + k, wide.at[me], wide.at[me], (to, z)).start()
        for r in range(2):
            chunk(size // 32 - 2 + r).wait()

    def small_end():
        for k, to in enumerate(peers):
            small(8 + k, wide.at[to], wide.at[to], (to, z)).wait_recv()
        total = wide[0]
        for i in range(1, 8):
            total = total + wide[i]
        wide_z[z] = total
        for k, to in enumerate(others):
            small(16 + k, wide_z.at[z], wide_z.at[z], (me, to)).start()

    def last_end():
        for k in range(n - 1):
            origin = lax.rem(z + n - 1 - k, n)
            small(16 + k, wide_z.at[origin], wide_z.at[origin], (me, origin)).wait_recv()
        total = wide_z[0]
        for i in range(1, n):
            total = total + wide_z[i]
        d_all[...] = total
        for k, to in enumerate(peers):
            small(k, narrow.at[to], narrow.at[to], (to, z)).wait_recv()
        total = narrow[0]
        for i in range(1, 8):
            total = total + narrow[i]
        d_bias[...] = total
        for k, to in enumerate(peers):
            small(k, narrow.at[me], narrow.at[me], (to, z)).wait_send()
            small(8 + k, wide.at[me], wide.at[me], (to, z)).wait_send()
        for k, to in enumerate(others):
            small(16 + k, wide_z.at[z], wide_z.at[z], (me, to)).wait_send()
        load(0, part_b.at[rows_at(z, size), :], layer_out).wait()

    narrow[me] = jnp.zeros(narrow.shape[1:], F32)
    wide[me] = jnp.zeros(wide.shape[1:], F32)
    pl.semaphore_wait(barrier, 7 + n - 1)

    tasks = {}

    def at(p, *work):
        tasks.setdefault(p, []).extend(work)

    loads[0].wait()
    for t in fold_b.tiles:
        fold_b.first(t)
    loads[1].wait()

    part = functools.partial
    at(0, part(turn, 0), part(turn, 1))
    at(1, loads[2].wait, part(normed_back, 0))
    at(2, part(normed_back, 1), part(fold_b.event, 2, 1))
    at(4, part(normed_back, 2), part(turn, 2), part(turn, 3), part(fold_b.event, 2, 2))
    at(5, part(fold_b.event, 3, 1))
    at(6, part(normed_back, 3), part(fold_g.event, 0, 1))
    at(7, part(fold_b.event, 2, 3), part(fold_b.event, 3, 2), part(fold_g.event, 1, 1))
    at(8, bias_sums, part(fold_g.event, 0, 2))
    at(9, part(fold_b.event, 3, 3), part(fold_g.event, 0, 3), part(fold_g.event, 2, 1))
    at(10, branch_end)
    at(11, part(fold_g.event, 1, 2), part(fold_g.event, 2, 2), part(fold_g.event, 3, 1))
    at(12, part(fold_g.event, 3, 2))
    at(13, part(fold_g.event, 1, 3))
    at(15, part(fold_g.event, 2, 3), part(fold_g.event, 3, 3), input_end, small_end, last_end)

    @pl.loop(0, max(pieces + 3, max(tasks) + 1))
    def _(p):
        @pl.when((p >= 1) & (p <= pieces))
        def _():
            stage_two(p - 1)

        @pl.when(p < pieces)
        def _():
            stage_one(p)

        @pl.when((p >= 2) & (p <= pieces + 1))
        def _():
            stage_three(p - 2)

        @pl.when((p >= 3) & (p <= pieces + 2))
        def _():
            stage_four(p - 3)

        for k, work in tasks.items():

            @pl.when(p == k)
            def _():
                for w in work:
                    w()

    for p in range(2):
        sib_copy(pieces - 2 + p).wait_send()
    for p in range(SLOTS):
        for c in out_copies(pieces - SLOTS + p)[1]:
            c.wait()
    fold_b.finish()
    fold_g.finish()


def backward_call(n, x, normed, cots, w_qkv, w_up, grads, joined, branch, gain, b_out, b_down):
    size, d = x.shape
    length, ff = n * size, w_up.shape[1]
    width = joined.shape[1] - ff
    vm, hbm = pl.BlockSpec(memory_space=pltpu.VMEM), pl.BlockSpec(memory_space=pl.ANY)
    shape = lambda s, t=BF: jax.ShapeDtypeStruct(s, t)
    dma = pltpu.SemaphoreType.DMA
    half, quarter = PIECE // 2, PIECE // 4
    late, tiles = (d // PIECE - EARLY) * (n - 1), d // PIECE * (n - 1)
    return pl.pallas_call(
        functools.partial(backward_scatter, n),
        out_shape=(
            shape((size, d)),
            shape((size, d), F32),
            shape((d // 8, 3 * width + ff), F32),
            shape((width + ff, d // 8), F32),
            shape((8, PIECE), F32),
            shape((16, PIECE), F32),
        ),
        in_specs=[hbm] * 8 + [vm] * 3,
        out_specs=(hbm,) * 4 + (vm,) * 2,
        scratch_shapes=[
            pltpu.VMEM((size, d), BF),
            pltpu.VMEM((length, d), BF),
            pltpu.VMEM((length, 3 * width + ff), BF),
            pltpu.VMEM((size, d), BF),
            pltpu.VMEM((d, length), BF),
            pltpu.VMEM((2, length, PIECE), BF),
            pltpu.VMEM((PIECE, length), BF),
            pltpu.VMEM((2, PIECE, 3 * width), BF),
            pltpu.VMEM((2, PIECE, ff), BF),
            pltpu.VMEM((length, d), BF),
            pltpu.VMEM((length, d), BF),
            pltpu.VMEM((2, late, size, PIECE), BF),
            pltpu.VMEM((2, tiles, size, PIECE), BF),
            pltpu.VMEM((2, 4, half, PIECE), BF),
            pltpu.VMEM((SIB_SLOTS, 4, half, PIECE), BF),
            pltpu.VMEM((SLOTS, 3, half, PIECE), BF),
            pltpu.VMEM((SLOTS, half, PIECE), F32),
            pltpu.VMEM((SLOTS, 2, quarter, PIECE), BF),
            pltpu.VMEM((SLOTS, 2, quarter, PIECE), BF),
            pltpu.VMEM((SLOTS, 2, quarter, PIECE), BF),
            pltpu.VMEM((2, 32, d), F32),
            pltpu.VMEM((8, 8, PIECE), F32),
            pltpu.VMEM((8, 16, PIECE), F32),
            pltpu.VMEM((n, 16, PIECE), F32),
            pltpu.VMEM((8, d), F32),
            dma((2, late)),
            dma((2, late)),
            dma((2, tiles)),
            dma((2, tiles)),
            dma((2,)),
            dma((SIB_SLOTS,)),
            dma((4, SLOTS)),
            dma((4, SLOTS)),
            dma((SLOTS, 2)),
            dma((4,)),
            dma((7,)),
            dma((16 + n - 1,)),
            dma((16 + n - 1,)),
        ],
        compiler_params=pltpu.CompilerParams(
            collective_id=2, has_side_effects=True, vmem_limit_bytes=63 << 20
        ),
        cost_estimate=pl.CostEstimate(flops=60_000_000_000, bytes_accessed=100_000_000, transcendentals=0),
    )(x, normed, cots, w_qkv, w_up, grads, joined, branch, gain[None], b_out[None], b_down[None])


def rotate(tensor, positions, direction):
    half_dim = ROT_DIM // 2
    freqs = rope_base ** (-(jnp.arange(half_dim).astype(jnp.float32) * 2.0 / ROT_DIM))
    angles = positions.astype(jnp.float32)[:, None] * freqs[None, :]
    cosine = jnp.cos(angles)[:, None, :]
    sine = direction * jnp.sin(angles)[:, None, :]
    first = tensor[..., :half_dim]
    second = tensor[..., half_dim:ROT_DIM]
    return jnp.concatenate(
        [first * cosine - second * sine, second * cosine + first * sine, tensor[..., ROT_DIM:]],
        axis=-1,
    )


def times_transposed(left, right):
    return lax.dot_general(
        left, right, (((1,), (1,)), ((), ())), preferred_element_type=jnp.float32
    )


def rows_transposed(left, right):
    return lax.dot_general(
        left, right, (((0,), (0,)), ((), ())), preferred_element_type=jnp.float32
    )


def plain_on_device(
    layer_input,
    ln_gain,
    ln_bias,
    w_query,
    b_query,
    w_key,
    b_key,
    w_value,
    b_value,
    w_out,
    b_out,
    w_up,
    b_up,
    w_down,
    b_down,
    prefix,
    cotangent,
):
    local_width = w_query.shape[1]
    hidden_here = w_up.shape[1]
    heads_here = local_width // HEAD_DIM
    score_scale = 1.0 / math.sqrt(HEAD_DIM)
    prefix_len = prefix[0]
    input_float = layer_input.astype(jnp.float32)
    row_mean = jnp.mean(input_float, axis=-1, keepdims=True)
    centred = input_float - row_mean
    inverse = lax.rsqrt(jnp.mean(centred * centred, axis=-1, keepdims=True) + epsilon)
    unit_rows = centred * inverse
    normed = (unit_rows * ln_gain + ln_bias).astype(jnp.bfloat16)
    normed_all = lax.all_gather(normed, "tensor", axis=0, tiled=True)
    length = normed_all.shape[0]
    positions = jnp.arange(length)
    block_rows = min(512, length)
    block_count = length // block_rows
    pieces = (
        lax.all_gather(w_query, "dp", axis=0, tiled=True),
        lax.all_gather(w_key, "dp", axis=0, tiled=True),
        lax.all_gather(w_value, "dp", axis=0, tiled=True),
        lax.all_gather(w_up, "dp", axis=0, tiled=True),
    )
    columns = normed_all
    query_acc, key_acc, value_acc, up_acc = tuple(
        (jnp.dot(columns, piece, preferred_element_type=jnp.float32) for piece in pieces)
    )
    query_pre = (query_acc + b_query).reshape(length, heads_here, HEAD_DIM)
    key_pre = (key_acc + b_key).reshape(length, heads_here, HEAD_DIM)
    query = rotate(query_pre, positions, 1.0).astype(jnp.bfloat16)
    key = rotate(key_pre, positions, 1.0).astype(jnp.bfloat16)
    value = (value_acc + b_value).reshape(length, heads_here, HEAD_DIM).astype(jnp.bfloat16)
    up_pre = up_acc + b_up
    hidden = jax.nn.gelu(up_pre, approximate=True).astype(jnp.bfloat16)

    def scores_for(query_rows, offset):
        raw = (
            jnp.einsum("qhd,khd->hqk", query_rows, key, preferred_element_type=jnp.float32)
            * score_scale
        )
        query_pos = offset + jnp.arange(block_rows)
        seen = (positions[None, :] <= query_pos[:, None]) | (positions[None, :] < prefix_len)
        return jnp.where(seen[None], raw, masked_score)

    def attend_block(index):
        offset = index * block_rows
        query_rows = lax.dynamic_slice_in_dim(query, offset, block_rows, 0)
        scores = scores_for(query_rows, offset)
        row_max = jnp.max(scores, axis=-1, keepdims=True)
        expo = jnp.exp(scores - row_max)
        totals = jnp.sum(expo, axis=-1, keepdims=True)
        probs_low = (expo / totals).astype(jnp.bfloat16)
        out_rows = jnp.einsum("hqk,khd->qhd", probs_low, value, preferred_element_type=jnp.float32)
        return (out_rows, (row_max + jnp.log(totals))[..., 0])

    indices = jnp.arange(block_count)
    out_blocks, log_totals = lax.map(attend_block, indices)
    attn = out_blocks.reshape(length, local_width).astype(jnp.bfloat16)
    pieces = (
        lax.all_gather(w_out, "dp", axis=1, tiled=True),
        lax.all_gather(w_down, "dp", axis=1, tiled=True),
    )
    part = jnp.dot(attn, pieces[0], preferred_element_type=jnp.float32) + jnp.dot(
        hidden, pieces[1], preferred_element_type=jnp.float32
    )
    partial_value = part
    branch = lax.psum_scatter(partial_value, "tensor", scatter_dimension=0, tiled=True)
    layer_out = (input_float + branch + b_out + b_down).astype(jnp.bfloat16)
    grad_all = lax.all_gather(cotangent, "tensor", axis=0, tiled=True)
    pieces = (
        lax.all_gather(w_out, "dp", axis=1, tiled=True),
        lax.all_gather(w_down, "dp", axis=1, tiled=True),
    )
    columns = grad_all
    attn_grad = times_transposed(columns, pieces[0])
    hidden_grad = times_transposed(columns, pieces[1])
    down_joined = jnp.concatenate([attn, hidden], axis=1)
    unused, gelu_pull = jax.vjp(lambda inner: jax.nn.gelu(inner, approximate=True), up_pre)
    up_grad_low = gelu_pull(hidden_grad)[0].astype(jnp.bfloat16)
    attn_grad_low = attn_grad.astype(jnp.bfloat16).reshape(length, heads_here, HEAD_DIM)

    def back_block(carry, item):
        key_grad, value_grad = carry
        index, lse_rows = item
        offset = index * block_rows
        query_rows = lax.dynamic_slice_in_dim(query, offset, block_rows, 0)
        grad_rows = lax.dynamic_slice_in_dim(attn_grad_low, offset, block_rows, 0)
        scores = scores_for(query_rows, offset)
        probs = jnp.exp(scores - lse_rows[..., None])
        value_grad = value_grad + jnp.einsum(
            "hqk,qhd->khd",
            probs.astype(jnp.bfloat16),
            grad_rows,
            preferred_element_type=jnp.float32,
        )
        prob_grad = jnp.einsum("qhd,khd->hqk", grad_rows, value, preferred_element_type=jnp.float32)
        delta = jnp.sum(probs * prob_grad, axis=-1, keepdims=True)
        score_grad = (probs * (prob_grad - delta)).astype(jnp.bfloat16)
        query_grad = (
            jnp.einsum("hqk,khd->qhd", score_grad, key, preferred_element_type=jnp.float32)
            * score_scale
        )
        key_grad = (
            key_grad
            + jnp.einsum("hqk,qhd->khd", score_grad, query_rows, preferred_element_type=jnp.float32)
            * score_scale
        )
        return ((key_grad, value_grad), query_grad)

    state_zeros = jnp.zeros((length, heads_here, HEAD_DIM), jnp.float32)
    (key_grad, value_grad), query_blocks = lax.scan(
        back_block, (state_zeros, state_zeros), (indices, log_totals)
    )
    query_grad = query_blocks.reshape(length, heads_here, HEAD_DIM)
    q_grad_low = (
        rotate(query_grad, positions, -1.0).reshape(length, local_width).astype(jnp.bfloat16)
    )
    k_grad_low = rotate(key_grad, positions, -1.0).reshape(length, local_width).astype(jnp.bfloat16)
    v_grad_low = value_grad.reshape(length, local_width).astype(jnp.bfloat16)
    up_joined = jnp.concatenate([q_grad_low, k_grad_low, v_grad_low, up_grad_low], axis=1)
    columns = grad_all
    joined_rows = lax.psum_scatter(
        jnp.concatenate(
            [rows_transposed(columns, down_joined), rows_transposed(normed_all, up_joined)], axis=1
        ),
        "dp",
        scatter_dimension=0,
        tiled=True,
    )
    down_rows = joined_rows[:, : local_width + hidden_here]
    up_rows = joined_rows[:, local_width + hidden_here :]
    d_w_out = down_rows[:, :local_width].T
    d_w_down = down_rows[:, local_width:].T
    d_w_query = up_rows[:, :local_width]
    d_w_key = up_rows[:, local_width : 2 * local_width]
    d_w_value = up_rows[:, 2 * local_width : 3 * local_width]
    d_w_up = up_rows[:, 3 * local_width :]
    pieces = (
        lax.all_gather(w_query, "dp", axis=0, tiled=True),
        lax.all_gather(w_key, "dp", axis=0, tiled=True),
        lax.all_gather(w_value, "dp", axis=0, tiled=True),
        lax.all_gather(w_up, "dp", axis=0, tiled=True),
    )
    part = (
        times_transposed(q_grad_low, pieces[0])
        + times_transposed(k_grad_low, pieces[1])
        + times_transposed(v_grad_low, pieces[2])
        + times_transposed(up_grad_low, pieces[3])
    )
    own_grad = lax.psum_scatter(part, "tensor", scatter_dimension=0, tiled=True)
    scaled_grad = own_grad * ln_gain
    norm_part = inverse * (
        scaled_grad
        - jnp.mean(scaled_grad, axis=-1, keepdims=True)
        - unit_rows * jnp.mean(scaled_grad * unit_rows, axis=-1, keepdims=True)
    )
    cot_float = cotangent.astype(jnp.float32)
    d_input = cot_float + norm_part
    d_ln_gain, d_ln_bias, d_b_out = lax.psum(
        (
            jnp.sum(own_grad * unit_rows, axis=0),
            jnp.sum(own_grad, axis=0),
            jnp.sum(cot_float, axis=0),
        ),
        ("dp", "tensor"),
    )
    d_b_query, d_b_key, d_b_value, d_b_up = lax.psum(
        (
            jnp.sum(q_grad_low.astype(jnp.float32), axis=0),
            jnp.sum(k_grad_low.astype(jnp.float32), axis=0),
            jnp.sum(v_grad_low.astype(jnp.float32), axis=0),
            jnp.sum(up_grad_low.astype(jnp.float32), axis=0),
        ),
        "dp",
    )
    return (
        layer_out,
        d_input,
        d_ln_gain,
        d_ln_bias,
        d_w_query,
        d_b_query,
        d_w_key,
        d_b_key,
        d_w_value,
        d_b_value,
        d_w_out,
        d_b_out,
        d_w_up,
        d_b_up,
        d_w_down,
        d_b_out,
    )


def finish(d_in_ref, d_dn_ref, d_input_ref, layer_ref, bias_ref, all_ref, *refs):
    (layer_out, d_input, d_ln_gain, d_ln_bias, d_wq, d_bq, d_wk, d_bk, d_wv, d_bv, d_wo, d_bo, d_wu, d_bu, d_wd, d_bd) = refs[:16]
    sems, holds = refs[16], refs[17:]
    width, ff = d_wq.shape[1], d_wu.shape[1]
    moves = [
        (d_in_ref.at[:, pl.ds(3 * width, ff)], d_wu),
        (d_dn_ref.at[pl.ds(width, ff), :], d_wd),
        (d_input_ref, d_input),
        (layer_ref, layer_out),
        (d_in_ref.at[:, pl.ds(0, width)], d_wq),
        (d_in_ref.at[:, pl.ds(width, width)], d_wk),
        (d_in_ref.at[:, pl.ds(2 * width, width)], d_wv),
        (d_dn_ref.at[pl.ds(0, width), :], d_wo),
    ]
    loads, stores = [], []
    for (src, dst), hold in zip(moves, holds):
        half = src.shape[0] // 2
        for i in range(2):
            part, k = pl.ds(i * half, half), len(loads)
            loads.append(pltpu.make_async_copy(src.at[part], hold.at[part], sems.at[0, k]))
            stores.append(pltpu.make_async_copy(hold.at[part], dst.at[part], sems.at[1, k]))
    for load in loads:
        load.start()
    rows = d_ln_gain.shape[0] // PIECE
    for i, out in enumerate((d_ln_gain, d_ln_bias, d_bo)):
        for q in range(rows):
            out[pl.ds(q * PIECE, PIECE)] = all_ref[i * rows + q, :]
    for q in range(rows):
        d_bd[pl.ds(q * PIECE, PIECE)] = all_ref[2 * rows + q, :]
    for i, out in enumerate((d_bq, d_bk, d_bv)):
        out[...] = bias_ref[i, :]
    for q in range(ff // PIECE):
        d_bu[pl.ds(q * PIECE, PIECE)] = bias_ref[3 + q, :]
    for load, store in zip(loads, stores):
        load.wait()
        store.start()
    for store in stores:
        store.wait()


def on_device(
    layer_input, ln_gain, ln_bias, w_query, b_query, w_key, b_key, w_value, b_value,
    w_out, b_out, w_up, b_up, w_down, b_down, prefix, cotangent,
):
    n = lax.axis_size("tensor")
    normed, cots, w_qkv, w_up_all, grads, joined, branch = forward_call(
        n, prefix, layer_input, cotangent, w_query, w_key, w_value, w_out, w_up, w_down,
        ln_gain, ln_bias, b_query, b_key, b_value, b_up,
    )
    layer_out, d_input, d_in, d_dn, d_bias, d_all = backward_call(
        n, layer_input, normed, cots, w_qkv, w_up_all, grads, joined, branch, ln_gain, b_out, b_down
    )
    vm, hbm = pl.BlockSpec(memory_space=pltpu.VMEM), pl.BlockSpec(memory_space=pltpu.HBM)
    like = lambda a, t=F32: jax.ShapeDtypeStruct(a.shape, t)
    return pl.pallas_call(
        finish,
        out_shape=(
            like(layer_input, BF), like(layer_input), like(ln_gain), like(ln_bias),
            like(w_query), like(b_query), like(w_key), like(b_key), like(w_value), like(b_value),
            like(w_out), like(b_out), like(w_up), like(b_up), like(w_down), like(b_down),
        ),
        in_specs=[hbm] * 4 + [vm] * 2,
        out_specs=(hbm, hbm, vm, vm, hbm, vm, hbm, vm, hbm, vm, hbm, vm, hbm, vm, hbm, vm),
        scratch_shapes=[pltpu.SemaphoreType.DMA((2, 16))]
        + [
            pltpu.VMEM(a.shape, t)
            for a, t in (
                (w_up, F32), (w_down, F32), (layer_input, F32), (layer_input, BF),
                (w_query, F32), (w_key, F32), (w_value, F32), (w_out, F32),
            )
        ],
        compiler_params=pltpu.CompilerParams(vmem_limit_bytes=63 << 20),
    )(d_in, d_dn, d_input, layer_out, d_bias, d_all)


def solution(mesh):
    fits = mesh.shape["dp"] == 8 and mesh.shape["tensor"] == 4
    return jax.shard_map(
        on_device if fits else plain_on_device,
        mesh=mesh,
        in_specs=(
            P(("dp", "tensor"), None),
            P(),
            P(),
            P("dp", "tensor"),
            P("tensor"),
            P("dp", "tensor"),
            P("tensor"),
            P("dp", "tensor"),
            P("tensor"),
            P("tensor", "dp"),
            P(),
            P("dp", "tensor"),
            P("tensor"),
            P("tensor", "dp"),
            P(),
            P("dp"),
            P(("dp", "tensor"), None),
        ),
        out_specs=(
            P(("dp", "tensor"), None),
            P(("dp", "tensor"), None),
            P(),
            P(),
            P("dp", "tensor"),
            P("tensor"),
            P("dp", "tensor"),
            P("tensor"),
            P("dp", "tensor"),
            P("tensor"),
            P("tensor", "dp"),
            P(),
            P("dp", "tensor"),
            P("tensor"),
            P("tensor", "dp"),
            P(),
        ),
        check_vma=False,
    )
```

```python
import functools
import math

import jax
import jax.numpy as jnp
import numpy as np
from jax import lax
from jax.experimental import pallas as pl
from jax.experimental.pallas import tpu as pltpu
from jax.sharding import PartitionSpec as P

HEAD_DIM = 64
ROT_DIM = 32
MESH = pl.DeviceIdType.MESH
BF = jnp.bfloat16
F32 = jnp.float32

epsilon = 1e-05
rope_base = 10000.0
masked_score = -1e30
root = math.sqrt(2.0 / math.pi)


def nn(a, b):
    return jnp.dot(a, b, preferred_element_type=F32)


def nt(a, b):
    return lax.dot_general(a, b, (((1,), (1,)), ((), ())), preferred_element_type=F32)


def tn(a, b):
    return lax.dot_general(a, b, (((0,), (0,)), ((), ())), preferred_element_type=F32)


def rows_at(index, size):
    return pl.ds(pl.multiple_of(index * size, size), size)


def flip(index, bit):
    return index + bit - 2 * bit * lax.rem(index // bit, 2)


class Copies:
    def __init__(self, send, recv):
        self.send, self.recv, self.count, self.sent = send, recv, 0, []

    def new(self):
        self.count += 1
        return self.count - 1

    def make(self, k, src, dst, device):
        return pltpu.make_async_remote_copy(
            src, dst, self.send.at[k], self.recv.at[k], device_id=device, device_id_type=MESH
        )

    def start(self, k, src, dst, device):
        copy = self.make(k, src, dst, device)
        copy.start()
        self.sent.append(copy)

    def wait(self, k, dst, device):
        self.make(k, dst, dst, device).wait_recv()

    def finish(self):
        for copy in self.sent:
            copy.wait_send()


class Spread:
    def __init__(self, copies, view, me, z):
        self.c, self.view, self.me, self.z = copies, view, me, z
        self.k = [copies.new() for _ in range(9)]

    def dev(self, bit):
        return (flip(self.me, bit), self.z)

    def own(self):
        v = self.view(self.me)
        self.c.start(self.k[1], v, v, self.dev(2))
        self.c.start(self.k[2], v, v, self.dev(4))
        self.c.start(self.k[0], v, v, self.dev(1))

    def forward(self):
        c, x, y = self.c, flip(self.me, 2), flip(self.me, 4)
        c.wait(self.k[1], self.view(x), self.dev(2))
        v = self.view(x, 0)
        c.start(self.k[3], v, v, self.dev(4))
        c.wait(self.k[2], self.view(y), self.dev(4))
        v = self.view(y, 1)
        c.start(self.k[4], v, v, self.dev(2))
        v = self.view(x)
        c.start(self.k[5], v, v, self.dev(1))
        v = self.view(y)
        c.start(self.k[6], v, v, self.dev(1))

    def last(self):
        c, far = self.c, flip(flip(self.me, 2), 4)
        c.wait(self.k[3], self.view(far, 0), self.dev(4))
        c.wait(self.k[4], self.view(far, 1), self.dev(2))
        v = self.view(far)
        c.start(self.k[7], v, v, self.dev(1))

    def ready(self):
        c, s = self.c, flip(self.me, 1)
        c.wait(self.k[0], self.view(s), self.dev(1))
        c.wait(self.k[5], self.view(flip(s, 2)), self.dev(1))
        c.wait(self.k[6], self.view(flip(s, 4)), self.dev(1))
        c.wait(self.k[7], self.view(flip(flip(s, 2), 4)), self.dev(1))


class Line:
    CHUNKS = 4

    def __init__(self, copies, buf, size, n, me, z):
        self.c, self.buf, self.size, self.n, self.me, self.z = copies, buf, size // self.CHUNKS, n, me, z
        self.k = [[[copies.new() for _ in range(self.CHUNKS)] for _ in range(2)] for _ in range(n - 1)]

    def copy(self, s, way, c, block):
        z, n = self.z, self.n
        to = jnp.minimum(z + 1, n - 1) if way == 0 else jnp.maximum(z - 1, 0)
        v = self.buf.at[rows_at(jnp.clip(block, 0, n - 1) * self.CHUNKS + c, self.size), :]
        return self.c.make(self.k[s][way][c], v, v, (self.me, to))

    def far(self, way):
        return self.z if way == 0 else self.n - 1 - self.z

    def block(self, way, s):
        return self.z - s if way == 0 else self.z + s

    def own(self, c):
        for way in range(2):

            @pl.when(self.far(way) < self.n - 1)
            def _():
                self.copy(0, way, c, self.z).start()

    def event(self, s, c):
        for way in range(2):
            far = self.far(way)

            @pl.when(far >= s + 1)
            def _():
                self.copy(s, way, c, self.block(way, s + 1)).wait_recv()

            if s + 1 < self.n - 1:

                @pl.when((far >= s + 1) & (far < self.n - 1))
                def _():
                    self.copy(s + 1, way, c, self.block(way, s + 1)).start()

    def finish(self):
        for s in range(self.n - 1):
            for way in range(2):
                far = self.far(way)

                @pl.when((far >= s) & (far < self.n - 1))
                def _():
                    for c in range(self.CHUNKS):
                        self.copy(s, way, c, self.z).wait_send()


class Fold:
    def __init__(self, part, slots, send, recv, tiles, size, n, me, z, begun=None, handed=None):
        self.part, self.slots, self.send, self.recv = part, slots, send, recv
        self.begun, self.handed = begun, handed
        self.tiles, self.size, self.n, self.me, self.z = list(tiles), size, n, me, z

    def far(self, way):
        return self.z if way == 0 else self.n - 1 - self.z

    def copy(self, way, t, i):
        z, n = self.z, self.n
        to = jnp.minimum(z + 1, n - 1) if way == 0 else jnp.maximum(z - 1, 0)
        goal = n - 1 - i if way == 0 else i
        k = self.tiles.index(t) * (n - 1) + i
        return pltpu.make_async_remote_copy(
            self.part.at[goal * self.size : (goal + 1) * self.size, t * PIECE : (t + 1) * PIECE],
            self.slots.at[way, k],
            self.send.at[way, k],
            self.recv.at[way, k],
            device_id=(self.me, to),
            device_id_type=MESH,
        )

    def first(self, t):
        for way in range(2):

            @pl.when(self.far(way) == 0)
            def _():
                for i in range(self.n - 1):
                    self.copy(way, t, i).start()

    def resume(self):
        for way in range(2):

            @pl.when(self.far(way) == 1)
            def _():
                for i in range(self.n - 2):
                    self.copy(way, self.begun, i).start()

    def event(self, t, far):
        n = self.n
        for way in range(2):

            @pl.when(self.far(way) == far)
            def _():
                for i in range(n - far):
                    goal = n - 1 - i if way == 0 else i
                    k = self.tiles.index(t) * (n - 1) + i
                    self.copy(way, t, i).wait_recv()
                    at = (slice(goal * self.size, (goal + 1) * self.size), slice(t * PIECE, (t + 1) * PIECE))
                    self.part[at] = (self.part[at].astype(F32) + self.slots[way, k].astype(F32)).astype(BF)
                    if i < n - 1 - far and t != self.handed:
                        self.copy(way, t, i).start()

    def finish(self):
        n = self.n
        for way in range(2):
            for far in range(n - 1):

                @pl.when(self.far(way) == far)
                def _():
                    for t in self.tiles:
                        if not (t == self.begun and far == 0 or t == self.handed and far > 0):
                            for i in range(n - 1 - far):
                                self.copy(way, t, i).wait_send()


PIECE = 512
EARLY = 2
ORDER = (
    "own.up0", "own.up1", "norm0", "nown0", "norm1", "nown1", "norm2", "nown2", "norm3", "nown3", "n00",
    "fwd.up0", "own.q0", "n01", "n02", "fwd.up1", "own.q1", "n03", "last.up0", "n10", "ready.up0", "raise00",
    "raise10", "n11", "fwd.q0", "n12", "last.up1", "ready.up1", "raise01", "n13", "cown", "raise11",
    "raise20", "fwd.q1", "own.dn0", "own.dn1", "n20", "raise21", "last.q0", "ready.q0", "n21", "last.q1",
    "ready.q1", "n22", "fwd.dn0", "own.dn2", "n23", "proj", "c00", "att0", "c01", "last.dn0", "fwd.dn1",
    "att1", "c02", "ready.dn0", "raise30", "c03", "raise31", "fwd.dn2", "ab0", "c10", "last.dn1", "ab1",
    "c11", "ready.dn1", "last.dn2", "ready.dn2", "c12", "lower0", "ffirst0", "lower1", "c13", "ffirst1",
    "lower2", "ffirst2", "c20", "lower3", "ab2", "c21", "hg0", "c22", "hg1", "f01", "hg2", "c23", "ab3",
    "hg3", "f02", "f11", "kb", "f03", "f12", "f21", "f13",
)


def turned(x, table, sign):
    return (
        x * table[0]
        + pltpu.roll(x, 112, 1) * (table[1] * sign)
        + pltpu.roll(x, 16, 1) * (table[2] * sign)
    )


def gather_forward(
    n,
    prefix,
    x,
    cot,
    wq,
    wk,
    wv,
    wo,
    wu,
    wd,
    gain,
    bias,
    bq,
    bk,
    bv,
    bu,
    table,
    normed_out,
    cots_out,
    w_qkv_out,
    w_up_out,
    grads_out,
    joined_out,
    branch_out,
    normed,
    cots,
    w_qkv,
    w_up,
    w_dn,
    qkv,
    joined,
    slope,
    d_attn,
    d_key,
    d_value,
    own_x,
    lse,
    lse_row,
    fold_slots,
    send,
    recv,
    local,
    outs,
    fold_send,
    fold_recv,
):
    me, z = lax.axis_index("dp"), lax.axis_index("tensor")
    size, d = x.shape
    length = n * size
    width = wq.shape[1]
    ff = wu.shape[1]
    shard = wq.shape[0]
    lanes = wo.shape[1]
    branch = normed

    barrier = pltpu.get_barrier_semaphore()
    for bit in (1, 2, 4):
        pl.semaphore_signal(barrier, 1, device_id=(flip(me, bit), z), device_id_type=MESH)

    @pl.when(z > 0)
    def _():
        pl.semaphore_signal(barrier, 1, device_id=(me, jnp.maximum(z - 1, 0)), device_id_type=MESH)

    @pl.when(z < n - 1)
    def _():
        pl.semaphore_signal(barrier, 1, device_id=(me, jnp.minimum(z + 1, n - 1)), device_id_type=MESH)

    mine, cols = rows_at(me, shard), rows_at(me, lanes)
    loads = [
        pltpu.make_async_copy(x, own_x, local.at[0]),
        pltpu.make_async_copy(wu, w_up.at[mine, :], local.at[1]),
        pltpu.make_async_copy(wq, w_qkv.at[mine, pl.ds(0, width)], local.at[2]),
        pltpu.make_async_copy(wk, w_qkv.at[mine, pl.ds(width, width)], local.at[3]),
        pltpu.make_async_copy(wv, w_qkv.at[mine, pl.ds(2 * width, width)], local.at[4]),
        pltpu.make_async_copy(wo, w_dn.at[pl.ds(0, width), cols], local.at[5]),
        pltpu.make_async_copy(wd, w_dn.at[pl.ds(width, ff), cols], local.at[6]),
        pltpu.make_async_copy(cot, cots.at[rows_at(z, size), :], local.at[7]),
    ]
    for load in loads:
        load.start()

    stores = []

    def store(src, dst):
        copy = pltpu.make_async_copy(src, dst, outs.at[len(stores)])
        stores.append(copy)
        copy.start()
        return copy

    copies = Copies(send, recv)

    def row_view(buf, first, count):
        def view(i, half=None):
            h = count if half is None else count // 2
            start = i * shard + first + (0 if half is None else half * h)
            return buf.at[pl.ds(pl.multiple_of(start, h), h), :]

        return view

    def col_view(first, count):
        def view(i, half=None):
            if half is None:
                return w_dn.at[pl.ds(first, count), rows_at(i, lanes)]
            h = count // 2
            return w_dn.at[pl.ds(first + half * h, h), rows_at(i, lanes)]

        return view

    def row_col_view(first, count):
        def view(i, half=None):
            h = shard if half is None else shard // 2
            start = i * shard + (0 if half is None else half * h)
            return w_up.at[pl.ds(pl.multiple_of(start, h), h), pl.ds(first, count)]

        return view

    s_up = [Spread(copies, row_col_view(i * ff // 2, ff // 2), me, z) for i in range(2)]
    s_qkv = [Spread(copies, row_view(w_qkv, i * shard // 2, shard // 2), me, z) for i in range(2)]
    s_dn = [Spread(copies, col_view(*v), me, z) for v in ((0, width), (width, ff // 2), (width + ff // 2, ff // 2))]
    l_n = Line(copies, normed, size, n, me, z)
    l_c = Line(copies, cots, size, n, me, z)
    fold = Fold(branch, fold_slots, fold_send, fold_recv, range(EARLY + 1), size, n, me, z, handed=EARLY)
    order = [z, flip(z, 1), flip(z, 2), flip(flip(z, 1), 2)]
    head = lax.broadcasted_iota(jnp.int32, (1, 128), 1) // HEAD_DIM

    def norm(r):
        rows = slice(r * 64, (r + 1) * 64)
        v = own_x[rows, :].astype(F32)
        mean = jnp.mean(v, axis=-1, keepdims=True)
        c = v - mean
        inv = lax.rsqrt(jnp.mean(c * c, axis=-1, keepdims=True) + epsilon)
        out = (c * inv) * gain[...] + bias[...]
        normed[pl.ds(pl.multiple_of(z * size + r * 64, 64), 64), :] = out.astype(BF)

    def project():
        tile = 512

        @pl.loop(0, length // tile)
        def _(m):
            rows = rows_at(m, tile)
            tab = [table[i, rows, :] for i in range(3)]
            for part in range(3):
                acc = nn(normed[rows, :], w_qkv[:, part * width : (part + 1) * width])
                acc = acc + (bq, bk, bv)[part][...]
                for p in range(width // 128):
                    piece = acc[:, p * 128 : (p + 1) * 128]
                    if part < 2:
                        piece = turned(piece, tab, 1.0)
                        if part == 0:
                            piece = piece * (1.0 / math.sqrt(HEAD_DIM))
                    qkv[rows, part * width + p * 128 : part * width + (p + 1) * 128] = piece.astype(BF)

    def raise_(j, part):
        rows = rows_at(j, size)
        tile = 512

        @pl.loop(part * ff // tile // 2, (part + 1) * ff // tile // 2)
        def _(t):
            cs = rows_at(t, tile)
            u = nn(normed[rows, :], w_up[:, cs]) + bu[:, cs]
            sq = u * u
            th = jnp.tanh(root * u * (1.0 + 0.044715 * sq))
            half = 0.5 * (1.0 + th)
            joined[rows, pl.ds(pl.multiple_of(width + t * tile, tile), tile)] = (u * half).astype(BF)
            slope[rows, cs] = (
                half + 0.5 * u * (1.0 - th * th) * (root * (1.0 + 3 * 0.044715 * sq))
            ).astype(BF)

    block = length // 4

    def visible(b):
        return (b if b > 0 else 0), max(b + 1, 2)

    def attend(first, count):
        @pl.loop(first, first + count)
        def _(p):
            ps = rows_at(p, 128)
            ks = pl.ds(pl.multiple_of(width + p * 128, 128), 128)
            vs = pl.ds(pl.multiple_of(2 * width + p * 128, 128), 128)
            lane = lax.broadcasted_iota(jnp.int32, (1, 128), 1)
            for b in range(4):
                full, some = visible(b)
                qs, kr = pl.ds(b * block, block), pl.ds(0, some * block)
                limit = jnp.maximum(
                    b * block + lax.broadcasted_iota(jnp.int32, (block, 1), 0), prefix[0] - 1
                )
                at = full * block + lax.broadcasted_iota(jnp.int32, (block, (some - full) * block), 1)
                q, outs_ = qkv[qs, ps], []
                scores = [nt(jnp.where(head == h, q, jnp.zeros_like(q)), qkv[kr, ks]) for h in range(2)]
                for h in range(2):
                    last = jnp.where(at <= limit, scores[h][:, full * block :], masked_score)
                    scores[h] = jnp.concatenate([scores[h][:, : full * block], last], 1) if full > 0 else last
                tops = [jnp.max(v, axis=-1, keepdims=True) for v in scores]
                exps = [jnp.exp(v - top) for v, top in zip(scores, tops)]
                totals = [jnp.sum(v, axis=-1, keepdims=True) for v in exps]
                outs_ = [nn((v * (1.0 / total)).astype(BF), qkv[kr, vs]) for v, total in zip(exps, totals)]
                logs = [top + jnp.log(total) for top, total in zip(tops, totals)]
                lse[qs, :] = jnp.where(
                    lane == 2 * p, logs[0], jnp.where(lane == 2 * p + 1, logs[1], lse[qs, :])
                )
                joined[qs, ps] = jnp.where(head == 0, outs_[0], outs_[1]).astype(BF)

    def lower(t):
        @pl.loop(0, length // 512)
        def _(m):
            rows = rows_at(m, 512)
            branch[rows, t * PIECE : (t + 1) * PIECE] = nn(
                joined[rows, :], w_dn[:, t * PIECE : (t + 1) * PIECE]
            ).astype(BF)

    def hidden_back(j):
        rows = rows_at(j, size)
        tile = 512

        @pl.loop(0, ff // tile)
        def _(t):
            g = nt(cots[rows, :], w_dn[pl.ds(pl.multiple_of(width + t * tile, tile), tile), :])
            cs = rows_at(t, tile)
            slope[rows, cs] = (g * slope[rows, cs].astype(F32)).astype(BF)

    def attend_back(b):
        full, some = visible(b)
        qs = pl.ds(b * block, block)
        limit = jnp.maximum(b * block + lax.broadcasted_iota(jnp.int32, (1, block), 1), prefix[0] - 1)

        @pl.loop(0, width // 128)
        def _(p):
            ps = rows_at(p, 128)
            ks = pl.ds(pl.multiple_of(width + p * 128, 128), 128)
            vs = pl.ds(pl.multiple_of(2 * width + p * 128, 128), 128)
            only = lambda a, h: jnp.where(head == h, a, jnp.zeros_like(a))
            q, g = qkv[qs, ps], d_attn[:, ps]
            kr = pl.ds(0, some * block)
            at = full * block + lax.broadcasted_iota(jnp.int32, ((some - full) * block, block), 0)
            qh, gh = [only(q, h) for h in range(2)], [only(g, h) for h in range(2)]
            scores = [nt(qkv[kr, ks], qh[h]) for h in range(2)]
            d_probs = [nt(qkv[kr, vs], gh[h]) for h in range(2)]
            probs, ds = [], []
            for h in range(2):
                e = jnp.exp(scores[h] - lse_row[pl.ds(2 * p + h, 1), qs])
                last = jnp.where(at <= limit, e[full * block :], 0.0)
                probs.append(jnp.concatenate([e[: full * block], last], 0) if full > 0 else last)
            for h in range(2):
                delta = jnp.sum(probs[h] * d_probs[h], axis=0, keepdims=True)
                ds.append((probs[h] * (d_probs[h] - delta)).astype(BF))
            d_value[kr, ps] += nn(probs[0].astype(BF), gh[0]) + nn(probs[1].astype(BF), gh[1])
            d_key[kr, ps] += nn(ds[0], qh[0]) + nn(ds[1], qh[1])
            dq = tn(ds[0], only(qkv[kr, ks], 0)) + tn(ds[1], only(qkv[kr, ks], 1))
            tab = [table[i, qs, :] for i in range(3)]
            qkv[qs, ps] = turned(dq * (1.0 / math.sqrt(HEAD_DIM)), tab, -1.0).astype(BF)

    def back(k):
        d_attn[...] = nt(cots[rows_at(order[k], size), :], w_dn[:width, :]).astype(BF)
        for b in range(4):

            @pl.when(order[k] == b)
            def _():
                attend_back(b)

    def keys_back():
        @pl.loop(0, width // 128)
        def _(p):
            ps = rows_at(p, 128)
            ks = pl.ds(pl.multiple_of(width + p * 128, 128), 128)
            vs = pl.ds(pl.multiple_of(2 * width + p * 128, 128), 128)
            tab = [table[i] for i in range(3)]
            qkv[:, ks] = turned(d_key[:, ps], tab, -1.0).astype(BF)
            qkv[:, vs] = d_value[:, ps].astype(BF)

    signals = 3 + jnp.where(z > 0, 1, 0) + jnp.where(z < n - 1, 1, 0)
    pl.semaphore_wait(barrier, signals)

    n_stored = []
    part = functools.partial

    def clear():
        lse[...] = jnp.zeros_like(lse)
        d_key[...] = jnp.zeros_like(d_key)
        d_value[...] = jnp.zeros_like(d_value)

    def wait_loads(*which):
        for i in which:
            loads[i].wait()

    def heads_end():
        lse_row[...] = lse[...].T[: lse_row.shape[0], :]

    def branch_free():
        l_n.finish()
        n_stored[0].wait()

    todo = {
        "own.up0": [part(wait_loads, 1), s_up[0].own],
        "own.q0": [part(wait_loads, 2, 3, 4), s_qkv[0].own],
        "own.dn0": [part(wait_loads, 5), s_dn[0].own],
        "own.dn1": [part(wait_loads, 6), s_dn[1].own],
        "norm0": [part(wait_loads, 0), part(norm, 0)],
        "nown3": [part(l_n.own, 3), clear],
        "ready.up1": [s_up[1].ready, part(store, w_up, w_up_out)],
        "ready.q1": [s_qkv[1].ready, part(store, w_qkv, w_qkv_out)],
        "n23": [part(l_n.event, 2, 3), lambda: n_stored.append(store(normed, normed_out))],
        "cown": [part(wait_loads, 7)] + [part(l_c.own, c) for c in range(Line.CHUNKS)],
        "c23": [part(l_c.event, 2, 3), part(store, cots, cots_out)],
        "proj": [project],
        "att0": [part(attend, 0, 2)],
        "att1": [part(attend, 2, 2), heads_end],
        "raise31": [part(raise_, order[3], 1), part(store, joined, joined_out)],
        "lower0": [branch_free, part(lower, 0)],
        "hg3": [part(hidden_back, order[3]), part(store, slope, grads_out.at[:, pl.ds(3 * width, ff)])],
        "kb": [keys_back, part(store, qkv, grads_out.at[:, pl.ds(0, 3 * width)])],
    }
    for name, spreads in (("up", s_up), ("q", s_qkv), ("dn", s_dn)):
        for i, s in enumerate(spreads):
            for what, call in (("own", s.own), ("fwd", s.forward), ("last", s.last), ("ready", s.ready)):
                todo.setdefault(what + "." + name + str(i), [call])
    for c in range(Line.CHUNKS):
        todo.setdefault("norm" + str(c), [part(norm, c)])
        todo.setdefault("nown" + str(c), [part(l_n.own, c)])
        for s in range(n - 1):
            todo.setdefault("n" + str(s) + str(c), [part(l_n.event, s, c)])
            todo.setdefault("c" + str(s) + str(c), [part(l_c.event, s, c)])
    for k in range(4):
        for i in range(2):
            todo.setdefault("raise" + str(k) + str(i), [part(raise_, order[k], i)])
        todo.setdefault("hg" + str(k), [part(hidden_back, order[k])])
        todo.setdefault("ab" + str(k), [part(back, k)])
        todo.setdefault("lower" + str(k), [part(lower, k)])
        todo.setdefault("ffirst" + str(k), [part(fold.first, k)])
        for far in range(1, n):
            todo.setdefault("f" + str(k) + str(far), [part(fold.event, k, far)])
    for name in ORDER:
        for call in todo[name]:
            call()
    store(branch, branch_out)
    for copy in stores:
        if copy is not n_stored[0]:
            copy.wait()
    fold.finish()
    l_c.finish()
    copies.finish()


def tables(length):
    half = ROT_DIM // 2
    freqs = rope_base ** (-(np.arange(half).astype(np.float32) * 2.0 / ROT_DIM))
    angles = np.arange(length).astype(np.float32)[:, None] * freqs[None, :].astype(np.float32)
    cos, sin = np.cos(angles), np.sin(angles)
    rest = np.zeros((length, HEAD_DIM - ROT_DIM), np.float32)
    none = np.zeros((length, half), np.float32)
    c = np.concatenate([cos, cos, rest + 1.0], 1)
    s1 = np.concatenate([-sin, none, rest], 1)
    s2 = np.concatenate([none, sin, rest], 1)
    return jnp.asarray(np.stack([np.concatenate([t, t], 1) for t in (c, s1, s2)]).astype(np.float32))


def forward_call(n, prefix, x, cot, wq, wk, wv, wo, wu, wd, gain, bias, bq, bk, bv, bu):
    size, d = x.shape
    length, width, ff = n * size, wq.shape[1], wu.shape[1]
    vm, hbm = pl.BlockSpec(memory_space=pltpu.VMEM), pl.BlockSpec(memory_space=pl.ANY)
    shape = lambda s, t=BF: jax.ShapeDtypeStruct(s, t)
    dma = pltpu.SemaphoreType.DMA
    count = 7 * 9 + 2 * (n - 1) * 2 * Line.CHUNKS
    return pl.pallas_call(
        functools.partial(gather_forward, n),
        out_shape=(
            shape((length, d)),
            shape((length, d)),
            shape((d, 3 * width)),
            shape((d, ff)),
            shape((length, 3 * width + ff)),
            shape((length, width + ff)),
            shape((length, d)),
        ),
        in_specs=[pl.BlockSpec(memory_space=pltpu.SMEM)] + [hbm] * 8 + [vm] * 7,
        out_specs=(hbm,) * 7,
        scratch_shapes=[
            pltpu.VMEM((length, d), BF),
            pltpu.VMEM((length, d), BF),
            pltpu.VMEM((d, 3 * width), BF),
            pltpu.VMEM((d, ff), BF),
            pltpu.VMEM((width + ff, d), BF),
            pltpu.VMEM((length, 3 * width), BF),
            pltpu.VMEM((length, width + ff), BF),
            pltpu.VMEM((length, ff), BF),
            pltpu.VMEM((size, width), BF),
            pltpu.VMEM((length, width), F32),
            pltpu.VMEM((length, width), F32),
            pltpu.VMEM((size, d), BF),
            pltpu.VMEM((length, 128), F32),
            pltpu.VMEM((width // HEAD_DIM, length), F32),
            pltpu.VMEM((2, (EARLY + 1) * (n - 1), size, PIECE), BF),
            dma((count,)),
            dma((count,)),
            dma((8,)),
            dma((8,)),
            dma((2, (EARLY + 1) * (n - 1))),
            dma((2, (EARLY + 1) * (n - 1))),
        ],
        compiler_params=pltpu.CompilerParams(
            collective_id=1, has_side_effects=True, vmem_limit_bytes=63 << 20
        ),
        cost_estimate=pl.CostEstimate(flops=50_000_000_000, bytes_accessed=100_000_000, transcendentals=0),
    )(
        prefix,
        x,
        cot,
        wq,
        wk,
        wv,
        wo,
        wu,
        wd,
        gain[None],
        bias[None],
        bq[None],
        bk[None],
        bv[None],
        bu[None],
        tables(length),
    )


SIB_SLOTS = 2
SLOTS = 4


def backward_scatter(
    n,
    x,
    normed,
    cots,
    w_qkv,
    w_up,
    grads_in,
    joined,
    branch,
    gain,
    b_out,
    b_down,
    layer_out,
    d_input,
    d_in,
    d_dn,
    d_bias,
    d_all,
    own_x,
    cot,
    grads,
    n_block,
    n_turned,
    j_block,
    j_turned,
    wq_block,
    wu_block,
    part_b,
    part_g,
    slots_b,
    slots_g,
    sib_out,
    sib_in,
    own_low,
    own_sum,
    x_in,
    y_in,
    end_in,
    d_rows,
    narrow,
    wide,
    wide_z,
    sums,
    b_send,
    b_recv,
    g_send,
    g_recv,
    sib_send,
    sib_recv,
    link_send,
    link_recv,
    out_sem,
    local,
    stream,
    small_send,
    small_recv,
):
    me, z = lax.axis_index("dp"), lax.axis_index("tensor")
    size, d = x.shape
    length = n * size
    ff = w_up.shape[1]
    width = joined.shape[1] - ff
    lanes = d // 8
    down_pieces = (width + ff) // PIECE
    up_pieces = (3 * width + ff) // PIECE
    pieces = down_pieces + up_pieces
    half, quarter = PIECE // 2, PIECE // 4
    sib = (flip(me, 1), z)
    x_to, y_to = (flip(me, 2), z), (flip(me, 4), z)

    barrier = pltpu.get_barrier_semaphore()
    peers = []
    for k in range(1, 8):
        to = me
        for bit in (1, 2, 4):
            if k & bit:
                to = flip(to, bit)
        peers.append(to)
        pl.semaphore_signal(barrier, 1, device_id=(to, z), device_id_type=MESH)
    others = [lax.rem(z + k, n) for k in range(1, n)]
    for to in others:
        pl.semaphore_signal(barrier, 1, device_id=(me, to), device_id_type=MESH)

    def load(k, src, dst):
        return pltpu.make_async_copy(src, dst, local.at[k])

    loads = [
        load(0, branch, part_b),
        load(1, cots, cot),
        load(2, grads_in, grads),
        load(3, x, own_x),
    ]

    def j_load(p):
        return pltpu.make_async_copy(
            joined.at[:, rows_at(jnp.minimum(p, down_pieces - 1), PIECE)],
            j_block.at[lax.rem(p, 2)],
            stream.at[lax.rem(p, 2)],
        )

    def w_loads(t):
        return [
            pltpu.make_async_copy(w_qkv.at[rows_at(t, PIECE), :], wq_block.at[t % 2], stream.at[2 + t % 2]),
            pltpu.make_async_copy(w_up.at[rows_at(t, PIECE), :], wu_block.at[t % 2], stream.at[4 + t % 2]),
        ]

    def n_load(j):
        return pltpu.make_async_copy(normed.at[rows_at(j, size), :], n_block, stream.at[6])

    j_load(0).start()
    for l in [loads[1], loads[0]] + [n_load(0)] + w_loads(0) + [loads[2], loads[3]] + w_loads(1):
        l.start()

    fold_b = Fold(part_b, slots_b, b_send, b_recv, range(EARLY, d // PIECE), size, n, me, z, begun=EARLY)
    fold_g = Fold(part_g, slots_g, g_send, g_recv, range(d // PIECE), size, n, me, z)

    goals = [flip(me, 2), flip(flip(me, 2), 4), flip(me, 4), me]

    def sib_copy(p):
        return pltpu.make_async_remote_copy(
            sib_out.at[lax.rem(p, 2)],
            sib_in.at[lax.rem(p, SIB_SLOTS)],
            sib_send.at[lax.rem(p, 2)],
            sib_recv.at[lax.rem(p, SIB_SLOTS)],
            device_id=sib,
            device_id_type=MESH,
        )

    def link_copy(k, p, src, dst, to):
        slot = lax.rem(p, SLOTS)
        return pltpu.make_async_remote_copy(
            src, dst, link_send.at[k, slot], link_recv.at[k, slot], device_id=to, device_id_type=MESH
        )

    def x_first(p):
        slot = lax.rem(p, SLOTS)
        return link_copy(0, p, own_low.at[slot, pl.ds(0, 2), pl.ds(0, quarter)], x_in.at[slot], x_to)

    def y_first(p):
        slot = lax.rem(p, SLOTS)
        return link_copy(1, p, own_low.at[slot, pl.ds(1, 2), pl.ds(quarter, quarter)], y_in.at[slot], y_to)

    def y_last(p):
        slot = lax.rem(p, SLOTS)
        return link_copy(2, p, own_low.at[slot, 2, pl.ds(0, quarter)], end_in.at[slot, 0], y_to)

    def x_last(p):
        slot = lax.rem(p, SLOTS)
        return link_copy(3, p, own_low.at[slot, 0, pl.ds(quarter, quarter)], end_in.at[slot, 1], x_to)

    def up_column(p):
        t = jnp.clip(p - down_pieces, 0, up_pieces - 1)
        return lax.rem(t + 3 * width // PIECE, up_pieces) * PIECE

    def out_copies(p):
        src = own_sum.at[lax.rem(p, SLOTS)]
        sem = out_sem.at[lax.rem(p, SLOTS)]
        row = jnp.minimum(p, down_pieces - 1) * PIECE
        down = [
            pltpu.make_async_copy(
                src.at[:, pl.ds(i * half, half)],
                d_dn.at[pl.ds(pl.multiple_of(row + i * half, half), half), :],
                sem.at[i],
            )
            for i in range(2)
        ]
        up = [
            pltpu.make_async_copy(
                src.at[:, pl.ds(i * half, half)],
                d_in.at[:, pl.ds(pl.multiple_of(up_column(p) + i * half, half), half)],
                sem.at[i],
            )
            for i in range(2)
        ]
        return down, up

    def first_down(p):
        slot, out = lax.rem(p, SLOTS), lax.rem(p, 2)
        j_load(p).wait()

        @pl.when(p + 1 < down_pieces)
        def _():
            j_load(p + 1).start()

        j_turned[...] = j_block[lax.rem(p, 2)].T
        for mine in range(2):
            for r, goal in enumerate(goals):
                to = flip(goal, 1) if mine == 0 else goal
                t = nn(j_turned[...], cot[:, rows_at(to, lanes)])
                for i in range(2):
                    v = t[i * half : (i + 1) * half, :]
                    cs = pl.ds(i * half, half)
                    if mine == 0:
                        sib_out[out, r, :, cs] = v.astype(BF)
                    elif r < 3:
                        own_low[slot, r, :, cs] = v.astype(BF)
                    else:
                        own_sum[slot, :, cs] = v
            if mine == 0:
                sib_copy(p).start()

    def first_up(p):
        slot, out = lax.rem(p, SLOTS), lax.rem(p, 2)
        g = grads[:, pl.ds(pl.multiple_of(up_column(p), PIECE), PIECE)]
        for mine in range(2):
            for r, goal in enumerate(goals):
                to = flip(goal, 1) if mine == 0 else goal
                t = nn(n_turned[rows_at(to, lanes), :], g)
                if mine == 0:
                    sib_out[out, r] = t.astype(BF)
                elif r < 3:
                    own_low[slot, r] = t.astype(BF)
                else:
                    own_sum[slot] = t
            if mine == 0:
                sib_copy(p).start()

    def stage_one(p):
        @pl.when(p >= 2)
        def _():
            sib_copy(p - 2).wait_send()

        @pl.when(p >= SLOTS)
        def _():
            for c in out_copies(p - SLOTS)[0]:
                c.wait()

        @pl.when(p < down_pieces)
        def _():
            first_down(p)

        @pl.when(p >= down_pieces)
        def _():
            first_up(p)

    def stage_two(p):
        slot, inn = lax.rem(p, SLOTS), lax.rem(p, SIB_SLOTS)
        sib_copy(p).wait_recv()
        a, b = pl.ds(0, quarter), pl.ds(quarter, quarter)

        def add(r, rows):
            own_low[slot, r, rows] = (own_low[slot, r, rows].astype(F32) + sib_in[inn, r, rows].astype(F32)).astype(BF)

        add(0, a)
        add(1, a)
        x_first(p).start()
        add(1, b)
        add(2, b)
        y_first(p).start()
        add(0, b)
        add(2, a)
        own_sum[slot] = own_sum[slot] + sib_in[inn, 3].astype(F32)

    def stage_three(p):
        slot = lax.rem(p, SLOTS)
        a, b = pl.ds(0, quarter), pl.ds(quarter, quarter)
        x_first(p).wait_recv()
        own_low[slot, 2, a] = (own_low[slot, 2, a].astype(F32) + x_in[slot, 1].astype(F32)).astype(BF)
        y_last(p).start()
        y_first(p).wait_recv()
        own_low[slot, 0, b] = (own_low[slot, 0, b].astype(F32) + y_in[slot, 0].astype(F32)).astype(BF)
        x_last(p).start()
        own_sum[slot, a] = own_sum[slot, a] + x_in[slot, 0].astype(F32)
        own_sum[slot, b] = own_sum[slot, b] + y_in[slot, 1].astype(F32)

    def stage_four(p):
        slot = lax.rem(p, SLOTS)
        a, b = pl.ds(0, quarter), pl.ds(quarter, quarter)
        y_last(p).wait_recv()
        own_sum[slot, a] = own_sum[slot, a] + end_in[slot, 0].astype(F32)
        x_last(p).wait_recv()
        own_sum[slot, b] = own_sum[slot, b] + end_in[slot, 1].astype(F32)
        down, up = out_copies(p)

        @pl.when(p < down_pieces)
        def _():
            for c in down:
                c.start()

        @pl.when(p >= down_pieces)
        def _():
            for c in up:
                c.start()

        for c in (x_first(p), y_first(p), x_last(p), y_last(p)):
            c.wait_send()

    def normed_back(t):
        for l in w_loads(t):
            l.wait()

        @pl.loop(0, length // 512)
        def _(m):
            rows = rows_at(m, 512)
            part_g[rows, t * PIECE : (t + 1) * PIECE] = (
                nt(grads[rows, : 3 * width], wq_block[t % 2]) + nt(grads[rows, 3 * width :], wu_block[t % 2])
            ).astype(BF)

        if t + 2 < d // PIECE:
            for l in w_loads(t + 2):
                l.start()
        fold_g.first(t)

    def turn(j):
        n_load(j).wait()
        n_turned[:, j * size : (j + 1) * size] = n_block[...].T
        if j + 1 < n:
            n_load(j + 1).start()

    def small(k, src, dst, to):
        return pltpu.make_async_remote_copy(
            src, dst, small_send.at[k], small_recv.at[k], device_id=to, device_id_type=MESH
        )

    def bias_sums():
        for i in range(up_pieces):
            narrow[me, i : i + 1, :] = jnp.sum(
                grads[:, i * PIECE : (i + 1) * PIECE].astype(F32), axis=0, keepdims=True
            )
        for k, to in enumerate(peers):
            small(k, narrow.at[me], narrow.at[me], (to, z)).start()

    def branch_end():
        loads[3].wait()

        @pl.loop(0, size // 32)
        def _(r):
            rows = pl.ds(pl.multiple_of(z * size + r * 32, 32), 32)
            v = own_x[rows_at(r, 32), :].astype(F32) + part_b[rows, :].astype(F32) + b_out[...] + b_down[...]
            part_b[rows, :] = v.astype(BF)

        load(0, part_b.at[rows_at(z, size), :], layer_out).start()

    def input_end():
        sums[...] = jnp.zeros_like(sums)

        def chunk(r):
            return pltpu.make_async_copy(
                d_rows.at[lax.rem(r, 2)], d_input.at[rows_at(r, 32), :], local.at[1 + lax.rem(r, 2)]
            )

        @pl.loop(0, size // 32)
        def _(r):
            mine = pl.ds(pl.multiple_of(z * size + r * 32, 32), 32)
            grad = part_g[mine, :].astype(F32)
            v = own_x[rows_at(r, 32), :].astype(F32)
            c = v - jnp.mean(v, axis=-1, keepdims=True)
            inv = lax.rsqrt(jnp.mean(c * c, axis=-1, keepdims=True) + epsilon)
            unit = c * inv
            own_cot = cot[mine, :].astype(F32)
            gu = grad * unit
            sums[0:1, :] += jnp.sum(gu, axis=0, keepdims=True)
            sums[1:2, :] += jnp.sum(grad, axis=0, keepdims=True)
            sums[2:3, :] += jnp.sum(own_cot, axis=0, keepdims=True)
            scaled = grad * gain[...]

            @pl.when(r >= 2)
            def _():
                chunk(r - 2).wait()

            d_rows[lax.rem(r, 2)] = own_cot + inv * (
                scaled
                - jnp.mean(scaled, axis=-1, keepdims=True)
                - unit * jnp.mean(scaled * unit, axis=-1, keepdims=True)
            )
            chunk(r).start()

        for i in range(3):
            for q in range(4):
                wide[me, 4 * i + q : 4 * i + q + 1, :] = sums[i : i + 1, q * PIECE : (q + 1) * PIECE]
        for k, to in enumerate(peers):
            small(8 + k, wide.at[me], wide.at[me], (to, z)).start()
        for r in range(2):
            chunk(size // 32 - 2 + r).wait()

    def small_end():
        for k, to in enumerate(peers):
            small(8 + k, wide.at[to], wide.at[to], (to, z)).wait_recv()
        total = wide[0]
        for i in range(1, 8):
            total = total + wide[i]
        wide_z[z] = total
        for k, to in enumerate(others):
            small(16 + k, wide_z.at[z], wide_z.at[z], (me, to)).start()

    def last_end():
        for k in range(n - 1):
            origin = lax.rem(z + n - 1 - k, n)
            small(16 + k, wide_z.at[origin], wide_z.at[origin], (me, origin)).wait_recv()
        total = wide_z[0]
        for i in range(1, n):
            total = total + wide_z[i]
        d_all[...] = total
        for k, to in enumerate(peers):
            small(k, narrow.at[to], narrow.at[to], (to, z)).wait_recv()
        total = narrow[0]
        for i in range(1, 8):
            total = total + narrow[i]
        d_bias[...] = total
        for k, to in enumerate(peers):
            small(k, narrow.at[me], narrow.at[me], (to, z)).wait_send()
            small(8 + k, wide.at[me], wide.at[me], (to, z)).wait_send()
        for k, to in enumerate(others):
            small(16 + k, wide_z.at[z], wide_z.at[z], (me, to)).wait_send()
        load(0, part_b.at[rows_at(z, size), :], layer_out).wait()

    narrow[me] = jnp.zeros(narrow.shape[1:], F32)
    wide[me] = jnp.zeros(wide.shape[1:], F32)
    pl.semaphore_wait(barrier, 7 + n - 1)

    tasks = {}

    def at(p, *work):
        tasks.setdefault(p, []).extend(work)

    loads[0].wait()
    fold_b.resume()
    for t in fold_b.tiles[1:]:
        fold_b.first(t)
    loads[1].wait()

    part = functools.partial
    at(0, loads[2].wait, part(normed_back, 0))
    at(1, part(turn, 0), part(turn, 1))
    at(2, part(turn, 2), part(turn, 3))
    at(3, part(normed_back, 1), part(fold_b.event, 2, 2), part(fold_b.event, 3, 1))
    at(4, part(fold_b.event, 2, 3))
    at(5, part(normed_back, 2), part(fold_g.event, 0, 1))
    at(6, part(fold_g.event, 1, 1))
    at(7, part(normed_back, 3))
    at(8, part(fold_b.event, 3, 2), part(fold_g.event, 2, 1))
    at(9, part(fold_g.event, 0, 2), part(fold_g.event, 1, 2))
    at(10, part(fold_b.event, 3, 3), part(fold_g.event, 2, 2), part(fold_g.event, 3, 1))
    at(11, bias_sums, part(fold_g.event, 0, 3), part(fold_g.event, 1, 3), part(fold_g.event, 3, 2), branch_end)
    at(12, part(fold_g.event, 2, 3), part(fold_g.event, 3, 3), input_end)
    at(13, small_end)
    at(14, last_end)

    @pl.loop(0, max(pieces + 3, max(tasks) + 1))
    def _(p):
        @pl.when((p >= 1) & (p <= pieces))
        def _():
            stage_two(p - 1)

        @pl.when(p < pieces)
        def _():
            stage_one(p)

        @pl.when((p >= 2) & (p <= pieces + 1))
        def _():
            stage_three(p - 2)

        @pl.when((p >= 3) & (p <= pieces + 2))
        def _():
            stage_four(p - 3)

        for k, work in tasks.items():

            @pl.when(p == k)
            def _():
                for w in work:
                    w()

    for p in range(2):
        sib_copy(pieces - 2 + p).wait_send()
    for p in range(SLOTS):
        for c in out_copies(pieces - SLOTS + p)[1]:
            c.wait()
    fold_b.finish()
    fold_g.finish()


def backward_call(n, x, normed, cots, w_qkv, w_up, grads, joined, branch, gain, b_out, b_down):
    size, d = x.shape
    length, ff = n * size, w_up.shape[1]
    width = joined.shape[1] - ff
    vm, hbm = pl.BlockSpec(memory_space=pltpu.VMEM), pl.BlockSpec(memory_space=pl.ANY)
    shape = lambda s, t=BF: jax.ShapeDtypeStruct(s, t)
    dma = pltpu.SemaphoreType.DMA
    half, quarter = PIECE // 2, PIECE // 4
    late, tiles = (d // PIECE - EARLY) * (n - 1), d // PIECE * (n - 1)
    return pl.pallas_call(
        functools.partial(backward_scatter, n),
        out_shape=(
            shape((size, d)),
            shape((size, d), F32),
            shape((d // 8, 3 * width + ff), F32),
            shape((width + ff, d // 8), F32),
            shape((8, PIECE), F32),
            shape((16, PIECE), F32),
        ),
        in_specs=[hbm] * 8 + [vm] * 3,
        out_specs=(hbm,) * 4 + (vm,) * 2,
        scratch_shapes=[
            pltpu.VMEM((size, d), BF),
            pltpu.VMEM((length, d), BF),
            pltpu.VMEM((length, 3 * width + ff), BF),
            pltpu.VMEM((size, d), BF),
            pltpu.VMEM((d, length), BF),
            pltpu.VMEM((2, length, PIECE), BF),
            pltpu.VMEM((PIECE, length), BF),
            pltpu.VMEM((2, PIECE, 3 * width), BF),
            pltpu.VMEM((2, PIECE, ff), BF),
            pltpu.VMEM((length, d), BF),
            pltpu.VMEM((length, d), BF),
            pltpu.VMEM((2, late, size, PIECE), BF),
            pltpu.VMEM((2, tiles, size, PIECE), BF),
            pltpu.VMEM((2, 4, half, PIECE), BF),
            pltpu.VMEM((SIB_SLOTS, 4, half, PIECE), BF),
            pltpu.VMEM((SLOTS, 3, half, PIECE), BF),
            pltpu.VMEM((SLOTS, half, PIECE), F32),
            pltpu.VMEM((SLOTS, 2, quarter, PIECE), BF),
            pltpu.VMEM((SLOTS, 2, quarter, PIECE), BF),
            pltpu.VMEM((SLOTS, 2, quarter, PIECE), BF),
            pltpu.VMEM((2, 32, d), F32),
            pltpu.VMEM((8, 8, PIECE), F32),
            pltpu.VMEM((8, 16, PIECE), F32),
            pltpu.VMEM((n, 16, PIECE), F32),
            pltpu.VMEM((8, d), F32),
            dma((2, late)),
            dma((2, late)),
            dma((2, tiles)),
            dma((2, tiles)),
            dma((2,)),
            dma((SIB_SLOTS,)),
            dma((4, SLOTS)),
            dma((4, SLOTS)),
            dma((SLOTS, 2)),
            dma((4,)),
            dma((7,)),
            dma((16 + n - 1,)),
            dma((16 + n - 1,)),
        ],
        compiler_params=pltpu.CompilerParams(
            collective_id=2, has_side_effects=True, vmem_limit_bytes=63 << 20
        ),
        cost_estimate=pl.CostEstimate(flops=60_000_000_000, bytes_accessed=100_000_000, transcendentals=0),
    )(x, normed, cots, w_qkv, w_up, grads, joined, branch, gain[None], b_out[None], b_down[None])


def rotate(tensor, positions, direction):
    half_dim = ROT_DIM // 2
    freqs = rope_base ** (-(jnp.arange(half_dim).astype(jnp.float32) * 2.0 / ROT_DIM))
    angles = positions.astype(jnp.float32)[:, None] * freqs[None, :]
    cosine = jnp.cos(angles)[:, None, :]
    sine = direction * jnp.sin(angles)[:, None, :]
    first = tensor[..., :half_dim]
    second = tensor[..., half_dim:ROT_DIM]
    return jnp.concatenate(
        [first * cosine - second * sine, second * cosine + first * sine, tensor[..., ROT_DIM:]],
        axis=-1,
    )


def times_transposed(left, right):
    return lax.dot_general(
        left, right, (((1,), (1,)), ((), ())), preferred_element_type=jnp.float32
    )


def rows_transposed(left, right):
    return lax.dot_general(
        left, right, (((0,), (0,)), ((), ())), preferred_element_type=jnp.float32
    )


def plain_on_device(
    layer_input,
    ln_gain,
    ln_bias,
    w_query,
    b_query,
    w_key,
    b_key,
    w_value,
    b_value,
    w_out,
    b_out,
    w_up,
    b_up,
    w_down,
    b_down,
    prefix,
    cotangent,
):
    local_width = w_query.shape[1]
    hidden_here = w_up.shape[1]
    heads_here = local_width // HEAD_DIM
    score_scale = 1.0 / math.sqrt(HEAD_DIM)
    prefix_len = prefix[0]
    input_float = layer_input.astype(jnp.float32)
    row_mean = jnp.mean(input_float, axis=-1, keepdims=True)
    centred = input_float - row_mean
    inverse = lax.rsqrt(jnp.mean(centred * centred, axis=-1, keepdims=True) + epsilon)
    unit_rows = centred * inverse
    normed = (unit_rows * ln_gain + ln_bias).astype(jnp.bfloat16)
    normed_all = lax.all_gather(normed, "tensor", axis=0, tiled=True)
    length = normed_all.shape[0]
    positions = jnp.arange(length)
    block_rows = min(512, length)
    block_count = length // block_rows
    pieces = (
        lax.all_gather(w_query, "dp", axis=0, tiled=True),
        lax.all_gather(w_key, "dp", axis=0, tiled=True),
        lax.all_gather(w_value, "dp", axis=0, tiled=True),
        lax.all_gather(w_up, "dp", axis=0, tiled=True),
    )
    columns = normed_all
    query_acc, key_acc, value_acc, up_acc = tuple(
        (jnp.dot(columns, piece, preferred_element_type=jnp.float32) for piece in pieces)
    )
    query_pre = (query_acc + b_query).reshape(length, heads_here, HEAD_DIM)
    key_pre = (key_acc + b_key).reshape(length, heads_here, HEAD_DIM)
    query = rotate(query_pre, positions, 1.0).astype(jnp.bfloat16)
    key = rotate(key_pre, positions, 1.0).astype(jnp.bfloat16)
    value = (value_acc + b_value).reshape(length, heads_here, HEAD_DIM).astype(jnp.bfloat16)
    up_pre = up_acc + b_up
    hidden = jax.nn.gelu(up_pre, approximate=True).astype(jnp.bfloat16)

    def scores_for(query_rows, offset):
        raw = (
            jnp.einsum("qhd,khd->hqk", query_rows, key, preferred_element_type=jnp.float32)
            * score_scale
        )
        query_pos = offset + jnp.arange(block_rows)
        seen = (positions[None, :] <= query_pos[:, None]) | (positions[None, :] < prefix_len)
        return jnp.where(seen[None], raw, masked_score)

    def attend_block(index):
        offset = index * block_rows
        query_rows = lax.dynamic_slice_in_dim(query, offset, block_rows, 0)
        scores = scores_for(query_rows, offset)
        row_max = jnp.max(scores, axis=-1, keepdims=True)
        expo = jnp.exp(scores - row_max)
        totals = jnp.sum(expo, axis=-1, keepdims=True)
        probs_low = (expo / totals).astype(jnp.bfloat16)
        out_rows = jnp.einsum("hqk,khd->qhd", probs_low, value, preferred_element_type=jnp.float32)
        return (out_rows, (row_max + jnp.log(totals))[..., 0])

    indices = jnp.arange(block_count)
    out_blocks, log_totals = lax.map(attend_block, indices)
    attn = out_blocks.reshape(length, local_width).astype(jnp.bfloat16)
    pieces = (
        lax.all_gather(w_out, "dp", axis=1, tiled=True),
        lax.all_gather(w_down, "dp", axis=1, tiled=True),
    )
    part = jnp.dot(attn, pieces[0], preferred_element_type=jnp.float32) + jnp.dot(
        hidden, pieces[1], preferred_element_type=jnp.float32
    )
    partial_value = part
    branch = lax.psum_scatter(partial_value, "tensor", scatter_dimension=0, tiled=True)
    layer_out = (input_float + branch + b_out + b_down).astype(jnp.bfloat16)
    grad_all = lax.all_gather(cotangent, "tensor", axis=0, tiled=True)
    pieces = (
        lax.all_gather(w_out, "dp", axis=1, tiled=True),
        lax.all_gather(w_down, "dp", axis=1, tiled=True),
    )
    columns = grad_all
    attn_grad = times_transposed(columns, pieces[0])
    hidden_grad = times_transposed(columns, pieces[1])
    down_joined = jnp.concatenate([attn, hidden], axis=1)
    unused, gelu_pull = jax.vjp(lambda inner: jax.nn.gelu(inner, approximate=True), up_pre)
    up_grad_low = gelu_pull(hidden_grad)[0].astype(jnp.bfloat16)
    attn_grad_low = attn_grad.astype(jnp.bfloat16).reshape(length, heads_here, HEAD_DIM)

    def back_block(carry, item):
        key_grad, value_grad = carry
        index, lse_rows = item
        offset = index * block_rows
        query_rows = lax.dynamic_slice_in_dim(query, offset, block_rows, 0)
        grad_rows = lax.dynamic_slice_in_dim(attn_grad_low, offset, block_rows, 0)
        scores = scores_for(query_rows, offset)
        probs = jnp.exp(scores - lse_rows[..., None])
        value_grad = value_grad + jnp.einsum(
            "hqk,qhd->khd",
            probs.astype(jnp.bfloat16),
            grad_rows,
            preferred_element_type=jnp.float32,
        )
        prob_grad = jnp.einsum("qhd,khd->hqk", grad_rows, value, preferred_element_type=jnp.float32)
        delta = jnp.sum(probs * prob_grad, axis=-1, keepdims=True)
        score_grad = (probs * (prob_grad - delta)).astype(jnp.bfloat16)
        query_grad = (
            jnp.einsum("hqk,khd->qhd", score_grad, key, preferred_element_type=jnp.float32)
            * score_scale
        )
        key_grad = (
            key_grad
            + jnp.einsum("hqk,qhd->khd", score_grad, query_rows, preferred_element_type=jnp.float32)
            * score_scale
        )
        return ((key_grad, value_grad), query_grad)

    state_zeros = jnp.zeros((length, heads_here, HEAD_DIM), jnp.float32)
    (key_grad, value_grad), query_blocks = lax.scan(
        back_block, (state_zeros, state_zeros), (indices, log_totals)
    )
    query_grad = query_blocks.reshape(length, heads_here, HEAD_DIM)
    q_grad_low = (
        rotate(query_grad, positions, -1.0).reshape(length, local_width).astype(jnp.bfloat16)
    )
    k_grad_low = rotate(key_grad, positions, -1.0).reshape(length, local_width).astype(jnp.bfloat16)
    v_grad_low = value_grad.reshape(length, local_width).astype(jnp.bfloat16)
    up_joined = jnp.concatenate([q_grad_low, k_grad_low, v_grad_low, up_grad_low], axis=1)
    columns = grad_all
    joined_rows = lax.psum_scatter(
        jnp.concatenate(
            [rows_transposed(columns, down_joined), rows_transposed(normed_all, up_joined)], axis=1
        ),
        "dp",
        scatter_dimension=0,
        tiled=True,
    )
    down_rows = joined_rows[:, : local_width + hidden_here]
    up_rows = joined_rows[:, local_width + hidden_here :]
    d_w_out = down_rows[:, :local_width].T
    d_w_down = down_rows[:, local_width:].T
    d_w_query = up_rows[:, :local_width]
    d_w_key = up_rows[:, local_width : 2 * local_width]
    d_w_value = up_rows[:, 2 * local_width : 3 * local_width]
    d_w_up = up_rows[:, 3 * local_width :]
    pieces = (
        lax.all_gather(w_query, "dp", axis=0, tiled=True),
        lax.all_gather(w_key, "dp", axis=0, tiled=True),
        lax.all_gather(w_value, "dp", axis=0, tiled=True),
        lax.all_gather(w_up, "dp", axis=0, tiled=True),
    )
    part = (
        times_transposed(q_grad_low, pieces[0])
        + times_transposed(k_grad_low, pieces[1])
        + times_transposed(v_grad_low, pieces[2])
        + times_transposed(up_grad_low, pieces[3])
    )
    own_grad = lax.psum_scatter(part, "tensor", scatter_dimension=0, tiled=True)
    scaled_grad = own_grad * ln_gain
    norm_part = inverse * (
        scaled_grad
        - jnp.mean(scaled_grad, axis=-1, keepdims=True)
        - unit_rows * jnp.mean(scaled_grad * unit_rows, axis=-1, keepdims=True)
    )
    cot_float = cotangent.astype(jnp.float32)
    d_input = cot_float + norm_part
    d_ln_gain, d_ln_bias, d_b_out = lax.psum(
        (
            jnp.sum(own_grad * unit_rows, axis=0),
            jnp.sum(own_grad, axis=0),
            jnp.sum(cot_float, axis=0),
        ),
        ("dp", "tensor"),
    )
    d_b_query, d_b_key, d_b_value, d_b_up = lax.psum(
        (
            jnp.sum(q_grad_low.astype(jnp.float32), axis=0),
            jnp.sum(k_grad_low.astype(jnp.float32), axis=0),
            jnp.sum(v_grad_low.astype(jnp.float32), axis=0),
            jnp.sum(up_grad_low.astype(jnp.float32), axis=0),
        ),
        "dp",
    )
    return (
        layer_out,
        d_input,
        d_ln_gain,
        d_ln_bias,
        d_w_query,
        d_b_query,
        d_w_key,
        d_b_key,
        d_w_value,
        d_b_value,
        d_w_out,
        d_b_out,
        d_w_up,
        d_b_up,
        d_w_down,
        d_b_out,
    )


def finish(d_in_ref, d_dn_ref, d_input_ref, layer_ref, bias_ref, all_ref, *refs):
    (layer_out, d_input, d_ln_gain, d_ln_bias, d_wq, d_bq, d_wk, d_bk, d_wv, d_bv, d_wo, d_bo, d_wu, d_bu, d_wd, d_bd) = refs[:16]
    sems, holds = refs[16], refs[17:]
    width, ff = d_wq.shape[1], d_wu.shape[1]
    moves = [
        (d_in_ref.at[:, pl.ds(3 * width, ff)], d_wu),
        (d_dn_ref.at[pl.ds(width, ff), :], d_wd),
        (d_input_ref, d_input),
        (layer_ref, layer_out),
        (d_in_ref.at[:, pl.ds(0, width)], d_wq),
        (d_in_ref.at[:, pl.ds(width, width)], d_wk),
        (d_in_ref.at[:, pl.ds(2 * width, width)], d_wv),
        (d_dn_ref.at[pl.ds(0, width), :], d_wo),
    ]
    loads, stores = [], []
    for (src, dst), hold in zip(moves, holds):
        half = src.shape[0] // 2
        for i in range(2):
            part, k = pl.ds(i * half, half), len(loads)
            loads.append(pltpu.make_async_copy(src.at[part], hold.at[part], sems.at[0, k]))
            stores.append(pltpu.make_async_copy(hold.at[part], dst.at[part], sems.at[1, k]))
    for load in loads:
        load.start()
    rows = d_ln_gain.shape[0] // PIECE
    for i, out in enumerate((d_ln_gain, d_ln_bias, d_bo)):
        for q in range(rows):
            out[pl.ds(q * PIECE, PIECE)] = all_ref[i * rows + q, :]
    for q in range(rows):
        d_bd[pl.ds(q * PIECE, PIECE)] = all_ref[2 * rows + q, :]
    for i, out in enumerate((d_bq, d_bk, d_bv)):
        out[...] = bias_ref[i, :]
    for q in range(ff // PIECE):
        d_bu[pl.ds(q * PIECE, PIECE)] = bias_ref[3 + q, :]
    for load, store in zip(loads, stores):
        load.wait()
        store.start()
    for store in stores:
        store.wait()


def on_device(
    layer_input, ln_gain, ln_bias, w_query, b_query, w_key, b_key, w_value, b_value,
    w_out, b_out, w_up, b_up, w_down, b_down, prefix, cotangent,
):
    n = lax.axis_size("tensor")
    normed, cots, w_qkv, w_up_all, grads, joined, branch = forward_call(
        n, prefix, layer_input, cotangent, w_query, w_key, w_value, w_out, w_up, w_down,
        ln_gain, ln_bias, b_query, b_key, b_value, b_up,
    )
    layer_out, d_input, d_in, d_dn, d_bias, d_all = backward_call(
        n, layer_input, normed, cots, w_qkv, w_up_all, grads, joined, branch, ln_gain, b_out, b_down
    )
    vm, hbm = pl.BlockSpec(memory_space=pltpu.VMEM), pl.BlockSpec(memory_space=pltpu.HBM)
    like = lambda a, t=F32: jax.ShapeDtypeStruct(a.shape, t)
    return pl.pallas_call(
        finish,
        out_shape=(
            like(layer_input, BF), like(layer_input), like(ln_gain), like(ln_bias),
            like(w_query), like(b_query), like(w_key), like(b_key), like(w_value), like(b_value),
            like(w_out), like(b_out), like(w_up), like(b_up), like(w_down), like(b_down),
        ),
        in_specs=[hbm] * 4 + [vm] * 2,
        out_specs=(hbm, hbm, vm, vm, hbm, vm, hbm, vm, hbm, vm, hbm, vm, hbm, vm, hbm, vm),
        scratch_shapes=[pltpu.SemaphoreType.DMA((2, 16))]
        + [
            pltpu.VMEM(a.shape, t)
            for a, t in (
                (w_up, F32), (w_down, F32), (layer_input, F32), (layer_input, BF),
                (w_query, F32), (w_key, F32), (w_value, F32), (w_out, F32),
            )
        ],
        compiler_params=pltpu.CompilerParams(vmem_limit_bytes=63 << 20),
    )(d_in, d_dn, d_input, layer_out, d_bias, d_all)


def solution(mesh):
    fits = mesh.shape["dp"] == 8 and mesh.shape["tensor"] == 4
    return jax.shard_map(
        on_device if fits else plain_on_device,
        mesh=mesh,
        in_specs=(
            P(("dp", "tensor"), None),
            P(),
            P(),
            P("dp", "tensor"),
            P("tensor"),
            P("dp", "tensor"),
            P("tensor"),
            P("dp", "tensor"),
            P("tensor"),
            P("tensor", "dp"),
            P(),
            P("dp", "tensor"),
            P("tensor"),
            P("tensor", "dp"),
            P(),
            P("dp"),
            P(("dp", "tensor"), None),
        ),
        out_specs=(
            P(("dp", "tensor"), None),
            P(("dp", "tensor"), None),
            P(),
            P(),
            P("dp", "tensor"),
            P("tensor"),
            P("dp", "tensor"),
            P("tensor"),
            P("dp", "tensor"),
            P("tensor"),
            P("tensor", "dp"),
            P(),
            P("dp", "tensor"),
            P("tensor"),
            P("tensor", "dp"),
            P(),
        ),
        check_vma=False,
    )
```

```python
import functools
import math

import jax
import jax.numpy as jnp
import numpy as np
from jax import lax
from jax.experimental import pallas as pl
from jax.experimental.pallas import tpu as pltpu
from jax.sharding import PartitionSpec as P

HEAD_DIM = 64
ROT_DIM = 32
MESH = pl.DeviceIdType.MESH
BF = jnp.bfloat16
F32 = jnp.float32

epsilon = 1e-05
rope_base = 10000.0
masked_score = -1e30
root = math.sqrt(2.0 / math.pi)


def nn(a, b):
    return jnp.dot(a, b, preferred_element_type=F32)


def nt(a, b):
    return lax.dot_general(a, b, (((1,), (1,)), ((), ())), preferred_element_type=F32)


def tn(a, b):
    return lax.dot_general(a, b, (((0,), (0,)), ((), ())), preferred_element_type=F32)


def rows_at(index, size):
    return pl.ds(pl.multiple_of(index * size, size), size)


def flip(index, bit):
    return index + bit - 2 * bit * lax.rem(index // bit, 2)


def chip_tiles(me):
    return [k // 2 for k in (me, flip(me, 2), flip(me, 4), flip(flip(me, 2), 4))]


class Copies:
    def __init__(self, send, recv):
        self.send, self.recv, self.count, self.sent = send, recv, 0, []

    def new(self):
        self.count += 1
        return self.count - 1

    def make(self, k, src, dst, device):
        return pltpu.make_async_remote_copy(
            src, dst, self.send.at[k], self.recv.at[k], device_id=device, device_id_type=MESH
        )

    def start(self, k, src, dst, device):
        copy = self.make(k, src, dst, device)
        copy.start()
        self.sent.append(copy)

    def wait(self, k, dst, device):
        self.make(k, dst, dst, device).wait_recv()

    def finish(self):
        for copy in self.sent:
            copy.wait_send()


class Spread:
    def __init__(self, copies, view, me, z):
        self.c, self.view, self.me, self.z = copies, view, me, z
        self.k = [copies.new() for _ in range(9)]

    def dev(self, bit):
        return (flip(self.me, bit), self.z)

    def own(self):
        v = self.view(self.me)
        self.c.start(self.k[1], v, v, self.dev(2))
        self.c.start(self.k[2], v, v, self.dev(4))
        self.c.start(self.k[0], v, v, self.dev(1))

    def forward(self):
        c, x, y = self.c, flip(self.me, 2), flip(self.me, 4)
        c.wait(self.k[1], self.view(x), self.dev(2))
        v = self.view(x, 0)
        c.start(self.k[3], v, v, self.dev(4))
        c.wait(self.k[2], self.view(y), self.dev(4))
        v = self.view(y, 1)
        c.start(self.k[4], v, v, self.dev(2))
        v = self.view(x)
        c.start(self.k[5], v, v, self.dev(1))
        v = self.view(y)
        c.start(self.k[6], v, v, self.dev(1))

    def last(self):
        c, far = self.c, flip(flip(self.me, 2), 4)
        c.wait(self.k[3], self.view(far, 0), self.dev(4))
        c.wait(self.k[4], self.view(far, 1), self.dev(2))
        v = self.view(far)
        c.start(self.k[7], v, v, self.dev(1))

    def ready_part(self, part):
        c, s = self.c, flip(self.me, 1)
        shards = ([(0, s)], [(5, flip(s, 2)), (6, flip(s, 4))], [(7, flip(flip(s, 2), 4))])
        for k, origin in shards[part]:
            c.wait(self.k[k], self.view(origin), self.dev(1))

    def ready(self):
        for part in range(3):
            self.ready_part(part)


class Line:
    CHUNKS = 4

    def __init__(self, copies, buf, size, n, me, z):
        self.c, self.buf, self.size, self.n, self.me, self.z = copies, buf, size // self.CHUNKS, n, me, z
        self.k = [[[copies.new() for _ in range(self.CHUNKS)] for _ in range(2)] for _ in range(n - 1)]

    def copy(self, s, way, c, block):
        z, n = self.z, self.n
        to = jnp.minimum(z + 1, n - 1) if way == 0 else jnp.maximum(z - 1, 0)
        v = self.buf.at[rows_at(jnp.clip(block, 0, n - 1) * self.CHUNKS + c, self.size), :]
        return self.c.make(self.k[s][way][c], v, v, (self.me, to))

    def far(self, way):
        return self.z if way == 0 else self.n - 1 - self.z

    def block(self, way, s):
        return self.z - s if way == 0 else self.z + s

    def own(self, c):
        for way in range(2):

            @pl.when(self.far(way) < self.n - 1)
            def _():
                self.copy(0, way, c, self.z).start()

    def event(self, s, c):
        for way in range(2):
            far = self.far(way)

            @pl.when(far >= s + 1)
            def _():
                self.copy(s, way, c, self.block(way, s + 1)).wait_recv()

            if s + 1 < self.n - 1:

                @pl.when((far >= s + 1) & (far < self.n - 1))
                def _():
                    self.copy(s + 1, way, c, self.block(way, s + 1)).start()

    def finish(self):
        for s in range(self.n - 1):
            for way in range(2):
                far = self.far(way)

                @pl.when((far >= s) & (far < self.n - 1))
                def _():
                    for c in range(self.CHUNKS):
                        self.copy(s, way, c, self.z).wait_send()


class Fold:
    def __init__(self, part, slots, send, recv, tiles, size, n, me, z, begun=None, handed=None, place=None):
        self.part, self.slots, self.send, self.recv = part, slots, send, recv
        self.begun, self.handed = begun, handed
        self.place = place or list(range(part.shape[1] // PIECE))
        self.tiles, self.size, self.n, self.me, self.z = list(tiles), size, n, me, z

    def far(self, way):
        return self.z if way == 0 else self.n - 1 - self.z

    def copy(self, way, t, i):
        z, n = self.z, self.n
        to = jnp.minimum(z + 1, n - 1) if way == 0 else jnp.maximum(z - 1, 0)
        goal = n - 1 - i if way == 0 else i
        k = self.tiles.index(t) * (n - 1) + i
        return pltpu.make_async_remote_copy(
            self.part.at[goal * self.size : (goal + 1) * self.size, rows_at(self.place[t], PIECE)],
            self.slots.at[way, k],
            self.send.at[way, k],
            self.recv.at[way, k],
            device_id=(self.me, to),
            device_id_type=MESH,
        )

    def first(self, t):
        for way in range(2):

            @pl.when(self.far(way) == 0)
            def _():
                for i in range(self.n - 1):
                    self.copy(way, t, i).start()

    def resume(self):
        for way in range(2):

            @pl.when(self.far(way) == 1)
            def _():
                for i in range(self.n - 2):
                    self.copy(way, self.begun, i).start()

    def event(self, t, far):
        n = self.n
        for way in range(2):

            @pl.when(self.far(way) == far)
            def _():
                for i in range(n - far):
                    goal = n - 1 - i if way == 0 else i
                    k = self.tiles.index(t) * (n - 1) + i
                    self.copy(way, t, i).wait_recv()
                    at = (slice(goal * self.size, (goal + 1) * self.size), rows_at(self.place[t], PIECE))
                    self.part[at] = (self.part[at].astype(F32) + self.slots[way, k].astype(F32)).astype(BF)
                    if i < n - 1 - far and t != self.handed:
                        self.copy(way, t, i).start()

    def finish(self):
        n = self.n
        for way in range(2):
            for far in range(n - 1):

                @pl.when(self.far(way) == far)
                def _():
                    for t in self.tiles:
                        if not (t == self.begun and far == 0 or t == self.handed and far > 0):
                            for i in range(n - 1 - far):
                                self.copy(way, t, i).wait_send()


PIECE = 512
EARLY = 2
ORDER = (
    "own.up0", "own.up1", "norm0", "nown0", "norm1", "nown1", "norm2", "nown2", "norm3", "nown3", "n00",
    "fwd.up0", "own.q0", "n01", "n02", "fwd.up1", "own.q1", "n03", "last.up0", "n10", "ready.up0", "raise00",
    "raise10", "n11", "fwd.q0", "n12", "last.up1", "ready.up1", "raise01", "n13", "cown", "raise11",
    "raise20", "fwd.q1", "own.dn0", "own.dn1", "n20", "raise21", "ready0.dn0", "ready0.dn1", "last.q0",
    "ready.q0", "n21", "last.q1", "ready.q1", "n22", "fwd.dn0", "own.dn2", "ready1.dn0", "ready0.dn2", "n23",
    "proj", "c00", "att0", "c01", "last.dn0", "fwd.dn1", "att1", "c02", "ready2.dn0", "ready1.dn1", "raise30",
    "c03", "fwd.dn2", "raise31", "lower0", "c10", "last.dn1", "ready1.dn2", "ffirst0", "lower1", "ready2.dn1",
    "ffirst1", "lower2", "c11", "last.dn2", "ffirst2", "ab0", "c12", "ready2.dn2", "lower3", "c13", "ab1",
    "c20", "f01", "ab2", "c21", "hg0", "hg1", "c22", "f02", "f11", "hg2", "c23", "ab3", "f03", "hg3", "f12",
    "f21", "kb", "f13",
)


def turned(x, table, sign):
    return (
        x * table[0]
        + pltpu.roll(x, 112, 1) * (table[1] * sign)
        + pltpu.roll(x, 16, 1) * (table[2] * sign)
    )


def gather_forward(
    n,
    prefix,
    x,
    cot,
    wq,
    wk,
    wv,
    wo,
    wu,
    wd,
    gain,
    bias,
    bq,
    bk,
    bv,
    bu,
    table,
    normed_out,
    cots_out,
    w_qkv_out,
    w_up_out,
    grads_out,
    joined_out,
    branch_out,
    normed,
    cots,
    w_qkv,
    w_up,
    w_dn,
    qkv,
    joined,
    slope,
    d_attn,
    d_key,
    d_value,
    own_x,
    lse,
    lse_row,
    fold_slots,
    send,
    recv,
    local,
    outs,
    fold_send,
    fold_recv,
):
    me, z = lax.axis_index("dp"), lax.axis_index("tensor")
    size, d = x.shape
    length = n * size
    width = wq.shape[1]
    ff = wu.shape[1]
    shard = wq.shape[0]
    lanes = wo.shape[1]
    branch = normed

    barrier = pltpu.get_barrier_semaphore()
    for bit in (1, 2, 4):
        pl.semaphore_signal(barrier, 1, device_id=(flip(me, bit), z), device_id_type=MESH)

    @pl.when(z > 0)
    def _():
        pl.semaphore_signal(barrier, 1, device_id=(me, jnp.maximum(z - 1, 0)), device_id_type=MESH)

    @pl.when(z < n - 1)
    def _():
        pl.semaphore_signal(barrier, 1, device_id=(me, jnp.minimum(z + 1, n - 1)), device_id_type=MESH)

    mine, cols = rows_at(me, shard), rows_at(me, lanes)
    loads = [
        pltpu.make_async_copy(x, own_x, local.at[0]),
        pltpu.make_async_copy(wu, w_up.at[mine, :], local.at[1]),
        pltpu.make_async_copy(wq, w_qkv.at[mine, pl.ds(0, width)], local.at[2]),
        pltpu.make_async_copy(wk, w_qkv.at[mine, pl.ds(width, width)], local.at[3]),
        pltpu.make_async_copy(wv, w_qkv.at[mine, pl.ds(2 * width, width)], local.at[4]),
        pltpu.make_async_copy(wo, w_dn.at[pl.ds(0, width), cols], local.at[5]),
        pltpu.make_async_copy(wd, w_dn.at[pl.ds(width, ff), cols], local.at[6]),
        pltpu.make_async_copy(cot, cots.at[rows_at(z, size), :], local.at[7]),
    ]
    for load in loads:
        load.start()

    stores = []

    def store(src, dst):
        copy = pltpu.make_async_copy(src, dst, outs.at[len(stores)])
        stores.append(copy)
        copy.start()
        return copy

    copies = Copies(send, recv)

    def row_view(buf, first, count):
        def view(i, half=None):
            h = count if half is None else count // 2
            start = i * shard + first + (0 if half is None else half * h)
            return buf.at[pl.ds(pl.multiple_of(start, h), h), :]

        return view

    def col_view(first, count):
        def view(i, half=None):
            if half is None:
                return w_dn.at[pl.ds(first, count), rows_at(i, lanes)]
            h = count // 2
            return w_dn.at[pl.ds(first + half * h, h), rows_at(i, lanes)]

        return view

    def row_col_view(first, count):
        def view(i, half=None):
            h = shard if half is None else shard // 2
            start = i * shard + (0 if half is None else half * h)
            return w_up.at[pl.ds(pl.multiple_of(start, h), h), pl.ds(first, count)]

        return view

    s_up = [Spread(copies, row_col_view(i * ff // 2, ff // 2), me, z) for i in range(2)]
    s_qkv = [Spread(copies, row_view(w_qkv, i * shard // 2, shard // 2), me, z) for i in range(2)]
    s_dn = [Spread(copies, col_view(*v), me, z) for v in ((0, width), (width, ff // 2), (width + ff // 2, ff // 2))]
    l_n = Line(copies, normed, size, n, me, z)
    l_c = Line(copies, cots, size, n, me, z)
    place = chip_tiles(me)
    fold = Fold(branch, fold_slots, fold_send, fold_recv, range(EARLY + 1), size, n, me, z, handed=EARLY, place=place)
    order = [z, flip(z, 1), flip(z, 2), flip(flip(z, 1), 2)]
    head = lax.broadcasted_iota(jnp.int32, (1, 128), 1) // HEAD_DIM

    def norm(r):
        rows = slice(r * 64, (r + 1) * 64)
        v = own_x[rows, :].astype(F32)
        mean = jnp.mean(v, axis=-1, keepdims=True)
        c = v - mean
        inv = lax.rsqrt(jnp.mean(c * c, axis=-1, keepdims=True) + epsilon)
        out = (c * inv) * gain[...] + bias[...]
        normed[pl.ds(pl.multiple_of(z * size + r * 64, 64), 64), :] = out.astype(BF)

    def project():
        tile = 512

        @pl.loop(0, length // tile)
        def _(m):
            rows = rows_at(m, tile)
            tab = [table[i, rows, :] for i in range(3)]
            for part in range(3):
                acc = nn(normed[rows, :], w_qkv[:, part * width : (part + 1) * width])
                acc = acc + (bq, bk, bv)[part][...]
                for p in range(width // 128):
                    piece = acc[:, p * 128 : (p + 1) * 128]
                    if part < 2:
                        piece = turned(piece, tab, 1.0)
                        if part == 0:
                            piece = piece * (1.0 / math.sqrt(HEAD_DIM))
                    qkv[rows, part * width + p * 128 : part * width + (p + 1) * 128] = piece.astype(BF)

    def raise_(j, part):
        rows = rows_at(j, size)
        tile = 512

        @pl.loop(part * ff // tile // 2, (part + 1) * ff // tile // 2)
        def _(t):
            cs = rows_at(t, tile)
            u = nn(normed[rows, :], w_up[:, cs]) + bu[:, cs]
            sq = u * u
            th = jnp.tanh(root * u * (1.0 + 0.044715 * sq))
            half = 0.5 * (1.0 + th)
            joined[rows, pl.ds(pl.multiple_of(width + t * tile, tile), tile)] = (u * half).astype(BF)
            slope[rows, cs] = (
                half + 0.5 * u * (1.0 - th * th) * (root * (1.0 + 3 * 0.044715 * sq))
            ).astype(BF)

    block = length // 4

    def visible(b):
        return (b if b > 0 else 0), max(b + 1, 2)

    def attend(first, count):
        @pl.loop(first, first + count)
        def _(p):
            ps = rows_at(p, 128)
            ks = pl.ds(pl.multiple_of(width + p * 128, 128), 128)
            vs = pl.ds(pl.multiple_of(2 * width + p * 128, 128), 128)
            lane = lax.broadcasted_iota(jnp.int32, (1, 128), 1)
            for b in range(4):
                full, some = visible(b)
                qs, kr = pl.ds(b * block, block), pl.ds(0, some * block)
                limit = jnp.maximum(
                    b * block + lax.broadcasted_iota(jnp.int32, (block, 1), 0), prefix[0] - 1
                )
                at = full * block + lax.broadcasted_iota(jnp.int32, (block, (some - full) * block), 1)
                q, outs_ = qkv[qs, ps], []
                scores = [nt(jnp.where(head == h, q, jnp.zeros_like(q)), qkv[kr, ks]) for h in range(2)]
                for h in range(2):
                    last = jnp.where(at <= limit, scores[h][:, full * block :], masked_score)
                    scores[h] = jnp.concatenate([scores[h][:, : full * block], last], 1) if full > 0 else last
                tops = [jnp.max(v, axis=-1, keepdims=True) for v in scores]
                exps = [jnp.exp(v - top) for v, top in zip(scores, tops)]
                totals = [jnp.sum(v, axis=-1, keepdims=True) for v in exps]
                outs_ = [nn((v * (1.0 / total)).astype(BF), qkv[kr, vs]) for v, total in zip(exps, totals)]
                logs = [top + jnp.log(total) for top, total in zip(tops, totals)]
                lse[qs, :] = jnp.where(
                    lane == 2 * p, logs[0], jnp.where(lane == 2 * p + 1, logs[1], lse[qs, :])
                )
                joined[qs, ps] = jnp.where(head == 0, outs_[0], outs_[1]).astype(BF)

    def lower(t):
        @pl.loop(0, length // 512)
        def _(m):
            rows = rows_at(m, 512)
            cs = rows_at(place[t], PIECE)
            branch[rows, cs] = nn(joined[rows, :], w_dn[:, cs]).astype(BF)

    def hidden_back(j):
        rows = rows_at(j, size)
        tile = 512

        @pl.loop(0, ff // tile)
        def _(t):
            g = nt(cots[rows, :], w_dn[pl.ds(pl.multiple_of(width + t * tile, tile), tile), :])
            cs = rows_at(t, tile)
            slope[rows, cs] = (g * slope[rows, cs].astype(F32)).astype(BF)

    def attend_back(b):
        full, some = visible(b)
        qs = pl.ds(b * block, block)
        limit = jnp.maximum(b * block + lax.broadcasted_iota(jnp.int32, (1, block), 1), prefix[0] - 1)

        @pl.loop(0, width // 128)
        def _(p):
            ps = rows_at(p, 128)
            ks = pl.ds(pl.multiple_of(width + p * 128, 128), 128)
            vs = pl.ds(pl.multiple_of(2 * width + p * 128, 128), 128)
            only = lambda a, h: jnp.where(head == h, a, jnp.zeros_like(a))
            q, g = qkv[qs, ps], d_attn[:, ps]
            kr = pl.ds(0, some * block)
            at = full * block + lax.broadcasted_iota(jnp.int32, ((some - full) * block, block), 0)
            qh, gh = [only(q, h) for h in range(2)], [only(g, h) for h in range(2)]
            scores = [nt(qkv[kr, ks], qh[h]) for h in range(2)]
            d_probs = [nt(qkv[kr, vs], gh[h]) for h in range(2)]
            probs, ds = [], []
            for h in range(2):
                e = jnp.exp(scores[h] - lse_row[pl.ds(2 * p + h, 1), qs])
                last = jnp.where(at <= limit, e[full * block :], 0.0)
                probs.append(jnp.concatenate([e[: full * block], last], 0) if full > 0 else last)
            for h in range(2):
                delta = jnp.sum(probs[h] * d_probs[h], axis=0, keepdims=True)
                ds.append((probs[h] * (d_probs[h] - delta)).astype(BF))
            d_value[kr, ps] += nn(probs[0].astype(BF), gh[0]) + nn(probs[1].astype(BF), gh[1])
            d_key[kr, ps] += nn(ds[0], qh[0]) + nn(ds[1], qh[1])
            dq = tn(ds[0], only(qkv[kr, ks], 0)) + tn(ds[1], only(qkv[kr, ks], 1))
            tab = [table[i, qs, :] for i in range(3)]
            qkv[qs, ps] = turned(dq * (1.0 / math.sqrt(HEAD_DIM)), tab, -1.0).astype(BF)

    def back(k):
        d_attn[...] = nt(cots[rows_at(order[k], size), :], w_dn[:width, :]).astype(BF)
        for b in range(4):

            @pl.when(order[k] == b)
            def _():
                attend_back(b)

    def keys_back():
        @pl.loop(0, width // 128)
        def _(p):
            ps = rows_at(p, 128)
            ks = pl.ds(pl.multiple_of(width + p * 128, 128), 128)
            vs = pl.ds(pl.multiple_of(2 * width + p * 128, 128), 128)
            tab = [table[i] for i in range(3)]
            qkv[:, ks] = turned(d_key[:, ps], tab, -1.0).astype(BF)
            qkv[:, vs] = d_value[:, ps].astype(BF)

    signals = 3 + jnp.where(z > 0, 1, 0) + jnp.where(z < n - 1, 1, 0)
    pl.semaphore_wait(barrier, signals)

    n_stored = []
    part = functools.partial

    def clear():
        lse[...] = jnp.zeros_like(lse)
        d_key[...] = jnp.zeros_like(d_key)
        d_value[...] = jnp.zeros_like(d_value)

    def wait_loads(*which):
        for i in which:
            loads[i].wait()

    def heads_end():
        lse_row[...] = lse[...].T[: lse_row.shape[0], :]

    def branch_free():
        l_n.finish()
        n_stored[0].wait()

    todo = {
        "own.up0": [part(wait_loads, 1), s_up[0].own],
        "own.q0": [part(wait_loads, 2, 3, 4), s_qkv[0].own],
        "own.dn0": [part(wait_loads, 5), s_dn[0].own],
        "own.dn1": [part(wait_loads, 6), s_dn[1].own],
        "norm0": [part(wait_loads, 0), part(norm, 0)],
        "nown3": [part(l_n.own, 3), clear],
        "ready.up1": [s_up[1].ready, part(store, w_up, w_up_out)],
        "ready.q1": [s_qkv[1].ready, part(store, w_qkv, w_qkv_out)],
        "n23": [part(l_n.event, 2, 3), lambda: n_stored.append(store(normed, normed_out))],
        "cown": [part(wait_loads, 7)] + [part(l_c.own, c) for c in range(Line.CHUNKS)],
        "c23": [part(l_c.event, 2, 3), part(store, cots, cots_out)],
        "proj": [project],
        "att0": [part(attend, 0, 2)],
        "att1": [part(attend, 2, 2), heads_end],
        "raise31": [part(raise_, order[3], 1), part(store, joined, joined_out)],
        "lower0": [branch_free, part(lower, 0)],
        "hg3": [part(hidden_back, order[3]), part(store, slope, grads_out.at[:, pl.ds(3 * width, ff)])],
        "kb": [keys_back, part(store, qkv, grads_out.at[:, pl.ds(0, 3 * width)])],
    }
    for name, spreads in (("up", s_up), ("q", s_qkv), ("dn", s_dn)):
        for i, s in enumerate(spreads):
            calls = [("own", s.own), ("fwd", s.forward), ("last", s.last), ("ready", s.ready)]
            calls += [("ready" + str(k), part(s.ready_part, k)) for k in range(3)]
            for what, call in calls:
                todo.setdefault(what + "." + name + str(i), [call])
    for c in range(Line.CHUNKS):
        todo.setdefault("norm" + str(c), [part(norm, c)])
        todo.setdefault("nown" + str(c), [part(l_n.own, c)])
        for s in range(n - 1):
            todo.setdefault("n" + str(s) + str(c), [part(l_n.event, s, c)])
            todo.setdefault("c" + str(s) + str(c), [part(l_c.event, s, c)])
    for k in range(4):
        for i in range(2):
            todo.setdefault("raise" + str(k) + str(i), [part(raise_, order[k], i)])
        todo.setdefault("hg" + str(k), [part(hidden_back, order[k])])
        todo.setdefault("ab" + str(k), [part(back, k)])
        todo.setdefault("lower" + str(k), [part(lower, k)])
        todo.setdefault("ffirst" + str(k), [part(fold.first, k)])
        for far in range(1, n):
            todo.setdefault("f" + str(k) + str(far), [part(fold.event, k, far)])
    for name in ORDER:
        for call in todo[name]:
            call()
    store(branch, branch_out)
    for copy in stores:
        if copy is not n_stored[0]:
            copy.wait()
    fold.finish()
    l_c.finish()
    copies.finish()


def tables(length):
    half = ROT_DIM // 2
    freqs = rope_base ** (-(np.arange(half).astype(np.float32) * 2.0 / ROT_DIM))
    angles = np.arange(length).astype(np.float32)[:, None] * freqs[None, :].astype(np.float32)
    cos, sin = np.cos(angles), np.sin(angles)
    rest = np.zeros((length, HEAD_DIM - ROT_DIM), np.float32)
    none = np.zeros((length, half), np.float32)
    c = np.concatenate([cos, cos, rest + 1.0], 1)
    s1 = np.concatenate([-sin, none, rest], 1)
    s2 = np.concatenate([none, sin, rest], 1)
    return jnp.asarray(np.stack([np.concatenate([t, t], 1) for t in (c, s1, s2)]).astype(np.float32))


def forward_call(n, prefix, x, cot, wq, wk, wv, wo, wu, wd, gain, bias, bq, bk, bv, bu):
    size, d = x.shape
    length, width, ff = n * size, wq.shape[1], wu.shape[1]
    vm, hbm = pl.BlockSpec(memory_space=pltpu.VMEM), pl.BlockSpec(memory_space=pl.ANY)
    shape = lambda s, t=BF: jax.ShapeDtypeStruct(s, t)
    dma = pltpu.SemaphoreType.DMA
    count = 7 * 9 + 2 * (n - 1) * 2 * Line.CHUNKS
    return pl.pallas_call(
        functools.partial(gather_forward, n),
        out_shape=(
            shape((length, d)),
            shape((length, d)),
            shape((d, 3 * width)),
            shape((d, ff)),
            shape((length, 3 * width + ff)),
            shape((length, width + ff)),
            shape((length, d)),
        ),
        in_specs=[pl.BlockSpec(memory_space=pltpu.SMEM)] + [hbm] * 8 + [vm] * 7,
        out_specs=(hbm,) * 7,
        scratch_shapes=[
            pltpu.VMEM((length, d), BF),
            pltpu.VMEM((length, d), BF),
            pltpu.VMEM((d, 3 * width), BF),
            pltpu.VMEM((d, ff), BF),
            pltpu.VMEM((width + ff, d), BF),
            pltpu.VMEM((length, 3 * width), BF),
            pltpu.VMEM((length, width + ff), BF),
            pltpu.VMEM((length, ff), BF),
            pltpu.VMEM((size, width), BF),
            pltpu.VMEM((length, width), F32),
            pltpu.VMEM((length, width), F32),
            pltpu.VMEM((size, d), BF),
            pltpu.VMEM((length, 128), F32),
            pltpu.VMEM((width // HEAD_DIM, length), F32),
            pltpu.VMEM((2, (EARLY + 1) * (n - 1), size, PIECE), BF),
            dma((count,)),
            dma((count,)),
            dma((8,)),
            dma((8,)),
            dma((2, (EARLY + 1) * (n - 1))),
            dma((2, (EARLY + 1) * (n - 1))),
        ],
        compiler_params=pltpu.CompilerParams(
            collective_id=1, has_side_effects=True, vmem_limit_bytes=63 << 20
        ),
        cost_estimate=pl.CostEstimate(flops=50_000_000_000, bytes_accessed=100_000_000, transcendentals=0),
    )(
        prefix,
        x,
        cot,
        wq,
        wk,
        wv,
        wo,
        wu,
        wd,
        gain[None],
        bias[None],
        bq[None],
        bk[None],
        bv[None],
        bu[None],
        tables(length),
    )


SIB_SLOTS = 2
SLOTS = 4


def backward_scatter(
    n,
    x,
    normed,
    cots,
    w_qkv,
    w_up,
    grads_in,
    joined,
    branch,
    gain,
    b_out,
    b_down,
    layer_out,
    d_input,
    d_in,
    d_dn,
    d_bias,
    d_all,
    own_x,
    cot,
    grads,
    n_block,
    n_turned,
    j_block,
    j_turned,
    wq_block,
    wu_block,
    part_b,
    part_g,
    slots_b,
    slots_g,
    sib_out,
    sib_in,
    own_low,
    own_sum,
    x_in,
    y_in,
    end_in,
    d_rows,
    narrow,
    wide,
    wide_z,
    sums,
    b_send,
    b_recv,
    g_send,
    g_recv,
    sib_send,
    sib_recv,
    link_send,
    link_recv,
    out_sem,
    local,
    stream,
    small_send,
    small_recv,
):
    me, z = lax.axis_index("dp"), lax.axis_index("tensor")
    size, d = x.shape
    length = n * size
    ff = w_up.shape[1]
    width = joined.shape[1] - ff
    lanes = d // 8
    down_pieces = (width + ff) // PIECE
    up_pieces = (3 * width + ff) // PIECE
    pieces = down_pieces + up_pieces
    half, quarter = PIECE // 2, PIECE // 4
    sib = (flip(me, 1), z)
    x_to, y_to = (flip(me, 2), z), (flip(me, 4), z)

    barrier = pltpu.get_barrier_semaphore()
    peers = []
    for k in range(1, 8):
        to = me
        for bit in (1, 2, 4):
            if k & bit:
                to = flip(to, bit)
        peers.append(to)
        pl.semaphore_signal(barrier, 1, device_id=(to, z), device_id_type=MESH)
    others = [lax.rem(z + k, n) for k in range(1, n)]
    for to in others:
        pl.semaphore_signal(barrier, 1, device_id=(me, to), device_id_type=MESH)

    def load(k, src, dst):
        return pltpu.make_async_copy(src, dst, local.at[k])

    loads = [
        load(0, branch, part_b),
        load(1, cots, cot),
        load(2, grads_in, grads),
        load(3, x, own_x),
    ]

    def j_load(p):
        return pltpu.make_async_copy(
            joined.at[:, rows_at(jnp.minimum(p, down_pieces - 1), PIECE)],
            j_block.at[lax.rem(p, 2)],
            stream.at[lax.rem(p, 2)],
        )

    def w_loads(t):
        return [
            pltpu.make_async_copy(w_qkv.at[rows_at(t, PIECE), :], wq_block.at[t % 2], stream.at[2 + t % 2]),
            pltpu.make_async_copy(w_up.at[rows_at(t, PIECE), :], wu_block.at[t % 2], stream.at[4 + t % 2]),
        ]

    def n_load(j):
        return pltpu.make_async_copy(normed.at[rows_at(j, size), :], n_block, stream.at[6])

    j_load(0).start()
    for l in [loads[1], loads[0]] + [n_load(0)] + w_loads(0) + [loads[2], loads[3]] + w_loads(1):
        l.start()

    fold_b = Fold(part_b, slots_b, b_send, b_recv, range(EARLY, d // PIECE), size, n, me, z, begun=EARLY, place=chip_tiles(me))
    fold_g = Fold(part_g, slots_g, g_send, g_recv, range(d // PIECE), size, n, me, z)

    goals = [flip(me, 2), flip(flip(me, 2), 4), flip(me, 4), me]

    def sib_copy(p):
        return pltpu.make_async_remote_copy(
            sib_out.at[lax.rem(p, 2)],
            sib_in.at[lax.rem(p, SIB_SLOTS)],
            sib_send.at[lax.rem(p, 2)],
            sib_recv.at[lax.rem(p, SIB_SLOTS)],
            device_id=sib,
            device_id_type=MESH,
        )

    def link_copy(k, p, src, dst, to):
        slot = lax.rem(p, SLOTS)
        return pltpu.make_async_remote_copy(
            src, dst, link_send.at[k, slot], link_recv.at[k, slot], device_id=to, device_id_type=MESH
        )

    def x_first(p):
        slot = lax.rem(p, SLOTS)
        return link_copy(0, p, own_low.at[slot, pl.ds(0, 2), pl.ds(0, quarter)], x_in.at[slot], x_to)

    def y_first(p):
        slot = lax.rem(p, SLOTS)
        return link_copy(1, p, own_low.at[slot, pl.ds(1, 2), pl.ds(quarter, quarter)], y_in.at[slot], y_to)

    def y_last(p):
        slot = lax.rem(p, SLOTS)
        return link_copy(2, p, own_low.at[slot, 2, pl.ds(0, quarter)], end_in.at[slot, 0], y_to)

    def x_last(p):
        slot = lax.rem(p, SLOTS)
        return link_copy(3, p, own_low.at[slot, 0, pl.ds(quarter, quarter)], end_in.at[slot, 1], x_to)

    def up_column(p):
        t = jnp.clip(p - down_pieces, 0, up_pieces - 1)
        return lax.rem(t + 3 * width // PIECE, up_pieces) * PIECE

    def out_copies(p):
        src = own_sum.at[lax.rem(p, SLOTS)]
        sem = out_sem.at[lax.rem(p, SLOTS)]
        row = jnp.minimum(p, down_pieces - 1) * PIECE
        down = [
            pltpu.make_async_copy(
                src.at[:, pl.ds(i * half, half)],
                d_dn.at[pl.ds(pl.multiple_of(row + i * half, half), half), :],
                sem.at[i],
            )
            for i in range(2)
        ]
        up = [
            pltpu.make_async_copy(
                src.at[:, pl.ds(i * half, half)],
                d_in.at[:, pl.ds(pl.multiple_of(up_column(p) + i * half, half), half)],
                sem.at[i],
            )
            for i in range(2)
        ]
        return down, up

    def first_down(p):
        slot, out = lax.rem(p, SLOTS), lax.rem(p, 2)
        j_load(p).wait()

        @pl.when(p + 1 < down_pieces)
        def _():
            j_load(p + 1).start()

        j_turned[...] = j_block[lax.rem(p, 2)].T
        for mine in range(2):
            for r, goal in enumerate(goals):
                to = flip(goal, 1) if mine == 0 else goal
                t = nn(j_turned[...], cot[:, rows_at(to, lanes)])
                for i in range(2):
                    v = t[i * half : (i + 1) * half, :]
                    cs = pl.ds(i * half, half)
                    if mine == 0:
                        sib_out[out, r, :, cs] = v.astype(BF)
                    elif r < 3:
                        own_low[slot, r, :, cs] = v.astype(BF)
                    else:
                        own_sum[slot, :, cs] = v
            if mine == 0:
                sib_copy(p).start()

    def first_up(p):
        slot, out = lax.rem(p, SLOTS), lax.rem(p, 2)
        g = grads[:, pl.ds(pl.multiple_of(up_column(p), PIECE), PIECE)]
        for mine in range(2):
            for r, goal in enumerate(goals):
                to = flip(goal, 1) if mine == 0 else goal
                t = nn(n_turned[rows_at(to, lanes), :], g)
                if mine == 0:
                    sib_out[out, r] = t.astype(BF)
                elif r < 3:
                    own_low[slot, r] = t.astype(BF)
                else:
                    own_sum[slot] = t
            if mine == 0:
                sib_copy(p).start()

    def stage_one(p):
        @pl.when(p >= 2)
        def _():
            sib_copy(p - 2).wait_send()

        @pl.when(p >= SLOTS)
        def _():
            for c in out_copies(p - SLOTS)[0]:
                c.wait()

        @pl.when(p < down_pieces)
        def _():
            first_down(p)

        @pl.when(p >= down_pieces)
        def _():
            first_up(p)

    def stage_two(p):
        slot, inn = lax.rem(p, SLOTS), lax.rem(p, SIB_SLOTS)
        sib_copy(p).wait_recv()
        a, b = pl.ds(0, quarter), pl.ds(quarter, quarter)

        def add(r, rows):
            own_low[slot, r, rows] = (own_low[slot, r, rows].astype(F32) + sib_in[inn, r, rows].astype(F32)).astype(BF)

        add(0, a)
        add(1, a)
        x_first(p).start()
        add(1, b)
        add(2, b)
        y_first(p).start()
        add(0, b)
        add(2, a)
        own_sum[slot] = own_sum[slot] + sib_in[inn, 3].astype(F32)

    def stage_three(p):
        slot = lax.rem(p, SLOTS)
        a, b = pl.ds(0, quarter), pl.ds(quarter, quarter)
        x_first(p).wait_recv()
        own_low[slot, 2, a] = (own_low[slot, 2, a].astype(F32) + x_in[slot, 1].astype(F32)).astype(BF)
        y_last(p).start()
        y_first(p).wait_recv()
        own_low[slot, 0, b] = (own_low[slot, 0, b].astype(F32) + y_in[slot, 0].astype(F32)).astype(BF)
        x_last(p).start()
        own_sum[slot, a] = own_sum[slot, a] + x_in[slot, 0].astype(F32)
        own_sum[slot, b] = own_sum[slot, b] + y_in[slot, 1].astype(F32)

    def stage_four(p):
        slot = lax.rem(p, SLOTS)
        a, b = pl.ds(0, quarter), pl.ds(quarter, quarter)
        y_last(p).wait_recv()
        own_sum[slot, a] = own_sum[slot, a] + end_in[slot, 0].astype(F32)
        x_last(p).wait_recv()
        own_sum[slot, b] = own_sum[slot, b] + end_in[slot, 1].astype(F32)
        down, up = out_copies(p)

        @pl.when(p < down_pieces)
        def _():
            for c in down:
                c.start()

        @pl.when(p >= down_pieces)
        def _():
            for c in up:
                c.start()

        for c in (x_first(p), y_first(p), x_last(p), y_last(p)):
            c.wait_send()

    def normed_back(t):
        for l in w_loads(t):
            l.wait()

        @pl.loop(0, length // 512)
        def _(m):
            rows = rows_at(m, 512)
            part_g[rows, t * PIECE : (t + 1) * PIECE] = (
                nt(grads[rows, : 3 * width], wq_block[t % 2]) + nt(grads[rows, 3 * width :], wu_block[t % 2])
            ).astype(BF)

        if t + 2 < d // PIECE:
            for l in w_loads(t + 2):
                l.start()
        fold_g.first(t)

    def turn(j):
        n_load(j).wait()
        n_turned[:, j * size : (j + 1) * size] = n_block[...].T
        if j + 1 < n:
            n_load(j + 1).start()

    def small(k, src, dst, to):
        return pltpu.make_async_remote_copy(
            src, dst, small_send.at[k], small_recv.at[k], device_id=to, device_id_type=MESH
        )

    def bias_sums():
        for i in range(up_pieces):
            narrow[me, i : i + 1, :] = jnp.sum(
                grads[:, i * PIECE : (i + 1) * PIECE].astype(F32), axis=0, keepdims=True
            )
        for k, to in enumerate(peers):
            small(k, narrow.at[me], narrow.at[me], (to, z)).start()

    def branch_end():
        loads[3].wait()

        @pl.loop(0, size // 32)
        def _(r):
            rows = pl.ds(pl.multiple_of(z * size + r * 32, 32), 32)
            v = own_x[rows_at(r, 32), :].astype(F32) + part_b[rows, :].astype(F32) + b_out[...] + b_down[...]
            part_b[rows, :] = v.astype(BF)

        load(0, part_b.at[rows_at(z, size), :], layer_out).start()

    def input_end():
        sums[...] = jnp.zeros_like(sums)

        def chunk(r):
            return pltpu.make_async_copy(
                d_rows.at[lax.rem(r, 2)], d_input.at[rows_at(r, 32), :], local.at[1 + lax.rem(r, 2)]
            )

        @pl.loop(0, size // 32)
        def _(r):
            mine = pl.ds(pl.multiple_of(z * size + r * 32, 32), 32)
            grad = part_g[mine, :].astype(F32)
            v = own_x[rows_at(r, 32), :].astype(F32)
            c = v - jnp.mean(v, axis=-1, keepdims=True)
            inv = lax.rsqrt(jnp.mean(c * c, axis=-1, keepdims=True) + epsilon)
            unit = c * inv
            own_cot = cot[mine, :].astype(F32)
            gu = grad * unit
            sums[0:1, :] += jnp.sum(gu, axis=0, keepdims=True)
            sums[1:2, :] += jnp.sum(grad, axis=0, keepdims=True)
            sums[2:3, :] += jnp.sum(own_cot, axis=0, keepdims=True)
            scaled = grad * gain[...]

            @pl.when(r >= 2)
            def _():
                chunk(r - 2).wait()

            d_rows[lax.rem(r, 2)] = own_cot + inv * (
                scaled
                - jnp.mean(scaled, axis=-1, keepdims=True)
                - unit * jnp.mean(scaled * unit, axis=-1, keepdims=True)
            )
            chunk(r).start()

        for i in range(3):
            for q in range(4):
                wide[me, 4 * i + q : 4 * i + q + 1, :] = sums[i : i + 1, q * PIECE : (q + 1) * PIECE]
        for k, to in enumerate(peers):
            small(8 + k, wide.at[me], wide.at[me], (to, z)).start()
        for r in range(2):
            chunk(size // 32 - 2 + r).wait()

    def small_end():
        for k, to in enumerate(peers):
            small(8 + k, wide.at[to], wide.at[to], (to, z)).wait_recv()
        total = wide[0]
        for i in range(1, 8):
            total = total + wide[i]
        wide_z[z] = total
        for k, to in enumerate(others):
            small(16 + k, wide_z.at[z], wide_z.at[z], (me, to)).start()

    def last_end():
        for k in range(n - 1):
            origin = lax.rem(z + n - 1 - k, n)
            small(16 + k, wide_z.at[origin], wide_z.at[origin], (me, origin)).wait_recv()
        total = wide_z[0]
        for i in range(1, n):
            total = total + wide_z[i]
        d_all[...] = total
        for k, to in enumerate(peers):
            small(k, narrow.at[to], narrow.at[to], (to, z)).wait_recv()
        total = narrow[0]
        for i in range(1, 8):
            total = total + narrow[i]
        d_bias[...] = total
        for k, to in enumerate(peers):
            small(k, narrow.at[me], narrow.at[me], (to, z)).wait_send()
            small(8 + k, wide.at[me], wide.at[me], (to, z)).wait_send()
        for k, to in enumerate(others):
            small(16 + k, wide_z.at[z], wide_z.at[z], (me, to)).wait_send()
        load(0, part_b.at[rows_at(z, size), :], layer_out).wait()

    narrow[me] = jnp.zeros(narrow.shape[1:], F32)
    wide[me] = jnp.zeros(wide.shape[1:], F32)
    pl.semaphore_wait(barrier, 7 + n - 1)

    tasks = {}

    def at(p, *work):
        tasks.setdefault(p, []).extend(work)

    loads[0].wait()
    fold_b.resume()
    for t in fold_b.tiles[1:]:
        fold_b.first(t)
    loads[1].wait()

    part = functools.partial
    at(0, loads[2].wait, part(normed_back, 0))
    at(1, part(turn, 0), part(turn, 1))
    at(2, part(turn, 2), part(turn, 3))
    at(3, part(normed_back, 1), part(fold_b.event, 2, 2), part(fold_b.event, 3, 1))
    at(4, part(fold_b.event, 2, 3))
    at(5, part(normed_back, 2), part(fold_g.event, 0, 1))
    at(6, part(fold_g.event, 1, 1))
    at(7, part(normed_back, 3))
    at(8, part(fold_b.event, 3, 2), part(fold_g.event, 2, 1))
    at(9, part(fold_g.event, 0, 2), part(fold_g.event, 1, 2))
    at(10, part(fold_b.event, 3, 3), part(fold_g.event, 2, 2), part(fold_g.event, 3, 1))
    at(11, bias_sums, part(fold_g.event, 0, 3), part(fold_g.event, 1, 3), part(fold_g.event, 3, 2), branch_end)
    at(12, part(fold_g.event, 2, 3), part(fold_g.event, 3, 3), input_end)
    at(13, small_end)
    at(14, last_end)

    @pl.loop(0, max(pieces + 3, max(tasks) + 1))
    def _(p):
        @pl.when((p >= 1) & (p <= pieces))
        def _():
            stage_two(p - 1)

        @pl.when(p < pieces)
        def _():
            stage_one(p)

        @pl.when((p >= 2) & (p <= pieces + 1))
        def _():
            stage_three(p - 2)

        @pl.when((p >= 3) & (p <= pieces + 2))
        def _():
            stage_four(p - 3)

        for k, work in tasks.items():

            @pl.when(p == k)
            def _():
                for w in work:
                    w()

    for p in range(2):
        sib_copy(pieces - 2 + p).wait_send()
    for p in range(SLOTS):
        for c in out_copies(pieces - SLOTS + p)[1]:
            c.wait()
    fold_b.finish()
    fold_g.finish()


def backward_call(n, x, normed, cots, w_qkv, w_up, grads, joined, branch, gain, b_out, b_down):
    size, d = x.shape
    length, ff = n * size, w_up.shape[1]
    width = joined.shape[1] - ff
    vm, hbm = pl.BlockSpec(memory_space=pltpu.VMEM), pl.BlockSpec(memory_space=pl.ANY)
    shape = lambda s, t=BF: jax.ShapeDtypeStruct(s, t)
    dma = pltpu.SemaphoreType.DMA
    half, quarter = PIECE // 2, PIECE // 4
    late, tiles = (d // PIECE - EARLY) * (n - 1), d // PIECE * (n - 1)
    return pl.pallas_call(
        functools.partial(backward_scatter, n),
        out_shape=(
            shape((size, d)),
            shape((size, d), F32),
            shape((d // 8, 3 * width + ff), F32),
            shape((width + ff, d // 8), F32),
            shape((8, PIECE), F32),
            shape((16, PIECE), F32),
        ),
        in_specs=[hbm] * 8 + [vm] * 3,
        out_specs=(hbm,) * 4 + (vm,) * 2,
        scratch_shapes=[
            pltpu.VMEM((size, d), BF),
            pltpu.VMEM((length, d), BF),
            pltpu.VMEM((length, 3 * width + ff), BF),
            pltpu.VMEM((size, d), BF),
            pltpu.VMEM((d, length), BF),
            pltpu.VMEM((2, length, PIECE), BF),
            pltpu.VMEM((PIECE, length), BF),
            pltpu.VMEM((2, PIECE, 3 * width), BF),
            pltpu.VMEM((2, PIECE, ff), BF),
            pltpu.VMEM((length, d), BF),
            pltpu.VMEM((length, d), BF),
            pltpu.VMEM((2, late, size, PIECE), BF),
            pltpu.VMEM((2, tiles, size, PIECE), BF),
            pltpu.VMEM((2, 4, half, PIECE), BF),
            pltpu.VMEM((SIB_SLOTS, 4, half, PIECE), BF),
            pltpu.VMEM((SLOTS, 3, half, PIECE), BF),
            pltpu.VMEM((SLOTS, half, PIECE), F32),
            pltpu.VMEM((SLOTS, 2, quarter, PIECE), BF),
            pltpu.VMEM((SLOTS, 2, quarter, PIECE), BF),
            pltpu.VMEM((SLOTS, 2, quarter, PIECE), BF),
            pltpu.VMEM((2, 32, d), F32),
            pltpu.VMEM((8, 8, PIECE), F32),
            pltpu.VMEM((8, 16, PIECE), F32),
            pltpu.VMEM((n, 16, PIECE), F32),
            pltpu.VMEM((8, d), F32),
            dma((2, late)),
            dma((2, late)),
            dma((2, tiles)),
            dma((2, tiles)),
            dma((2,)),
            dma((SIB_SLOTS,)),
            dma((4, SLOTS)),
            dma((4, SLOTS)),
            dma((SLOTS, 2)),
            dma((4,)),
            dma((7,)),
            dma((16 + n - 1,)),
            dma((16 + n - 1,)),
        ],
        compiler_params=pltpu.CompilerParams(
            collective_id=2, has_side_effects=True, vmem_limit_bytes=63 << 20
        ),
        cost_estimate=pl.CostEstimate(flops=60_000_000_000, bytes_accessed=100_000_000, transcendentals=0),
    )(x, normed, cots, w_qkv, w_up, grads, joined, branch, gain[None], b_out[None], b_down[None])


def rotate(tensor, positions, direction):
    half_dim = ROT_DIM // 2
    freqs = rope_base ** (-(jnp.arange(half_dim).astype(jnp.float32) * 2.0 / ROT_DIM))
    angles = positions.astype(jnp.float32)[:, None] * freqs[None, :]
    cosine = jnp.cos(angles)[:, None, :]
    sine = direction * jnp.sin(angles)[:, None, :]
    first = tensor[..., :half_dim]
    second = tensor[..., half_dim:ROT_DIM]
    return jnp.concatenate(
        [first * cosine - second * sine, second * cosine + first * sine, tensor[..., ROT_DIM:]],
        axis=-1,
    )


def times_transposed(left, right):
    return lax.dot_general(
        left, right, (((1,), (1,)), ((), ())), preferred_element_type=jnp.float32
    )


def rows_transposed(left, right):
    return lax.dot_general(
        left, right, (((0,), (0,)), ((), ())), preferred_element_type=jnp.float32
    )


def plain_on_device(
    layer_input,
    ln_gain,
    ln_bias,
    w_query,
    b_query,
    w_key,
    b_key,
    w_value,
    b_value,
    w_out,
    b_out,
    w_up,
    b_up,
    w_down,
    b_down,
    prefix,
    cotangent,
):
    local_width = w_query.shape[1]
    hidden_here = w_up.shape[1]
    heads_here = local_width // HEAD_DIM
    score_scale = 1.0 / math.sqrt(HEAD_DIM)
    prefix_len = prefix[0]
    input_float = layer_input.astype(jnp.float32)
    row_mean = jnp.mean(input_float, axis=-1, keepdims=True)
    centred = input_float - row_mean
    inverse = lax.rsqrt(jnp.mean(centred * centred, axis=-1, keepdims=True) + epsilon)
    unit_rows = centred * inverse
    normed = (unit_rows * ln_gain + ln_bias).astype(jnp.bfloat16)
    normed_all = lax.all_gather(normed, "tensor", axis=0, tiled=True)
    length = normed_all.shape[0]
    positions = jnp.arange(length)
    block_rows = min(512, length)
    block_count = length // block_rows
    pieces = (
        lax.all_gather(w_query, "dp", axis=0, tiled=True),
        lax.all_gather(w_key, "dp", axis=0, tiled=True),
        lax.all_gather(w_value, "dp", axis=0, tiled=True),
        lax.all_gather(w_up, "dp", axis=0, tiled=True),
    )
    columns = normed_all
    query_acc, key_acc, value_acc, up_acc = tuple(
        (jnp.dot(columns, piece, preferred_element_type=jnp.float32) for piece in pieces)
    )
    query_pre = (query_acc + b_query).reshape(length, heads_here, HEAD_DIM)
    key_pre = (key_acc + b_key).reshape(length, heads_here, HEAD_DIM)
    query = rotate(query_pre, positions, 1.0).astype(jnp.bfloat16)
    key = rotate(key_pre, positions, 1.0).astype(jnp.bfloat16)
    value = (value_acc + b_value).reshape(length, heads_here, HEAD_DIM).astype(jnp.bfloat16)
    up_pre = up_acc + b_up
    hidden = jax.nn.gelu(up_pre, approximate=True).astype(jnp.bfloat16)

    def scores_for(query_rows, offset):
        raw = (
            jnp.einsum("qhd,khd->hqk", query_rows, key, preferred_element_type=jnp.float32)
            * score_scale
        )
        query_pos = offset + jnp.arange(block_rows)
        seen = (positions[None, :] <= query_pos[:, None]) | (positions[None, :] < prefix_len)
        return jnp.where(seen[None], raw, masked_score)

    def attend_block(index):
        offset = index * block_rows
        query_rows = lax.dynamic_slice_in_dim(query, offset, block_rows, 0)
        scores = scores_for(query_rows, offset)
        row_max = jnp.max(scores, axis=-1, keepdims=True)
        expo = jnp.exp(scores - row_max)
        totals = jnp.sum(expo, axis=-1, keepdims=True)
        probs_low = (expo / totals).astype(jnp.bfloat16)
        out_rows = jnp.einsum("hqk,khd->qhd", probs_low, value, preferred_element_type=jnp.float32)
        return (out_rows, (row_max + jnp.log(totals))[..., 0])

    indices = jnp.arange(block_count)
    out_blocks, log_totals = lax.map(attend_block, indices)
    attn = out_blocks.reshape(length, local_width).astype(jnp.bfloat16)
    pieces = (
        lax.all_gather(w_out, "dp", axis=1, tiled=True),
        lax.all_gather(w_down, "dp", axis=1, tiled=True),
    )
    part = jnp.dot(attn, pieces[0], preferred_element_type=jnp.float32) + jnp.dot(
        hidden, pieces[1], preferred_element_type=jnp.float32
    )
    partial_value = part
    branch = lax.psum_scatter(partial_value, "tensor", scatter_dimension=0, tiled=True)
    layer_out = (input_float + branch + b_out + b_down).astype(jnp.bfloat16)
    grad_all = lax.all_gather(cotangent, "tensor", axis=0, tiled=True)
    pieces = (
        lax.all_gather(w_out, "dp", axis=1, tiled=True),
        lax.all_gather(w_down, "dp", axis=1, tiled=True),
    )
    columns = grad_all
    attn_grad = times_transposed(columns, pieces[0])
    hidden_grad = times_transposed(columns, pieces[1])
    down_joined = jnp.concatenate([attn, hidden], axis=1)
    unused, gelu_pull = jax.vjp(lambda inner: jax.nn.gelu(inner, approximate=True), up_pre)
    up_grad_low = gelu_pull(hidden_grad)[0].astype(jnp.bfloat16)
    attn_grad_low = attn_grad.astype(jnp.bfloat16).reshape(length, heads_here, HEAD_DIM)

    def back_block(carry, item):
        key_grad, value_grad = carry
        index, lse_rows = item
        offset = index * block_rows
        query_rows = lax.dynamic_slice_in_dim(query, offset, block_rows, 0)
        grad_rows = lax.dynamic_slice_in_dim(attn_grad_low, offset, block_rows, 0)
        scores = scores_for(query_rows, offset)
        probs = jnp.exp(scores - lse_rows[..., None])
        value_grad = value_grad + jnp.einsum(
            "hqk,qhd->khd",
            probs.astype(jnp.bfloat16),
            grad_rows,
            preferred_element_type=jnp.float32,
        )
        prob_grad = jnp.einsum("qhd,khd->hqk", grad_rows, value, preferred_element_type=jnp.float32)
        delta = jnp.sum(probs * prob_grad, axis=-1, keepdims=True)
        score_grad = (probs * (prob_grad - delta)).astype(jnp.bfloat16)
        query_grad = (
            jnp.einsum("hqk,khd->qhd", score_grad, key, preferred_element_type=jnp.float32)
            * score_scale
        )
        key_grad = (
            key_grad
            + jnp.einsum("hqk,qhd->khd", score_grad, query_rows, preferred_element_type=jnp.float32)
            * score_scale
        )
        return ((key_grad, value_grad), query_grad)

    state_zeros = jnp.zeros((length, heads_here, HEAD_DIM), jnp.float32)
    (key_grad, value_grad), query_blocks = lax.scan(
        back_block, (state_zeros, state_zeros), (indices, log_totals)
    )
    query_grad = query_blocks.reshape(length, heads_here, HEAD_DIM)
    q_grad_low = (
        rotate(query_grad, positions, -1.0).reshape(length, local_width).astype(jnp.bfloat16)
    )
    k_grad_low = rotate(key_grad, positions, -1.0).reshape(length, local_width).astype(jnp.bfloat16)
    v_grad_low = value_grad.reshape(length, local_width).astype(jnp.bfloat16)
    up_joined = jnp.concatenate([q_grad_low, k_grad_low, v_grad_low, up_grad_low], axis=1)
    columns = grad_all
    joined_rows = lax.psum_scatter(
        jnp.concatenate(
            [rows_transposed(columns, down_joined), rows_transposed(normed_all, up_joined)], axis=1
        ),
        "dp",
        scatter_dimension=0,
        tiled=True,
    )
    down_rows = joined_rows[:, : local_width + hidden_here]
    up_rows = joined_rows[:, local_width + hidden_here :]
    d_w_out = down_rows[:, :local_width].T
    d_w_down = down_rows[:, local_width:].T
    d_w_query = up_rows[:, :local_width]
    d_w_key = up_rows[:, local_width : 2 * local_width]
    d_w_value = up_rows[:, 2 * local_width : 3 * local_width]
    d_w_up = up_rows[:, 3 * local_width :]
    pieces = (
        lax.all_gather(w_query, "dp", axis=0, tiled=True),
        lax.all_gather(w_key, "dp", axis=0, tiled=True),
        lax.all_gather(w_value, "dp", axis=0, tiled=True),
        lax.all_gather(w_up, "dp", axis=0, tiled=True),
    )
    part = (
        times_transposed(q_grad_low, pieces[0])
        + times_transposed(k_grad_low, pieces[1])
        + times_transposed(v_grad_low, pieces[2])
        + times_transposed(up_grad_low, pieces[3])
    )
    own_grad = lax.psum_scatter(part, "tensor", scatter_dimension=0, tiled=True)
    scaled_grad = own_grad * ln_gain
    norm_part = inverse * (
        scaled_grad
        - jnp.mean(scaled_grad, axis=-1, keepdims=True)
        - unit_rows * jnp.mean(scaled_grad * unit_rows, axis=-1, keepdims=True)
    )
    cot_float = cotangent.astype(jnp.float32)
    d_input = cot_float + norm_part
    d_ln_gain, d_ln_bias, d_b_out = lax.psum(
        (
            jnp.sum(own_grad * unit_rows, axis=0),
            jnp.sum(own_grad, axis=0),
            jnp.sum(cot_float, axis=0),
        ),
        ("dp", "tensor"),
    )
    d_b_query, d_b_key, d_b_value, d_b_up = lax.psum(
        (
            jnp.sum(q_grad_low.astype(jnp.float32), axis=0),
            jnp.sum(k_grad_low.astype(jnp.float32), axis=0),
            jnp.sum(v_grad_low.astype(jnp.float32), axis=0),
            jnp.sum(up_grad_low.astype(jnp.float32), axis=0),
        ),
        "dp",
    )
    return (
        layer_out,
        d_input,
        d_ln_gain,
        d_ln_bias,
        d_w_query,
        d_b_query,
        d_w_key,
        d_b_key,
        d_w_value,
        d_b_value,
        d_w_out,
        d_b_out,
        d_w_up,
        d_b_up,
        d_w_down,
        d_b_out,
    )


def finish(d_in_ref, d_dn_ref, d_input_ref, layer_ref, bias_ref, all_ref, *refs):
    (layer_out, d_input, d_ln_gain, d_ln_bias, d_wq, d_bq, d_wk, d_bk, d_wv, d_bv, d_wo, d_bo, d_wu, d_bu, d_wd, d_bd) = refs[:16]
    sems, holds = refs[16], refs[17:]
    width, ff = d_wq.shape[1], d_wu.shape[1]
    moves = [
        (d_in_ref.at[:, pl.ds(3 * width, ff)], d_wu),
        (d_dn_ref.at[pl.ds(width, ff), :], d_wd),
        (d_input_ref, d_input),
        (layer_ref, layer_out),
        (d_in_ref.at[:, pl.ds(0, width)], d_wq),
        (d_in_ref.at[:, pl.ds(width, width)], d_wk),
        (d_in_ref.at[:, pl.ds(2 * width, width)], d_wv),
        (d_dn_ref.at[pl.ds(0, width), :], d_wo),
    ]
    loads, stores = [], []
    for (src, dst), hold in zip(moves, holds):
        half = src.shape[0] // 2
        for i in range(2):
            part, k = pl.ds(i * half, half), len(loads)
            loads.append(pltpu.make_async_copy(src.at[part], hold.at[part], sems.at[0, k]))
            stores.append(pltpu.make_async_copy(hold.at[part], dst.at[part], sems.at[1, k]))
    for load in loads:
        load.start()
    rows = d_ln_gain.shape[0] // PIECE
    for i, out in enumerate((d_ln_gain, d_ln_bias, d_bo)):
        for q in range(rows):
            out[pl.ds(q * PIECE, PIECE)] = all_ref[i * rows + q, :]
    for q in range(rows):
        d_bd[pl.ds(q * PIECE, PIECE)] = all_ref[2 * rows + q, :]
    for i, out in enumerate((d_bq, d_bk, d_bv)):
        out[...] = bias_ref[i, :]
    for q in range(ff // PIECE):
        d_bu[pl.ds(q * PIECE, PIECE)] = bias_ref[3 + q, :]
    for load, store in zip(loads, stores):
        load.wait()
        store.start()
    for store in stores:
        store.wait()


def on_device(
    layer_input, ln_gain, ln_bias, w_query, b_query, w_key, b_key, w_value, b_value,
    w_out, b_out, w_up, b_up, w_down, b_down, prefix, cotangent,
):
    n = lax.axis_size("tensor")
    normed, cots, w_qkv, w_up_all, grads, joined, branch = forward_call(
        n, prefix, layer_input, cotangent, w_query, w_key, w_value, w_out, w_up, w_down,
        ln_gain, ln_bias, b_query, b_key, b_value, b_up,
    )
    layer_out, d_input, d_in, d_dn, d_bias, d_all = backward_call(
        n, layer_input, normed, cots, w_qkv, w_up_all, grads, joined, branch, ln_gain, b_out, b_down
    )
    vm, hbm = pl.BlockSpec(memory_space=pltpu.VMEM), pl.BlockSpec(memory_space=pltpu.HBM)
    like = lambda a, t=F32: jax.ShapeDtypeStruct(a.shape, t)
    return pl.pallas_call(
        finish,
        out_shape=(
            like(layer_input, BF), like(layer_input), like(ln_gain), like(ln_bias),
            like(w_query), like(b_query), like(w_key), like(b_key), like(w_value), like(b_value),
            like(w_out), like(b_out), like(w_up), like(b_up), like(w_down), like(b_down),
        ),
        in_specs=[hbm] * 4 + [vm] * 2,
        out_specs=(hbm, hbm, vm, vm, hbm, vm, hbm, vm, hbm, vm, hbm, vm, hbm, vm, hbm, vm),
        scratch_shapes=[pltpu.SemaphoreType.DMA((2, 16))]
        + [
            pltpu.VMEM(a.shape, t)
            for a, t in (
                (w_up, F32), (w_down, F32), (layer_input, F32), (layer_input, BF),
                (w_query, F32), (w_key, F32), (w_value, F32), (w_out, F32),
            )
        ],
        compiler_params=pltpu.CompilerParams(vmem_limit_bytes=63 << 20),
    )(d_in, d_dn, d_input, layer_out, d_bias, d_all)


def solution(mesh):
    fits = mesh.shape["dp"] == 8 and mesh.shape["tensor"] == 4
    return jax.shard_map(
        on_device if fits else plain_on_device,
        mesh=mesh,
        in_specs=(
            P(("dp", "tensor"), None),
            P(),
            P(),
            P("dp", "tensor"),
            P("tensor"),
            P("dp", "tensor"),
            P("tensor"),
            P("dp", "tensor"),
            P("tensor"),
            P("tensor", "dp"),
            P(),
            P("dp", "tensor"),
            P("tensor"),
            P("tensor", "dp"),
            P(),
            P("dp"),
            P(("dp", "tensor"), None),
        ),
        out_specs=(
            P(("dp", "tensor"), None),
            P(("dp", "tensor"), None),
            P(),
            P(),
            P("dp", "tensor"),
            P("tensor"),
            P("dp", "tensor"),
            P("tensor"),
            P("dp", "tensor"),
            P("tensor"),
            P("tensor", "dp"),
            P(),
            P("dp", "tensor"),
            P("tensor"),
            P("tensor", "dp"),
            P(),
        ),
        check_vma=False,
    )
```

```python
import functools
import math

import jax
import jax.numpy as jnp
import numpy as np
from jax import lax
from jax.experimental import pallas as pl
from jax.experimental.pallas import tpu as pltpu
from jax.sharding import PartitionSpec as P

HEAD_DIM = 64
ROT_DIM = 32
MESH = pl.DeviceIdType.MESH
BF = jnp.bfloat16
F32 = jnp.float32

epsilon = 1e-05
rope_base = 10000.0
masked_score = -1e30
root = math.sqrt(2.0 / math.pi)


def nn(a, b):
    return jnp.dot(a, b, preferred_element_type=F32)


def nt(a, b):
    return lax.dot_general(a, b, (((1,), (1,)), ((), ())), preferred_element_type=F32)


def tn(a, b):
    return lax.dot_general(a, b, (((0,), (0,)), ((), ())), preferred_element_type=F32)


def rows_at(index, size):
    return pl.ds(pl.multiple_of(index * size, size), size)


def flip(index, bit):
    return index + bit - 2 * bit * lax.rem(index // bit, 2)


def chip_tiles(me):
    return [k // 2 for k in (me, flip(me, 2), flip(me, 4), flip(flip(me, 2), 4))]


class Copies:
    def __init__(self, send, recv):
        self.send, self.recv, self.count, self.sent = send, recv, 0, []

    def new(self):
        self.count += 1
        return self.count - 1

    def make(self, k, src, dst, device):
        return pltpu.make_async_remote_copy(
            src, dst, self.send.at[k], self.recv.at[k], device_id=device, device_id_type=MESH
        )

    def start(self, k, src, dst, device):
        copy = self.make(k, src, dst, device)
        copy.start()
        self.sent.append(copy)

    def wait(self, k, dst, device):
        self.make(k, dst, dst, device).wait_recv()

    def finish(self):
        for copy in self.sent:
            copy.wait_send()


class Spread:
    def __init__(self, copies, view, me, z):
        self.c, self.view, self.me, self.z = copies, view, me, z
        self.k = [copies.new() for _ in range(9)]

    def dev(self, bit):
        return (flip(self.me, bit), self.z)

    def own(self):
        v = self.view(self.me)
        self.c.start(self.k[1], v, v, self.dev(2))
        self.c.start(self.k[2], v, v, self.dev(4))
        self.c.start(self.k[0], v, v, self.dev(1))

    def forward(self):
        c, x, y = self.c, flip(self.me, 2), flip(self.me, 4)
        c.wait(self.k[1], self.view(x), self.dev(2))
        v = self.view(x, 0)
        c.start(self.k[3], v, v, self.dev(4))
        c.wait(self.k[2], self.view(y), self.dev(4))
        v = self.view(y, 1)
        c.start(self.k[4], v, v, self.dev(2))
        v = self.view(x)
        c.start(self.k[5], v, v, self.dev(1))
        v = self.view(y)
        c.start(self.k[6], v, v, self.dev(1))

    def last(self):
        c, far = self.c, flip(flip(self.me, 2), 4)
        c.wait(self.k[3], self.view(far, 0), self.dev(4))
        c.wait(self.k[4], self.view(far, 1), self.dev(2))
        v = self.view(far)
        c.start(self.k[7], v, v, self.dev(1))

    def ready_part(self, part):
        c, s = self.c, flip(self.me, 1)
        shards = ([(0, s)], [(5, flip(s, 2)), (6, flip(s, 4))], [(7, flip(flip(s, 2), 4))])
        for k, origin in shards[part]:
            c.wait(self.k[k], self.view(origin), self.dev(1))

    def ready(self):
        for part in range(3):
            self.ready_part(part)


class Line:
    CHUNKS = 4

    def __init__(self, copies, buf, size, n, me, z):
        self.c, self.buf, self.size, self.n, self.me, self.z = copies, buf, size // self.CHUNKS, n, me, z
        self.k = [[[copies.new() for _ in range(self.CHUNKS)] for _ in range(2)] for _ in range(n - 1)]

    def copy(self, s, way, c, block):
        z, n = self.z, self.n
        to = jnp.minimum(z + 1, n - 1) if way == 0 else jnp.maximum(z - 1, 0)
        v = self.buf.at[rows_at(jnp.clip(block, 0, n - 1) * self.CHUNKS + c, self.size), :]
        return self.c.make(self.k[s][way][c], v, v, (self.me, to))

    def far(self, way):
        return self.z if way == 0 else self.n - 1 - self.z

    def block(self, way, s):
        return self.z - s if way == 0 else self.z + s

    def own(self, c):
        for way in range(2):

            @pl.when(self.far(way) < self.n - 1)
            def _():
                self.copy(0, way, c, self.z).start()

    def event(self, s, c):
        for way in range(2):
            far = self.far(way)

            @pl.when(far >= s + 1)
            def _():
                self.copy(s, way, c, self.block(way, s + 1)).wait_recv()

            if s + 1 < self.n - 1:

                @pl.when((far >= s + 1) & (far < self.n - 1))
                def _():
                    self.copy(s + 1, way, c, self.block(way, s + 1)).start()

    def finish(self):
        for s in range(self.n - 1):
            for way in range(2):
                far = self.far(way)

                @pl.when((far >= s) & (far < self.n - 1))
                def _():
                    for c in range(self.CHUNKS):
                        self.copy(s, way, c, self.z).wait_send()


class Fold:
    def __init__(self, part, slots, send, recv, tiles, size, n, me, z, begun=None, handed=None, place=None):
        self.part, self.slots, self.send, self.recv = part, slots, send, recv
        self.begun, self.handed = begun, handed
        self.place = place or list(range(part.shape[1] // PIECE))
        self.tiles, self.size, self.n, self.me, self.z = list(tiles), size, n, me, z

    def far(self, way):
        return self.z if way == 0 else self.n - 1 - self.z

    def copy(self, way, t, i):
        z, n = self.z, self.n
        to = jnp.minimum(z + 1, n - 1) if way == 0 else jnp.maximum(z - 1, 0)
        goal = n - 1 - i if way == 0 else i
        k = self.tiles.index(t) * (n - 1) + i
        return pltpu.make_async_remote_copy(
            self.part.at[goal * self.size : (goal + 1) * self.size, rows_at(self.place[t], PIECE)],
            self.slots.at[way, k],
            self.send.at[way, k],
            self.recv.at[way, k],
            device_id=(self.me, to),
            device_id_type=MESH,
        )

    def first(self, t):
        for way in range(2):

            @pl.when(self.far(way) == 0)
            def _():
                for i in range(self.n - 1):
                    self.copy(way, t, i).start()

    def resume(self):
        for way in range(2):

            @pl.when(self.far(way) == 1)
            def _():
                for i in range(self.n - 2):
                    self.copy(way, self.begun, i).start()

    def event(self, t, far):
        n = self.n
        for way in range(2):

            @pl.when(self.far(way) == far)
            def _():
                for i in range(n - far):
                    goal = n - 1 - i if way == 0 else i
                    k = self.tiles.index(t) * (n - 1) + i
                    self.copy(way, t, i).wait_recv()
                    at = (slice(goal * self.size, (goal + 1) * self.size), rows_at(self.place[t], PIECE))
                    self.part[at] = (self.part[at].astype(F32) + self.slots[way, k].astype(F32)).astype(BF)
                    if i < n - 1 - far and t != self.handed:
                        self.copy(way, t, i).start()

    def finish(self):
        n = self.n
        for way in range(2):
            for far in range(n - 1):

                @pl.when(self.far(way) == far)
                def _():
                    for t in self.tiles:
                        if not (t == self.begun and far == 0 or t == self.handed and far > 0):
                            for i in range(n - 1 - far):
                                self.copy(way, t, i).wait_send()


PIECE = 512
EARLY = 2
(OWN, HAND, FAR, READY, READY_0, READY_1, READY_2, NORM, SEND, ATTEND, HEADS_BACK) = range(11)
(HIDDEN_BACK, LOWER, FOLD_FIRST, LINE_N, LINE_C, RAISE, FOLD, SEND_C, PROJECT, KEYS_BACK) = range(11, 21)
UP, QKV, DOWN = range(3)
ORDER = (
    (OWN, UP, 0), (OWN, UP, 1), (NORM, 0, 0), (SEND, 0, 0), (NORM, 1, 0), (SEND, 1, 0), (NORM, 2, 0),
    (SEND, 2, 0), (NORM, 3, 0), (SEND, 3, 0), (LINE_N, 0, 0), (HAND, UP, 0), (OWN, QKV, 0), (LINE_N, 0, 1),
    (LINE_N, 0, 2), (HAND, UP, 1), (OWN, QKV, 1), (LINE_N, 0, 3), (FAR, UP, 0), (LINE_N, 1, 0), (READY, UP, 0),
    (RAISE, 0, 0), (RAISE, 1, 0), (LINE_N, 1, 1), (HAND, QKV, 0), (LINE_N, 1, 2), (FAR, UP, 1), (READY, UP, 1),
    (RAISE, 0, 1), (LINE_N, 1, 3), (SEND_C, 0, 0), (RAISE, 1, 1), (RAISE, 2, 0), (HAND, QKV, 1), (OWN, DOWN, 0),
    (OWN, DOWN, 1), (LINE_N, 2, 0), (RAISE, 2, 1), (READY_0, DOWN, 0), (READY_0, DOWN, 1), (FAR, QKV, 0),
    (READY, QKV, 0), (LINE_N, 2, 1), (FAR, QKV, 1), (READY, QKV, 1), (LINE_N, 2, 2), (HAND, DOWN, 0),
    (OWN, DOWN, 2), (READY_1, DOWN, 0), (READY_0, DOWN, 2), (LINE_N, 2, 3), (PROJECT, 0, 0), (LINE_C, 0, 0),
    (ATTEND, 0, 0), (LINE_C, 0, 1), (FAR, DOWN, 0), (HAND, DOWN, 1), (ATTEND, 1, 0), (LINE_C, 0, 2),
    (READY_2, DOWN, 0), (READY_1, DOWN, 1), (RAISE, 3, 0), (LINE_C, 0, 3), (HAND, DOWN, 2), (RAISE, 3, 1),
    (LOWER, 0, 0), (LINE_C, 1, 0), (FAR, DOWN, 1), (READY_1, DOWN, 2), (FOLD_FIRST, 0, 0), (LOWER, 1, 0),
    (READY_2, DOWN, 1), (FOLD_FIRST, 1, 0), (LOWER, 2, 0), (LINE_C, 1, 1), (FAR, DOWN, 2), (FOLD_FIRST, 2, 0),
    (HEADS_BACK, 0, 0), (LINE_C, 1, 2), (READY_2, DOWN, 2), (LOWER, 3, 0), (LINE_C, 1, 3), (HEADS_BACK, 1, 0),
    (LINE_C, 2, 0), (FOLD, 0, 1), (HEADS_BACK, 2, 0), (LINE_C, 2, 1), (HIDDEN_BACK, 0, 0), (HIDDEN_BACK, 1, 0),
    (LINE_C, 2, 2), (FOLD, 0, 2), (FOLD, 1, 1), (HIDDEN_BACK, 2, 0), (LINE_C, 2, 3), (HEADS_BACK, 3, 0),
    (FOLD, 0, 3), (HIDDEN_BACK, 3, 0), (FOLD, 1, 2), (FOLD, 2, 1), (KEYS_BACK, 0, 0), (FOLD, 1, 3),
)


def turned(x, table, sign):
    return (
        x * table[0]
        + pltpu.roll(x, 112, 1) * (table[1] * sign)
        + pltpu.roll(x, 16, 1) * (table[2] * sign)
    )


def gather_forward(
    n,
    prefix,
    x,
    cot,
    wq,
    wk,
    wv,
    wo,
    wu,
    wd,
    gain,
    bias,
    bq,
    bk,
    bv,
    bu,
    table,
    normed_out,
    cots_out,
    w_qkv_out,
    w_up_out,
    grads_out,
    joined_out,
    branch_out,
    normed,
    cots,
    w_qkv,
    w_up,
    w_dn,
    qkv,
    joined,
    slope,
    d_attn,
    d_key,
    d_value,
    own_x,
    lse,
    lse_row,
    fold_slots,
    send,
    recv,
    local,
    outs,
    fold_send,
    fold_recv,
):
    me, z = lax.axis_index("dp"), lax.axis_index("tensor")
    size, d = x.shape
    length = n * size
    width = wq.shape[1]
    ff = wu.shape[1]
    shard = wq.shape[0]
    lanes = wo.shape[1]
    branch = normed

    barrier = pltpu.get_barrier_semaphore()
    for bit in (1, 2, 4):
        pl.semaphore_signal(barrier, 1, device_id=(flip(me, bit), z), device_id_type=MESH)

    @pl.when(z > 0)
    def _():
        pl.semaphore_signal(barrier, 1, device_id=(me, jnp.maximum(z - 1, 0)), device_id_type=MESH)

    @pl.when(z < n - 1)
    def _():
        pl.semaphore_signal(barrier, 1, device_id=(me, jnp.minimum(z + 1, n - 1)), device_id_type=MESH)

    mine, cols = rows_at(me, shard), rows_at(me, lanes)
    loads = [
        pltpu.make_async_copy(x, own_x, local.at[0]),
        pltpu.make_async_copy(wu, w_up.at[mine, :], local.at[1]),
        pltpu.make_async_copy(wq, w_qkv.at[mine, pl.ds(0, width)], local.at[2]),
        pltpu.make_async_copy(wk, w_qkv.at[mine, pl.ds(width, width)], local.at[3]),
        pltpu.make_async_copy(wv, w_qkv.at[mine, pl.ds(2 * width, width)], local.at[4]),
        pltpu.make_async_copy(wo, w_dn.at[pl.ds(0, width), cols], local.at[5]),
        pltpu.make_async_copy(wd, w_dn.at[pl.ds(width, ff), cols], local.at[6]),
        pltpu.make_async_copy(cot, cots.at[rows_at(z, size), :], local.at[7]),
    ]
    for load in loads:
        load.start()

    stores = []

    def store(src, dst):
        copy = pltpu.make_async_copy(src, dst, outs.at[len(stores)])
        stores.append(copy)
        copy.start()
        return copy

    copies = Copies(send, recv)

    def row_view(buf, first, count):
        def view(i, half=None):
            h = count if half is None else count // 2
            start = i * shard + first + (0 if half is None else half * h)
            return buf.at[pl.ds(pl.multiple_of(start, h), h), :]

        return view

    def col_view(first, count):
        def view(i, half=None):
            if half is None:
                return w_dn.at[pl.ds(first, count), rows_at(i, lanes)]
            h = count // 2
            return w_dn.at[pl.ds(first + half * h, h), rows_at(i, lanes)]

        return view

    def row_col_view(first, count):
        def view(i, half=None):
            h = shard if half is None else shard // 2
            start = i * shard + (0 if half is None else half * h)
            return w_up.at[pl.ds(pl.multiple_of(start, h), h), pl.ds(first, count)]

        return view

    s_up = [Spread(copies, row_col_view(i * ff // 2, ff // 2), me, z) for i in range(2)]
    s_qkv = [Spread(copies, row_view(w_qkv, i * shard // 2, shard // 2), me, z) for i in range(2)]
    s_dn = [Spread(copies, col_view(*v), me, z) for v in ((0, width), (width, ff // 2), (width + ff // 2, ff // 2))]
    l_n = Line(copies, normed, size, n, me, z)
    l_c = Line(copies, cots, size, n, me, z)
    place = chip_tiles(me)
    fold = Fold(branch, fold_slots, fold_send, fold_recv, range(EARLY + 1), size, n, me, z, handed=EARLY, place=place)
    order = [z, flip(z, 1), flip(z, 2), flip(flip(z, 1), 2)]
    head = lax.broadcasted_iota(jnp.int32, (1, 128), 1) // HEAD_DIM

    def norm(r):
        rows = slice(r * 64, (r + 1) * 64)
        v = own_x[rows, :].astype(F32)
        mean = jnp.mean(v, axis=-1, keepdims=True)
        c = v - mean
        inv = lax.rsqrt(jnp.mean(c * c, axis=-1, keepdims=True) + epsilon)
        out = (c * inv) * gain[...] + bias[...]
        normed[pl.ds(pl.multiple_of(z * size + r * 64, 64), 64), :] = out.astype(BF)

    def project():
        tile = 512

        @pl.loop(0, length // tile)
        def _(m):
            rows = rows_at(m, tile)
            tab = [table[i, rows, :] for i in range(3)]
            for part in range(3):
                acc = nn(normed[rows, :], w_qkv[:, part * width : (part + 1) * width])
                acc = acc + (bq, bk, bv)[part][...]
                for p in range(width // 128):
                    piece = acc[:, p * 128 : (p + 1) * 128]
                    if part < 2:
                        piece = turned(piece, tab, 1.0)
                        if part == 0:
                            piece = piece * (1.0 / math.sqrt(HEAD_DIM))
                    qkv[rows, part * width + p * 128 : part * width + (p + 1) * 128] = piece.astype(BF)

    def raise_(j, part):
        rows = rows_at(j, size)
        tile = 512

        @pl.loop(part * ff // tile // 2, (part + 1) * ff // tile // 2)
        def _(t):
            cs = rows_at(t, tile)
            u = nn(normed[rows, :], w_up[:, cs]) + bu[:, cs]
            sq = u * u
            th = jnp.tanh(root * u * (1.0 + 0.044715 * sq))
            half = 0.5 * (1.0 + th)
            joined[rows, pl.ds(pl.multiple_of(width + t * tile, tile), tile)] = (u * half).astype(BF)
            slope[rows, cs] = (
                half + 0.5 * u * (1.0 - th * th) * (root * (1.0 + 3 * 0.044715 * sq))
            ).astype(BF)

    block = length // 4

    def visible(b):
        return (b if b > 0 else 0), max(b + 1, 2)

    def attend(first, count):
        @pl.loop(first, first + count)
        def _(p):
            ps = rows_at(p, 128)
            ks = pl.ds(pl.multiple_of(width + p * 128, 128), 128)
            vs = pl.ds(pl.multiple_of(2 * width + p * 128, 128), 128)
            lane = lax.broadcasted_iota(jnp.int32, (1, 128), 1)
            for b in range(4):
                full, some = visible(b)
                qs, kr = pl.ds(b * block, block), pl.ds(0, some * block)
                limit = jnp.maximum(
                    b * block + lax.broadcasted_iota(jnp.int32, (block, 1), 0), prefix[0] - 1
                )
                at = full * block + lax.broadcasted_iota(jnp.int32, (block, (some - full) * block), 1)
                q, outs_ = qkv[qs, ps], []
                scores = [nt(jnp.where(head == h, q, jnp.zeros_like(q)), qkv[kr, ks]) for h in range(2)]
                for h in range(2):
                    last = jnp.where(at <= limit, scores[h][:, full * block :], masked_score)
                    scores[h] = jnp.concatenate([scores[h][:, : full * block], last], 1) if full > 0 else last
                tops = [jnp.max(v, axis=-1, keepdims=True) for v in scores]
                exps = [jnp.exp(v - top) for v, top in zip(scores, tops)]
                totals = [jnp.sum(v, axis=-1, keepdims=True) for v in exps]
                outs_ = [nn((v * (1.0 / total)).astype(BF), qkv[kr, vs]) for v, total in zip(exps, totals)]
                logs = [top + jnp.log(total) for top, total in zip(tops, totals)]
                lse[qs, :] = jnp.where(
                    lane == 2 * p, logs[0], jnp.where(lane == 2 * p + 1, logs[1], lse[qs, :])
                )
                joined[qs, ps] = jnp.where(head == 0, outs_[0], outs_[1]).astype(BF)

    def lower(t):
        @pl.loop(0, length // 512)
        def _(m):
            rows = rows_at(m, 512)
            cs = rows_at(place[t], PIECE)
            branch[rows, cs] = nn(joined[rows, :], w_dn[:, cs]).astype(BF)

    def hidden_back(j):
        rows = rows_at(j, size)
        tile = 512

        @pl.loop(0, ff // tile)
        def _(t):
            g = nt(cots[rows, :], w_dn[pl.ds(pl.multiple_of(width + t * tile, tile), tile), :])
            cs = rows_at(t, tile)
            slope[rows, cs] = (g * slope[rows, cs].astype(F32)).astype(BF)

    def attend_back(b):
        full, some = visible(b)
        qs = pl.ds(b * block, block)
        limit = jnp.maximum(b * block + lax.broadcasted_iota(jnp.int32, (1, block), 1), prefix[0] - 1)

        @pl.loop(0, width // 128)
        def _(p):
            ps = rows_at(p, 128)
            ks = pl.ds(pl.multiple_of(width + p * 128, 128), 128)
            vs = pl.ds(pl.multiple_of(2 * width + p * 128, 128), 128)
            only = lambda a, h: jnp.where(head == h, a, jnp.zeros_like(a))
            q, g = qkv[qs, ps], d_attn[:, ps]
            kr = pl.ds(0, some * block)
            at = full * block + lax.broadcasted_iota(jnp.int32, ((some - full) * block, block), 0)
            qh, gh = [only(q, h) for h in range(2)], [only(g, h) for h in range(2)]
            scores = [nt(qkv[kr, ks], qh[h]) for h in range(2)]
            d_probs = [nt(qkv[kr, vs], gh[h]) for h in range(2)]
            probs, ds = [], []
            for h in range(2):
                e = jnp.exp(scores[h] - lse_row[pl.ds(2 * p + h, 1), qs])
                last = jnp.where(at <= limit, e[full * block :], 0.0)
                probs.append(jnp.concatenate([e[: full * block], last], 0) if full > 0 else last)
            for h in range(2):
                delta = jnp.sum(probs[h] * d_probs[h], axis=0, keepdims=True)
                ds.append((probs[h] * (d_probs[h] - delta)).astype(BF))
            d_value[kr, ps] += nn(probs[0].astype(BF), gh[0]) + nn(probs[1].astype(BF), gh[1])
            d_key[kr, ps] += nn(ds[0], qh[0]) + nn(ds[1], qh[1])
            dq = tn(ds[0], only(qkv[kr, ks], 0)) + tn(ds[1], only(qkv[kr, ks], 1))
            tab = [table[i, qs, :] for i in range(3)]
            qkv[qs, ps] = turned(dq * (1.0 / math.sqrt(HEAD_DIM)), tab, -1.0).astype(BF)

    def back(k):
        d_attn[...] = nt(cots[rows_at(order[k], size), :], w_dn[:width, :]).astype(BF)
        for b in range(4):

            @pl.when(order[k] == b)
            def _():
                attend_back(b)

    def keys_back():
        @pl.loop(0, width // 128)
        def _(p):
            ps = rows_at(p, 128)
            ks = pl.ds(pl.multiple_of(width + p * 128, 128), 128)
            vs = pl.ds(pl.multiple_of(2 * width + p * 128, 128), 128)
            tab = [table[i] for i in range(3)]
            qkv[:, ks] = turned(d_key[:, ps], tab, -1.0).astype(BF)
            qkv[:, vs] = d_value[:, ps].astype(BF)

    signals = 3 + jnp.where(z > 0, 1, 0) + jnp.where(z < n - 1, 1, 0)
    pl.semaphore_wait(barrier, signals)

    n_stored = []
    part = functools.partial

    def clear():
        lse[...] = jnp.zeros_like(lse)
        d_key[...] = jnp.zeros_like(d_key)
        d_value[...] = jnp.zeros_like(d_value)

    def wait_loads(*which):
        for i in which:
            loads[i].wait()

    def heads_end():
        lse_row[...] = lse[...].T[: lse_row.shape[0], :]

    def branch_free():
        l_n.finish()
        n_stored[0].wait()

    todo = {
        (OWN, UP, 0): [part(wait_loads, 1), s_up[0].own],
        (OWN, QKV, 0): [part(wait_loads, 2, 3, 4), s_qkv[0].own],
        (OWN, DOWN, 0): [part(wait_loads, 5), s_dn[0].own],
        (OWN, DOWN, 1): [part(wait_loads, 6), s_dn[1].own],
        (NORM, 0, 0): [part(wait_loads, 0), part(norm, 0)],
        (SEND, 3, 0): [part(l_n.own, 3), clear],
        (READY, UP, 1): [s_up[1].ready, part(store, w_up, w_up_out)],
        (READY, QKV, 1): [s_qkv[1].ready, part(store, w_qkv, w_qkv_out)],
        (LINE_N, 2, 3): [part(l_n.event, 2, 3), lambda: n_stored.append(store(normed, normed_out))],
        (SEND_C, 0, 0): [part(wait_loads, 7)] + [part(l_c.own, c) for c in range(Line.CHUNKS)],
        (LINE_C, 2, 3): [part(l_c.event, 2, 3), part(store, cots, cots_out)],
        (PROJECT, 0, 0): [project],
        (ATTEND, 0, 0): [part(attend, 0, 2)],
        (ATTEND, 1, 0): [part(attend, 2, 2), heads_end],
        (RAISE, 3, 1): [part(raise_, order[3], 1), part(store, joined, joined_out)],
        (LOWER, 0, 0): [branch_free, part(lower, 0)],
        (HIDDEN_BACK, 3, 0): [part(hidden_back, order[3]), part(store, slope, grads_out.at[:, pl.ds(3 * width, ff)])],
        (KEYS_BACK, 0, 0): [keys_back, part(store, qkv, grads_out.at[:, pl.ds(0, 3 * width)])],
    }
    for kind, spreads in ((UP, s_up), (QKV, s_qkv), (DOWN, s_dn)):
        for i, s in enumerate(spreads):
            calls = [(OWN, s.own), (HAND, s.forward), (FAR, s.last), (READY, s.ready)]
            calls += [(READY_0 + k, part(s.ready_part, k)) for k in range(3)]
            for what, call in calls:
                todo.setdefault((what, kind, i), [call])
    for c in range(Line.CHUNKS):
        todo.setdefault((NORM, c, 0), [part(norm, c)])
        todo.setdefault((SEND, c, 0), [part(l_n.own, c)])
        for s in range(n - 1):
            todo.setdefault((LINE_N, s, c), [part(l_n.event, s, c)])
            todo.setdefault((LINE_C, s, c), [part(l_c.event, s, c)])
    for k in range(4):
        for i in range(2):
            todo.setdefault((RAISE, k, i), [part(raise_, order[k], i)])
        todo.setdefault((HIDDEN_BACK, k, 0), [part(hidden_back, order[k])])
        todo.setdefault((HEADS_BACK, k, 0), [part(back, k)])
        todo.setdefault((LOWER, k, 0), [part(lower, k)])
        todo.setdefault((FOLD_FIRST, k, 0), [part(fold.first, k)])
        for far in range(1, n):
            todo.setdefault((FOLD, k, far), [part(fold.event, k, far)])
    for name in ORDER:
        for call in todo[name]:
            call()
    store(branch, branch_out)
    for copy in stores:
        if copy is not n_stored[0]:
            copy.wait()
    fold.finish()
    l_c.finish()
    copies.finish()


def tables(length):
    half = ROT_DIM // 2
    freqs = rope_base ** (-(np.arange(half).astype(np.float32) * 2.0 / ROT_DIM))
    angles = np.arange(length).astype(np.float32)[:, None] * freqs[None, :].astype(np.float32)
    cos, sin = np.cos(angles), np.sin(angles)
    rest = np.zeros((length, HEAD_DIM - ROT_DIM), np.float32)
    none = np.zeros((length, half), np.float32)
    c = np.concatenate([cos, cos, rest + 1.0], 1)
    s1 = np.concatenate([-sin, none, rest], 1)
    s2 = np.concatenate([none, sin, rest], 1)
    return jnp.asarray(np.stack([np.concatenate([t, t], 1) for t in (c, s1, s2)]).astype(np.float32))


def forward_call(n, prefix, x, cot, wq, wk, wv, wo, wu, wd, gain, bias, bq, bk, bv, bu):
    size, d = x.shape
    length, width, ff = n * size, wq.shape[1], wu.shape[1]
    vm, hbm = pl.BlockSpec(memory_space=pltpu.VMEM), pl.BlockSpec(memory_space=pl.ANY)
    shape = lambda s, t=BF: jax.ShapeDtypeStruct(s, t)
    dma = pltpu.SemaphoreType.DMA
    count = 7 * 9 + 2 * (n - 1) * 2 * Line.CHUNKS
    return pl.pallas_call(
        functools.partial(gather_forward, n),
        out_shape=(
            shape((length, d)),
            shape((length, d)),
            shape((d, 3 * width)),
            shape((d, ff)),
            shape((length, 3 * width + ff)),
            shape((length, width + ff)),
            shape((length, d)),
        ),
        in_specs=[pl.BlockSpec(memory_space=pltpu.SMEM)] + [hbm] * 8 + [vm] * 7,
        out_specs=(hbm,) * 7,
        scratch_shapes=[
            pltpu.VMEM((length, d), BF),
            pltpu.VMEM((length, d), BF),
            pltpu.VMEM((d, 3 * width), BF),
            pltpu.VMEM((d, ff), BF),
            pltpu.VMEM((width + ff, d), BF),
            pltpu.VMEM((length, 3 * width), BF),
            pltpu.VMEM((length, width + ff), BF),
            pltpu.VMEM((length, ff), BF),
            pltpu.VMEM((size, width), BF),
            pltpu.VMEM((length, width), F32),
            pltpu.VMEM((length, width), F32),
            pltpu.VMEM((size, d), BF),
            pltpu.VMEM((length, 128), F32),
            pltpu.VMEM((width // HEAD_DIM, length), F32),
            pltpu.VMEM((2, (EARLY + 1) * (n - 1), size, PIECE), BF),
            dma((count,)),
            dma((count,)),
            dma((8,)),
            dma((8,)),
            dma((2, (EARLY + 1) * (n - 1))),
            dma((2, (EARLY + 1) * (n - 1))),
        ],
        compiler_params=pltpu.CompilerParams(
            collective_id=1, has_side_effects=True, vmem_limit_bytes=63 << 20
        ),
        cost_estimate=pl.CostEstimate(flops=50_000_000_000, bytes_accessed=100_000_000, transcendentals=0),
    )(
        prefix,
        x,
        cot,
        wq,
        wk,
        wv,
        wo,
        wu,
        wd,
        gain[None],
        bias[None],
        bq[None],
        bk[None],
        bv[None],
        bu[None],
        tables(length),
    )


SIB_SLOTS = 2
SLOTS = 4


def backward_scatter(
    n,
    x,
    normed,
    cots,
    w_qkv,
    w_up,
    grads_in,
    joined,
    branch,
    gain,
    b_out,
    b_down,
    layer_out,
    d_input,
    d_in,
    d_dn,
    d_bias,
    d_all,
    own_x,
    cot,
    grads,
    n_block,
    n_turned,
    j_block,
    j_turned,
    wq_block,
    wu_block,
    part_b,
    part_g,
    slots_b,
    slots_g,
    sib_out,
    sib_in,
    own_low,
    own_sum,
    x_in,
    y_in,
    end_in,
    d_rows,
    narrow,
    wide,
    wide_z,
    sums,
    b_send,
    b_recv,
    g_send,
    g_recv,
    sib_send,
    sib_recv,
    link_send,
    link_recv,
    out_sem,
    local,
    stream,
    small_send,
    small_recv,
):
    me, z = lax.axis_index("dp"), lax.axis_index("tensor")
    size, d = x.shape
    length = n * size
    ff = w_up.shape[1]
    width = joined.shape[1] - ff
    lanes = d // 8
    down_pieces = (width + ff) // PIECE
    up_pieces = (3 * width + ff) // PIECE
    pieces = down_pieces + up_pieces
    half, quarter = PIECE // 2, PIECE // 4
    sib = (flip(me, 1), z)
    x_to, y_to = (flip(me, 2), z), (flip(me, 4), z)

    barrier = pltpu.get_barrier_semaphore()
    peers = []
    for k in range(1, 8):
        to = me
        for bit in (1, 2, 4):
            if k & bit:
                to = flip(to, bit)
        peers.append(to)
        pl.semaphore_signal(barrier, 1, device_id=(to, z), device_id_type=MESH)
    others = [lax.rem(z + k, n) for k in range(1, n)]
    for to in others:
        pl.semaphore_signal(barrier, 1, device_id=(me, to), device_id_type=MESH)

    def load(k, src, dst):
        return pltpu.make_async_copy(src, dst, local.at[k])

    loads = [
        load(0, branch, part_b),
        load(1, cots, cot),
        load(2, grads_in, grads),
        load(3, x, own_x),
    ]

    def j_load(p):
        return pltpu.make_async_copy(
            joined.at[:, rows_at(jnp.minimum(p, down_pieces - 1), PIECE)],
            j_block.at[lax.rem(p, 2)],
            stream.at[lax.rem(p, 2)],
        )

    def w_loads(t):
        return [
            pltpu.make_async_copy(w_qkv.at[rows_at(t, PIECE), :], wq_block.at[t % 2], stream.at[2 + t % 2]),
            pltpu.make_async_copy(w_up.at[rows_at(t, PIECE), :], wu_block.at[t % 2], stream.at[4 + t % 2]),
        ]

    def n_load(j):
        return pltpu.make_async_copy(normed.at[rows_at(j, size), :], n_block, stream.at[6])

    j_load(0).start()
    for l in [loads[1], loads[0]] + [n_load(0)] + w_loads(0) + [loads[2], loads[3]] + w_loads(1):
        l.start()

    fold_b = Fold(part_b, slots_b, b_send, b_recv, range(EARLY, d // PIECE), size, n, me, z, begun=EARLY, place=chip_tiles(me))
    fold_g = Fold(part_g, slots_g, g_send, g_recv, range(d // PIECE), size, n, me, z)

    goals = [flip(me, 2), flip(flip(me, 2), 4), flip(me, 4), me]

    def sib_copy(p):
        return pltpu.make_async_remote_copy(
            sib_out.at[lax.rem(p, 2)],
            sib_in.at[lax.rem(p, SIB_SLOTS)],
            sib_send.at[lax.rem(p, 2)],
            sib_recv.at[lax.rem(p, SIB_SLOTS)],
            device_id=sib,
            device_id_type=MESH,
        )

    def link_copy(k, p, src, dst, to):
        slot = lax.rem(p, SLOTS)
        return pltpu.make_async_remote_copy(
            src, dst, link_send.at[k, slot], link_recv.at[k, slot], device_id=to, device_id_type=MESH
        )

    def x_first(p):
        slot = lax.rem(p, SLOTS)
        return link_copy(0, p, own_low.at[slot, pl.ds(0, 2), pl.ds(0, quarter)], x_in.at[slot], x_to)

    def y_first(p):
        slot = lax.rem(p, SLOTS)
        return link_copy(1, p, own_low.at[slot, pl.ds(1, 2), pl.ds(quarter, quarter)], y_in.at[slot], y_to)

    def y_last(p):
        slot = lax.rem(p, SLOTS)
        return link_copy(2, p, own_low.at[slot, 2, pl.ds(0, quarter)], end_in.at[slot, 0], y_to)

    def x_last(p):
        slot = lax.rem(p, SLOTS)
        return link_copy(3, p, own_low.at[slot, 0, pl.ds(quarter, quarter)], end_in.at[slot, 1], x_to)

    def up_column(p):
        t = jnp.clip(p - down_pieces, 0, up_pieces - 1)
        return lax.rem(t + 3 * width // PIECE, up_pieces) * PIECE

    def out_copies(p):
        src = own_sum.at[lax.rem(p, SLOTS)]
        sem = out_sem.at[lax.rem(p, SLOTS)]
        row = jnp.minimum(p, down_pieces - 1) * PIECE
        down = [
            pltpu.make_async_copy(
                src.at[:, pl.ds(i * half, half)],
                d_dn.at[pl.ds(pl.multiple_of(row + i * half, half), half), :],
                sem.at[i],
            )
            for i in range(2)
        ]
        up = [
            pltpu.make_async_copy(
                src.at[:, pl.ds(i * half, half)],
                d_in.at[:, pl.ds(pl.multiple_of(up_column(p) + i * half, half), half)],
                sem.at[i],
            )
            for i in range(2)
        ]
        return down, up

    def first_down(p):
        slot, out = lax.rem(p, SLOTS), lax.rem(p, 2)
        j_load(p).wait()

        @pl.when(p + 1 < down_pieces)
        def _():
            j_load(p + 1).start()

        j_turned[...] = j_block[lax.rem(p, 2)].T
        for mine in range(2):
            for r, goal in enumerate(goals):
                to = flip(goal, 1) if mine == 0 else goal
                t = nn(j_turned[...], cot[:, rows_at(to, lanes)])
                for i in range(2):
                    v = t[i * half : (i + 1) * half, :]
                    cs = pl.ds(i * half, half)
                    if mine == 0:
                        sib_out[out, r, :, cs] = v.astype(BF)
                    elif r < 3:
                        own_low[slot, r, :, cs] = v.astype(BF)
                    else:
                        own_sum[slot, :, cs] = v
            if mine == 0:
                sib_copy(p).start()

    def first_up(p):
        slot, out = lax.rem(p, SLOTS), lax.rem(p, 2)
        g = grads[:, pl.ds(pl.multiple_of(up_column(p), PIECE), PIECE)]
        for mine in range(2):
            for r, goal in enumerate(goals):
                to = flip(goal, 1) if mine == 0 else goal
                t = nn(n_turned[rows_at(to, lanes), :], g)
                if mine == 0:
                    sib_out[out, r] = t.astype(BF)
                elif r < 3:
                    own_low[slot, r] = t.astype(BF)
                else:
                    own_sum[slot] = t
            if mine == 0:
                sib_copy(p).start()

    def stage_one(p):
        @pl.when(p >= 2)
        def _():
            sib_copy(p - 2).wait_send()

        @pl.when(p >= SLOTS)
        def _():
            for c in out_copies(p - SLOTS)[0]:
                c.wait()

        @pl.when(p < down_pieces)
        def _():
            first_down(p)

        @pl.when(p >= down_pieces)
        def _():
            first_up(p)

    def stage_two(p):
        slot, inn = lax.rem(p, SLOTS), lax.rem(p, SIB_SLOTS)
        sib_copy(p).wait_recv()
        a, b = pl.ds(0, quarter), pl.ds(quarter, quarter)

        def add(r, rows):
            own_low[slot, r, rows] = (own_low[slot, r, rows].astype(F32) + sib_in[inn, r, rows].astype(F32)).astype(BF)

        add(0, a)
        add(1, a)
        x_first(p).start()
        add(1, b)
        add(2, b)
        y_first(p).start()
        add(0, b)
        add(2, a)
        own_sum[slot] = own_sum[slot] + sib_in[inn, 3].astype(F32)

    def stage_three(p):
        slot = lax.rem(p, SLOTS)
        a, b = pl.ds(0, quarter), pl.ds(quarter, quarter)
        x_first(p).wait_recv()
        own_low[slot, 2, a] = (own_low[slot, 2, a].astype(F32) + x_in[slot, 1].astype(F32)).astype(BF)
        y_last(p).start()
        y_first(p).wait_recv()
        own_low[slot, 0, b] = (own_low[slot, 0, b].astype(F32) + y_in[slot, 0].astype(F32)).astype(BF)
        x_last(p).start()
        own_sum[slot, a] = own_sum[slot, a] + x_in[slot, 0].astype(F32)
        own_sum[slot, b] = own_sum[slot, b] + y_in[slot, 1].astype(F32)

    def stage_four(p):
        slot = lax.rem(p, SLOTS)
        a, b = pl.ds(0, quarter), pl.ds(quarter, quarter)
        y_last(p).wait_recv()
        own_sum[slot, a] = own_sum[slot, a] + end_in[slot, 0].astype(F32)
        x_last(p).wait_recv()
        own_sum[slot, b] = own_sum[slot, b] + end_in[slot, 1].astype(F32)
        down, up = out_copies(p)

        @pl.when(p < down_pieces)
        def _():
            for c in down:
                c.start()

        @pl.when(p >= down_pieces)
        def _():
            for c in up:
                c.start()

        for c in (x_first(p), y_first(p), x_last(p), y_last(p)):
            c.wait_send()

    def normed_back(t):
        for l in w_loads(t):
            l.wait()

        @pl.loop(0, length // 512)
        def _(m):
            rows = rows_at(m, 512)
            part_g[rows, t * PIECE : (t + 1) * PIECE] = (
                nt(grads[rows, : 3 * width], wq_block[t % 2]) + nt(grads[rows, 3 * width :], wu_block[t % 2])
            ).astype(BF)

        if t + 2 < d // PIECE:
            for l in w_loads(t + 2):
                l.start()
        fold_g.first(t)

    def turn(j):
        n_load(j).wait()
        n_turned[:, j * size : (j + 1) * size] = n_block[...].T
        if j + 1 < n:
            n_load(j + 1).start()

    def small(k, src, dst, to):
        return pltpu.make_async_remote_copy(
            src, dst, small_send.at[k], small_recv.at[k], device_id=to, device_id_type=MESH
        )

    def bias_sums():
        for i in range(up_pieces):
            narrow[me, i : i + 1, :] = jnp.sum(
                grads[:, i * PIECE : (i + 1) * PIECE].astype(F32), axis=0, keepdims=True
            )
        for k, to in enumerate(peers):
            small(k, narrow.at[me], narrow.at[me], (to, z)).start()

    def branch_end():
        loads[3].wait()

        @pl.loop(0, size // 32)
        def _(r):
            rows = pl.ds(pl.multiple_of(z * size + r * 32, 32), 32)
            v = own_x[rows_at(r, 32), :].astype(F32) + part_b[rows, :].astype(F32) + b_out[...] + b_down[...]
            part_b[rows, :] = v.astype(BF)

        load(0, part_b.at[rows_at(z, size), :], layer_out).start()

    def input_end():
        sums[...] = jnp.zeros_like(sums)

        def chunk(r):
            return pltpu.make_async_copy(
                d_rows.at[lax.rem(r, 2)], d_input.at[rows_at(r, 32), :], local.at[1 + lax.rem(r, 2)]
            )

        @pl.loop(0, size // 32)
        def _(r):
            mine = pl.ds(pl.multiple_of(z * size + r * 32, 32), 32)
            grad = part_g[mine, :].astype(F32)
            v = own_x[rows_at(r, 32), :].astype(F32)
            c = v - jnp.mean(v, axis=-1, keepdims=True)
            inv = lax.rsqrt(jnp.mean(c * c, axis=-1, keepdims=True) + epsilon)
            unit = c * inv
            own_cot = cot[mine, :].astype(F32)
            gu = grad * unit
            sums[0:1, :] += jnp.sum(gu, axis=0, keepdims=True)
            sums[1:2, :] += jnp.sum(grad, axis=0, keepdims=True)
            sums[2:3, :] += jnp.sum(own_cot, axis=0, keepdims=True)
            scaled = grad * gain[...]

            @pl.when(r >= 2)
            def _():
                chunk(r - 2).wait()

            d_rows[lax.rem(r, 2)] = own_cot + inv * (
                scaled
                - jnp.mean(scaled, axis=-1, keepdims=True)
                - unit * jnp.mean(scaled * unit, axis=-1, keepdims=True)
            )
            chunk(r).start()

        for i in range(3):
            for q in range(4):
                wide[me, 4 * i + q : 4 * i + q + 1, :] = sums[i : i + 1, q * PIECE : (q + 1) * PIECE]
        for k, to in enumerate(peers):
            small(8 + k, wide.at[me], wide.at[me], (to, z)).start()
        for r in range(2):
            chunk(size // 32 - 2 + r).wait()

    def small_end():
        for k, to in enumerate(peers):
            small(8 + k, wide.at[to], wide.at[to], (to, z)).wait_recv()
        total = wide[0]
        for i in range(1, 8):
            total = total + wide[i]
        wide_z[z] = total
        for k, to in enumerate(others):
            small(16 + k, wide_z.at[z], wide_z.at[z], (me, to)).start()

    def last_end():
        for k in range(n - 1):
            origin = lax.rem(z + n - 1 - k, n)
            small(16 + k, wide_z.at[origin], wide_z.at[origin], (me, origin)).wait_recv()
        total = wide_z[0]
        for i in range(1, n):
            total = total + wide_z[i]
        d_all[...] = total
        for k, to in enumerate(peers):
            small(k, narrow.at[to], narrow.at[to], (to, z)).wait_recv()
        total = narrow[0]
        for i in range(1, 8):
            total = total + narrow[i]
        d_bias[...] = total
        for k, to in enumerate(peers):
            small(k, narrow.at[me], narrow.at[me], (to, z)).wait_send()
            small(8 + k, wide.at[me], wide.at[me], (to, z)).wait_send()
        for k, to in enumerate(others):
            small(16 + k, wide_z.at[z], wide_z.at[z], (me, to)).wait_send()
        load(0, part_b.at[rows_at(z, size), :], layer_out).wait()

    narrow[me] = jnp.zeros(narrow.shape[1:], F32)
    wide[me] = jnp.zeros(wide.shape[1:], F32)
    pl.semaphore_wait(barrier, 7 + n - 1)

    tasks = {}

    def at(p, *work):
        tasks.setdefault(p, []).extend(work)

    loads[0].wait()
    fold_b.resume()
    for t in fold_b.tiles[1:]:
        fold_b.first(t)
    loads[1].wait()

    part = functools.partial
    at(0, loads[2].wait, part(normed_back, 0))
    at(1, part(turn, 0), part(turn, 1))
    at(2, part(turn, 2), part(turn, 3))
    at(3, part(normed_back, 1), part(fold_b.event, 2, 2), part(fold_b.event, 3, 1))
    at(4, part(fold_b.event, 2, 3))
    at(5, part(normed_back, 2), part(fold_g.event, 0, 1))
    at(6, part(fold_g.event, 1, 1))
    at(7, part(normed_back, 3))
    at(8, part(fold_b.event, 3, 2), part(fold_g.event, 2, 1))
    at(9, part(fold_g.event, 0, 2), part(fold_g.event, 1, 2))
    at(10, part(fold_b.event, 3, 3), part(fold_g.event, 2, 2), part(fold_g.event, 3, 1))
    at(11, bias_sums, part(fold_g.event, 0, 3), part(fold_g.event, 1, 3), part(fold_g.event, 3, 2), branch_end)
    at(12, part(fold_g.event, 2, 3), part(fold_g.event, 3, 3), input_end)
    at(13, small_end)
    at(14, last_end)

    @pl.loop(0, max(pieces + 3, max(tasks) + 1))
    def _(p):
        @pl.when((p >= 1) & (p <= pieces))
        def _():
            stage_two(p - 1)

        @pl.when(p < pieces)
        def _():
            stage_one(p)

        @pl.when((p >= 2) & (p <= pieces + 1))
        def _():
            stage_three(p - 2)

        @pl.when((p >= 3) & (p <= pieces + 2))
        def _():
            stage_four(p - 3)

        for k, work in tasks.items():

            @pl.when(p == k)
            def _():
                for w in work:
                    w()

    for p in range(2):
        sib_copy(pieces - 2 + p).wait_send()
    for p in range(SLOTS):
        for c in out_copies(pieces - SLOTS + p)[1]:
            c.wait()
    fold_b.finish()
    fold_g.finish()


def backward_call(n, x, normed, cots, w_qkv, w_up, grads, joined, branch, gain, b_out, b_down):
    size, d = x.shape
    length, ff = n * size, w_up.shape[1]
    width = joined.shape[1] - ff
    vm, hbm = pl.BlockSpec(memory_space=pltpu.VMEM), pl.BlockSpec(memory_space=pl.ANY)
    shape = lambda s, t=BF: jax.ShapeDtypeStruct(s, t)
    dma = pltpu.SemaphoreType.DMA
    half, quarter = PIECE // 2, PIECE // 4
    late, tiles = (d // PIECE - EARLY) * (n - 1), d // PIECE * (n - 1)
    return pl.pallas_call(
        functools.partial(backward_scatter, n),
        out_shape=(
            shape((size, d)),
            shape((size, d), F32),
            shape((d // 8, 3 * width + ff), F32),
            shape((width + ff, d // 8), F32),
            shape((8, PIECE), F32),
            shape((16, PIECE), F32),
        ),
        in_specs=[hbm] * 8 + [vm] * 3,
        out_specs=(hbm,) * 4 + (vm,) * 2,
        scratch_shapes=[
            pltpu.VMEM((size, d), BF),
            pltpu.VMEM((length, d), BF),
            pltpu.VMEM((length, 3 * width + ff), BF),
            pltpu.VMEM((size, d), BF),
            pltpu.VMEM((d, length), BF),
            pltpu.VMEM((2, length, PIECE), BF),
            pltpu.VMEM((PIECE, length), BF),
            pltpu.VMEM((2, PIECE, 3 * width), BF),
            pltpu.VMEM((2, PIECE, ff), BF),
            pltpu.VMEM((length, d), BF),
            pltpu.VMEM((length, d), BF),
            pltpu.VMEM((2, late, size, PIECE), BF),
            pltpu.VMEM((2, tiles, size, PIECE), BF),
            pltpu.VMEM((2, 4, half, PIECE), BF),
            pltpu.VMEM((SIB_SLOTS, 4, half, PIECE), BF),
            pltpu.VMEM((SLOTS, 3, half, PIECE), BF),
            pltpu.VMEM((SLOTS, half, PIECE), F32),
            pltpu.VMEM((SLOTS, 2, quarter, PIECE), BF),
            pltpu.VMEM((SLOTS, 2, quarter, PIECE), BF),
            pltpu.VMEM((SLOTS, 2, quarter, PIECE), BF),
            pltpu.VMEM((2, 32, d), F32),
            pltpu.VMEM((8, 8, PIECE), F32),
            pltpu.VMEM((8, 16, PIECE), F32),
            pltpu.VMEM((n, 16, PIECE), F32),
            pltpu.VMEM((8, d), F32),
            dma((2, late)),
            dma((2, late)),
            dma((2, tiles)),
            dma((2, tiles)),
            dma((2,)),
            dma((SIB_SLOTS,)),
            dma((4, SLOTS)),
            dma((4, SLOTS)),
            dma((SLOTS, 2)),
            dma((4,)),
            dma((7,)),
            dma((16 + n - 1,)),
            dma((16 + n - 1,)),
        ],
        compiler_params=pltpu.CompilerParams(
            collective_id=2, has_side_effects=True, vmem_limit_bytes=63 << 20
        ),
        cost_estimate=pl.CostEstimate(flops=60_000_000_000, bytes_accessed=100_000_000, transcendentals=0),
    )(x, normed, cots, w_qkv, w_up, grads, joined, branch, gain[None], b_out[None], b_down[None])


def rotate(tensor, positions, direction):
    half_dim = ROT_DIM // 2
    freqs = rope_base ** (-(jnp.arange(half_dim).astype(jnp.float32) * 2.0 / ROT_DIM))
    angles = positions.astype(jnp.float32)[:, None] * freqs[None, :]
    cosine = jnp.cos(angles)[:, None, :]
    sine = direction * jnp.sin(angles)[:, None, :]
    first = tensor[..., :half_dim]
    second = tensor[..., half_dim:ROT_DIM]
    return jnp.concatenate(
        [first * cosine - second * sine, second * cosine + first * sine, tensor[..., ROT_DIM:]],
        axis=-1,
    )


def times_transposed(left, right):
    return lax.dot_general(
        left, right, (((1,), (1,)), ((), ())), preferred_element_type=jnp.float32
    )


def rows_transposed(left, right):
    return lax.dot_general(
        left, right, (((0,), (0,)), ((), ())), preferred_element_type=jnp.float32
    )


def plain_on_device(
    layer_input,
    ln_gain,
    ln_bias,
    w_query,
    b_query,
    w_key,
    b_key,
    w_value,
    b_value,
    w_out,
    b_out,
    w_up,
    b_up,
    w_down,
    b_down,
    prefix,
    cotangent,
):
    local_width = w_query.shape[1]
    hidden_here = w_up.shape[1]
    heads_here = local_width // HEAD_DIM
    score_scale = 1.0 / math.sqrt(HEAD_DIM)
    prefix_len = prefix[0]
    input_float = layer_input.astype(jnp.float32)
    row_mean = jnp.mean(input_float, axis=-1, keepdims=True)
    centred = input_float - row_mean
    inverse = lax.rsqrt(jnp.mean(centred * centred, axis=-1, keepdims=True) + epsilon)
    unit_rows = centred * inverse
    normed = (unit_rows * ln_gain + ln_bias).astype(jnp.bfloat16)
    normed_all = lax.all_gather(normed, "tensor", axis=0, tiled=True)
    length = normed_all.shape[0]
    positions = jnp.arange(length)
    block_rows = min(512, length)
    block_count = length // block_rows
    pieces = (
        lax.all_gather(w_query, "dp", axis=0, tiled=True),
        lax.all_gather(w_key, "dp", axis=0, tiled=True),
        lax.all_gather(w_value, "dp", axis=0, tiled=True),
        lax.all_gather(w_up, "dp", axis=0, tiled=True),
    )
    columns = normed_all
    query_acc, key_acc, value_acc, up_acc = tuple(
        (jnp.dot(columns, piece, preferred_element_type=jnp.float32) for piece in pieces)
    )
    query_pre = (query_acc + b_query).reshape(length, heads_here, HEAD_DIM)
    key_pre = (key_acc + b_key).reshape(length, heads_here, HEAD_DIM)
    query = rotate(query_pre, positions, 1.0).astype(jnp.bfloat16)
    key = rotate(key_pre, positions, 1.0).astype(jnp.bfloat16)
    value = (value_acc + b_value).reshape(length, heads_here, HEAD_DIM).astype(jnp.bfloat16)
    up_pre = up_acc + b_up
    hidden = jax.nn.gelu(up_pre, approximate=True).astype(jnp.bfloat16)

    def scores_for(query_rows, offset):
        raw = (
            jnp.einsum("qhd,khd->hqk", query_rows, key, preferred_element_type=jnp.float32)
            * score_scale
        )
        query_pos = offset + jnp.arange(block_rows)
        seen = (positions[None, :] <= query_pos[:, None]) | (positions[None, :] < prefix_len)
        return jnp.where(seen[None], raw, masked_score)

    def attend_block(index):
        offset = index * block_rows
        query_rows = lax.dynamic_slice_in_dim(query, offset, block_rows, 0)
        scores = scores_for(query_rows, offset)
        row_max = jnp.max(scores, axis=-1, keepdims=True)
        expo = jnp.exp(scores - row_max)
        totals = jnp.sum(expo, axis=-1, keepdims=True)
        probs_low = (expo / totals).astype(jnp.bfloat16)
        out_rows = jnp.einsum("hqk,khd->qhd", probs_low, value, preferred_element_type=jnp.float32)
        return (out_rows, (row_max + jnp.log(totals))[..., 0])

    indices = jnp.arange(block_count)
    out_blocks, log_totals = lax.map(attend_block, indices)
    attn = out_blocks.reshape(length, local_width).astype(jnp.bfloat16)
    pieces = (
        lax.all_gather(w_out, "dp", axis=1, tiled=True),
        lax.all_gather(w_down, "dp", axis=1, tiled=True),
    )
    part = jnp.dot(attn, pieces[0], preferred_element_type=jnp.float32) + jnp.dot(
        hidden, pieces[1], preferred_element_type=jnp.float32
    )
    partial_value = part
    branch = lax.psum_scatter(partial_value, "tensor", scatter_dimension=0, tiled=True)
    layer_out = (input_float + branch + b_out + b_down).astype(jnp.bfloat16)
    grad_all = lax.all_gather(cotangent, "tensor", axis=0, tiled=True)
    pieces = (
        lax.all_gather(w_out, "dp", axis=1, tiled=True),
        lax.all_gather(w_down, "dp", axis=1, tiled=True),
    )
    columns = grad_all
    attn_grad = times_transposed(columns, pieces[0])
    hidden_grad = times_transposed(columns, pieces[1])
    down_joined = jnp.concatenate([attn, hidden], axis=1)
    unused, gelu_pull = jax.vjp(lambda inner: jax.nn.gelu(inner, approximate=True), up_pre)
    up_grad_low = gelu_pull(hidden_grad)[0].astype(jnp.bfloat16)
    attn_grad_low = attn_grad.astype(jnp.bfloat16).reshape(length, heads_here, HEAD_DIM)

    def back_block(carry, item):
        key_grad, value_grad = carry
        index, lse_rows = item
        offset = index * block_rows
        query_rows = lax.dynamic_slice_in_dim(query, offset, block_rows, 0)
        grad_rows = lax.dynamic_slice_in_dim(attn_grad_low, offset, block_rows, 0)
        scores = scores_for(query_rows, offset)
        probs = jnp.exp(scores - lse_rows[..., None])
        value_grad = value_grad + jnp.einsum(
            "hqk,qhd->khd",
            probs.astype(jnp.bfloat16),
            grad_rows,
            preferred_element_type=jnp.float32,
        )
        prob_grad = jnp.einsum("qhd,khd->hqk", grad_rows, value, preferred_element_type=jnp.float32)
        delta = jnp.sum(probs * prob_grad, axis=-1, keepdims=True)
        score_grad = (probs * (prob_grad - delta)).astype(jnp.bfloat16)
        query_grad = (
            jnp.einsum("hqk,khd->qhd", score_grad, key, preferred_element_type=jnp.float32)
            * score_scale
        )
        key_grad = (
            key_grad
            + jnp.einsum("hqk,qhd->khd", score_grad, query_rows, preferred_element_type=jnp.float32)
            * score_scale
        )
        return ((key_grad, value_grad), query_grad)

    state_zeros = jnp.zeros((length, heads_here, HEAD_DIM), jnp.float32)
    (key_grad, value_grad), query_blocks = lax.scan(
        back_block, (state_zeros, state_zeros), (indices, log_totals)
    )
    query_grad = query_blocks.reshape(length, heads_here, HEAD_DIM)
    q_grad_low = (
        rotate(query_grad, positions, -1.0).reshape(length, local_width).astype(jnp.bfloat16)
    )
    k_grad_low = rotate(key_grad, positions, -1.0).reshape(length, local_width).astype(jnp.bfloat16)
    v_grad_low = value_grad.reshape(length, local_width).astype(jnp.bfloat16)
    up_joined = jnp.concatenate([q_grad_low, k_grad_low, v_grad_low, up_grad_low], axis=1)
    columns = grad_all
    joined_rows = lax.psum_scatter(
        jnp.concatenate(
            [rows_transposed(columns, down_joined), rows_transposed(normed_all, up_joined)], axis=1
        ),
        "dp",
        scatter_dimension=0,
        tiled=True,
    )
    down_rows = joined_rows[:, : local_width + hidden_here]
    up_rows = joined_rows[:, local_width + hidden_here :]
    d_w_out = down_rows[:, :local_width].T
    d_w_down = down_rows[:, local_width:].T
    d_w_query = up_rows[:, :local_width]
    d_w_key = up_rows[:, local_width : 2 * local_width]
    d_w_value = up_rows[:, 2 * local_width : 3 * local_width]
    d_w_up = up_rows[:, 3 * local_width :]
    pieces = (
        lax.all_gather(w_query, "dp", axis=0, tiled=True),
        lax.all_gather(w_key, "dp", axis=0, tiled=True),
        lax.all_gather(w_value, "dp", axis=0, tiled=True),
        lax.all_gather(w_up, "dp", axis=0, tiled=True),
    )
    part = (
        times_transposed(q_grad_low, pieces[0])
        + times_transposed(k_grad_low, pieces[1])
        + times_transposed(v_grad_low, pieces[2])
        + times_transposed(up_grad_low, pieces[3])
    )
    own_grad = lax.psum_scatter(part, "tensor", scatter_dimension=0, tiled=True)
    scaled_grad = own_grad * ln_gain
    norm_part = inverse * (
        scaled_grad
        - jnp.mean(scaled_grad, axis=-1, keepdims=True)
        - unit_rows * jnp.mean(scaled_grad * unit_rows, axis=-1, keepdims=True)
    )
    cot_float = cotangent.astype(jnp.float32)
    d_input = cot_float + norm_part
    d_ln_gain, d_ln_bias, d_b_out = lax.psum(
        (
            jnp.sum(own_grad * unit_rows, axis=0),
            jnp.sum(own_grad, axis=0),
            jnp.sum(cot_float, axis=0),
        ),
        ("dp", "tensor"),
    )
    d_b_query, d_b_key, d_b_value, d_b_up = lax.psum(
        (
            jnp.sum(q_grad_low.astype(jnp.float32), axis=0),
            jnp.sum(k_grad_low.astype(jnp.float32), axis=0),
            jnp.sum(v_grad_low.astype(jnp.float32), axis=0),
            jnp.sum(up_grad_low.astype(jnp.float32), axis=0),
        ),
        "dp",
    )
    return (
        layer_out,
        d_input,
        d_ln_gain,
        d_ln_bias,
        d_w_query,
        d_b_query,
        d_w_key,
        d_b_key,
        d_w_value,
        d_b_value,
        d_w_out,
        d_b_out,
        d_w_up,
        d_b_up,
        d_w_down,
        d_b_out,
    )


def finish(d_in_ref, d_dn_ref, d_input_ref, layer_ref, bias_ref, all_ref, *refs):
    (layer_out, d_input, d_ln_gain, d_ln_bias, d_wq, d_bq, d_wk, d_bk, d_wv, d_bv, d_wo, d_bo, d_wu, d_bu, d_wd, d_bd) = refs[:16]
    sems, holds = refs[16], refs[17:]
    width, ff = d_wq.shape[1], d_wu.shape[1]
    moves = [
        (d_in_ref.at[:, pl.ds(3 * width, ff)], d_wu),
        (d_dn_ref.at[pl.ds(width, ff), :], d_wd),
        (d_input_ref, d_input),
        (layer_ref, layer_out),
        (d_in_ref.at[:, pl.ds(0, width)], d_wq),
        (d_in_ref.at[:, pl.ds(width, width)], d_wk),
        (d_in_ref.at[:, pl.ds(2 * width, width)], d_wv),
        (d_dn_ref.at[pl.ds(0, width), :], d_wo),
    ]
    loads, stores = [], []
    for (src, dst), hold in zip(moves, holds):
        half = src.shape[0] // 2
        for i in range(2):
            part, k = pl.ds(i * half, half), len(loads)
            loads.append(pltpu.make_async_copy(src.at[part], hold.at[part], sems.at[0, k]))
            stores.append(pltpu.make_async_copy(hold.at[part], dst.at[part], sems.at[1, k]))
    for load in loads:
        load.start()
    rows = d_ln_gain.shape[0] // PIECE
    for i, out in enumerate((d_ln_gain, d_ln_bias, d_bo)):
        for q in range(rows):
            out[pl.ds(q * PIECE, PIECE)] = all_ref[i * rows + q, :]
    for q in range(rows):
        d_bd[pl.ds(q * PIECE, PIECE)] = all_ref[2 * rows + q, :]
    for i, out in enumerate((d_bq, d_bk, d_bv)):
        out[...] = bias_ref[i, :]
    for q in range(ff // PIECE):
        d_bu[pl.ds(q * PIECE, PIECE)] = bias_ref[3 + q, :]
    for load, store in zip(loads, stores):
        load.wait()
        store.start()
    for store in stores:
        store.wait()


def on_device(
    layer_input, ln_gain, ln_bias, w_query, b_query, w_key, b_key, w_value, b_value,
    w_out, b_out, w_up, b_up, w_down, b_down, prefix, cotangent,
):
    n = lax.axis_size("tensor")
    normed, cots, w_qkv, w_up_all, grads, joined, branch = forward_call(
        n, prefix, layer_input, cotangent, w_query, w_key, w_value, w_out, w_up, w_down,
        ln_gain, ln_bias, b_query, b_key, b_value, b_up,
    )
    layer_out, d_input, d_in, d_dn, d_bias, d_all = backward_call(
        n, layer_input, normed, cots, w_qkv, w_up_all, grads, joined, branch, ln_gain, b_out, b_down
    )
    vm, hbm = pl.BlockSpec(memory_space=pltpu.VMEM), pl.BlockSpec(memory_space=pltpu.HBM)
    like = lambda a, t=F32: jax.ShapeDtypeStruct(a.shape, t)
    return pl.pallas_call(
        finish,
        out_shape=(
            like(layer_input, BF), like(layer_input), like(ln_gain), like(ln_bias),
            like(w_query), like(b_query), like(w_key), like(b_key), like(w_value), like(b_value),
            like(w_out), like(b_out), like(w_up), like(b_up), like(w_down), like(b_down),
        ),
        in_specs=[hbm] * 4 + [vm] * 2,
        out_specs=(hbm, hbm, vm, vm, hbm, vm, hbm, vm, hbm, vm, hbm, vm, hbm, vm, hbm, vm),
        scratch_shapes=[pltpu.SemaphoreType.DMA((2, 16))]
        + [
            pltpu.VMEM(a.shape, t)
            for a, t in (
                (w_up, F32), (w_down, F32), (layer_input, F32), (layer_input, BF),
                (w_query, F32), (w_key, F32), (w_value, F32), (w_out, F32),
            )
        ],
        compiler_params=pltpu.CompilerParams(vmem_limit_bytes=63 << 20),
    )(d_in, d_dn, d_input, layer_out, d_bias, d_all)


def solution(mesh):
    fits = mesh.shape["dp"] == 8 and mesh.shape["tensor"] == 4
    return jax.shard_map(
        on_device if fits else plain_on_device,
        mesh=mesh,
        in_specs=(
            P(("dp", "tensor"), None),
            P(),
            P(),
            P("dp", "tensor"),
            P("tensor"),
            P("dp", "tensor"),
            P("tensor"),
            P("dp", "tensor"),
            P("tensor"),
            P("tensor", "dp"),
            P(),
            P("dp", "tensor"),
            P("tensor"),
            P("tensor", "dp"),
            P(),
            P("dp"),
            P(("dp", "tensor"), None),
        ),
        out_specs=(
            P(("dp", "tensor"), None),
            P(("dp", "tensor"), None),
            P(),
            P(),
            P("dp", "tensor"),
            P("tensor"),
            P("dp", "tensor"),
            P("tensor"),
            P("dp", "tensor"),
            P("tensor"),
            P("tensor", "dp"),
            P(),
            P("dp", "tensor"),
            P("tensor"),
            P("tensor", "dp"),
            P(),
        ),
        check_vma=False,
    )
```
